32 devices in a mesh: groups: 2 (over x), section: 2 (over core), tp: 8 (over z, y).
Axes of the slice: x: 2, y: 2, z: 4, core: 2. Of those that a mesh axis runs over, the one named last changes fastest.
Arguments:
- prefill_query: bfloat16 [2, 4096, 8192], P('section', ('groups', 'tp')), parts along dimension 1, may hold values from -5 to 5
- prefill_key: bfloat16 [2, 4096, 1024], P('section', ('groups', 'tp')), parts along dimension 1, may hold values from -5 to 5
- prefill_value: bfloat16 [2, 4096, 1024], P('section', ('groups', 'tp')), parts along dimension 1, may hold values from -4 to 4
- page_counts: int32 [2, 8], P(None, 'groups'), parts along dimension 1, may hold values from 1 to 8, 16 in all within a row
- last_fill: int32 [2, 8], P(None, 'groups'), parts along dimension 1, may hold values from 1 to 128
- dec_query: bfloat16 [2, 4, 8, 8192], P('section', None, 'groups', 'tp'), parts along dimension 2, may hold values from -5 to 5
- dec_key: bfloat16 [2, 4, 8, 1024], P('section', None, 'groups'), parts along dimension 2, may hold values from -5 to 5
- dec_value: bfloat16 [2, 4, 8, 1024], P('section', None, 'groups'), parts along dimension 2, may hold values from -4 to 4
Outputs:
- prefill_out: bfloat16 [2, 4096, 8192], P('section', ('groups', 'tp')), parts along dimension 1
- dec_out: bfloat16 [2, 4, 8, 8192], P('section', None, 'groups', 'tp'), parts along dimension 2
The draws below stay inside these ranges and needn't reach their ends.
There are 2 independent parts, one for each index of `groups`. The reference program is written for one: setup_inputs(seed, part) draws one part's arguments, and reference() takes and returns one part's arrays. A program takes and returns all parts, laid end to end along the dimension named above; each array names one. Nothing has to cross between parts.
Inputs may be any that keep to these rules, and one draw needn't show every extreme that they name: `page_counts`: in each half the page counts of the 4 prompts sum to 16, and some prompt has exactly 8 pages.
All inputs are finite; a program needn't handle non-finite values.
Results may differ from the reference program's by a relative error of at most 0.0036.
Values may be sent and summed in bfloat16 or wider, within the bound.
No kernel may reach another device: no remote copies, remote signals or barrier semaphores. Data moves between devices by JAX's collectives and lax.ppermute only.
A program may use at most 128 MiB of HBM per device.

```python
import math
import jax
import jax.numpy as jnp
import numpy as np
from jax import lax

QH = 64
KVH = 8
HD = 128
PAGE = 128
BACK = 4
STEPS = 4
TOK_DEV = 256
HALVES = 2
TOKENS = 2048
PAGES = 16
MAXP = 8
REQ = 4


def common_rows(key, shape):
    return jnp.clip(jax.random.normal(key, shape, jnp.float32), -4.0, 4.0)


def draw_prefill_key(key, part):
    base = common_rows(key, (HALVES, TOKENS, KVH * HD))
    return base.astype(jnp.bfloat16)


def draw_prefill_query(key, part):
    key = jax.random.fold_in(key, 6)
    first = jax.random.fold_in(key, 0)
    return common_rows(first, (HALVES, TOKENS, QH * HD)).astype(jnp.bfloat16)


def draw_dec_key(key, part):
    base = common_rows(key, (HALVES, STEPS, REQ, KVH * HD))
    return base.astype(jnp.bfloat16)


def draw_dec_query(key, part):
    key = jax.random.fold_in(key, 8)
    first = jax.random.fold_in(key, 0)
    return common_rows(first, (HALVES, STEPS, REQ, QH * HD)).astype(jnp.bfloat16)


def touch_ends(drawn, key, smallest, high):
    place = [jax.random.randint(jax.random.fold_in(key, axis), (), 0, length) for axis, length in enumerate(drawn.shape)]
    longest = drawn.shape.index(max(drawn.shape))
    beside = place[:longest] + [(place[longest] + 1) % drawn.shape[longest]] + place[longest + 1:]
    return drawn.at[tuple(place)].set(smallest).at[tuple(beside)].set(high)


def steps_of(key, dims, pieces, low, top_value):
    def one(dim, shards_of):
        steps = jax.random.uniform(jax.random.fold_in(jax.random.fold_in(key, 6), dim), (shards_of,), jnp.float32, low / len(pieces), top_value / len(pieces))
        return jnp.repeat(jnp.exp(steps), dims[dim] // shards_of).reshape((-1,) + (1,) * (len(dims) - dim - 1))

    factor_of = one(*pieces[0])
    for cut in pieces[1:]:
        factor_of = factor_of * one(*cut)
    return factor_of


def split_up(count, total, reach, lean):
    weights = [(1 << 20) // math.isqrt(rank ** lean) + 1 for rank in range(2, count + 1)]
    rest, given = total - reach - (count - 1), [1] * (count - 1)
    while rest > 0:
        free = [i for i in range(count - 1) if given[i] < reach]
        pool, budget = sum([weights[i] for i in free]), rest
        for i in free:
            extra = min(reach - given[i], max(1, budget * weights[i] // pool), rest)
            given[i] = given[i] + extra
            rest = rest - extra
    return np.array([reach] + given)


def ragged_sizes(rng, count, total, most, lean):
    if count == 2:
        one = jax.random.randint(rng, (), max(1, total - most), min(most, total - 1) + 1)
        return jnp.stack([one, total - one])
    sizes = jnp.asarray(split_up(count, total, most, lean), jnp.int32)
    twos = (count - 1) // 2
    giver, receiver = sizes[1:1 + 2 * twos:2], sizes[2:2 + 2 * twos:2]
    room = jnp.minimum(giver - 1, most - receiver)
    shifted = jax.random.randint(jax.random.fold_in(rng, 1), (twos,), 0, 1 << 20) % (room + 1)
    sizes = sizes.at[1:1 + 2 * twos:2].set(giver - shifted).at[2:2 + 2 * twos:2].set(receiver + shifted)
    return sizes[jax.random.permutation(jax.random.fold_in(rng, 2), count)]


def normal_values(key, shape, scale, reach, shards=(), kind=jnp.bfloat16):
    entries = jax.random.normal(key, shape, jnp.float32) * scale
    if len(shards) > 0:
        entries = steps_of(key, shape, shards, -0.22, 0.18) * entries
    return jnp.clip(entries, min=-reach, max=reach).astype(kind)


def setup_inputs(seed: int = 0, part: int = 0) -> dict:
    streams_of = jax.random.split(jax.random.key(seed), 9)
    part_splits = jax.random.split(jax.random.fold_in(streams_of[8], part), 9)
    return {
        "prefill_query": draw_prefill_query(jax.random.fold_in(jax.random.fold_in(streams_of[8], part), 71), part),
        "prefill_key": draw_prefill_key(jax.random.fold_in(jax.random.fold_in(streams_of[8], part), 71), part),
        "prefill_value": normal_values(part_splits[2], (HALVES, TOKENS, KVH * HD), 1.0, 4.0, ((0, 2), (1, 8))),
        "page_counts": jax.vmap(lambda own: ragged_sizes(own, REQ, PAGES, MAXP, 2))(jax.random.split(part_splits[3], HALVES)).reshape((HALVES, REQ)).astype(jnp.int32),
        "last_fill": touch_ends(jax.random.randint(part_splits[4], (HALVES, REQ), 1, PAGE + 1), jax.random.fold_in(part_splits[4], 1), 1, PAGE).astype(jnp.int32),
        "dec_query": draw_dec_query(jax.random.fold_in(jax.random.fold_in(streams_of[8], part), 71), part),
        "dec_key": draw_dec_key(jax.random.fold_in(jax.random.fold_in(streams_of[8], part), 71), part),
        "dec_value": normal_values(part_splits[7], (HALVES, STEPS, REQ, KVH * HD), 1.0, 4.0, ((0, 2),)),
    }


def layout(counts, fills):
    ends = jnp.cumsum(counts)
    starts = (ends - counts).astype(jnp.int32)
    return starts, (PAGE * (counts - 1) + fills).astype(jnp.int32)


def token_info(starts, lengths, positions):
    page = jnp.floor_divide(positions, PAGE)
    owner = jnp.sum((page[:, None] >= starts[None, :]).astype(jnp.int32), axis=1) - 1
    chosen = owner[:, None] == jnp.arange(starts.shape[0], dtype=jnp.int32)[None, :]
    first = jnp.sum(jnp.where(chosen, starts[None, :], 0), axis=1) * PAGE
    length = jnp.sum(jnp.where(chosen, lengths[None, :], 0), axis=1)
    offset = positions - first
    return owner, offset, offset < length


def softmax_terms(score, allowed):
    masked = jnp.where(allowed, score, -1e30)
    top = jnp.max(masked, axis=-1, keepdims=True)
    terms = jnp.where(allowed, jnp.exp(masked - top), 0.0)
    return terms, jnp.sum(terms, axis=-1)


def rounded(terms):
    return lax.optimization_barrier(terms.astype(jnp.bfloat16)).astype(jnp.float32)


def prefill_half(query, keys, values, counts, fills):
    starts, lengths = layout(counts, fills)
    group = QH // KVH
    width = (BACK + 1) * TOK_DEV
    front = jnp.zeros((BACK * TOK_DEV, KVH * HD), keys.dtype)
    keys_padded = jnp.concatenate([front, keys], axis=0)
    values_padded = jnp.concatenate([front, values], axis=0)

    def block(index):
        base = index * TOK_DEV
        qpos = base + jnp.arange(TOK_DEV, dtype=jnp.int32)
        kpos = base - BACK * TOK_DEV + jnp.arange(width, dtype=jnp.int32)
        qown, qoff, qlive = token_info(starts, lengths, qpos)
        kown, koff, klive = token_info(starts, lengths, kpos)
        allowed = (qown[:, None] == kown[None, :]) & (koff[None, :] <= qoff[:, None]) & klive[None, :] & qlive[:, None]
        rows = lax.dynamic_slice_in_dim(query, base, TOK_DEV, 0).astype(jnp.float32).reshape(TOK_DEV, KVH, group, HD)
        kblock = lax.dynamic_slice_in_dim(keys_padded, base, width, 0).astype(jnp.float32).reshape(width, KVH, HD)
        vblock = lax.dynamic_slice_in_dim(values_padded, base, width, 0).astype(jnp.float32).reshape(width, KVH, HD)
        score = jnp.einsum('tkgd,skd->kgts', rows, kblock) * (HD ** -0.5)
        terms, total = softmax_terms(score, allowed[None, None])
        total = jnp.where(qlive[None, None, :], total, 1.0)
        mixed = jnp.einsum('kgts,skd->tkgd', rounded(terms), vblock)
        mixed = mixed / jnp.transpose(total, (2, 0, 1))[..., None]
        mixed = jnp.where(qlive[:, None, None, None], mixed, 0.0)
        return mixed.reshape(TOK_DEV, QH * HD).astype(jnp.bfloat16)

    out = lax.map(block, jnp.arange(TOKENS // TOK_DEV, dtype=jnp.int32))
    return out.reshape(TOKENS, QH * HD)


def decode_half(query, new_key, new_value, keys, values, counts, fills):
    starts, lengths = layout(counts, fills)
    group = QH // KVH
    span = MAXP * PAGE
    index = jnp.minimum(starts[:, None] + jnp.arange(MAXP, dtype=jnp.int32)[None, :], PAGES - 1)
    pool_keys = keys.reshape(PAGES, PAGE, KVH * HD)[index].reshape(REQ, span, KVH, HD)
    pool_values = values.reshape(PAGES, PAGE, KVH * HD)[index].reshape(REQ, span, KVH, HD)
    fresh_keys = jnp.transpose(new_key.reshape(STEPS, REQ, KVH, HD), (1, 0, 2, 3))
    fresh_values = jnp.transpose(new_value.reshape(STEPS, REQ, KVH, HD), (1, 0, 2, 3))
    all_keys = jnp.concatenate([pool_keys, fresh_keys], axis=1).astype(jnp.float32)
    all_values = jnp.concatenate([pool_values, fresh_values], axis=1).astype(jnp.float32)
    rows = query.astype(jnp.float32).reshape(STEPS, REQ, KVH, group, HD)
    score = jnp.einsum('srkgd,rckd->rkgsc', rows, all_keys) * (HD ** -0.5)
    live = jnp.arange(span, dtype=jnp.int32)[None, :] < lengths[:, None]
    causal = jnp.arange(STEPS)[None, :] <= jnp.arange(STEPS)[:, None]
    allowed = jnp.concatenate([jnp.broadcast_to(live[:, None, :], (REQ, STEPS, span)), jnp.broadcast_to(causal[None], (REQ, STEPS, STEPS))], axis=2)
    terms, total = softmax_terms(score, allowed[:, None, None])
    mixed = jnp.einsum('rkgsc,rckd->srkgd', terms, all_values, precision=lax.Precision.HIGHEST)
    mixed = mixed / jnp.transpose(total, (3, 0, 1, 2))[..., None]
    return mixed.reshape(STEPS, REQ, QH * HD).astype(jnp.bfloat16)


def reference(prefill_query, prefill_key, prefill_value, page_counts, last_fill, dec_query, dec_key, dec_value):
    prefill_out = jnp.stack([prefill_half(prefill_query[h], prefill_key[h], prefill_value[h], page_counts[h], last_fill[h]) for h in range(2)])
    dec_out = jnp.stack([decode_half(dec_query[h], dec_key[h], dec_value[h], prefill_key[1 - h], prefill_value[1 - h], page_counts[1 - h], last_fill[1 - h]) for h in range(2)])
    return prefill_out, dec_out
```

```python
import functools
import math

import jax
import jax.numpy as jnp
from jax import lax
from jax.experimental import pallas as pl
from jax.experimental.pallas import tpu as pltpu
from jax.sharding import PartitionSpec as P

QH = 64
KVH = 8
HD = 128
PAGE = 128
STEPS = 4
GROUP = QH // KVH
SCALE = HD ** (-0.5)
EXP2_SCALE = SCALE * math.log2(math.e)
LOW = -1e30
CHUNKS = 4
HEADS_AT_ONCE = 2
STAT_ROWS = 16


def transposed_dot(a, b):
    return lax.dot_general(a, b, (((1,), (1,)), ((), ())), preferred_element_type=jnp.float32)


def plain_dot(a, b):
    return jnp.dot(a, b, preferred_element_type=jnp.float32)


def page_facts(counts, fills, pages):
    ids = jnp.arange(counts.shape[0], dtype=jnp.int32)
    ends = jnp.sum(jnp.where(ids[None, :] <= ids[:, None], counts[None, :], 0), axis=1)
    starts = ends - counts
    begun = starts[None, :] <= pages[:, None]
    owner = jnp.sum(begun.astype(jnp.int32), axis=1) - 1
    first = jnp.max(jnp.where(begun, starts[None, :], 0), axis=1)
    missing = jnp.where(ends[None, :] - 1 == pages[:, None], PAGE - fills[None, :], 0)
    return owner, first, PAGE - jnp.sum(missing, axis=1)


def prompt_kernel(
    meta, q_ref, ko, vo, ka, va, kb, vb, kc, vc, kd, vd, ke, ve, *rest
):
    o_ref = rest[-1]
    place = meta[0]
    even = place % 2 == 0
    near, far = 2 * place - 2, 2 * place - 6
    page_a = 2 * place - 4
    page_c = jnp.where(even, near, far)
    page_be = jnp.where(even, far, near)
    page_d = 2 * place - 7
    choose = jnp.full((2 * PAGE, HD), even)
    k_be = jnp.where(choose, ke[...], kb[...])
    v_be = jnp.where(choose, ve[...], vb[...])
    ones = jnp.ones((2 * PAGE, HD), jnp.bfloat16)
    lane = lax.broadcasted_iota(jnp.int32, (1, 2 * PAGE), 1)
    row = lax.broadcasted_iota(jnp.int32, (PAGE, PAGE), 0)
    col = lax.broadcasted_iota(jnp.int32, (PAGE, PAGE), 1)
    causal = jnp.where(col <= row, 0.0, LOW)
    shared_keys = [ka[...], kc[...], k_be]
    shared_values = [jnp.concatenate([v, ones], axis=1) for v in (va[...], vc[...], v_be)]
    m_rows = HEADS_AT_ONCE * PAGE

    for i in range(2):
        first, live = meta[1 + 2 * i], meta[2 + 2 * i]

        def off(page):
            return jnp.where(page >= first, 0.0, LOW)

        if i == 0:
            keys_own = jnp.concatenate([kd[...], ko[:PAGE, :]], axis=0)
            values_own = jnp.concatenate([vd[...], vo[:PAGE, :]], axis=0)
            before = off(page_d)
        else:
            keys_own, values_own = ko[...], vo[...]
            before = off(2 * place)
        own_bias = jnp.concatenate(
            [jnp.concatenate([jnp.full((PAGE, PAGE), before), causal], axis=1)] * HEADS_AT_ONCE, axis=0
        )
        keys = [keys_own] + shared_keys
        values = [jnp.concatenate([values_own, ones], axis=1)] + shared_values
        biases = [own_bias] + [
            jnp.where(lane < PAGE, off(p), off(p + 1)) for p in (page_a, page_c, page_be)
        ]
        token = lax.broadcasted_iota(jnp.int32, (m_rows, HD), 0) % PAGE
        for start in range(0, GROUP, HEADS_AT_ONCE):
            heads = range(start, start + HEADS_AT_ONCE)
            q = jnp.concatenate(
                [q_ref[i * PAGE:(i + 1) * PAGE, h * HD:(h + 1) * HD] for h in heads], axis=0
            )
            scores = [transposed_dot(q, k) + b for k, b in zip(keys, biases)]
            top = functools.reduce(jnp.maximum, scores)
            top = jnp.max(top, axis=1, keepdims=True)
            mixed = None
            for s, v in zip(scores, values):
                prob = jnp.exp2((s - top) * EXP2_SCALE).astype(jnp.bfloat16)
                part = plain_dot(prob, v)
                mixed = part if mixed is None else mixed + part
            out = mixed[:, :HD] / mixed[:, HD:]
            out = jnp.where(token < live, out, 0.0).astype(jnp.bfloat16)
            for slot, h in enumerate(heads):
                o_ref[i * PAGE:(i + 1) * PAGE, h * HD:(h + 1) * HD] = out[slot * PAGE:(slot + 1) * PAGE]


def prompt_chunk(chunk, meta, query, key, value, blocks, done):
    tok = query.shape[0]
    n = KVH // CHUNKS
    base = chunk * n
    own = pl.BlockSpec((tok, HD), lambda j, meta: (0, base + j))
    whole_k = pl.BlockSpec((tok, HD), lambda j, meta: (0, j))
    whole_v = pl.BlockSpec((tok, HD), lambda j, meta: (0, n + j))
    late_k = pl.BlockSpec((PAGE, HD), lambda j, meta: (1, j))
    late_v = pl.BlockSpec((PAGE, HD), lambda j, meta: (1, n + j))
    wide = pl.BlockSpec((tok, GROUP * HD), lambda j, meta: (0, base + j))
    a, b, c, d, e = blocks
    operands = [meta, query, key, value, a, a, b, b, c, c, d, d, e, e]
    specs = [wide, own, own] + [whole_k, whole_v] * 3 + [late_k, late_v] + [whole_k, whole_v]
    aliases = {}
    if done is not None:
        aliases = {len(operands): 0}
        operands.append(done)
        specs.append(pl.BlockSpec(memory_space=pl.ANY))
    pairs = n * QH // KVH * tok * 8 * PAGE
    return pl.pallas_call(
        prompt_kernel,
        out_shape=jax.ShapeDtypeStruct(query.shape, jnp.bfloat16),
        grid_spec=pltpu.PrefetchScalarGridSpec(
            num_scalar_prefetch=1, grid=(n,), in_specs=specs, out_specs=wide
        ),
        input_output_aliases=aliases,
        compiler_params=pltpu.CompilerParams(vmem_limit_bytes=48 << 20),
        cost_estimate=pl.CostEstimate(
            flops=pairs * HD * 8, bytes_accessed=4 * n * tok * GROUP * HD, transcendentals=pairs
        ),
        name="prompt_attention",
    )(*operands)


def partial_kernel(meta, q_ref, k_ref, v_ref, o_ref, stat_ref):
    rows = GROUP * STEPS
    lane = lax.broadcasted_iota(jnp.int32, (rows, PAGE), 1)
    spot = lax.broadcasted_iota(jnp.int32, (2 * rows, PAGE), 0)
    across = lax.broadcasted_iota(jnp.int32, (2 * rows, PAGE), 1)
    line = lax.broadcasted_iota(jnp.int32, (STAT_ROWS, PAGE), 0)
    for k in range(KVH):
        sums = []
        for i in range(2):
            live = meta[2 + 2 * i]
            keys = k_ref[i * PAGE:(i + 1) * PAGE, k * HD:(k + 1) * HD]
            values = v_ref[i * PAGE:(i + 1) * PAGE, k * HD:(k + 1) * HD]
            score = transposed_dot(q_ref[k, i * rows:(i + 1) * rows], keys) * SCALE
            score = jnp.where(lane < live, score, LOW)
            top = jnp.max(score, axis=1, keepdims=True)
            terms = jnp.exp(score - top)
            total = jnp.sum(terms, axis=1, keepdims=True)
            high = terms.astype(jnp.bfloat16)
            low = (terms - high.astype(jnp.float32)).astype(jnp.bfloat16)
            mixed = plain_dot(high, values) + plain_dot(low, values)
            o_ref[k, i * rows:(i + 1) * rows] = (mixed / total).astype(jnp.bfloat16)
            sums.append(top + jnp.log(total))
        both = jnp.concatenate(sums, axis=0)
        turned = jnp.sum(jnp.where(spot == across, both, 0.0), axis=0, keepdims=True)
        first = turned.astype(jnp.bfloat16).astype(jnp.float32)
        rest = turned - first
        second = rest.astype(jnp.bfloat16).astype(jnp.float32)
        third = rest - second
        stat = jnp.where(line == 0, first, jnp.where(line == 1, second, jnp.where(line == 2, third, 0.0)))
        stat_ref[k] = stat.astype(jnp.bfloat16)


def partial_decode(meta, query, key, value):
    rows = 2 * GROUP * STEPS
    vmem = pl.BlockSpec(memory_space=pltpu.VMEM)
    return pl.pallas_call(
        partial_kernel,
        out_shape=(
            jax.ShapeDtypeStruct((KVH, rows, HD), jnp.bfloat16),
            jax.ShapeDtypeStruct((KVH, STAT_ROWS, HD), jnp.bfloat16),
        ),
        in_specs=[pl.BlockSpec(memory_space=pltpu.SMEM), vmem, vmem, vmem],
        out_specs=(vmem, vmem),
        compiler_params=pltpu.CompilerParams(vmem_limit_bytes=32 << 20),
        name="partial_decode",
    )(meta, query, key, value)


def other_half(x):
    return lax.ppermute(x, "section", [(0, 1), (1, 0)])


def combined(arrived, query, new_key, new_value, owner, place, lanes):
    requests = query.shape[1]
    here = QH // lanes
    width = 2 * here * STEPS
    head = place * here // GROUP
    fresh_keys = lax.dynamic_slice_in_dim(new_key, head * HD, HD, 2)
    fresh_values = lax.dynamic_slice_in_dim(new_value, head * HD, HD, 2).astype(jnp.float32)
    score = jnp.einsum(
        "srhd,urd->rhsu",
        query.reshape(STEPS, requests, here, HD),
        fresh_keys,
        preferred_element_type=jnp.float32,
    ) * SCALE
    causal = jnp.arange(STEPS)[None, :] <= jnp.arange(STEPS)[:, None]
    score = jnp.where(causal, score, LOW)
    parts = arrived[:, :width].astype(jnp.float32).reshape(2 * lanes, here, STEPS, HD)
    stats = jnp.sum(arrived[:, width:width + 3, :width].astype(jnp.float32), axis=1)
    stats = stats.reshape(2 * lanes, here, STEPS)
    mine = owner[None, :] == jnp.arange(requests, dtype=jnp.int32)[:, None]
    held = jnp.where(mine[:, :, None, None], stats[None], LOW)
    top = jnp.maximum(jnp.max(held, axis=1), jnp.max(score, axis=3))
    weight = jnp.exp(held - top[:, None])
    terms = jnp.exp(score - top[..., None])
    total = jnp.sum(weight, axis=1) + jnp.sum(terms, axis=3)
    mixed = jnp.sum(weight[..., None] * parts[None], axis=1)
    mixed = mixed + jnp.sum(
        terms[..., None] * jnp.transpose(fresh_values, (1, 0, 2))[:, None, None], axis=3
    )
    mixed = mixed / total[..., None]
    mixed = jnp.transpose(mixed, (2, 0, 1, 3))
    return mixed.reshape(STEPS, requests, here * HD).astype(jnp.bfloat16)


def on_device(
    prefill_query, prefill_key, prefill_value, page_counts, last_fill, dec_query, dec_key, dec_value
):
    half = lax.axis_index("section")
    place = lax.axis_index("tp")
    lanes = lax.axis_size("tp")
    here = QH // lanes
    requests = page_counts.shape[1]
    query, key, value = prefill_query[0], prefill_key[0], prefill_value[0]

    counts = lax.dynamic_index_in_dim(page_counts, half, 0, keepdims=False)
    fills = lax.dynamic_index_in_dim(last_fill, half, 0, keepdims=False)
    owner, first, live = page_facts(counts, fills, 2 * place + jnp.arange(2, dtype=jnp.int32))
    meta = jnp.stack([place, first[0], live[0], first[1], live[1]]).astype(jnp.int32)
    other_counts = lax.dynamic_index_in_dim(page_counts, 1 - half, 0, keepdims=False)
    other_fills = lax.dynamic_index_in_dim(last_fill, 1 - half, 0, keepdims=False)
    other_owner, _, _ = page_facts(
        other_counts, other_fills, jnp.arange(2 * lanes, dtype=jnp.int32)
    )

    wanted = lax.all_gather(other_half(dec_query[0]), "tp")
    picked = jnp.stack(
        [lax.dynamic_index_in_dim(wanted, owner[i], 2, keepdims=False) for i in range(2)], axis=0
    )
    picked = picked.reshape(2, lanes, STEPS, here, HD)
    picked = jnp.transpose(picked, (1, 3, 0, 2, 4)).reshape(KVH, GROUP, 2, STEPS, HD)
    picked = jnp.transpose(picked, (0, 2, 1, 3, 4)).reshape(KVH, 2 * GROUP * STEPS, HD)
    parts, stats = partial_decode(meta, picked, key, value)
    split = GROUP // here
    parts = jnp.transpose(
        parts.reshape(KVH, 2, split, here * STEPS, HD), (0, 2, 1, 3, 4)
    ).reshape(lanes, 2 * here * STEPS, HD)
    stats = stats[:, :, : 2 * GROUP * STEPS].reshape(KVH, STAT_ROWS, 2, split, here * STEPS)
    stats = jnp.transpose(stats, (0, 3, 1, 2, 4)).reshape(lanes, STAT_ROWS, 2 * here * STEPS)
    stats = jnp.pad(stats, ((0, 0), (0, 0), (0, HD - 2 * here * STEPS)))
    packed = jnp.concatenate([parts, stats], axis=1)
    arrived = lax.all_to_all(packed, "tp", split_axis=0, concat_axis=0, tiled=True)
    arrived = other_half(arrived)
    dec_out = combined(
        arrived, dec_query[0], dec_key[0], dec_value[0], other_owner, place, lanes
    )

    n = KVH // CHUNKS * HD
    ahead = [(i, i + 2) for i in range(lanes - 2)]
    ahead_again = [(i, i + 2) for i in range(2, lanes - 2)]
    beside = [(i, i + 1) for i in range(0, lanes, 2)]
    trade = [(i, i ^ 1) for i in range(2, lanes)]
    back = [(i, i - 1) for i in range(5, lanes, 2)]
    mine = [
        jnp.concatenate([key[:, g * n:(g + 1) * n], value[:, g * n:(g + 1) * n]], axis=1)
        for g in range(CHUNKS)
    ]
    out = None
    for g in range(CHUNKS):
        a = lax.ppermute(mine[g], "tp", ahead)
        b = lax.ppermute(mine[g], "tp", beside)
        c = lax.ppermute(a, "tp", trade)
        d = lax.ppermute(a, "tp", ahead_again)
        e = lax.ppermute(d, "tp", back)
        out = prompt_chunk(g, meta, query, key, value, (a, b, c, d, e), out)
    return (out[None], dec_out[None])


def solution(mesh):
    placed = (
        P("section", ("groups", "tp"), None),
        P("section", ("groups", "tp"), None),
        P("section", ("groups", "tp"), None),
        P(None, "groups"),
        P(None, "groups"),
        P("section", None, "groups", "tp"),
        P("section", None, "groups", None),
        P("section", None, "groups", None),
    )
    return jax.shard_map(
        on_device,
        mesh=mesh,
        in_specs=placed,
        out_specs=(P("section", ("groups", "tp"), None), P("section", None, "groups", "tp")),
        check_vma=False,
    )
```

```python
import functools
import math

import jax
import jax.numpy as jnp
from jax import lax
from jax.experimental import pallas as pl
from jax.experimental.pallas import tpu as pltpu
from jax.sharding import PartitionSpec as P

QH = 64
KVH = 8
HD = 128
PAGE = 128
STEPS = 4
GROUP = QH // KVH
SCALE = HD ** (-0.5)
EXP2_SCALE = SCALE * math.log2(math.e)
LOW = -1e30
CHUNKS = (3, 3, 2)
ROWS = 512
STAT_ROWS = 16


def transposed_dot(a, b):
    return lax.dot_general(a, b, (((1,), (1,)), ((), ())), preferred_element_type=jnp.float32)


def plain_dot(a, b):
    return jnp.dot(a, b, preferred_element_type=jnp.float32)


def page_facts(counts, fills, pages):
    ids = jnp.arange(counts.shape[0], dtype=jnp.int32)
    ends = jnp.sum(jnp.where(ids[None, :] <= ids[:, None], counts[None, :], 0), axis=1)
    starts = ends - counts
    begun = starts[None, :] <= pages[:, None]
    owner = jnp.sum(begun.astype(jnp.int32), axis=1) - 1
    first = jnp.max(jnp.where(begun, starts[None, :], 0), axis=1)
    missing = jnp.where(ends[None, :] - 1 == pages[:, None], PAGE - fills[None, :], 0)
    return owner, first, PAGE - jnp.sum(missing, axis=1)


def prompt_kernel(
    meta, q_ref, ko, vo, ka, va, kb, vb, kc, vc, kd, vd, ke, ve, *rest
):
    o_ref = rest[-1]
    place = meta[0]
    even = place % 2 == 0
    near, far = 2 * place - 2, 2 * place - 6
    page_a = 2 * place - 4
    page_c = jnp.where(even, near, far)
    page_be = jnp.where(even, far, near)
    choose = jnp.full((2 * PAGE, HD), even)
    k_be = jnp.where(choose, ke[...], kb[...])
    v_be = jnp.where(choose, ve[...], vb[...])
    row = lax.broadcasted_iota(jnp.int32, (PAGE, PAGE), 0)
    col = lax.broadcasted_iota(jnp.int32, (PAGE, PAGE), 1)
    heads_at_once = ROWS // PAGE
    causal = jnp.concatenate([jnp.where(col <= row, 0.0, LOW)] * heads_at_once, axis=0)
    token = lax.broadcasted_iota(jnp.int32, (ROWS, HD), 0) % PAGE
    one = jnp.ones((PAGE, HD), jnp.bfloat16)
    zero = jnp.zeros((PAGE, HD), jnp.bfloat16)

    def window(i):
        first = meta[1 + 2 * i]
        own = slice(i * PAGE, (i + 1) * PAGE)
        stand_in = jnp.broadcast_to(ko[i * PAGE:i * PAGE + 1, :], (PAGE, HD))

        def page(k, v, number):
            seen = jnp.full((PAGE, HD), number >= first)
            k = jnp.where(seen, k, stand_in)
            v = jnp.where(seen, v, zero)
            return jnp.concatenate([k, k], axis=1), jnp.concatenate([v, jnp.where(seen, one, zero)], axis=1)

        if i == 0:
            pages = [page(kd[...], vd[...], 2 * place - 7)]
        else:
            pages = [page(ko[:PAGE, :], vo[:PAGE, :], 2 * place)]
        k, v = ko[own, :], vo[own, :]
        pages.append((jnp.concatenate([k, k], axis=1), jnp.concatenate([v, one], axis=1)))
        for k, v, number in ((ka, va, page_a), (kc, vc, page_c)):
            pages.append(page(k[:PAGE, :], v[:PAGE, :], number))
            pages.append(page(k[PAGE:, :], v[PAGE:, :], number + 1))
        pages.append(page(k_be[:PAGE, :], v_be[:PAGE, :], page_be))
        pages.append(page(k_be[PAGE:, :], v_be[PAGE:, :], page_be + 1))
        tiles = range(0, len(pages), 2)
        return (
            [jnp.concatenate([pages[t][0], pages[t + 1][0]], axis=0) for t in tiles],
            [jnp.concatenate([pages[t][1], pages[t + 1][1]], axis=0) for t in tiles],
        )

    windows = [window(0), window(1)]

    def scores(i, start):
        q = jnp.concatenate(
            [
                q_ref[i * PAGE:(i + 1) * PAGE, h * HD:(h + 1) * HD]
                for h in range(start, start + heads_at_once)
            ],
            axis=0,
        ).astype(jnp.float32) * EXP2_SCALE
        high = q.astype(jnp.bfloat16)
        low = (q - high.astype(jnp.float32)).astype(jnp.bfloat16)
        both = jnp.concatenate([high, low], axis=1)
        tiles = [transposed_dot(both, k) for k in windows[i][0]]
        tiles[0] = jnp.concatenate([tiles[0][:, :PAGE], tiles[0][:, PAGE:] + causal], axis=1)
        return tiles

    def finish(i, start, tiles):
        live = meta[2 + 2 * i]
        top = jnp.max(functools.reduce(jnp.maximum, tiles), axis=1, keepdims=True)
        mixed = None
        for s, v in zip(tiles, windows[i][1]):
            part = plain_dot(jnp.exp2(s - top).astype(jnp.bfloat16), v)
            mixed = part if mixed is None else mixed + part
        out = mixed[:, :HD] / mixed[:, HD:]
        out = jnp.where(token < live, out, 0.0).astype(jnp.bfloat16)
        for slot in range(heads_at_once):
            h = start + slot
            o_ref[i * PAGE:(i + 1) * PAGE, h * HD:(h + 1) * HD] = out[slot * PAGE:(slot + 1) * PAGE]

    blocks = [(i, start) for i in range(2) for start in range(0, GROUP, heads_at_once)]
    ready = scores(*blocks[0])
    for index, block in enumerate(blocks):
        following = scores(*blocks[index + 1]) if index + 1 < len(blocks) else None
        finish(*block, ready)
        ready = following


def prompt_chunk(base, n, meta, query, key, value, blocks, done):
    tok = query.shape[0]
    own = pl.BlockSpec((tok, HD), lambda j, meta: (0, base + j))
    later = pl.BlockSpec((tok, HD), lambda j, meta: (0, KVH + base + j))
    part_k = pl.BlockSpec((tok, HD), lambda j, meta: (0, j))
    part_v = pl.BlockSpec((tok, HD), lambda j, meta: (0, n + j))
    late_k = pl.BlockSpec((PAGE, HD), lambda j, meta: (1, j))
    late_v = pl.BlockSpec((PAGE, HD), lambda j, meta: (1, n + j))
    wide = pl.BlockSpec((tok, GROUP * HD), lambda j, meta: (0, base + j))
    a, b, c, d, e = blocks
    operands = [meta, query, key, value, a, a, b, b, c, c, d, d, e, e]
    specs = [wide, own, own, part_k, part_v, own, later]
    specs += [part_k, part_v, late_k, late_v, part_k, part_v]
    aliases = {}
    if done is not None:
        aliases = {len(operands): 0}
        operands.append(done)
        specs.append(pl.BlockSpec(memory_space=pl.ANY))
    return pl.pallas_call(
        prompt_kernel,
        out_shape=jax.ShapeDtypeStruct(query.shape, jnp.bfloat16),
        grid_spec=pltpu.PrefetchScalarGridSpec(
            num_scalar_prefetch=1, grid=(n,), in_specs=specs, out_specs=wide
        ),
        input_output_aliases=aliases,
        compiler_params=pltpu.CompilerParams(vmem_limit_bytes=48 << 20),
        cost_estimate=pl.CostEstimate(
            flops=1, bytes_accessed=1, transcendentals=0
        ),
        name="prompt_attention",
    )(*operands)


def partial_kernel(meta, q_ref, k_ref, v_ref, o_ref, stat_ref):
    rows = GROUP * STEPS
    lane = lax.broadcasted_iota(jnp.int32, (rows, PAGE), 1)
    spot = lax.broadcasted_iota(jnp.int32, (2 * rows, PAGE), 0)
    across = lax.broadcasted_iota(jnp.int32, (2 * rows, PAGE), 1)
    line = lax.broadcasted_iota(jnp.int32, (STAT_ROWS, PAGE), 0)
    for k in range(KVH):
        sums = []
        for i in range(2):
            live = meta[2 + 2 * i]
            keys = k_ref[i * PAGE:(i + 1) * PAGE, k * HD:(k + 1) * HD]
            values = v_ref[i * PAGE:(i + 1) * PAGE, k * HD:(k + 1) * HD]
            score = transposed_dot(q_ref[k, i * rows:(i + 1) * rows], keys) * SCALE
            score = jnp.where(lane < live, score, LOW)
            top = jnp.max(score, axis=1, keepdims=True)
            terms = jnp.exp(score - top)
            total = jnp.sum(terms, axis=1, keepdims=True)
            high = terms.astype(jnp.bfloat16)
            low = (terms - high.astype(jnp.float32)).astype(jnp.bfloat16)
            mixed = plain_dot(high, values) + plain_dot(low, values)
            o_ref[k, i * rows:(i + 1) * rows] = (mixed / total).astype(jnp.bfloat16)
            sums.append(top + jnp.log(total))
        both = jnp.concatenate(sums, axis=0)
        turned = jnp.sum(jnp.where(spot == across, both, 0.0), axis=0, keepdims=True)
        first = turned.astype(jnp.bfloat16).astype(jnp.float32)
        rest = turned - first
        second = rest.astype(jnp.bfloat16).astype(jnp.float32)
        third = rest - second
        stat = jnp.where(line == 0, first, jnp.where(line == 1, second, jnp.where(line == 2, third, 0.0)))
        stat_ref[k] = stat.astype(jnp.bfloat16)


def partial_decode(meta, query, key, value):
    rows = 2 * GROUP * STEPS
    vmem = pl.BlockSpec(memory_space=pltpu.VMEM)
    return pl.pallas_call(
        partial_kernel,
        out_shape=(
            jax.ShapeDtypeStruct((KVH, rows, HD), jnp.bfloat16),
            jax.ShapeDtypeStruct((KVH, STAT_ROWS, HD), jnp.bfloat16),
        ),
        in_specs=[pl.BlockSpec(memory_space=pltpu.SMEM), vmem, vmem, vmem],
        out_specs=(vmem, vmem),
        compiler_params=pltpu.CompilerParams(vmem_limit_bytes=32 << 20),
        cost_estimate=pl.CostEstimate(flops=1, bytes_accessed=1, transcendentals=0),
        name="partial_decode",
    )(meta, query, key, value)


def other_half(x):
    return lax.ppermute(x, "section", [(0, 1), (1, 0)])


def combined(arrived, query, new_key, new_value, owner, place, lanes):
    requests = query.shape[1]
    here = QH // lanes
    width = 2 * here * STEPS
    head = place * here // GROUP
    fresh_keys = lax.dynamic_slice_in_dim(new_key, head * HD, HD, 2)
    fresh_values = lax.dynamic_slice_in_dim(new_value, head * HD, HD, 2).astype(jnp.float32)
    score = jnp.einsum(
        "srhd,urd->rhsu",
        query.reshape(STEPS, requests, here, HD),
        fresh_keys,
        preferred_element_type=jnp.float32,
    ) * SCALE
    causal = jnp.arange(STEPS)[None, :] <= jnp.arange(STEPS)[:, None]
    score = jnp.where(causal, score, LOW)
    parts = arrived[:, :width].astype(jnp.float32).reshape(2 * lanes, here, STEPS, HD)
    stats = jnp.sum(arrived[:, width:width + 3, :width].astype(jnp.float32), axis=1)
    stats = stats.reshape(2 * lanes, here, STEPS)
    mine = owner[None, :] == jnp.arange(requests, dtype=jnp.int32)[:, None]
    held = jnp.where(mine[:, :, None, None], stats[None], LOW)
    top = jnp.maximum(jnp.max(held, axis=1), jnp.max(score, axis=3))
    weight = jnp.exp(held - top[:, None])
    terms = jnp.exp(score - top[..., None])
    total = jnp.sum(weight, axis=1) + jnp.sum(terms, axis=3)
    mixed = jnp.sum(weight[..., None] * parts[None], axis=1)
    mixed = mixed + jnp.sum(
        terms[..., None] * jnp.transpose(fresh_values, (1, 0, 2))[:, None, None], axis=3
    )
    mixed = mixed / total[..., None]
    mixed = jnp.transpose(mixed, (2, 0, 1, 3))
    return mixed.reshape(STEPS, requests, here * HD).astype(jnp.bfloat16)


def on_device(
    prefill_query, prefill_key, prefill_value, page_counts, last_fill, dec_query, dec_key, dec_value
):
    half = lax.axis_index("section")
    place = lax.axis_index("tp")
    lanes = lax.axis_size("tp")
    here = QH // lanes
    requests = page_counts.shape[1]
    query, key, value = prefill_query[0], prefill_key[0], prefill_value[0]

    counts = lax.dynamic_index_in_dim(page_counts, half, 0, keepdims=False)
    fills = lax.dynamic_index_in_dim(last_fill, half, 0, keepdims=False)
    owner, first, live = page_facts(counts, fills, 2 * place + jnp.arange(2, dtype=jnp.int32))
    meta = jnp.stack([place, first[0], live[0], first[1], live[1]]).astype(jnp.int32)
    other_counts = lax.dynamic_index_in_dim(page_counts, 1 - half, 0, keepdims=False)
    other_fills = lax.dynamic_index_in_dim(last_fill, 1 - half, 0, keepdims=False)
    other_owner, _, _ = page_facts(
        other_counts, other_fills, jnp.arange(2 * lanes, dtype=jnp.int32)
    )

    ahead = [(i, i + 2) for i in range(lanes - 2)]
    ahead_again = [(i, i + 2) for i in range(2, lanes - 2)]
    beside = [(i, i + 1) for i in range(0, lanes, 2)]
    trade = [(i, i ^ 1) for i in range(2, lanes)]
    back = [(i, i - 1) for i in range(5, lanes, 2)]
    asked = other_half(dec_query[0])
    bases = [sum(CHUNKS[:g]) for g in range(len(CHUNKS))]
    received = []
    for base, n in zip(bases, CHUNKS):
        columns = slice(base * HD, (base + n) * HD)
        mine = jnp.concatenate([key[:, columns], value[:, columns]], axis=1)
        a = lax.ppermute(mine, "tp", ahead)
        c = lax.ppermute(a, "tp", trade)
        d = lax.ppermute(a, "tp", ahead_again)
        e = lax.ppermute(d, "tp", back)
        received.append((a, c, d, e))
    b = lax.ppermute(jnp.concatenate([key, value], axis=1), "tp", beside)

    wanted = lax.all_gather(asked, "tp")
    wanted, _ = lax.optimization_barrier((wanted, received[0][0]))
    picked = jnp.stack(
        [lax.dynamic_index_in_dim(wanted, owner[i], 2, keepdims=False) for i in range(2)], axis=0
    )
    picked = picked.reshape(2, lanes, STEPS, here, HD)
    picked = jnp.transpose(picked, (1, 3, 0, 2, 4)).reshape(KVH, GROUP, 2, STEPS, HD)
    picked = jnp.transpose(picked, (0, 2, 1, 3, 4)).reshape(KVH, 2 * GROUP * STEPS, HD)
    parts, stats = partial_decode(meta, picked, key, value)
    split = GROUP // here
    parts = jnp.transpose(
        parts.reshape(KVH, 2, split, here * STEPS, HD), (0, 2, 1, 3, 4)
    ).reshape(lanes, 2 * here * STEPS, HD)
    stats = stats[:, :, : 2 * GROUP * STEPS].reshape(KVH, STAT_ROWS, 2, split, here * STEPS)
    stats = jnp.transpose(stats, (0, 3, 1, 2, 4)).reshape(lanes, STAT_ROWS, 2 * here * STEPS)
    stats = jnp.pad(stats, ((0, 0), (0, 0), (0, HD - 2 * here * STEPS)))
    packed = jnp.concatenate([parts, stats], axis=1)
    arrived = lax.all_to_all(packed, "tp", split_axis=0, concat_axis=0, tiled=True)
    arrived = other_half(arrived)

    out = None
    for base, n, (a, c, d, e) in zip(bases, CHUNKS, received):
        out = prompt_chunk(base, n, meta, query, key, value, (a, b, c, d, e), out)
        if base == 0:
            arrived, _ = lax.optimization_barrier((arrived, c))
    dec_out = combined(
        arrived, dec_query[0], dec_key[0], dec_value[0], other_owner, place, lanes
    )
    return (out[None], dec_out[None])


def solution(mesh):
    placed = (
        P("section", ("groups", "tp"), None),
        P("section", ("groups", "tp"), None),
        P("section", ("groups", "tp"), None),
        P(None, "groups"),
        P(None, "groups"),
        P("section", None, "groups", "tp"),
        P("section", None, "groups", None),
        P("section", None, "groups", None),
    )
    return jax.shard_map(
        on_device,
        mesh=mesh,
        in_specs=placed,
        out_specs=(P("section", ("groups", "tp"), None), P("section", None, "groups", "tp")),
        check_vma=False,
    )
```

```python
import functools
import math

import jax
import jax.numpy as jnp
from jax import lax
from jax.experimental import pallas as pl
from jax.experimental.pallas import tpu as pltpu
from jax.sharding import PartitionSpec as P

QH = 64
KVH = 8
HD = 128
PAGE = 128
MAXP = 8
STEPS = 4
GROUP = QH // KVH
SCALE = HD ** (-0.5)
EXP2_SCALE = SCALE * math.log2(math.e)
LOW = -1e30
CHUNKS = (4, 4)
ROWS = 512
SMEM = pl.BlockSpec(memory_space=pltpu.SMEM)
VMEM = pl.BlockSpec(memory_space=pltpu.VMEM)


def dot(a, b):
    return jnp.dot(a, b, preferred_element_type=jnp.float32)


def transposed_dot(a, b):
    return lax.dot_general(a, b, (((1,), (1,)), ((), ())), preferred_element_type=jnp.float32)


def page_facts(counts, fills, half, page):
    owner, first, live, end = -1, 0, PAGE, 0
    for r in range(counts.shape[1]):
        start, end = end, end + counts[half, r]
        begun = start <= page
        owner = jnp.where(begun, r, owner)
        first = jnp.where(begun, start, first)
        live = jnp.where(end - 1 == page, fills[half, r], live)
    return owner, first, live


def pack_kernel(k_ref, v_ref, *outs):
    whole = outs[-1]
    base = 0
    for n, out in zip(CHUNKS, outs):
        for j in range(n):
            h = base + j
            for p in range(2):
                rows, columns = slice(p * PAGE, (p + 1) * PAGE), slice(h * HD, (h + 1) * HD)
                turned = jnp.transpose(k_ref[rows, columns].astype(jnp.float32)).astype(jnp.bfloat16)
                value = v_ref[rows, columns]
                out[j * HD:(j + 1) * HD, rows] = turned
                out[(n + j) * HD:(n + j + 1) * HD, rows] = value
                whole[h * HD:(h + 1) * HD, rows] = turned
                whole[(KVH + h) * HD:(KVH + h + 1) * HD, rows] = value
        base += n


def pack(key, value):
    tok = key.shape[0]
    shapes = [jax.ShapeDtypeStruct((2 * n * HD, tok), jnp.bfloat16) for n in (*CHUNKS, KVH)]
    return pl.pallas_call(
        pack_kernel,
        out_shape=shapes,
        in_specs=[VMEM, VMEM],
        out_specs=[VMEM] * len(shapes),
        compiler_params=pltpu.CompilerParams(vmem_limit_bytes=32 << 20),
        cost_estimate=pl.CostEstimate(flops=1, bytes_accessed=1, transcendentals=0),
        name="pack",
    )(key, value)


def prompt_kernel(counts, fills, q_ref, ko, vo, ka, va, kb, vb, kc, vc, kd, vd, ke, ve, *rest):
    o_ref = rest[-1]
    half, place = lax.axis_index("section"), lax.axis_index("tp")
    even = place % 2 == 0
    near, far = 2 * place - 2, 2 * place - 6
    page_a = 2 * place - 4
    page_c = jnp.where(even, near, far)
    page_be = jnp.where(even, far, near)
    choose = jnp.full((HD, PAGE), even)
    one_page, other_page = slice(0, PAGE), slice(PAGE, 2 * PAGE)
    k_be = [jnp.where(choose, kd[:, other_page], kb[:, one_page]), jnp.where(choose, ke[...], kb[:, other_page])]
    v_be = [jnp.where(choose, vd[:, other_page], vb[:, one_page]), jnp.where(choose, ve[...], vb[:, other_page])]
    row = lax.broadcasted_iota(jnp.int32, (PAGE, PAGE), 0)
    col = lax.broadcasted_iota(jnp.int32, (PAGE, PAGE), 1)
    heads_at_once = ROWS // PAGE
    causal = jnp.concatenate([jnp.where(col <= row, 0.0, LOW)] * heads_at_once, axis=0)
    token = lax.broadcasted_iota(jnp.int32, (ROWS, HD), 0) % PAGE
    one = jnp.ones((PAGE, HD), jnp.bfloat16)
    zero = jnp.zeros((PAGE, HD), jnp.bfloat16)
    facts = [page_facts(counts, fills, half, 2 * place + i) for i in range(2)]

    def window(i):
        first = facts[i][1]
        own = slice(i * PAGE, (i + 1) * PAGE)
        stand_in = jnp.broadcast_to(ko[:, i * PAGE:i * PAGE + 1], (HD, PAGE))

        def page(k, v, number):
            seen = jnp.full((PAGE, HD), number >= first)
            return jnp.where(seen, k, stand_in), jnp.concatenate(
                [jnp.where(seen, v, zero), jnp.where(seen, one, zero)], axis=1
            )

        if i == 0:
            pages = [page(kd[:, one_page], vd[:, one_page], 2 * place - 7)]
        else:
            pages = [page(ko[:, one_page], vo[:, one_page], 2 * place)]
        pages.append((ko[:, own], jnp.concatenate([vo[:, own], one], axis=1)))
        for k, v, number in ((ka, va, page_a), (kc, vc, page_c)):
            pages.append(page(k[:, one_page], v[:, one_page], number))
            pages.append(page(k[:, other_page], v[:, other_page], number + 1))
        pages.append(page(k_be[0], v_be[0], page_be))
        pages.append(page(k_be[1], v_be[1], page_be + 1))
        keys, values = [], []
        for t in range(0, len(pages), 2):
            both = jnp.concatenate([pages[t][0], pages[t + 1][0]], axis=1)
            keys.append(jnp.concatenate([both, both], axis=0))
            values.append(jnp.concatenate([pages[t][1], pages[t + 1][1]], axis=0))
        return keys, values

    windows = [window(0), window(1)]

    def scores(i, start):
        q = jnp.concatenate(
            [
                q_ref[i * PAGE:(i + 1) * PAGE, h * HD:(h + 1) * HD]
                for h in range(start, start + heads_at_once)
            ],
            axis=0,
        ).astype(jnp.float32) * EXP2_SCALE
        high = q.astype(jnp.bfloat16)
        low = (q - high.astype(jnp.float32)).astype(jnp.bfloat16)
        both = jnp.concatenate([high, low], axis=1)
        tiles = [dot(both, k) for k in windows[i][0]]
        tiles[0] = jnp.concatenate([tiles[0][:, :PAGE], tiles[0][:, PAGE:] + causal], axis=1)
        return tiles

    def finish(i, start, tiles):
        live = facts[i][2]
        top = jnp.max(functools.reduce(jnp.maximum, tiles), axis=1, keepdims=True)
        mixed = None
        for s, v in zip(tiles, windows[i][1]):
            part = dot(jnp.exp2(s - top).astype(jnp.bfloat16), v)
            mixed = part if mixed is None else mixed + part
        out = mixed[:, :HD] / mixed[:, HD:]
        out = jnp.where(token < live, out, 0.0).astype(jnp.bfloat16)
        for slot in range(heads_at_once):
            h = start + slot
            o_ref[i * PAGE:(i + 1) * PAGE, h * HD:(h + 1) * HD] = out[slot * PAGE:(slot + 1) * PAGE]

    blocks = [(i, start) for i in range(2) for start in range(0, GROUP, heads_at_once)]
    ready = scores(*blocks[0])
    for index, block in enumerate(blocks):
        following = scores(*blocks[index + 1]) if index + 1 < len(blocks) else None
        finish(*block, ready)
        ready = following


def prompt_heads(base, n, low, high, counts, fills, query, blocks, done):
    tok = query.shape[0]

    def block(first, width=tok):
        return pl.BlockSpec((HD, width), lambda j, *_: (first + low + j, 0))

    wide = pl.BlockSpec((tok, GROUP * HD), lambda j, *_: (0, base + low + j))
    mine, a, b, c, d, e = blocks
    operands = [counts, fills, query, mine, mine, a, a, b, b, c, c, d, d, e, e]
    specs = [wide, block(0), block(n), block(0), block(n), block(base), block(KVH + base)]
    specs += [block(0), block(n), block(0), block(n), block(0, PAGE), block(n, PAGE)]
    aliases = {}
    if done is not None:
        aliases = {len(operands): 0}
        operands.append(done)
        specs.append(pl.BlockSpec(memory_space=pl.ANY))
    return pl.pallas_call(
        prompt_kernel,
        out_shape=jax.ShapeDtypeStruct(query.shape, jnp.bfloat16),
        grid_spec=pltpu.PrefetchScalarGridSpec(
            num_scalar_prefetch=2, grid=(high - low,), in_specs=specs, out_specs=wide
        ),
        input_output_aliases=aliases,
        compiler_params=pltpu.CompilerParams(vmem_limit_bytes=48 << 20),
        cost_estimate=pl.CostEstimate(flops=1, bytes_accessed=1, transcendentals=0),
        name="prompt_attention",
    )(*operands)


def stat_rows(rows):
    return 16 - rows % 16


def partial_kernel(lanes, counts, fills, q_ref, k_ref, v_ref, o_ref):
    here = QH // lanes
    split = GROUP // here
    width = here * STEPS
    extra = stat_rows(2 * width)
    half, place = lax.axis_index("section"), lax.axis_index("tp")
    lane = lax.broadcasted_iota(jnp.int32, (GROUP * STEPS, PAGE), 1)
    spot = lax.broadcasted_iota(jnp.int32, (2 * width, PAGE), 0)
    across = lax.broadcasted_iota(jnp.int32, (2 * width, PAGE), 1)
    line = lax.broadcasted_iota(jnp.int32, (extra, PAGE), 0)
    facts = [page_facts(counts, fills, half, 2 * place + i) for i in range(2)]
    for k in range(KVH):
        mixed, sums = [], []
        for i in range(2):
            owner, _, live = facts[i]
            query = [q_ref[owner, place ^ (k * split + t)] for t in range(split)]
            query = jnp.concatenate(query, axis=0) if split > 1 else query[0]
            keys = k_ref[i * PAGE:(i + 1) * PAGE, k * HD:(k + 1) * HD]
            values = v_ref[i * PAGE:(i + 1) * PAGE, k * HD:(k + 1) * HD]
            score = transposed_dot(query, keys) * SCALE
            score = jnp.where(lane < live, score, LOW)
            top = jnp.max(score, axis=1, keepdims=True)
            terms = jnp.exp(score - top)
            total = jnp.sum(terms, axis=1, keepdims=True)
            high = terms.astype(jnp.bfloat16)
            low = (terms - high.astype(jnp.float32)).astype(jnp.bfloat16)
            mixed.append((dot(high, values) + dot(low, values)) / total)
            sums.append(top + jnp.log(total))
        for t in range(split):
            rows = slice(t * width, (t + 1) * width)
            both = jnp.concatenate([sums[0][rows], sums[1][rows]], axis=0)
            turned = jnp.sum(jnp.where(spot == across, both, 0.0), axis=0, keepdims=True)
            first = turned.astype(jnp.bfloat16).astype(jnp.float32)
            rest = turned - first
            second = rest.astype(jnp.bfloat16).astype(jnp.float32)
            stat = jnp.where(line == 0, first, jnp.where(line == 1, second, rest - second))
            stat = jnp.where(line < 3, stat, 0.0)
            block = jnp.concatenate([mixed[0][rows], mixed[1][rows], stat], axis=0)
            o_ref[place ^ (k * split + t)] = block.astype(jnp.bfloat16)


def partial_decode(counts, fills, query, key, value, lanes):
    rows = 2 * (QH // lanes) * STEPS
    return pl.pallas_call(
        functools.partial(partial_kernel, lanes),
        out_shape=jax.ShapeDtypeStruct((lanes, rows + stat_rows(rows), HD), jnp.bfloat16),
        in_specs=[SMEM, SMEM, VMEM, VMEM, VMEM],
        out_specs=VMEM,
        compiler_params=pltpu.CompilerParams(vmem_limit_bytes=32 << 20),
        cost_estimate=pl.CostEstimate(flops=1, bytes_accessed=1, transcendentals=0),
        name="partial_decode",
    )(counts, fills, query, key, value)


def merge_kernel(lanes, counts, parts_ref, q_ref, k_ref, v_ref, o_ref):
    requests = q_ref.shape[0]
    width = (QH // lanes) * STEPS
    other, place = 1 - lax.axis_index("section"), lax.axis_index("tp")
    head = place * (QH // lanes) // GROUP
    spot = lax.broadcasted_iota(jnp.int32, (width, PAGE), 0)
    across = lax.broadcasted_iota(jnp.int32, (width, PAGE), 1)
    step = lax.broadcasted_iota(jnp.int32, (width, 1), 0) % STEPS
    end = 0
    for r in range(requests):
        start, end = end, end + counts[other, r]
        query = q_ref[r].astype(jnp.float32)
        keys = k_ref[r, head].astype(jnp.float32)
        values = v_ref[r, head].astype(jnp.float32)
        tops, vectors = [], []
        for u in range(STEPS):
            score = jnp.sum(query * keys[u:u + 1], axis=1, keepdims=True) * SCALE
            tops.append(jnp.where(u <= step, score, LOW))
            vectors.append(values[u:u + 1])
        for j in range(MAXP):
            page = jnp.minimum(start + j, 2 * lanes - 1)
            block = parts_ref[(page // 2) ^ place].astype(jnp.float32)
            later = jnp.full((width, HD), page % 2 == 1)
            vectors.append(jnp.where(later, block[width:2 * width], block[:width]))
            stat = jnp.sum(block[2 * width:2 * width + 8], axis=0, keepdims=True)
            stat = jnp.sum(
                jnp.where(across - page % 2 * width == spot, stat, 0.0), axis=1, keepdims=True
            )
            tops.append(jnp.where(jnp.full((width, 1), start + j < end), stat, LOW))
        top = functools.reduce(jnp.maximum, tops)
        weights = [jnp.exp(t - top) for t in tops]
        total = functools.reduce(jnp.add, weights)
        mixed = functools.reduce(jnp.add, [w * x for w, x in zip(weights, vectors)])
        o_ref[r] = (mixed / total).astype(jnp.bfloat16)


def merged(counts, parts, query, new_key, new_value, lanes):
    requests = query.shape[1]
    here = QH // lanes
    query = jnp.transpose(query.reshape(STEPS, requests, here, HD), (1, 2, 0, 3))
    query = query.reshape(requests, here * STEPS, HD)
    fresh = [
        jnp.transpose(x.reshape(STEPS, requests, KVH, HD), (1, 2, 0, 3)) for x in (new_key, new_value)
    ]
    out = pl.pallas_call(
        functools.partial(merge_kernel, lanes),
        out_shape=jax.ShapeDtypeStruct(query.shape, jnp.bfloat16),
        in_specs=[SMEM, VMEM, VMEM, VMEM, VMEM],
        out_specs=VMEM,
        compiler_params=pltpu.CompilerParams(vmem_limit_bytes=32 << 20),
        cost_estimate=pl.CostEstimate(flops=1, bytes_accessed=1, transcendentals=0),
        name="merge_decode",
    )(counts, parts, query, *fresh)
    out = jnp.transpose(out.reshape(requests, here, STEPS, HD), (2, 0, 1, 3))
    return out.reshape(STEPS, requests, here * HD)


def other_half(x):
    return lax.ppermute(x, "section", [(0, 1), (1, 0)])


def swap_bit(x, lanes, bit):
    return lax.ppermute(x, "tp", [(i, i ^ bit) for i in range(lanes)])


def bits_of(lanes):
    return [1 << b for b in range(lanes.bit_length() - 1)]


def gathered(x, lanes):
    held = x[None]
    for bit in bits_of(lanes):
        held = jnp.concatenate([held, swap_bit(held, lanes, bit)], axis=0)
    return held


def exchanged(x, lanes):
    for bit in bits_of(lanes):
        split = x.reshape(lanes // (2 * bit), 2, bit, *x.shape[1:])
        x = jnp.stack([split[:, 0], swap_bit(split[:, 1], lanes, bit)], axis=1).reshape(x.shape)
    return x


def after(x, *earlier):
    return lax.optimization_barrier((x, *earlier))[0]


def on_device(
    prefill_query, prefill_key, prefill_value, counts, fills, dec_query, dec_key, dec_value
):
    lanes = lax.axis_size("tp")
    here = QH // lanes
    requests = counts.shape[1]
    query, key, value = prefill_query[0], prefill_key[0], prefill_value[0]

    ahead = [(i, i + 2) for i in range(lanes - 2)]
    ahead_again = [(i, i + 2) for i in range(2, lanes - 2)]
    beside = [(i, i + 1) for i in range(0, lanes, 2)]
    trade = [(i, i ^ 1) for i in range(2, lanes)]
    back = [(i, i - 1) for i in range(5, lanes, 2)]
    asked = other_half(dec_query[0])
    *mine, whole = pack(key, value)
    received = []
    for block in mine:
        a = lax.ppermute(block, "tp", ahead)
        c = lax.ppermute(a, "tp", trade)
        d = lax.ppermute(jnp.concatenate([a[:, PAGE:], c[:, :PAGE]], axis=1), "tp", ahead_again)
        e = lax.ppermute(d[:, :PAGE], "tp", back)
        received.append((a, c, d, e))
    b = lax.ppermute(whole, "tp", beside)

    wanted = gathered(asked, lanes).reshape(lanes, STEPS, requests, here, HD)
    wanted = jnp.transpose(wanted, (2, 0, 3, 1, 4)).reshape(requests, lanes, here * STEPS, HD)
    parts = partial_decode(counts, fills, wanted, key, value, lanes)
    parts = exchanged(parts, lanes)
    dec_out = merged(counts, other_half(parts), dec_query[0], dec_key[0], dec_value[0], lanes)

    out, base = None, 0
    for g, n in enumerate(CHUNKS):
        a, c, d, e = received[g]
        blocks = (mine[g], a, b, c, d, e)
        if g + 1 < len(CHUNKS):
            cut = n // 2
            out = prompt_heads(base, n, 0, cut, counts, fills, query, blocks, out)
            out = after(out, received[g + 1][2])
            out = prompt_heads(base, n, cut, n, counts, fills, query, blocks, out)
        else:
            out = after(out, dec_out)
            out = prompt_heads(base, n, 0, n, counts, fills, query, blocks, out)
        base += n
    return (out[None], dec_out[None])


def solution(mesh):
    placed = (
        P("section", ("groups", "tp"), None),
        P("section", ("groups", "tp"), None),
        P("section", ("groups", "tp"), None),
        P(None, "groups"),
        P(None, "groups"),
        P("section", None, "groups", "tp"),
        P("section", None, "groups", None),
        P("section", None, "groups", None),
    )
    return jax.shard_map(
        on_device,
        mesh=mesh,
        in_specs=placed,
        out_specs=(P("section", ("groups", "tp"), None), P("section", None, "groups", "tp")),
        check_vma=False,
    )
```

```python
import functools
import math

import jax
import jax.numpy as jnp
from jax import lax
from jax.experimental import pallas as pl
from jax.experimental.pallas import tpu as pltpu
from jax.sharding import PartitionSpec as P

QH = 64
KVH = 8
HD = 128
PAGE = 128
MAXP = 8
STEPS = 4
GROUP = QH // KVH
SCALE = HD ** (-0.5)
EXP2_SCALE = SCALE * math.log2(math.e)
LOW = -1e30
CHUNKS = (4, 4)
ROWS = 512
UNIT = 64
SMEM = pl.BlockSpec(memory_space=pltpu.SMEM)
VMEM = pl.BlockSpec(memory_space=pltpu.VMEM)


def dot(a, b):
    return jnp.dot(a, b, preferred_element_type=jnp.float32)


def transposed_dot(a, b):
    return lax.dot_general(a, b, (((1,), (1,)), ((), ())), preferred_element_type=jnp.float32)


def page_facts(facts, half, page):
    requests = facts.shape[1] // 2
    owner, first, live, end = -1, 0, PAGE, 0
    for r in range(requests):
        start, end = end, end + facts[half, r]
        begun = start <= page
        owner = jnp.where(begun, r, owner)
        first = jnp.where(begun, start, first)
        live = jnp.where(end - 1 == page, facts[half, requests + r], live)
    return owner, first, live


def params(limit):
    return dict(
        compiler_params=pltpu.CompilerParams(vmem_limit_bytes=limit << 20),
        cost_estimate=pl.CostEstimate(flops=1, bytes_accessed=1, transcendentals=0),
    )


def pack_kernel(k_ref, v_ref, *outs):
    base = 0
    for n, out in zip(CHUNKS, outs):
        for j in range(n):
            h = base + j
            for p in range(2):
                rows, columns = slice(p * PAGE, (p + 1) * PAGE), slice(h * HD, (h + 1) * HD)
                turned = jnp.transpose(k_ref[rows, columns].astype(jnp.float32)).astype(jnp.bfloat16)
                value = v_ref[rows, columns]
                out[p, j * HD:(j + 1) * HD] = turned
                out[p, (n + j) * HD:(n + j + 1) * HD] = value
        base += n


def pack(key, value):
    shapes = [jax.ShapeDtypeStruct((2, 2 * n * HD, PAGE), jnp.bfloat16) for n in CHUNKS]
    return pl.pallas_call(
        pack_kernel,
        out_shape=shapes,
        in_specs=[VMEM, VMEM],
        out_specs=[VMEM] * len(shapes),
        name="pack",
        **params(32),
    )(key, value)


def prompt_kernel(facts, q_ref, ko, vo, ka, va, kb, vb, kc, vc, kd, vd, ke, ve, *rest):
    o_ref, keys, values, causal, *slots = rest[-8:]
    score_slots, prob_slots = slots[:2], slots[2:]
    half, place = lax.axis_index("section"), lax.axis_index("tp")
    even = place % 2 == 0
    near, far = 2 * place - 2, 2 * place - 6
    page_c = jnp.where(even, near, far)
    page_be = jnp.where(even, far, near)
    choose = jnp.full((HD, PAGE), even)
    k_be = [jnp.where(choose, kd[1], kb[0]), jnp.where(choose, ke[...], kb[1])]
    v_be = [jnp.where(choose, vd[1], vb[0]), jnp.where(choose, ve[...], vb[1])]
    row = lax.broadcasted_iota(jnp.int32, (PAGE, PAGE), 0)
    col = lax.broadcasted_iota(jnp.int32, (PAGE, PAGE), 1)
    causal[...] = jnp.where(col <= row, 0.0, LOW)
    one = jnp.ones((PAGE, HD), jnp.bfloat16)
    zero = jnp.zeros((PAGE, HD), jnp.bfloat16)
    lives = []

    for i in range(2):
        _, first, live = page_facts(facts, half, 2 * place + i)
        lives.append(live)
        stand_in = jnp.broadcast_to(ko[i, :, :1], (HD, PAGE))
        if i == 0:
            pages = [(kd[0], vd[0], 2 * place - 7)]
        else:
            pages = [(ko[0], vo[0], 2 * place)]
        pages.append((ko[i], vo[i], None))
        pages += [(ka[p], va[p], 2 * place - 4 + p) for p in range(2)]
        pages += [(kc[p], vc[p], page_c + p) for p in range(2)]
        pages += [(k_be[p], v_be[p], page_be + p) for p in range(2)]
        for spot, (k, v, number) in enumerate(pages):
            count = one
            if number is not None:
                seen = jnp.full((PAGE, HD), number >= first)
                k = jnp.where(seen, k, stand_in)
                v = jnp.where(seen, v, zero)
                count = jnp.where(seen, one, zero)
            at = slice(spot * PAGE, (spot + 1) * PAGE)
            keys[i, :HD, at] = k
            keys[i, HD:, at] = k
            values[i, at, :HD] = v
            values[i, at, HD:] = count

    heads_at_once = ROWS // PAGE
    blocks = [(i, start) for i in range(2) for start in range(0, GROUP, heads_at_once)]

    def queries(i, start):
        q = jnp.concatenate(
            [
                q_ref[i * PAGE:(i + 1) * PAGE, h * HD:(h + 1) * HD]
                for h in range(start, start + heads_at_once)
            ],
            axis=0,
        ).astype(jnp.float32) * EXP2_SCALE
        high = q.astype(jnp.bfloat16)
        low = (q - high.astype(jnp.float32)).astype(jnp.bfloat16)
        return jnp.concatenate([high, low], axis=1)

    def score(block, slot, query, tile):
        at = slice(tile * 2 * PAGE, (tile + 1) * 2 * PAGE)
        score_slots[slot][:, at] = dot(query, keys[block[0], :, at])

    def soften(slot, unit):
        rows = slice(unit * UNIT, (unit + 1) * UNIT)
        spots = [slice(c * PAGE, (c + 1) * PAGE) for c in range(MAXP)]
        pieces = [score_slots[slot][rows, at] for at in spots]
        begin = unit * UNIT % PAGE
        pieces[1] = pieces[1] + causal[begin:begin + UNIT]
        top = jnp.max(functools.reduce(jnp.maximum, pieces), axis=1, keepdims=True)
        for piece, at in zip(pieces, spots):
            prob_slots[slot][rows, at] = jnp.exp2(piece - top).astype(jnp.bfloat16)

    def mix(block, slot):
        i, start = block
        mixed = dot(prob_slots[slot][...], values[i])
        token = lax.broadcasted_iota(jnp.int32, (ROWS, HD), 0) % PAGE
        total = mixed[:, HD:]
        near = pl.reciprocal(total, approx=True)
        near = near * (2.0 - total * near)
        out = jnp.where(token < lives[i], mixed[:, :HD] * near, 0.0).astype(jnp.bfloat16)
        for number in range(heads_at_once):
            h = start + number
            o_ref[i * PAGE:(i + 1) * PAGE, h * HD:(h + 1) * HD] = out[number * PAGE:(number + 1) * PAGE]

    tiles = MAXP // 2
    share = ROWS // UNIT // tiles
    query = queries(*blocks[0])
    for tile in range(tiles):
        score(blocks[0], 0, query, tile)
    for index in range(len(blocks) + 1):
        slot = index % 2
        if index > 0:
            mix(blocks[index - 1], 1 - slot)
        if index + 1 < len(blocks):
            query = queries(*blocks[index + 1])
        for tile in range(tiles):
            if index + 1 < len(blocks):
                score(blocks[index + 1], 1 - slot, query, tile)
            if index < len(blocks):
                for unit in range(tile * share, (tile + 1) * share):
                    soften(slot, unit)


def prompt_heads(base, n, low, high, facts, query, blocks, done):
    tok = query.shape[0]

    def block(first):
        return pl.BlockSpec((2, HD, PAGE), lambda j, *_: (0, first + low + j, 0))

    def half_block(first):
        return pl.BlockSpec((HD, PAGE), lambda j, *_: (first + low + j, 0))

    wide = pl.BlockSpec((tok, GROUP * HD), lambda j, *_: (0, base + low + j))
    mine, a, b, c, d, e = blocks
    operands = [facts, query, mine, mine, a, a, b, b, c, c, d, d, e, e]
    specs = [wide, block(0), block(n), block(0), block(n), block(0), block(n)]
    specs += [block(0), block(n), block(0), block(n), half_block(0), half_block(n)]
    aliases = {}
    if done is not None:
        aliases = {len(operands): 0}
        operands.append(done)
        specs.append(pl.BlockSpec(memory_space=pl.ANY))
    return pl.pallas_call(
        prompt_kernel,
        out_shape=jax.ShapeDtypeStruct(query.shape, jnp.bfloat16),
        grid_spec=pltpu.PrefetchScalarGridSpec(
            num_scalar_prefetch=1,
            grid=(high - low,),
            in_specs=specs,
            out_specs=wide,
            scratch_shapes=[
                pltpu.VMEM((2, 2 * HD, MAXP * PAGE), jnp.bfloat16),
                pltpu.VMEM((2, MAXP * PAGE, 2 * HD), jnp.bfloat16),
                pltpu.VMEM((PAGE, PAGE), jnp.float32),
                pltpu.VMEM((ROWS, MAXP * PAGE), jnp.float32),
                pltpu.VMEM((ROWS, MAXP * PAGE), jnp.float32),
                pltpu.VMEM((ROWS, MAXP * PAGE), jnp.bfloat16),
                pltpu.VMEM((ROWS, MAXP * PAGE), jnp.bfloat16),
            ],
        ),
        input_output_aliases=aliases,
        name="prompt_attention",
        **params(48),
    )(*operands)


def stat_rows(rows):
    return 16 - rows % 16


def choose_kernel(facts, q_ref, o_ref):
    half = lax.axis_index("section")

    def one(lane, carry):
        for i in range(2):
            o_ref[lane, i] = q_ref[page_facts(facts, half, 2 * lane + i)[0]]
        return carry

    lax.fori_loop(0, o_ref.shape[0], one, 0)


def chosen_queries(facts, query, lanes):
    return pl.pallas_call(
        choose_kernel,
        out_shape=jax.ShapeDtypeStruct((lanes, 2, *query.shape[1:]), jnp.bfloat16),
        in_specs=[SMEM, VMEM],
        out_specs=VMEM,
        name="choose_queries",
        **params(32),
    )(facts, query)


def partial_kernel(lanes, facts, q_ref, k_ref, v_ref, o_ref):
    split = GROUP // (QH // lanes)
    width = QH // lanes * STEPS
    extra = stat_rows(2 * width)
    half, place = lax.axis_index("section"), lax.axis_index("tp")
    lane = lax.broadcasted_iota(jnp.int32, (GROUP * STEPS, PAGE), 1)
    spot = lax.broadcasted_iota(jnp.int32, (2 * width, PAGE), 0)
    across = lax.broadcasted_iota(jnp.int32, (2 * width, PAGE), 1)
    line = lax.broadcasted_iota(jnp.int32, (extra, PAGE), 0)
    lives = [page_facts(facts, half, 2 * place + i)[2] for i in range(2)]
    for k in range(KVH):
        mixed, sums = [], []
        for i in range(2):
            query = jnp.concatenate([q_ref[k * split + t, i] for t in range(split)], axis=0)
            keys = k_ref[i * PAGE:(i + 1) * PAGE, k * HD:(k + 1) * HD]
            values = v_ref[i * PAGE:(i + 1) * PAGE, k * HD:(k + 1) * HD]
            score = transposed_dot(query, keys) * SCALE
            score = jnp.where(lane < lives[i], score, LOW)
            top = jnp.max(score, axis=1, keepdims=True)
            terms = jnp.exp(score - top)
            total = jnp.sum(terms, axis=1, keepdims=True)
            high = terms.astype(jnp.bfloat16)
            low = (terms - high.astype(jnp.float32)).astype(jnp.bfloat16)
            mixed.append((dot(high, values) + dot(low, values)) / total)
            sums.append(top + jnp.log(total))
        for t in range(split):
            rows = slice(t * width, (t + 1) * width)
            both = jnp.concatenate([sums[0][rows], sums[1][rows]], axis=0)
            turned = jnp.sum(jnp.where(spot == across, both, 0.0), axis=0, keepdims=True)
            first = turned.astype(jnp.bfloat16).astype(jnp.float32)
            rest = turned - first
            second = rest.astype(jnp.bfloat16).astype(jnp.float32)
            stat = jnp.where(line == 0, first, jnp.where(line == 1, second, rest - second))
            stat = jnp.where(line < 3, stat, 0.0)
            block = jnp.concatenate([mixed[0][rows], mixed[1][rows], stat], axis=0)
            o_ref[k * split + t] = block.astype(jnp.bfloat16)


def partial_decode(facts, query, key, value, lanes):
    rows = 2 * (QH // lanes) * STEPS
    return pl.pallas_call(
        functools.partial(partial_kernel, lanes),
        out_shape=jax.ShapeDtypeStruct((lanes, rows + stat_rows(rows), HD), jnp.bfloat16),
        in_specs=[SMEM, VMEM, VMEM, VMEM],
        out_specs=VMEM,
        name="partial_decode",
        **params(32),
    )(facts, query, key, value)


def merge_kernel(lanes, facts, parts_ref, q_ref, k_ref, v_ref, o_ref):
    requests = q_ref.shape[0]
    width = (QH // lanes) * STEPS
    other, place = 1 - lax.axis_index("section"), lax.axis_index("tp")
    head = place * (QH // lanes) // GROUP
    spot = lax.broadcasted_iota(jnp.int32, (width, PAGE), 0)
    across = lax.broadcasted_iota(jnp.int32, (width, PAGE), 1)
    step = lax.broadcasted_iota(jnp.int32, (width, 1), 0) % STEPS
    end = 0
    for r in range(requests):
        start, end = end, end + facts[other, r]
        query = q_ref[r].astype(jnp.float32)
        keys = k_ref[r, head].astype(jnp.float32)
        values = v_ref[r, head].astype(jnp.float32)
        tops, vectors = [], []
        for u in range(STEPS):
            score = jnp.sum(query * keys[u:u + 1], axis=1, keepdims=True) * SCALE
            tops.append(jnp.where(u <= step, score, LOW))
            vectors.append(values[u:u + 1])
        for j in range(MAXP):
            page = jnp.minimum(start + j, 2 * lanes - 1)
            block = parts_ref[page // 2].astype(jnp.float32)
            later = jnp.full((width, HD), page % 2 == 1)
            vectors.append(jnp.where(later, block[width:2 * width], block[:width]))
            stat = jnp.sum(block[2 * width:2 * width + 8], axis=0, keepdims=True)
            stat = jnp.sum(
                jnp.where(across - page % 2 * width == spot, stat, 0.0), axis=1, keepdims=True
            )
            tops.append(jnp.where(jnp.full((width, 1), start + j < end), stat, LOW))
        top = functools.reduce(jnp.maximum, tops)
        weights = [jnp.exp(t - top) for t in tops]
        total = functools.reduce(jnp.add, weights)
        mixed = functools.reduce(jnp.add, [w * x for w, x in zip(weights, vectors)])
        o_ref[r] = (mixed / total).astype(jnp.bfloat16)


def merged(facts, parts, query, new_key, new_value, lanes):
    requests = query.shape[0]
    fresh = [
        jnp.transpose(x.reshape(STEPS, requests, KVH, HD), (1, 2, 0, 3)) for x in (new_key, new_value)
    ]
    out = pl.pallas_call(
        functools.partial(merge_kernel, lanes),
        out_shape=jax.ShapeDtypeStruct(query.shape, jnp.bfloat16),
        in_specs=[SMEM, VMEM, VMEM, VMEM, VMEM],
        out_specs=VMEM,
        name="merge_decode",
        **params(32),
    )(facts, parts, query, *fresh)
    out = jnp.transpose(out.reshape(requests, QH // lanes, STEPS, HD), (2, 0, 1, 3))
    return out.reshape(STEPS, requests, QH // lanes * HD)


def other_half(x):
    return lax.ppermute(x, "section", [(0, 1), (1, 0)])


def after(x, *earlier):
    return lax.optimization_barrier((x, *earlier))[0]


def on_device(
    prefill_query, prefill_key, prefill_value, counts, fills, dec_query, dec_key, dec_value
):
    lanes = lax.axis_size("tp")
    here = QH // lanes
    requests = counts.shape[1]
    query, key, value = prefill_query[0], prefill_key[0], prefill_value[0]
    facts = jnp.concatenate([counts, fills], axis=1)
    dec_rows = jnp.transpose(dec_query[0].reshape(STEPS, requests, here, HD), (1, 2, 0, 3))
    dec_rows = dec_rows.reshape(requests, here * STEPS, HD)
    asked = other_half(dec_rows)

    ahead = [(i, i + 2) for i in range(lanes - 2)]
    ahead_again = [(i, i + 2) for i in range(2, lanes - 2)]
    beside = [(i, i + 1) for i in range(0, lanes, 2)]
    trade = [(i, i ^ 1) for i in range(2, lanes)]
    back = [(i, i - 1) for i in range(5, lanes, 2)]
    mine = pack(key, value)
    ahead_blocks = [lax.ppermute(block, "tp", ahead) for block in mine]

    wanted = chosen_queries(facts, asked, lanes)
    wanted = lax.all_to_all(wanted, "tp", split_axis=0, concat_axis=0, tiled=True)
    parts = partial_decode(facts, wanted, key, value, lanes)
    parts = lax.all_to_all(parts, "tp", split_axis=0, concat_axis=0, tiled=True)
    dec_out = merged(facts, other_half(parts), dec_rows, dec_key[0], dec_value[0], lanes)

    received = []
    for block, a, done in zip(mine, ahead_blocks, (wanted, parts)):
        b = lax.ppermute(after(block, received[0][2]) if received else block, "tp", beside)
        c = lax.ppermute(after(a, done) if received else after(a, done, b), "tp", trade)
        d = lax.ppermute(jnp.concatenate([a[1:], c[:1]], axis=0), "tp", ahead_again)
        e = lax.ppermute(d[0], "tp", back)
        received.append((a, b, c, d, e))

    out, base = None, 0
    for g, n in enumerate(CHUNKS):
        blocks = (mine[g], *received[g])
        if g + 1 < len(CHUNKS):
            cut = n // 2
            out = prompt_heads(base, n, 0, cut, facts, query, blocks, out)
            out = after(out, received[g + 1][3])
            out = prompt_heads(base, n, cut, n, facts, query, blocks, out)
        else:
            out = after(out, dec_out)
            out = prompt_heads(base, n, 0, n, facts, query, blocks, out)
        base += n
    return (out[None], dec_out[None])


def solution(mesh):
    placed = (
        P("section", ("groups", "tp"), None),
        P("section", ("groups", "tp"), None),
        P("section", ("groups", "tp"), None),
        P(None, "groups"),
        P(None, "groups"),
        P("section", None, "groups", "tp"),
        P("section", None, "groups", None),
        P("section", None, "groups", None),
    )
    return jax.shard_map(
        on_device,
        mesh=mesh,
        in_specs=placed,
        out_specs=(P("section", ("groups", "tp"), None), P("section", None, "groups", "tp")),
        check_vma=False,
    )
```

```python
import functools
import math

import jax
import jax.numpy as jnp
from jax import lax
from jax.experimental import pallas as pl
from jax.experimental.pallas import tpu as pltpu
from jax.sharding import PartitionSpec as P

QH = 64
KVH = 8
HD = 128
PAGE = 128
MAXP = 8
STEPS = 4
GROUP = QH // KVH
SCALE = HD ** (-0.5)
EXP2_SCALE = SCALE * math.log2(math.e)
LOW = -1e30
CHUNKS = (4, 4)
ROWS = 512
SMEM = pl.BlockSpec(memory_space=pltpu.SMEM)
VMEM = pl.BlockSpec(memory_space=pltpu.VMEM)


def dot(a, b):
    return jnp.dot(a, b, preferred_element_type=jnp.float32)


def page_facts(facts, half, page):
    requests = facts.shape[1] // 2
    owner, first, live, end = -1, 0, PAGE, 0
    for r in range(requests):
        start, end = end, end + facts[half, r]
        begun = start <= page
        owner = jnp.where(begun, r, owner)
        first = jnp.where(begun, start, first)
        live = jnp.where(end - 1 == page, facts[half, requests + r], live)
    return owner, first, live


def params(limit):
    return dict(
        compiler_params=pltpu.CompilerParams(vmem_limit_bytes=limit << 20),
        cost_estimate=pl.CostEstimate(flops=1, bytes_accessed=1, transcendentals=0),
    )


def pack_kernel(k_ref, v_ref, o_ref):
    for p in range(2):
        rows = slice(p * PAGE, (p + 1) * PAGE)
        o_ref[p, 0] = jnp.transpose(k_ref[rows].astype(jnp.float32)).astype(jnp.bfloat16)
        o_ref[p, 1] = v_ref[rows]


def pack(base, n, key, value):
    tok = key.shape[0]
    column = pl.BlockSpec((tok, HD), lambda j: (0, base + j))
    out = pl.pallas_call(
        pack_kernel,
        out_shape=jax.ShapeDtypeStruct((2, 2, n * HD, PAGE), jnp.bfloat16),
        grid=(n,),
        in_specs=[column, column],
        out_specs=pl.BlockSpec((2, 2, HD, PAGE), lambda j: (0, 0, j, 0)),
        name="pack",
        **params(32),
    )(key, value)
    return out.reshape(2, 2 * n * HD, PAGE)


def prompt_kernel(facts, q_ref, ko, vo, ka, va, kb, vb, kc, vc, kd, vd, ke, ve, *rest):
    o_ref, keys, values, causal, *probs = rest[-6:]
    half, place = lax.axis_index("section"), lax.axis_index("tp")
    even = place % 2 == 0
    near, far = 2 * place - 2, 2 * place - 6
    page_c = jnp.where(even, near, far)
    page_be = jnp.where(even, far, near)
    choose = jnp.full((HD, PAGE), even)
    k_be = [jnp.where(choose, kd[1], kb[0]), jnp.where(choose, ke[...], kb[1])]
    v_be = [jnp.where(choose, vd[1], vb[0]), jnp.where(choose, ve[...], vb[1])]
    row = lax.broadcasted_iota(jnp.int32, (PAGE, PAGE), 0)
    col = lax.broadcasted_iota(jnp.int32, (PAGE, PAGE), 1)
    causal[...] = jnp.where(col <= row, 0.0, LOW)
    one = jnp.ones((PAGE, HD), jnp.bfloat16)
    zero = jnp.zeros((PAGE, HD), jnp.bfloat16)
    lives = []

    for i in range(2):
        _, first, live = page_facts(facts, half, 2 * place + i)
        lives.append(live)
        stand_in = jnp.broadcast_to(ko[i, :, :1], (HD, PAGE))
        if i == 0:
            pages = [(kd[0], vd[0], 2 * place - 7)]
        else:
            pages = [(ko[0], vo[0], 2 * place)]
        pages.append((ko[i], vo[i], None))
        pages += [(ka[p], va[p], 2 * place - 4 + p) for p in range(2)]
        pages += [(kc[p], vc[p], page_c + p) for p in range(2)]
        pages += [(k_be[p], v_be[p], page_be + p) for p in range(2)]
        for spot, (k, v, number) in enumerate(pages):
            count = one
            if number is not None:
                seen = jnp.full((PAGE, HD), number >= first)
                k = jnp.where(seen, k, stand_in)
                v = jnp.where(seen, v, zero)
                count = jnp.where(seen, one, zero)
            at = slice(spot * PAGE, (spot + 1) * PAGE)
            keys[i, :HD, at] = k
            keys[i, HD:, at] = k
            values[i, at, :HD] = v
            values[i, at, HD:] = count

    heads_at_once = ROWS // PAGE
    blocks = [(i, start) for i in range(2) for start in range(0, GROUP, heads_at_once)]

    def halves(query):
        query = query.astype(jnp.float32) * EXP2_SCALE
        high = query.astype(jnp.bfloat16)
        low = (query - high.astype(jnp.float32)).astype(jnp.bfloat16)
        return jnp.concatenate([high, low], axis=1)

    def queries(i, start):
        return halves(
            jnp.concatenate(
                [
                    q_ref[i * PAGE:(i + 1) * PAGE, h * HD:(h + 1) * HD]
                    for h in range(start, start + heads_at_once)
                ],
                axis=0,
            )
        )

    def divided(mixed, live):
        total = mixed[:, HD:]
        near = pl.reciprocal(total, approx=True)
        near = near * (2.0 - total * near)
        token = lax.broadcasted_iota(jnp.int32, (total.shape[0], HD), 0) % PAGE
        return jnp.where(token < live, mixed[:, :HD] * near, 0.0).astype(jnp.bfloat16)

    tiles = [slice(t, t + 2 * PAGE) for t in range(0, MAXP * PAGE, 2 * PAGE)]

    def own_scores(query, i, repeat):
        own = dot(query, keys[i, :, tiles[0]])
        bias = jnp.concatenate([causal[...]] * repeat, axis=0)
        return jnp.concatenate([own[:, :PAGE], own[:, PAGE:] + bias], axis=1)

    def mix(block, slot, largest):
        i, start = block
        mixed = dot(probs[slot][...], values[i])
        out = divided(mixed, lives[i])
        for number in range(heads_at_once):
            h = start + number
            o_ref[i * PAGE:(i + 1) * PAGE, h * HD:(h + 1) * HD] = out[number * PAGE:(number + 1) * PAGE]
        return jnp.maximum(largest, mixed[:, HD:])

    largest = jnp.zeros((ROWS, HD), jnp.float32)
    for index in range(len(blocks) + 1):
        if index < len(blocks):
            i, slot = blocks[index][0], index % 2
            query = queries(*blocks[index])
            own = own_scores(query, i, heads_at_once)
            top = jnp.max(own, axis=1, keepdims=True)
            probs[slot][:, tiles[0]] = jnp.exp2(own - top).astype(jnp.bfloat16)
        if index > 0:
            largest = mix(blocks[index - 1], 1 - slot if index < len(blocks) else slot, largest)
        if index < len(blocks):
            for at in tiles[1:]:
                other = dot(query, keys[i, :, at])
                probs[slot][:, at] = jnp.exp2(other - top).astype(jnp.bfloat16)

    @pl.when(jnp.logical_not(jnp.max(largest) < 2.0 ** 100))
    def _():
        def one(index, carry):
            i, h = index // GROUP, index % GROUP
            rows = pl.ds(pl.multiple_of(i * PAGE, PAGE), PAGE)
            columns = pl.ds(pl.multiple_of(h * HD, HD), HD)
            query = halves(q_ref[rows, columns])
            scores = [own_scores(query, i, 1)] + [dot(query, keys[i, :, at]) for at in tiles[1:]]
            top = jnp.max(functools.reduce(jnp.maximum, scores), axis=1, keepdims=True)
            mixed = jnp.zeros((PAGE, 2 * HD), jnp.float32)
            for score, at in zip(scores, tiles):
                mixed = mixed + dot(jnp.exp2(score - top).astype(jnp.bfloat16), values[i, at])
            o_ref[rows, columns] = divided(mixed, jnp.where(i == 0, lives[0], lives[1]))
            return carry

        lax.fori_loop(0, 2 * GROUP, one, 0)


def prompt_heads(base, n, low, high, facts, query, blocks, done):
    tok = query.shape[0]

    def block(first):
        return pl.BlockSpec((2, HD, PAGE), lambda j, *_: (0, first + low + j, 0))

    def half_block(first):
        return pl.BlockSpec((HD, PAGE), lambda j, *_: (first + low + j, 0))

    wide = pl.BlockSpec((tok, GROUP * HD), lambda j, *_: (0, base + low + j))
    mine, a, b, c, d, e = blocks
    operands = [facts, query, mine, mine, a, a, b, b, c, c, d, d, e, e]
    specs = [wide, block(0), block(n), block(0), block(n), block(0), block(n)]
    specs += [block(0), block(n), block(0), block(n), half_block(0), half_block(n)]
    aliases = {}
    if done is not None:
        aliases = {len(operands): 0}
        operands.append(done)
        specs.append(pl.BlockSpec(memory_space=pl.ANY))
    return pl.pallas_call(
        prompt_kernel,
        out_shape=jax.ShapeDtypeStruct(query.shape, jnp.bfloat16),
        grid_spec=pltpu.PrefetchScalarGridSpec(
            num_scalar_prefetch=1,
            grid=(high - low,),
            in_specs=specs,
            out_specs=wide,
            scratch_shapes=[
                pltpu.VMEM((2, 2 * HD, MAXP * PAGE), jnp.bfloat16),
                pltpu.VMEM((2, MAXP * PAGE, 2 * HD), jnp.bfloat16),
                pltpu.VMEM((PAGE, PAGE), jnp.float32),
                pltpu.VMEM((ROWS, MAXP * PAGE), jnp.bfloat16),
                pltpu.VMEM((ROWS, MAXP * PAGE), jnp.bfloat16),
            ],
        ),
        input_output_aliases=aliases,
        name="prompt_attention",
        **params(48),
    )(*operands)


def stat_rows(rows):
    return 16 - rows % 16


def choose_kernel(facts, q_ref, o_ref):
    half = lax.axis_index("section")

    def one(lane, carry):
        for i in range(2):
            o_ref[lane, i] = q_ref[page_facts(facts, half, 2 * lane + i)[0]]
        return carry

    lax.fori_loop(0, o_ref.shape[0], one, 0)


def chosen_queries(facts, query, lanes):
    return pl.pallas_call(
        choose_kernel,
        out_shape=jax.ShapeDtypeStruct((lanes, 2, *query.shape[1:]), jnp.bfloat16),
        in_specs=[SMEM, VMEM],
        out_specs=VMEM,
        name="choose_queries",
        **params(32),
    )(facts, query)


def partial_kernel(lanes, facts, q_ref, *rest):
    *packed, o_ref = rest
    split = GROUP // (QH // lanes)
    width = QH // lanes * STEPS
    extra = stat_rows(2 * width)
    half, place = lax.axis_index("section"), lax.axis_index("tp")
    lane = lax.broadcasted_iota(jnp.int32, (GROUP * STEPS, PAGE), 1)
    spot = lax.broadcasted_iota(jnp.int32, (2 * width, PAGE), 0)
    across = lax.broadcasted_iota(jnp.int32, (2 * width, PAGE), 1)
    line = lax.broadcasted_iota(jnp.int32, (extra, PAGE), 0)
    lives = [page_facts(facts, half, 2 * place + i)[2] for i in range(2)]
    places = [(block, j, n) for block, n in zip(packed, CHUNKS) for j in range(n)]
    for k, (block, j, n) in enumerate(places):
        mixed, sums = [], []
        for i in range(2):
            query = jnp.concatenate([q_ref[k * split + t, i] for t in range(split)], axis=0)
            keys = block[i, j * HD:(j + 1) * HD]
            values = block[i, (n + j) * HD:(n + j + 1) * HD]
            score = dot(query, keys) * SCALE
            score = jnp.where(lane < lives[i], score, LOW)
            top = jnp.max(score, axis=1, keepdims=True)
            terms = jnp.exp(score - top)
            total = jnp.sum(terms, axis=1, keepdims=True)
            high = terms.astype(jnp.bfloat16)
            low = (terms - high.astype(jnp.float32)).astype(jnp.bfloat16)
            mixed.append((dot(high, values) + dot(low, values)) / total)
            sums.append(top + jnp.log(total))
        for t in range(split):
            rows = slice(t * width, (t + 1) * width)
            both = jnp.concatenate([sums[0][rows], sums[1][rows]], axis=0)
            turned = jnp.sum(jnp.where(spot == across, both, 0.0), axis=0, keepdims=True)
            first = turned.astype(jnp.bfloat16).astype(jnp.float32)
            rest = turned - first
            second = rest.astype(jnp.bfloat16).astype(jnp.float32)
            stat = jnp.where(line == 0, first, jnp.where(line == 1, second, rest - second))
            stat = jnp.where(line < 3, stat, 0.0)
            block = jnp.concatenate([mixed[0][rows], mixed[1][rows], stat], axis=0)
            o_ref[k * split + t] = block.astype(jnp.bfloat16)


def partial_decode(facts, query, packed, lanes):
    rows = 2 * (QH // lanes) * STEPS
    return pl.pallas_call(
        functools.partial(partial_kernel, lanes),
        out_shape=jax.ShapeDtypeStruct((lanes, rows + stat_rows(rows), HD), jnp.bfloat16),
        in_specs=[SMEM, VMEM] + [VMEM] * len(packed),
        out_specs=VMEM,
        name="partial_decode",
        **params(32),
    )(facts, query, *packed)


def merge_kernel(lanes, facts, parts_ref, q_ref, k_ref, v_ref, o_ref):
    requests = q_ref.shape[0]
    width = (QH // lanes) * STEPS
    other, place = 1 - lax.axis_index("section"), lax.axis_index("tp")
    head = place * (QH // lanes) // GROUP
    spot = lax.broadcasted_iota(jnp.int32, (width, PAGE), 0)
    across = lax.broadcasted_iota(jnp.int32, (width, PAGE), 1)
    step = lax.broadcasted_iota(jnp.int32, (width, 1), 0) % STEPS
    end = 0
    for r in range(requests):
        start, end = end, end + facts[other, r]
        query = q_ref[r].astype(jnp.float32)
        keys = k_ref[r, head].astype(jnp.float32)
        values = v_ref[r, head].astype(jnp.float32)
        tops, vectors = [], []
        for u in range(STEPS):
            score = jnp.sum(query * keys[u:u + 1], axis=1, keepdims=True) * SCALE
            tops.append(jnp.where(u <= step, score, LOW))
            vectors.append(values[u:u + 1])
        for j in range(MAXP):
            page = jnp.minimum(start + j, 2 * lanes - 1)
            block = parts_ref[page // 2].astype(jnp.float32)
            later = jnp.full((width, HD), page % 2 == 1)
            vectors.append(jnp.where(later, block[width:2 * width], block[:width]))
            stat = jnp.sum(block[2 * width:2 * width + 8], axis=0, keepdims=True)
            stat = jnp.sum(
                jnp.where(across - page % 2 * width == spot, stat, 0.0), axis=1, keepdims=True
            )
            tops.append(jnp.where(jnp.full((width, 1), start + j < end), stat, LOW))
        top = functools.reduce(jnp.maximum, tops)
        weights = [jnp.exp(t - top) for t in tops]
        total = functools.reduce(jnp.add, weights)
        mixed = functools.reduce(jnp.add, [w * x for w, x in zip(weights, vectors)])
        o_ref[r] = (mixed / total).astype(jnp.bfloat16)


def merged(facts, parts, query, new_key, new_value, lanes):
    requests = query.shape[0]
    fresh = [
        jnp.transpose(x.reshape(STEPS, requests, KVH, HD), (1, 2, 0, 3)) for x in (new_key, new_value)
    ]
    out = pl.pallas_call(
        functools.partial(merge_kernel, lanes),
        out_shape=jax.ShapeDtypeStruct(query.shape, jnp.bfloat16),
        in_specs=[SMEM, VMEM, VMEM, VMEM, VMEM],
        out_specs=VMEM,
        name="merge_decode",
        **params(32),
    )(facts, parts, query, *fresh)
    out = jnp.transpose(out.reshape(requests, QH // lanes, STEPS, HD), (2, 0, 1, 3))
    return out.reshape(STEPS, requests, QH // lanes * HD)


def other_half(x):
    return lax.ppermute(x, "section", [(0, 1), (1, 0)])


def after(x, *earlier):
    return lax.optimization_barrier((x, *earlier))[0]


def on_device(
    prefill_query, prefill_key, prefill_value, counts, fills, dec_query, dec_key, dec_value
):
    lanes = lax.axis_size("tp")
    here = QH // lanes
    requests = counts.shape[1]
    query, key, value = prefill_query[0], prefill_key[0], prefill_value[0]
    facts = jnp.concatenate([counts, fills], axis=1)
    dec_rows = jnp.transpose(dec_query[0].reshape(STEPS, requests, here, HD), (1, 2, 0, 3))
    dec_rows = dec_rows.reshape(requests, here * STEPS, HD)
    asked = other_half(dec_rows)

    ahead = [(i, i + 2) for i in range(lanes - 2)]
    ahead_again = [(i, i + 2) for i in range(2, lanes - 2)]
    beside = [(i, i + 1) for i in range(0, lanes, 2)]
    trade = [(i, i ^ 1) for i in range(2, lanes)]
    back = [(i, i - 1) for i in range(5, lanes, 2)]
    bases = [sum(CHUNKS[:g]) for g in range(len(CHUNKS))]
    mine = [pack(base, n, key, value) for base, n in zip(bases, CHUNKS)]
    received = []
    for block in mine:
        a = lax.ppermute(block, "tp", ahead)
        b = lax.ppermute(after(block, received[0][2]) if received else block, "tp", beside)
        c = lax.ppermute(a if received else after(a, b), "tp", trade)
        d = lax.ppermute(jnp.concatenate([a[1:], c[:1]], axis=0), "tp", ahead_again)
        e = lax.ppermute(d[0], "tp", back)
        received.append((a, b, c, d, e))

    wanted = chosen_queries(facts, asked, lanes)
    wanted = lax.all_to_all(wanted, "tp", split_axis=0, concat_axis=0, tiled=True)
    wanted = after(wanted, received[0][2])
    parts = partial_decode(facts, wanted, mine, lanes)
    parts = lax.all_to_all(parts, "tp", split_axis=0, concat_axis=0, tiled=True)
    dec_out = merged(facts, other_half(parts), dec_rows, dec_key[0], dec_value[0], lanes)

    out = None
    for g, (base, n) in enumerate(zip(bases, CHUNKS)):
        blocks = (mine[g], *received[g])
        if g + 1 < len(CHUNKS):
            cut = n // 2
            out = prompt_heads(base, n, 0, cut, facts, query, blocks, out)
            out = after(out, received[g + 1][3])
            out = prompt_heads(base, n, cut, n, facts, query, blocks, out)
        else:
            out = after(out, dec_out)
            out = prompt_heads(base, n, 0, n, facts, query, blocks, out)
    return (out[None], dec_out[None])


def solution(mesh):
    placed = (
        P("section", ("groups", "tp"), None),
        P("section", ("groups", "tp"), None),
        P("section", ("groups", "tp"), None),
        P(None, "groups"),
        P(None, "groups"),
        P("section", None, "groups", "tp"),
        P("section", None, "groups", None),
        P("section", None, "groups", None),
    )
    return jax.shard_map(
        on_device,
        mesh=mesh,
        in_specs=placed,
        out_specs=(P("section", ("groups", "tp"), None), P("section", None, "groups", "tp")),
        check_vma=False,
    )
```

```python
import functools
import math

import jax
import jax.numpy as jnp
from jax import lax
from jax.experimental import pallas as pl
from jax.experimental.pallas import tpu as pltpu
from jax.sharding import PartitionSpec as P

QH = 64
KVH = 8
HD = 128
PAGE = 128
MAXP = 8
STEPS = 4
GROUP = QH // KVH
SCALE = HD ** (-0.5)
EXP2_SCALE = SCALE * math.log2(math.e)
LOW = -1e30
CHUNKS = (4, 4)
ROWS = 512
SMEM = pl.BlockSpec(memory_space=pltpu.SMEM)
VMEM = pl.BlockSpec(memory_space=pltpu.VMEM)


def dot(a, b):
    return jnp.dot(a, b, preferred_element_type=jnp.float32)


def page_facts(facts, half, page):
    requests = facts.shape[1] // 2
    owner, first, live, end = -1, 0, PAGE, 0
    for r in range(requests):
        start, end = end, end + facts[half, r]
        begun = start <= page
        owner = jnp.where(begun, r, owner)
        first = jnp.where(begun, start, first)
        live = jnp.where(end - 1 == page, facts[half, requests + r], live)
    return owner, first, live


def params(limit):
    return dict(
        compiler_params=pltpu.CompilerParams(vmem_limit_bytes=limit << 20),
        cost_estimate=pl.CostEstimate(flops=1, bytes_accessed=1, transcendentals=0),
    )


def pack_kernel(k_ref, v_ref, o_ref):
    for p in range(2):
        rows = slice(p * PAGE, (p + 1) * PAGE)
        o_ref[p, 0] = jnp.transpose(k_ref[rows].astype(jnp.float32)).astype(jnp.bfloat16)
        o_ref[p, 1] = v_ref[rows]


def pack(base, n, key, value):
    tok = key.shape[0]
    column = pl.BlockSpec((tok, HD), lambda j: (0, base + j))
    out = pl.pallas_call(
        pack_kernel,
        out_shape=jax.ShapeDtypeStruct((2, 2, n * HD, PAGE), jnp.bfloat16),
        grid=(n,),
        in_specs=[column, column],
        out_specs=pl.BlockSpec((2, 2, HD, PAGE), lambda j: (0, 0, j, 0)),
        name="pack",
        **params(32),
    )(key, value)
    return out.reshape(2, 2 * n * HD, PAGE)


def prompt_kernel(base, n, low, facts, q_ref, *rest):
    o_ref, keys, values, causal, *probs = rest[-6:]
    head = low + pl.program_id(0)
    spots = [pl.ds(pl.multiple_of((x + head) * HD, HD), HD) for x in (0, n)]
    mine, a, b, c, d = [[[x[p, at] for at in spots] for p in range(2)] for x in rest[:5]]
    e = [rest[5][at] for at in spots]
    columns = [
        pl.ds(pl.multiple_of((base + head) * GROUP * HD + h * HD, HD), HD) for h in range(GROUP)
    ]
    half, place = lax.axis_index("section"), lax.axis_index("tp")
    even = place % 2 == 0
    near, far = 2 * place - 2, 2 * place - 6
    page_c = jnp.where(even, near, far)
    page_be = jnp.where(even, far, near)
    choose = jnp.full((HD, PAGE), even)
    be = [
        [jnp.where(choose, x, y) for x, y in zip(late, b[p])] for p, late in enumerate((d[1], e))
    ]
    row = lax.broadcasted_iota(jnp.int32, (PAGE, PAGE), 0)
    col = lax.broadcasted_iota(jnp.int32, (PAGE, PAGE), 1)
    causal[...] = jnp.where(col <= row, 0.0, LOW)
    one = jnp.ones((PAGE, HD), jnp.bfloat16)
    zero = jnp.zeros((PAGE, HD), jnp.bfloat16)
    lives = []

    for i in range(2):
        _, first, live = page_facts(facts, half, 2 * place + i)
        lives.append(live)
        stand_in = jnp.broadcast_to(mine[i][0][:, :1], (HD, PAGE))
        if i == 0:
            pages = [(*d[0], 2 * place - 7)]
        else:
            pages = [(*mine[0], 2 * place)]
        pages.append((*mine[i], None))
        pages += [(*a[p], 2 * place - 4 + p) for p in range(2)]
        pages += [(*c[p], page_c + p) for p in range(2)]
        pages += [(*be[p], page_be + p) for p in range(2)]
        for spot, (k, v, number) in enumerate(pages):
            count = one
            if number is not None:
                seen = jnp.full((PAGE, HD), number >= first)
                k = jnp.where(seen, k, stand_in)
                v = jnp.where(seen, v, zero)
                count = jnp.where(seen, one, zero)
            at = slice(spot * PAGE, (spot + 1) * PAGE)
            keys[i, :HD, at] = k
            keys[i, HD:, at] = k
            values[i, at, :HD] = v
            values[i, at, HD:] = count

    heads_at_once = ROWS // PAGE
    blocks = [(i, start) for i in range(2) for start in range(0, GROUP, heads_at_once)]

    def halves(query):
        query = query.astype(jnp.float32) * EXP2_SCALE
        high = query.astype(jnp.bfloat16)
        low = (query - high.astype(jnp.float32)).astype(jnp.bfloat16)
        return jnp.concatenate([high, low], axis=1)

    def queries(i, start):
        return halves(
            jnp.concatenate(
                [
                    q_ref[i * PAGE:(i + 1) * PAGE, columns[h]]
                    for h in range(start, start + heads_at_once)
                ],
                axis=0,
            )
        )

    def divided(mixed, live):
        total = mixed[:, HD:]
        near = pl.reciprocal(total, approx=True)
        near = near * (2.0 - total * near)
        token = lax.broadcasted_iota(jnp.int32, (total.shape[0], HD), 0) % PAGE
        return jnp.where(token < live, mixed[:, :HD] * near, 0.0).astype(jnp.bfloat16)

    tiles = [slice(t, t + 2 * PAGE) for t in range(0, MAXP * PAGE, 2 * PAGE)]

    def own_scores(query, i, repeat):
        own = dot(query, keys[i, :, tiles[0]])
        bias = jnp.concatenate([causal[...]] * repeat, axis=0)
        return jnp.concatenate([own[:, :PAGE], own[:, PAGE:] + bias], axis=1)

    def mix(block, slot, largest):
        i, start = block
        mixed = dot(probs[slot][...], values[i])
        out = divided(mixed, lives[i])
        for number in range(heads_at_once):
            h = start + number
            o_ref[i * PAGE:(i + 1) * PAGE, h * HD:(h + 1) * HD] = out[number * PAGE:(number + 1) * PAGE]
        return jnp.maximum(largest, mixed[:, HD:])

    largest = jnp.zeros((ROWS, HD), jnp.float32)
    for index in range(len(blocks) + 1):
        if index < len(blocks):
            i, slot = blocks[index][0], index % 2
            query = queries(*blocks[index])
            own = own_scores(query, i, heads_at_once)
            top = jnp.max(own, axis=1, keepdims=True)
            probs[slot][:, tiles[0]] = jnp.exp2(own - top).astype(jnp.bfloat16)
        if index > 0:
            largest = mix(blocks[index - 1], 1 - slot if index < len(blocks) else slot, largest)
        if index < len(blocks):
            for at in tiles[1:]:
                other = dot(query, keys[i, :, at])
                probs[slot][:, at] = jnp.exp2(other - top).astype(jnp.bfloat16)

    @pl.when(jnp.logical_not(jnp.max(largest) < 2.0 ** 100))
    def _():
        def one(index, carry):
            i, h = index // GROUP, index % GROUP
            rows = pl.ds(pl.multiple_of(i * PAGE, PAGE), PAGE)
            columns = pl.ds(pl.multiple_of(h * HD, HD), HD)
            from_all = pl.ds(pl.multiple_of(((base + head) * GROUP + h) * HD, HD), HD)
            query = halves(q_ref[rows, from_all])
            scores = [own_scores(query, i, 1)] + [dot(query, keys[i, :, at]) for at in tiles[1:]]
            top = jnp.max(functools.reduce(jnp.maximum, scores), axis=1, keepdims=True)
            mixed = jnp.zeros((PAGE, 2 * HD), jnp.float32)
            for score, at in zip(scores, tiles):
                mixed = mixed + dot(jnp.exp2(score - top).astype(jnp.bfloat16), values[i, at])
            o_ref[rows, columns] = divided(mixed, jnp.where(i == 0, lives[0], lives[1]))
            return carry

        lax.fori_loop(0, 2 * GROUP, one, 0)


def prompt_heads(base, n, low, high, facts, query, blocks, done):
    tok = query.shape[0]

    wide = pl.BlockSpec((tok, GROUP * HD), lambda j, *_: (0, base + low + j))
    operands = [facts, query, *blocks]
    specs = [VMEM] * (1 + len(blocks))
    aliases = {}
    if done is not None:
        aliases = {len(operands): 0}
        operands.append(done)
        specs.append(pl.BlockSpec(memory_space=pl.ANY))
    return pl.pallas_call(
        functools.partial(prompt_kernel, base, n, low),
        out_shape=jax.ShapeDtypeStruct(query.shape, jnp.bfloat16),
        grid_spec=pltpu.PrefetchScalarGridSpec(
            num_scalar_prefetch=1,
            grid=(high - low,),
            in_specs=specs,
            out_specs=wide,
            scratch_shapes=[
                pltpu.VMEM((2, 2 * HD, MAXP * PAGE), jnp.bfloat16),
                pltpu.VMEM((2, MAXP * PAGE, 2 * HD), jnp.bfloat16),
                pltpu.VMEM((PAGE, PAGE), jnp.float32),
                pltpu.VMEM((ROWS, MAXP * PAGE), jnp.bfloat16),
                pltpu.VMEM((ROWS, MAXP * PAGE), jnp.bfloat16),
            ],
        ),
        input_output_aliases=aliases,
        name="prompt_attention",
        **params(20),
    )(*operands)


def stat_rows(rows):
    return 16 - rows % 16


def choose_kernel(facts, q_ref, o_ref):
    half = lax.axis_index("section")

    def one(lane, carry):
        for i in range(2):
            o_ref[lane, i] = q_ref[page_facts(facts, half, 2 * lane + i)[0]]
        return carry

    lax.fori_loop(0, o_ref.shape[0], one, 0)


def chosen_queries(facts, query, lanes):
    return pl.pallas_call(
        choose_kernel,
        out_shape=jax.ShapeDtypeStruct((lanes, 2, *query.shape[1:]), jnp.bfloat16),
        in_specs=[SMEM, VMEM],
        out_specs=VMEM,
        name="choose_queries",
        **params(32),
    )(facts, query)


def partial_kernel(lanes, facts, q_ref, *rest):
    *packed, o_ref = rest
    split = GROUP // (QH // lanes)
    width = QH // lanes * STEPS
    extra = stat_rows(2 * width)
    half, place = lax.axis_index("section"), lax.axis_index("tp")
    lane = lax.broadcasted_iota(jnp.int32, (GROUP * STEPS, PAGE), 1)
    spot = lax.broadcasted_iota(jnp.int32, (2 * width, PAGE), 0)
    across = lax.broadcasted_iota(jnp.int32, (2 * width, PAGE), 1)
    line = lax.broadcasted_iota(jnp.int32, (extra, PAGE), 0)
    lives = [page_facts(facts, half, 2 * place + i)[2] for i in range(2)]
    places = [(block, j, n) for block, n in zip(packed, CHUNKS) for j in range(n)]
    for k, (block, j, n) in enumerate(places):
        mixed, sums = [], []
        for i in range(2):
            query = jnp.concatenate([q_ref[k * split + t, i] for t in range(split)], axis=0)
            keys = block[i, j * HD:(j + 1) * HD]
            values = block[i, (n + j) * HD:(n + j + 1) * HD]
            score = dot(query, keys) * SCALE
            score = jnp.where(lane < lives[i], score, LOW)
            top = jnp.max(score, axis=1, keepdims=True)
            terms = jnp.exp(score - top)
            total = jnp.sum(terms, axis=1, keepdims=True)
            high = terms.astype(jnp.bfloat16)
            low = (terms - high.astype(jnp.float32)).astype(jnp.bfloat16)
            mixed.append((dot(high, values) + dot(low, values)) / total)
            sums.append(top + jnp.log(total))
        for t in range(split):
            rows = slice(t * width, (t + 1) * width)
            both = jnp.concatenate([sums[0][rows], sums[1][rows]], axis=0)
            turned = jnp.sum(jnp.where(spot == across, both, 0.0), axis=0, keepdims=True)
            first = turned.astype(jnp.bfloat16).astype(jnp.float32)
            rest = turned - first
            second = rest.astype(jnp.bfloat16).astype(jnp.float32)
            stat = jnp.where(line == 0, first, jnp.where(line == 1, second, rest - second))
            stat = jnp.where(line < 3, stat, 0.0)
            block = jnp.concatenate([mixed[0][rows], mixed[1][rows], stat], axis=0)
            o_ref[k * split + t] = block.astype(jnp.bfloat16)


def partial_decode(facts, query, packed, lanes):
    rows = 2 * (QH // lanes) * STEPS
    return pl.pallas_call(
        functools.partial(partial_kernel, lanes),
        out_shape=jax.ShapeDtypeStruct((lanes, rows + stat_rows(rows), HD), jnp.bfloat16),
        in_specs=[SMEM, VMEM] + [VMEM] * len(packed),
        out_specs=VMEM,
        name="partial_decode",
        **params(32),
    )(facts, query, *packed)


def merge_kernel(lanes, facts, parts_ref, q_ref, k_ref, v_ref, o_ref):
    requests = q_ref.shape[0]
    width = (QH // lanes) * STEPS
    other, place = 1 - lax.axis_index("section"), lax.axis_index("tp")
    head = place * (QH // lanes) // GROUP
    spot = lax.broadcasted_iota(jnp.int32, (width, PAGE), 0)
    across = lax.broadcasted_iota(jnp.int32, (width, PAGE), 1)
    step = lax.broadcasted_iota(jnp.int32, (width, 1), 0) % STEPS
    end = 0
    for r in range(requests):
        start, end = end, end + facts[other, r]
        query = q_ref[r].astype(jnp.float32)
        keys = k_ref[r, head].astype(jnp.float32)
        values = v_ref[r, head].astype(jnp.float32)
        tops, vectors = [], []
        for u in range(STEPS):
            score = jnp.sum(query * keys[u:u + 1], axis=1, keepdims=True) * SCALE
            tops.append(jnp.where(u <= step, score, LOW))
            vectors.append(values[u:u + 1])
        for j in range(MAXP):
            page = jnp.minimum(start + j, 2 * lanes - 1)
            block = parts_ref[page // 2].astype(jnp.float32)
            later = jnp.full((width, HD), page % 2 == 1)
            vectors.append(jnp.where(later, block[width:2 * width], block[:width]))
            stat = jnp.sum(block[2 * width:2 * width + 8], axis=0, keepdims=True)
            stat = jnp.sum(
                jnp.where(across - page % 2 * width == spot, stat, 0.0), axis=1, keepdims=True
            )
            tops.append(jnp.where(jnp.full((width, 1), start + j < end), stat, LOW))
        top = functools.reduce(jnp.maximum, tops)
        weights = [jnp.exp(t - top) for t in tops]
        total = functools.reduce(jnp.add, weights)
        mixed = functools.reduce(jnp.add, [w * x for w, x in zip(weights, vectors)])
        o_ref[r] = (mixed / total).astype(jnp.bfloat16)


def merged(facts, parts, query, new_key, new_value, lanes):
    requests = query.shape[0]
    fresh = [
        jnp.transpose(x.reshape(STEPS, requests, KVH, HD), (1, 2, 0, 3)) for x in (new_key, new_value)
    ]
    out = pl.pallas_call(
        functools.partial(merge_kernel, lanes),
        out_shape=jax.ShapeDtypeStruct(query.shape, jnp.bfloat16),
        in_specs=[SMEM, VMEM, VMEM, VMEM, VMEM],
        out_specs=VMEM,
        name="merge_decode",
        **params(32),
    )(facts, parts, query, *fresh)
    out = jnp.transpose(out.reshape(requests, QH // lanes, STEPS, HD), (2, 0, 1, 3))
    return out.reshape(STEPS, requests, QH // lanes * HD)


def other_half(x):
    return lax.ppermute(x, "section", [(0, 1), (1, 0)])


def after(x, *earlier):
    return lax.optimization_barrier((x, *earlier))[0]


def on_device(
    prefill_query, prefill_key, prefill_value, counts, fills, dec_query, dec_key, dec_value
):
    lanes = lax.axis_size("tp")
    here = QH // lanes
    requests = counts.shape[1]
    query, key, value = prefill_query[0], prefill_key[0], prefill_value[0]
    facts = jnp.concatenate([counts, fills], axis=1)
    dec_rows = jnp.transpose(dec_query[0].reshape(STEPS, requests, here, HD), (1, 2, 0, 3))
    dec_rows = dec_rows.reshape(requests, here * STEPS, HD)
    asked = other_half(dec_rows)

    ahead = [(i, i + 2) for i in range(lanes - 2)]
    ahead_again = [(i, i + 2) for i in range(2, lanes - 2)]
    beside = [(i, i + 1) for i in range(0, lanes, 2)]
    trade = [(i, i ^ 1) for i in range(2, lanes)]
    back = [(i, i - 1) for i in range(5, lanes, 2)]
    bases = [sum(CHUNKS[:g]) for g in range(len(CHUNKS))]
    mine = [pack(base, n, key, value) for base, n in zip(bases, CHUNKS)]
    chosen = chosen_queries(facts, asked, lanes)
    wanted = lax.all_to_all(chosen, "tp", split_axis=0, concat_axis=0, tiled=True)
    parts = partial_decode(facts, wanted, mine, lanes)
    parts = lax.all_to_all(parts, "tp", split_axis=0, concat_axis=0, tiled=True)
    dec_out = merged(facts, other_half(parts), dec_rows, dec_key[0], dec_value[0], lanes)

    received = []
    for g, block in enumerate(mine):
        a = lax.ppermute(after(block, chosen) if g else block, "tp", ahead)
        b = lax.ppermute(after(block, received[0][2]) if g else block, "tp", beside)
        c = lax.ppermute(after(a, wanted if g else b), "tp", trade)
        d = jnp.concatenate([a[1:], c[:1]], axis=0)
        d = lax.ppermute(after(d, parts) if g else d, "tp", ahead_again)
        e = lax.ppermute(d[0], "tp", back)
        received.append((a, b, c, d, e))

    out = None
    for g, (base, n) in enumerate(zip(bases, CHUNKS)):
        blocks = (mine[g], *received[g])
        if g > 0:
            out = after(out, dec_out)
        out = prompt_heads(base, n, 0, n, facts, query, blocks, out)
    return (out[None], dec_out[None])


def solution(mesh):
    placed = (
        P("section", ("groups", "tp"), None),
        P("section", ("groups", "tp"), None),
        P("section", ("groups", "tp"), None),
        P(None, "groups"),
        P(None, "groups"),
        P("section", None, "groups", "tp"),
        P("section", None, "groups", None),
        P("section", None, "groups", None),
    )
    return jax.shard_map(
        on_device,
        mesh=mesh,
        in_specs=placed,
        out_specs=(P("section", ("groups", "tp"), None), P("section", None, "groups", "tp")),
        check_vma=False,
    )
```

```python
import functools

import jax
import jax.numpy as jnp
from jax import lax
from jax.experimental import pallas as pl
from jax.experimental.pallas import tpu as pltpu
from jax.sharding import PartitionSpec as P

QH = 64
KVH = 8
HD = 128
PAGE = 128
MAXP = 8
STEPS = 4
GROUP = QH // KVH
SCALE = HD ** (-0.5)
LOW = -1e30
CHUNKS = (4, 4)
ROWS = 1024
SMEM = pl.BlockSpec(memory_space=pltpu.SMEM)
VMEM = pl.BlockSpec(memory_space=pltpu.VMEM)


def dot(a, b):
    return jnp.dot(a, b, preferred_element_type=jnp.float32)


def page_facts(facts, half, page):
    requests = facts.shape[1] // 2
    owner, first, live, end = -1, 0, PAGE, 0
    for r in range(requests):
        start, end = end, end + facts[half, r]
        begun = start <= page
        owner = jnp.where(begun, r, owner)
        first = jnp.where(begun, start, first)
        live = jnp.where(end - 1 == page, facts[half, requests + r], live)
    return owner, first, live


def params(limit):
    return dict(
        compiler_params=pltpu.CompilerParams(vmem_limit_bytes=limit << 20),
        cost_estimate=pl.CostEstimate(flops=1, bytes_accessed=1, transcendentals=0),
    )


def pack_kernel(k_ref, v_ref, o_ref):
    for p in range(2):
        rows = slice(p * PAGE, (p + 1) * PAGE)
        o_ref[p, 0] = jnp.transpose(k_ref[rows].astype(jnp.float32)).astype(jnp.bfloat16)
        o_ref[p, 1] = v_ref[rows]


def pack(base, n, key, value):
    tok = key.shape[0]
    column = pl.BlockSpec((tok, HD), lambda j: (0, base + j))
    out = pl.pallas_call(
        pack_kernel,
        out_shape=jax.ShapeDtypeStruct((2, 2, n * HD, PAGE), jnp.bfloat16),
        grid=(n,),
        in_specs=[column, column],
        out_specs=pl.BlockSpec((2, 2, HD, PAGE), lambda j: (0, 0, j, 0)),
        name="pack",
        **params(56),
    )(key, value)
    return out.reshape(2, 2 * n * HD, PAGE)


def prompt_kernel(n, low, facts, q_ref, *rest):
    o_ref, keys, values, causal, *probs = rest[-6:]
    head = low + pl.program_id(0)
    spots = [pl.ds(pl.multiple_of((x + head) * HD, HD), HD) for x in (0, n)]
    mine, a, b, c, d = [[[x[p, at] for at in spots] for p in range(2)] for x in rest[:5]]
    e = [rest[5][at] for at in spots]
    half, place = lax.axis_index("section"), lax.axis_index("tp")
    even = place % 2 == 0
    near, far = 2 * place - 2, 2 * place - 6
    page_c = jnp.where(even, near, far)
    page_be = jnp.where(even, far, near)
    choose = jnp.full((HD, PAGE), even)
    be = [
        [jnp.where(choose, x, y) for x, y in zip(late, b[p])] for p, late in enumerate((d[1], e))
    ]
    row = lax.broadcasted_iota(jnp.int32, (PAGE, PAGE), 0)
    col = lax.broadcasted_iota(jnp.int32, (PAGE, PAGE), 1)
    causal[...] = jnp.where(col <= row, 0.0, LOW)
    one = jnp.ones((PAGE, HD), jnp.bfloat16)
    zero = jnp.zeros((PAGE, HD), jnp.bfloat16)
    lives = []

    for i in range(2):
        _, first, live = page_facts(facts, half, 2 * place + i)
        lives.append(live)
        stand_in = jnp.broadcast_to(mine[i][0][:, :1], (HD, PAGE))
        if i == 0:
            pages = [(*d[0], 2 * place - 7)]
        else:
            pages = [(*mine[0], 2 * place)]
        pages.append((*mine[i], None))
        pages += [(*a[p], 2 * place - 4 + p) for p in range(2)]
        pages += [(*c[p], page_c + p) for p in range(2)]
        pages += [(*be[p], page_be + p) for p in range(2)]
        for spot, (k, v, number) in enumerate(pages):
            count = one
            if number is not None:
                seen = jnp.full((PAGE, HD), number >= first)
                k = jnp.where(seen, k, stand_in)
                v = jnp.where(seen, v, zero)
                count = jnp.where(seen, one, zero)
            at = slice(spot * PAGE, (spot + 1) * PAGE)
            keys[i, :HD, at] = k
            keys[i, HD:, at] = k
            values[i, at, :HD] = v
            values[i, at, HD:] = count

    heads_at_once = ROWS // PAGE
    blocks = [(i, start) for i in range(2) for start in range(0, GROUP, heads_at_once)]

    def halves(query):
        query = query.astype(jnp.float32) * SCALE
        high = query.astype(jnp.bfloat16)
        low = (query - high.astype(jnp.float32)).astype(jnp.bfloat16)
        return jnp.concatenate([high, low], axis=1)

    def queries(i, start):
        return halves(
            jnp.concatenate(
                [
                    q_ref[i * PAGE:(i + 1) * PAGE, h * HD:(h + 1) * HD]
                    for h in range(start, start + heads_at_once)
                ],
                axis=0,
            )
        )

    def divided(mixed, live):
        total = mixed[:, HD:]
        near = pl.reciprocal(total, approx=True)
        near = near * (2.0 - total * near)
        token = lax.broadcasted_iota(jnp.int32, (total.shape[0], HD), 0) % PAGE
        return jnp.where(token < live, mixed[:, :HD] * near, 0.0).astype(jnp.bfloat16)

    tiles = [slice(t, t + 2 * PAGE) for t in range(0, MAXP * PAGE, 2 * PAGE)]

    def own_scores(query, i, repeat):
        own = dot(query, keys[i, :, tiles[0]])
        bias = jnp.concatenate([causal[...]] * repeat, axis=0)
        return jnp.concatenate([own[:, :PAGE], own[:, PAGE:] + bias], axis=1)

    def mix(block, slot, largest):
        i, start = block
        mixed = dot(probs[slot][...], values[i])
        out = divided(mixed, lives[i])
        for number in range(heads_at_once):
            h = start + number
            o_ref[i * PAGE:(i + 1) * PAGE, h * HD:(h + 1) * HD] = out[number * PAGE:(number + 1) * PAGE]
        return jnp.maximum(largest, mixed[:, HD:])

    largest = jnp.zeros((ROWS, HD), jnp.float32)
    for index in range(len(blocks) + 1):
        if index < len(blocks):
            i, slot = blocks[index][0], index % 2
            query = queries(*blocks[index])
            own = own_scores(query, i, heads_at_once)
            top = jnp.max(own, axis=1, keepdims=True)
            probs[slot][:, tiles[0]] = jnp.exp(own - top).astype(jnp.bfloat16)
        if index > 0:
            largest = mix(blocks[index - 1], 1 - slot if index < len(blocks) else slot, largest)
        if index < len(blocks):
            for at in tiles[1:]:
                other = dot(query, keys[i, :, at])
                probs[slot][:, at] = jnp.exp(other - top).astype(jnp.bfloat16)

    @pl.when(jnp.logical_not(jnp.max(largest) < 1e30))
    def _():
        def one(index, carry):
            i, h = index // GROUP, index % GROUP
            rows = pl.ds(pl.multiple_of(i * PAGE, PAGE), PAGE)
            columns = pl.ds(pl.multiple_of(h * HD, HD), HD)
            query = halves(q_ref[rows, columns])
            scores = [own_scores(query, i, 1)] + [dot(query, keys[i, :, at]) for at in tiles[1:]]
            top = jnp.max(functools.reduce(jnp.maximum, scores), axis=1, keepdims=True)
            mixed = jnp.zeros((PAGE, 2 * HD), jnp.float32)
            for score, at in zip(scores, tiles):
                mixed = mixed + dot(jnp.exp(score - top).astype(jnp.bfloat16), values[i, at])
            o_ref[rows, columns] = divided(mixed, jnp.where(i == 0, lives[0], lives[1]))
            return carry

        lax.fori_loop(0, 2 * GROUP, one, 0)


def prompt_heads(base, n, low, high, facts, query, blocks, done):
    tok = query.shape[0]

    wide = pl.BlockSpec((tok, GROUP * HD), lambda j, *_: (0, base + low + j))
    operands = [facts, query, *blocks]
    specs = [wide] + [VMEM] * len(blocks)
    aliases = {}
    if done is not None:
        aliases = {len(operands): 0}
        operands.append(done)
        specs.append(pl.BlockSpec(memory_space=pl.ANY))
    return pl.pallas_call(
        functools.partial(prompt_kernel, n, low),
        out_shape=jax.ShapeDtypeStruct(query.shape, jnp.bfloat16),
        grid_spec=pltpu.PrefetchScalarGridSpec(
            num_scalar_prefetch=1,
            grid=(high - low,),
            in_specs=specs,
            out_specs=wide,
            scratch_shapes=[
                pltpu.VMEM((2, 2 * HD, MAXP * PAGE), jnp.bfloat16),
                pltpu.VMEM((2, MAXP * PAGE, 2 * HD), jnp.bfloat16),
                pltpu.VMEM((PAGE, PAGE), jnp.float32),
                pltpu.VMEM((ROWS, MAXP * PAGE), jnp.bfloat16),
                pltpu.VMEM((ROWS, MAXP * PAGE), jnp.bfloat16),
            ],
        ),
        input_output_aliases=aliases,
        name="prompt_attention",
        **params(20),
    )(*operands)


def stat_rows(rows):
    return 16 - rows % 16


def choose_kernel(facts, q_ref, o_ref, rows_ref, turned):
    requests, here = q_ref.shape[1], q_ref.shape[2] // HD
    other = 1 - lax.axis_index("section")
    for s in range(STEPS):
        query = q_ref[s].astype(jnp.float32)
        for r in range(requests):
            for h in range(here):
                row = h * STEPS + s
                turned[r, row:row + 1] = query[r:r + 1, h * HD:(h + 1) * HD]
    rows_ref[...] = turned[...].astype(jnp.bfloat16)

    def one(lane, carry):
        for i in range(2):
            owner = page_facts(facts, other, 2 * lane + i)[0]
            o_ref[lane, i] = turned[owner].astype(jnp.bfloat16)
        return carry

    lax.fori_loop(0, o_ref.shape[0], one, 0)


def chosen_queries(facts, query, lanes):
    rows = (query.shape[1], QH // lanes * STEPS, HD)
    return pl.pallas_call(
        choose_kernel,
        out_shape=(
            jax.ShapeDtypeStruct((lanes, 2, *rows[1:]), jnp.bfloat16),
            jax.ShapeDtypeStruct(rows, jnp.bfloat16),
        ),
        in_specs=[SMEM, VMEM],
        out_specs=(VMEM, VMEM),
        scratch_shapes=[pltpu.VMEM(rows, jnp.float32)],
        name="choose_queries",
        **params(32),
    )(facts, query)


def partial_kernel(lanes, facts, q_ref, *rest):
    *packed, o_ref = rest
    split = GROUP // (QH // lanes)
    width = QH // lanes * STEPS
    extra = stat_rows(2 * width)
    half, place = lax.axis_index("section"), lax.axis_index("tp")
    group = GROUP * STEPS
    height = 2 * KVH * group
    lane = lax.broadcasted_iota(jnp.int32, (height, PAGE), 1)
    later = lax.broadcasted_iota(jnp.int32, (height, PAGE), 0) // group % 2 == 1
    spot = lax.broadcasted_iota(jnp.int32, (2 * width, PAGE), 0)
    across = lax.broadcasted_iota(jnp.int32, (2 * width, PAGE), 1)
    line = lax.broadcasted_iota(jnp.int32, (extra, PAGE), 0)
    lives = [page_facts(facts, half, 2 * place + i)[2] for i in range(2)]
    places = [(block, j, n) for block, n in zip(packed, CHUNKS) for j in range(n)]
    scores, values = [], []
    for k, (block, j, n) in enumerate(places):
        for i in range(2):
            query = jnp.concatenate([q_ref[k * split + t, i] for t in range(split)], axis=0)
            scores.append(dot(query, block[i, j * HD:(j + 1) * HD]))
            values.append(block[i, (n + j) * HD:(n + j + 1) * HD])
    score = jnp.concatenate(scores, axis=0) * SCALE
    score = jnp.where(lane < jnp.where(later, lives[1], lives[0]), score, LOW)
    top = jnp.max(score, axis=1, keepdims=True)
    terms = jnp.exp(score - top)
    total = jnp.sum(terms, axis=1, keepdims=True)
    high = terms.astype(jnp.bfloat16)
    low = (terms - high.astype(jnp.float32)).astype(jnp.bfloat16)
    mixed = jnp.concatenate(
        [
            dot(high[m * group:(m + 1) * group], v) + dot(low[m * group:(m + 1) * group], v)
            for m, v in enumerate(values)
        ],
        axis=0,
    ) / total
    sums = top + jnp.log(total)
    for k in range(KVH):
        for t in range(split):
            begins = [(2 * k + i) * group + t * width for i in range(2)]
            both = jnp.concatenate([sums[at:at + width] for at in begins], axis=0)
            turned = jnp.sum(jnp.where(spot == across, both, 0.0), axis=0, keepdims=True)
            first = turned.astype(jnp.bfloat16).astype(jnp.float32)
            rest = turned - first
            second = rest.astype(jnp.bfloat16).astype(jnp.float32)
            stat = jnp.where(line == 0, first, jnp.where(line == 1, second, rest - second))
            stat = jnp.where(line < 3, stat, 0.0)
            block = jnp.concatenate([mixed[at:at + width] for at in begins] + [stat], axis=0)
            o_ref[k * split + t] = block.astype(jnp.bfloat16)


def partial_decode(facts, query, packed, lanes):
    rows = 2 * (QH // lanes) * STEPS
    return pl.pallas_call(
        functools.partial(partial_kernel, lanes),
        out_shape=jax.ShapeDtypeStruct((lanes, rows + stat_rows(rows), HD), jnp.bfloat16),
        in_specs=[SMEM, VMEM] + [VMEM] * len(packed),
        out_specs=VMEM,
        name="partial_decode",
        **params(32),
    )(facts, query, *packed)


def merge_kernel(lanes, facts, parts_ref, q_ref, k_ref, v_ref, o_ref):
    requests = q_ref.shape[0]
    width = (QH // lanes) * STEPS
    other, place = 1 - lax.axis_index("section"), lax.axis_index("tp")
    head = place * (QH // lanes) // GROUP
    spot = lax.broadcasted_iota(jnp.int32, (width, PAGE), 0)
    across = lax.broadcasted_iota(jnp.int32, (width, PAGE), 1)
    step = lax.broadcasted_iota(jnp.int32, (width, 1), 0) % STEPS
    end = 0
    for r in range(requests):
        start, end = end, end + facts[other, r]
        query = q_ref[r].astype(jnp.float32)
        keys = k_ref[r, head].astype(jnp.float32)
        values = v_ref[r, head].astype(jnp.float32)
        tops, vectors = [], []
        for u in range(STEPS):
            score = jnp.sum(query * keys[u:u + 1], axis=1, keepdims=True) * SCALE
            tops.append(jnp.where(u <= step, score, LOW))
            vectors.append(values[u:u + 1])
        for j in range(MAXP):
            page = jnp.minimum(start + j, 2 * lanes - 1)
            block = parts_ref[page // 2].astype(jnp.float32)
            later = jnp.full((width, HD), page % 2 == 1)
            vectors.append(jnp.where(later, block[width:2 * width], block[:width]))
            stat = jnp.sum(block[2 * width:2 * width + 8], axis=0, keepdims=True)
            stat = jnp.sum(
                jnp.where(across - page % 2 * width == spot, stat, 0.0), axis=1, keepdims=True
            )
            tops.append(jnp.where(jnp.full((width, 1), start + j < end), stat, LOW))
        top = functools.reduce(jnp.maximum, tops)
        weights = [jnp.exp(t - top) for t in tops]
        total = functools.reduce(jnp.add, weights)
        mixed = functools.reduce(jnp.add, [w * x for w, x in zip(weights, vectors)])
        o_ref[r] = (mixed / total).astype(jnp.bfloat16)


def merged(facts, parts, query, new_key, new_value, lanes):
    requests = query.shape[0]
    fresh = [
        jnp.transpose(x.reshape(STEPS, requests, KVH, HD), (1, 2, 0, 3)) for x in (new_key, new_value)
    ]
    out = pl.pallas_call(
        functools.partial(merge_kernel, lanes),
        out_shape=jax.ShapeDtypeStruct(query.shape, jnp.bfloat16),
        in_specs=[SMEM, VMEM, VMEM, VMEM, VMEM],
        out_specs=VMEM,
        name="merge_decode",
        **params(32),
    )(facts, parts, query, *fresh)
    out = jnp.transpose(out.reshape(requests, QH // lanes, STEPS, HD), (2, 0, 1, 3))
    return out.reshape(STEPS, requests, QH // lanes * HD)


def other_half(x):
    return lax.ppermute(x, "section", [(0, 1), (1, 0)])


def after(x, *earlier):
    return lax.optimization_barrier((x, *earlier))[0]


def on_device(
    prefill_query, prefill_key, prefill_value, counts, fills, dec_query, dec_key, dec_value
):
    lanes = lax.axis_size("tp")
    query, key, value = prefill_query[0], prefill_key[0], prefill_value[0]
    facts = jnp.concatenate([counts, fills], axis=1)
    ahead = [(i, i + 2) for i in range(lanes - 2)]
    ahead_again = [(i, i + 2) for i in range(2, lanes - 2)]
    beside = [(i, i + 1) for i in range(0, lanes, 2)]
    trade = [(i, i ^ 1) for i in range(2, lanes)]
    back = [(i, i - 1) for i in range(5, lanes, 2)]
    bases = [sum(CHUNKS[:g]) for g in range(len(CHUNKS))]
    mine = [pack(base, n, key, value) for base, n in zip(bases, CHUNKS)]
    chosen, dec_rows = chosen_queries(facts, dec_query[0], lanes)
    wanted = lax.all_to_all(chosen, "tp", split_axis=0, concat_axis=0, tiled=True)
    parts = partial_decode(facts, other_half(wanted), mine, lanes)
    parts = lax.all_to_all(parts, "tp", split_axis=0, concat_axis=0, tiled=True)
    dec_out = merged(facts, other_half(parts), dec_rows, dec_key[0], dec_value[0], lanes)

    received = []
    for g, block in enumerate(mine):
        a = lax.ppermute(after(block, wanted) if g else block, "tp", ahead)
        b = lax.ppermute(after(block, received[0][2]) if g else block, "tp", beside)
        c = lax.ppermute(a if g else after(a, b), "tp", trade)
        d = jnp.concatenate([a[1:], c[:1]], axis=0)
        d = lax.ppermute(after(d, parts) if g else d, "tp", ahead_again)
        late = d
        if g:
            base, n = bases[0], CHUNKS[0]
            blocks = (mine[0], *received[0])
            out = prompt_heads(base, n, 0, n // 2, facts, query, blocks, None)
            late = after(d, out)
            out = after(out, d)
            out = prompt_heads(base, n, n // 2, n, facts, query, blocks, out)
        e = lax.ppermute(late[0], "tp", back)
        received.append((a, b, c, d, e))
    out = after(out, dec_out)
    out = prompt_heads(bases[1], CHUNKS[1], 0, CHUNKS[1], facts, query, (mine[1], *received[1]), out)
    return (out[None], dec_out[None])


def solution(mesh):
    placed = (
        P("section", ("groups", "tp"), None),
        P("section", ("groups", "tp"), None),
        P("section", ("groups", "tp"), None),
        P(None, "groups"),
        P(None, "groups"),
        P("section", None, "groups", "tp"),
        P("section", None, "groups", None),
        P("section", None, "groups", None),
    )
    return jax.shard_map(
        on_device,
        mesh=mesh,
        in_specs=placed,
        out_specs=(P("section", ("groups", "tp"), None), P("section", None, "groups", "tp")),
        check_vma=False,
    )
```

```python
import functools
import math

import jax
import jax.numpy as jnp
from jax import lax
from jax.experimental import pallas as pl
from jax.experimental.pallas import tpu as pltpu
from jax.sharding import PartitionSpec as P

QH = 64
KVH = 8
HD = 128
PAGE = 128
MAXP = 8
STEPS = 4
GROUP = QH // KVH
SCALE = HD ** (-0.5)
EXP2_SCALE = SCALE * math.log2(math.e)
LOW = -1e30
BACK = 4
CHUNKS = (3, 3, 2)
ROWS = 512
SMEM = pl.BlockSpec(memory_space=pltpu.SMEM)
VMEM = pl.BlockSpec(memory_space=pltpu.VMEM)


def dot(a, b):
    return jnp.dot(a, b, preferred_element_type=jnp.float32)


def page_facts(facts, half, page):
    requests = facts.shape[1] // 2
    owner, first, live, end = -1, 0, PAGE, 0
    for r in range(requests):
        start, end = end, end + facts[half, r]
        begun = start <= page
        owner = jnp.where(begun, r, owner)
        first = jnp.where(begun, start, first)
        live = jnp.where(end - 1 == page, facts[half, requests + r], live)
    return owner, first, live


def params(limit):
    return dict(
        compiler_params=pltpu.CompilerParams(vmem_limit_bytes=limit << 20),
        cost_estimate=pl.CostEstimate(flops=1, bytes_accessed=1, transcendentals=0),
    )


def pack_kernel(k_ref, v_ref, o_ref):
    for j in range(o_ref.shape[2] // HD):
        columns = slice(j * HD, (j + 1) * HD)
        for p in range(2):
            rows = slice(p * PAGE, (p + 1) * PAGE)
            turned = jnp.transpose(k_ref[rows, columns].astype(jnp.float32))
            o_ref[p, 0, columns] = turned.astype(jnp.bfloat16)
            o_ref[p, 1, columns] = v_ref[rows, columns]


def pack(base, n, key, value):
    return pl.pallas_call(
        pack_kernel,
        out_shape=jax.ShapeDtypeStruct((2, 2, n * HD, PAGE), jnp.bfloat16),
        in_specs=[VMEM, VMEM],
        out_specs=VMEM,
        name="pack",
        **params(32),
    )(*(x[:, base * HD:(base + n) * HD] for x in (key, value)))


def prompt_kernel(facts, place_ref, q_ref, *rest):
    blocks, (o_ref, keys, values, causal, *probs) = rest[:2 * (BACK + 1)], rest[-6:]
    half, place = lax.axis_index("section"), place_ref[0]
    row = lax.broadcasted_iota(jnp.int32, (PAGE, PAGE), 0)
    col = lax.broadcasted_iota(jnp.int32, (PAGE, PAGE), 1)
    causal[...] = jnp.where(col <= row, 0.0, LOW)
    zero = jnp.zeros((PAGE, HD), jnp.bfloat16)
    lives, counted = [], []

    for i in range(2):
        _, first, live = page_facts(facts, half, 2 * place + i)
        lives.append(live)
        stand_in = jnp.broadcast_to(blocks[0][0, i, 0, :, :1], (HD, PAGE))
        pages = [(BACK, 1) if i == 0 else (0, 0), (0, i)]
        pages += [(back, p) for back in range(1, BACK) for p in range(2)]
        seen = [2 * (place - back) + p >= first for back, p in pages]
        counted.append([jnp.where(x, 1.0, 0.0) for x in seen])
        for spot, (back, p) in enumerate(pages):
            mask = jnp.full((PAGE, HD), seen[spot])
            at = slice(spot * PAGE, (spot + 1) * PAGE)
            keys[i, :, at] = jnp.where(mask, blocks[2 * back][0, p, 0], stand_in)
            values[i, at] = jnp.where(mask, blocks[2 * back + 1][0, p, 0], zero)

    heads_at_once = ROWS // PAGE
    blocks_of_rows = [(i, start) for i in range(2) for start in range(0, GROUP, heads_at_once)]
    tiles = [slice(t, t + 2 * PAGE) for t in range(0, MAXP * PAGE, 2 * PAGE)]

    def own_scores(query, i, repeat):
        own = dot(query, keys[i, :, tiles[0]]) * EXP2_SCALE
        bias = jnp.concatenate([causal[...]] * repeat, axis=0)
        return jnp.concatenate([own[:, :PAGE], own[:, PAGE:] + bias], axis=1)

    def weighed(terms, i, tile):
        counts = counted[i][2 * tile:2 * tile + 2]
        return terms[:, :PAGE] * counts[0] + terms[:, PAGE:] * counts[1]

    def divided(mixed, total, live):
        token = lax.broadcasted_iota(jnp.int32, mixed.shape, 0) % PAGE
        return jnp.where(token < live, mixed / total, 0.0).astype(jnp.bfloat16)

    def mix(block, slot, total):
        i, start = block
        out = divided(dot(probs[slot][...], values[i]), total, lives[i])
        for number in range(heads_at_once):
            h = start + number
            o_ref[i * PAGE:(i + 1) * PAGE, h * HD:(h + 1) * HD] = out[number * PAGE:(number + 1) * PAGE]

    largest = jnp.zeros((ROWS, 1), jnp.float32)
    before = None
    for index, (i, start) in enumerate(blocks_of_rows):
        slot = index % 2
        query = jnp.concatenate(
            [
                q_ref[i * PAGE:(i + 1) * PAGE, h * HD:(h + 1) * HD]
                for h in range(start, start + heads_at_once)
            ],
            axis=0,
        )
        own = own_scores(query, i, heads_at_once)
        top = jnp.max(own, axis=1, keepdims=True)
        terms = jnp.exp2(own - top)
        probs[slot][:, tiles[0]] = terms.astype(jnp.bfloat16)
        total = weighed(terms, i, 0)
        if before is not None:
            mix(*before)
        for tile in range(1, len(tiles)):
            other = dot(query, keys[i, :, tiles[tile]]) * EXP2_SCALE
            terms = jnp.exp2(other - top)
            probs[slot][:, tiles[tile]] = terms.astype(jnp.bfloat16)
            total = total + weighed(terms, i, tile)
        total = jnp.sum(total, axis=1, keepdims=True)
        largest = jnp.maximum(largest, total)
        before = (i, start), slot, total
    mix(*before)

    @pl.when(jnp.logical_not(jnp.max(largest) < 1e30))
    def _():
        def one(index, carry):
            i, h = index // GROUP, index % GROUP
            rows = pl.ds(pl.multiple_of(i * PAGE, PAGE), PAGE)
            columns = pl.ds(pl.multiple_of(h * HD, HD), HD)
            query = q_ref[rows, columns]
            scores = [own_scores(query, i, 1)]
            scores += [dot(query, keys[i, :, at]) * EXP2_SCALE for at in tiles[1:]]
            top = jnp.max(functools.reduce(jnp.maximum, scores), axis=1, keepdims=True)
            mixed = jnp.zeros((PAGE, HD), jnp.float32)
            total = jnp.zeros((PAGE, HD), jnp.float32)
            for tile, (score, at) in enumerate(zip(scores, tiles)):
                terms = jnp.exp2(score - top)
                mixed = mixed + dot(terms.astype(jnp.bfloat16), values[i, at])
                for p in range(2):
                    count = jnp.where(i == 0, counted[0][2 * tile + p], counted[1][2 * tile + p])
                    total = total + terms[:, p * PAGE:(p + 1) * PAGE] * count
            total = jnp.sum(total, axis=1, keepdims=True)
            o_ref[rows, columns] = divided(mixed, total, jnp.where(i == 0, lives[0], lives[1]))
            return carry

        lax.fori_loop(0, 2 * GROUP, one, 0)


def prompt_heads(base, n, facts, place, query, held, done):
    tok = query.shape[0]

    def block(back, which):
        return pl.BlockSpec(
            (1, 2, 1, HD, PAGE),
            lambda j, facts, place: (jnp.maximum(place[0] - back, 0), 0, which, j, 0),
        )

    wide = pl.BlockSpec((tok, GROUP * HD), lambda j, *_: (0, base + j))
    specs = [wide] + [block(back, which) for back in range(BACK + 1) for which in range(2)]
    operands = [facts, place, query] + [held] * (len(specs) - 1)
    aliases = {}
    if done is not None:
        aliases = {len(operands): 0}
        operands.append(done)
        specs.append(pl.BlockSpec(memory_space=pl.ANY))
    return pl.pallas_call(
        prompt_kernel,
        out_shape=jax.ShapeDtypeStruct(query.shape, jnp.bfloat16),
        grid_spec=pltpu.PrefetchScalarGridSpec(
            num_scalar_prefetch=2,
            grid=(n,),
            in_specs=specs,
            out_specs=wide,
            scratch_shapes=[
                pltpu.VMEM((2, HD, MAXP * PAGE), jnp.bfloat16),
                pltpu.VMEM((2, MAXP * PAGE, HD), jnp.bfloat16),
                pltpu.VMEM((PAGE, PAGE), jnp.float32),
                pltpu.VMEM((ROWS, MAXP * PAGE), jnp.bfloat16),
                pltpu.VMEM((ROWS, MAXP * PAGE), jnp.bfloat16),
            ],
        ),
        input_output_aliases=aliases,
        name="prompt_attention",
        **params(48),
    )(*operands)


def pick_kernel(bases, head_ref, *rest):
    *held, o_ref, sem = rest
    for base, ref in zip(bases, held):
        local = head_ref[0] - base

        @pl.when((local >= 0) & (local < ref.shape[3] // HD))
        def _():
            rows = pl.ds(pl.multiple_of(local * HD, HD), HD)
            copy = pltpu.make_async_copy(ref.at[:, :, :, rows], o_ref, sem)
            copy.start()
            copy.wait()


def picked_head(bases, head, held):
    spread = pl.BlockSpec(memory_space=pl.ANY)
    return pl.pallas_call(
        functools.partial(pick_kernel, bases),
        out_shape=jax.ShapeDtypeStruct((*held[0].shape[:3], HD, PAGE), jnp.bfloat16),
        in_specs=[SMEM] + [spread] * len(held),
        out_specs=spread,
        scratch_shapes=[pltpu.SemaphoreType.DMA],
        name="pick_head",
        **params(48),
    )(head, *held)


def decode_kernel(facts, head_ref, pool_ref, q_ref, k_ref, v_ref, o_ref):
    requests, width = q_ref.shape[:2]
    last = 2 * pool_ref.shape[0] - 1
    other = 1 - lax.axis_index("section")
    lane = lax.broadcasted_iota(jnp.int32, (width, PAGE), 1)
    step = lax.broadcasted_iota(jnp.int32, (width, 1), 0) % STEPS
    scores, fresh, pages = [], [], []
    end = 0
    for r in range(requests):
        start, end = end, end + facts[other, r]
        length = PAGE * (end - start - 1) + facts[other, requests + r]
        query = q_ref[r]
        numbers = [jnp.minimum(start + j, last) for j in range(MAXP)]
        pages.append([(number // 2, number % 2) for number in numbers])
        tiles = []
        for j, at in enumerate(pages[r]):
            score = dot(query, pool_ref[at[0], at[1], 0]) * SCALE
            tiles.append(jnp.where(lane < length - j * PAGE, score, LOW))
        scores.append(jnp.concatenate(tiles, axis=1))
        keys = k_ref[r, head_ref[0]].astype(jnp.float32)
        wide = query.astype(jnp.float32)
        news = [jnp.sum(wide * keys[u:u + 1], axis=1, keepdims=True) * SCALE for u in range(STEPS)]
        fresh.append([jnp.where(u <= step, x, LOW) for u, x in enumerate(news)])
    score = jnp.concatenate(scores, axis=0)
    fresh = [jnp.concatenate([x[u] for x in fresh], axis=0) for u in range(STEPS)]
    top = functools.reduce(jnp.maximum, fresh + [jnp.max(score, axis=1, keepdims=True)])
    terms = jnp.exp(score - top)
    fresh = [jnp.exp(x - top) for x in fresh]
    total = functools.reduce(jnp.add, fresh + [jnp.sum(terms, axis=1, keepdims=True)])
    high = terms.astype(jnp.bfloat16)
    low = (terms - high.astype(jnp.float32)).astype(jnp.bfloat16)
    for r in range(requests):
        rows = slice(r * width, (r + 1) * width)
        new_values = v_ref[r, head_ref[0]].astype(jnp.float32)
        mixed = functools.reduce(
            jnp.add, [fresh[u][rows] * new_values[u:u + 1] for u in range(STEPS)]
        )
        for j, at in enumerate(pages[r]):
            values = pool_ref[at[0], at[1], 1]
            columns = slice(j * PAGE, (j + 1) * PAGE)
            mixed = mixed + dot(high[rows, columns], values) + dot(low[rows, columns], values)
        o_ref[r] = (mixed / total[rows]).astype(jnp.bfloat16)


def decoded(facts, head, pool, query, new_key, new_value, lanes):
    requests, here = query.shape[1], QH // lanes
    query = jnp.transpose(query.reshape(STEPS, requests, here, HD), (1, 2, 0, 3))
    query = query.reshape(requests, here * STEPS, HD)
    fresh = [
        jnp.transpose(x.reshape(STEPS, requests, KVH, HD), (1, 2, 0, 3)) for x in (new_key, new_value)
    ]
    out = pl.pallas_call(
        decode_kernel,
        out_shape=jax.ShapeDtypeStruct(query.shape, jnp.bfloat16),
        in_specs=[SMEM, SMEM, VMEM, VMEM, VMEM, VMEM],
        out_specs=VMEM,
        name="decode_attention",
        **params(32),
    )(facts, head, pool, query, *fresh)
    out = jnp.transpose(out.reshape(requests, here, STEPS, HD), (2, 0, 1, 3))
    return out.reshape(STEPS, requests, here * HD)


def after(x, *earlier):
    return lax.optimization_barrier((x, *earlier))[0]


def on_device(
    prefill_query, prefill_key, prefill_value, counts, fills, dec_query, dec_key, dec_value
):
    lanes = lax.axis_size("tp")
    query, key, value = prefill_query[0], prefill_key[0], prefill_value[0]
    facts = jnp.concatenate([counts, fills], axis=1)
    place = lax.axis_index("tp").reshape(1)
    head = place * (QH // lanes) // GROUP
    bases = [sum(CHUNKS[:g]) for g in range(len(CHUNKS))]

    held, packed = [], None
    for base, n in zip(bases, CHUNKS):
        packed = pack(base, n, key if packed is None else after(key, packed), value)
        held.append(lax.all_gather(packed, "tp"))
    out = None
    for g, (base, n) in enumerate(zip(bases, CHUNKS)):
        if g + 1 == len(CHUNKS):
            head = after(head, out)
            pool = lax.ppermute(picked_head(bases, head, held), "section", [(0, 1), (1, 0)])
        out = prompt_heads(base, n, facts, place, query, held[g], out)
    dec_out = decoded(facts, head, pool, dec_query[0], dec_key[0], dec_value[0], lanes)
    return (out[None], dec_out[None])


def solution(mesh):
    placed = (
        P("section", ("groups", "tp"), None),
        P("section", ("groups", "tp"), None),
        P("section", ("groups", "tp"), None),
        P(None, "groups"),
        P(None, "groups"),
        P("section", None, "groups", "tp"),
        P("section", None, "groups", None),
        P("section", None, "groups", None),
    )
    return jax.shard_map(
        on_device,
        mesh=mesh,
        in_specs=placed,
        out_specs=(P("section", ("groups", "tp"), None), P("section", None, "groups", "tp")),
        check_vma=False,
    )
```

```python
import functools
import math

import jax
import jax.numpy as jnp
from jax import lax
from jax.experimental import pallas as pl
from jax.experimental.pallas import tpu as pltpu
from jax.sharding import PartitionSpec as P

QH = 64
KVH = 8
HD = 128
PAGE = 128
MAXP = 8
STEPS = 4
GROUP = QH // KVH
SCALE = HD ** (-0.5)
EXP2_SCALE = SCALE * math.log2(math.e)
LOW = -1e30
CHUNKS = (3, 5)
CUTS = (2, 3)
ROWS = 512
SMEM = pl.BlockSpec(memory_space=pltpu.SMEM)
VMEM = pl.BlockSpec(memory_space=pltpu.VMEM)


def dot(a, b):
    return jnp.dot(a, b, preferred_element_type=jnp.float32)


def page_facts(facts, half, page):
    requests = facts.shape[1] // 2
    owner, first, live, end = -1, 0, PAGE, 0
    for r in range(requests):
        start, end = end, end + facts[half, r]
        begun = start <= page
        owner = jnp.where(begun, r, owner)
        first = jnp.where(begun, start, first)
        live = jnp.where(end - 1 == page, facts[half, requests + r], live)
    return owner, first, live


def params(limit):
    return dict(
        compiler_params=pltpu.CompilerParams(vmem_limit_bytes=limit << 20),
        cost_estimate=pl.CostEstimate(flops=1, bytes_accessed=1, transcendentals=0),
    )


def pack_kernel(base, by_head, k_ref, v_ref, *rest):
    o_ref, k_part, v_part, sems = rest[-4:]
    n = k_part.shape[1] // HD
    own = slice(base * HD, (base + n) * HD)
    copies = [
        pltpu.make_async_copy(source.at[:, own], part, sems.at[spot])
        for spot, (source, part) in enumerate(((k_ref, k_part), (v_ref, v_part)))
    ]
    for copy in copies:
        copy.start()
    for copy in copies:
        copy.wait()
    for j in range(n):
        columns = slice(j * HD, (j + 1) * HD)
        for p in range(2):
            rows = slice(p * PAGE, (p + 1) * PAGE)
            turned = jnp.transpose(k_part[rows, columns].astype(jnp.float32)).astype(jnp.bfloat16)
            if by_head:
                o_ref[j, p, 0] = turned
                o_ref[j, p, 1] = v_part[rows, columns]
            else:
                o_ref[p, columns] = turned
                o_ref[p, (n + j) * HD:(n + j + 1) * HD] = v_part[rows, columns]


def pack(base, n, key, value, by_head=False):
    shape = (n, 2, 2, HD, PAGE) if by_head else (2, 2 * n * HD, PAGE)
    part = pltpu.VMEM((key.shape[0], n * HD), jnp.bfloat16)
    return pl.pallas_call(
        functools.partial(pack_kernel, base, by_head),
        out_shape=jax.ShapeDtypeStruct(shape, jnp.bfloat16),
        in_specs=[pl.BlockSpec(memory_space=pl.ANY)] * 2,
        out_specs=VMEM,
        scratch_shapes=[part, part, pltpu.SemaphoreType.DMA((2,))],
        name="pack",
        **params(48),
    )(key, value)


def prompt_kernel(n, low, facts, q_ref, *rest):
    o_ref, keys, values, causal, *slots = rest[-8:]
    scores, probs = slots[:2], slots[2:]
    half, place = lax.axis_index("section"), lax.axis_index("tp")
    head = low + pl.program_id(0)
    spots = [pl.ds(pl.multiple_of((x + head) * HD, HD), HD) for x in (0, n)]
    mine, a, b, c, d = [[[x[p, at] for at in spots] for p in range(2)] for x in rest[:5]]
    e = [rest[5][at] for at in spots]
    even = place % 2 == 0
    near, far = 2 * place - 2, 2 * place - 6
    page_c = jnp.where(even, near, far)
    page_be = jnp.where(even, far, near)
    choose = jnp.full((HD, PAGE), even)
    be = [
        [jnp.where(choose, x, y) for x, y in zip(late, b[p])] for p, late in enumerate((d[1], e))
    ]
    row = lax.broadcasted_iota(jnp.int32, (PAGE, PAGE), 0)
    col = lax.broadcasted_iota(jnp.int32, (PAGE, PAGE), 1)
    causal[...] = jnp.where(col <= row, 0.0, LOW)
    zero = jnp.zeros((PAGE, HD), jnp.bfloat16)
    lives, counted = [], []

    for i in range(2):
        _, first, live = page_facts(facts, half, 2 * place + i)
        lives.append(live)
        stand_in = jnp.broadcast_to(mine[i][0][:, :1], (HD, PAGE))
        pages = [(*d[0], 2 * place - 7) if i == 0 else (*mine[0], 2 * place)]
        pages.append((*mine[i], 2 * place + i))
        pages += [(*a[p], 2 * place - 4 + p) for p in range(2)]
        pages += [(*c[p], page_c + p) for p in range(2)]
        pages += [(*be[p], page_be + p) for p in range(2)]
        counted.append([jnp.where(page[2] >= first, 1.0, 0.0) for page in pages])
        for spot, (k, v, number) in enumerate(pages):
            seen = jnp.full((PAGE, HD), number >= first)
            at = slice(spot * PAGE, (spot + 1) * PAGE)
            keys[i, :, at] = jnp.where(seen, k, stand_in)
            values[i, at] = jnp.where(seen, v, zero)

    heads_at_once = ROWS // PAGE
    blocks = [(i, start) for i in range(2) for start in range(0, GROUP, heads_at_once)]
    pages = [slice(t, t + PAGE) for t in range(0, MAXP * PAGE, PAGE)]
    token = lax.broadcasted_iota(jnp.int32, (ROWS, HD), 0) % PAGE

    def score(index):
        i, start = blocks[index]
        query = jnp.concatenate(
            [
                q_ref[i * PAGE:(i + 1) * PAGE, h * HD:(h + 1) * HD]
                for h in range(start, start + heads_at_once)
            ],
            axis=0,
        )
        scores[index % 2][...] = dot(query, keys[i])

    def soften(index):
        i = blocks[index][0]
        pieces = [scores[index % 2][:, at] for at in pages]
        pieces[1] = pieces[1] + jnp.concatenate([causal[...]] * heads_at_once, axis=0)
        top = jnp.max(functools.reduce(jnp.maximum, pieces), axis=1, keepdims=True) * EXP2_SCALE
        total = None
        for piece, at, count in zip(pieces, pages, counted[i]):
            terms = jnp.exp2(piece * EXP2_SCALE - top)
            probs[index % 2][:, at] = terms.astype(jnp.bfloat16)
            total = terms * count if total is None else total + terms * count
        return jnp.sum(total, axis=1, keepdims=True)

    def mix(index, total):
        i, start = blocks[index]
        middle = MAXP * PAGE // 2
        mixed = dot(probs[index % 2][:, :middle], values[i, :middle])
        mixed = mixed + dot(probs[index % 2][:, middle:], values[i, middle:])
        out = jnp.where(token < lives[i], mixed / total, 0.0).astype(jnp.bfloat16)
        for number in range(heads_at_once):
            h = start + number
            o_ref[i * PAGE:(i + 1) * PAGE, h * HD:(h + 1) * HD] = out[number * PAGE:(number + 1) * PAGE]

    score(0)
    total = None
    for index in range(len(blocks)):
        if index + 1 < len(blocks):
            score(index + 1)
        if index > 0:
            mix(index - 1, total)
        total = soften(index)
    mix(len(blocks) - 1, total)


def prompt_heads(base, n, low, high, facts, query, blocks, done):
    tok = query.shape[0]
    wide = pl.BlockSpec((tok, GROUP * HD), lambda j, *_: (0, base + low + j))
    operands = [facts, query, *blocks]
    specs = [wide] + [VMEM] * len(blocks)
    aliases = {}
    if done is not None:
        aliases = {len(operands): 0}
        operands.append(done)
        specs.append(pl.BlockSpec(memory_space=pl.ANY))
    return pl.pallas_call(
        functools.partial(prompt_kernel, n, low),
        out_shape=jax.ShapeDtypeStruct(query.shape, jnp.bfloat16),
        grid_spec=pltpu.PrefetchScalarGridSpec(
            num_scalar_prefetch=1,
            grid=(high - low,),
            in_specs=specs,
            out_specs=wide,
            scratch_shapes=[
                pltpu.VMEM((2, HD, MAXP * PAGE), jnp.bfloat16),
                pltpu.VMEM((2, MAXP * PAGE, HD), jnp.bfloat16),
                pltpu.VMEM((PAGE, PAGE), jnp.float32),
                pltpu.VMEM((ROWS, MAXP * PAGE), jnp.float32),
                pltpu.VMEM((ROWS, MAXP * PAGE), jnp.float32),
                pltpu.VMEM((ROWS, MAXP * PAGE), jnp.bfloat16),
                pltpu.VMEM((ROWS, MAXP * PAGE), jnp.bfloat16),
            ],
        ),
        input_output_aliases=aliases,
        name="prompt_attention",
        **params(48),
    )(*operands)


def decode_kernel(facts, head_ref, pool_ref, q_ref, k_ref, v_ref, o_ref):
    requests, width = q_ref.shape[:2]
    last = 2 * pool_ref.shape[0] - 1
    other = 1 - lax.axis_index("section")
    lane = lax.broadcasted_iota(jnp.int32, (width, PAGE), 1)
    step = lax.broadcasted_iota(jnp.int32, (width, 1), 0) % STEPS
    scores, fresh, pages = [], [], []
    end = 0
    for r in range(requests):
        start, end = end, end + facts[other, r]
        length = PAGE * (end - start - 1) + facts[other, requests + r]
        query = q_ref[r]
        numbers = [jnp.minimum(start + j, last) for j in range(MAXP)]
        pages.append([(number // 2, number % 2) for number in numbers])
        tiles = []
        for j, at in enumerate(pages[r]):
            score = dot(query, pool_ref[at[0], at[1], 0]) * SCALE
            tiles.append(jnp.where(lane < length - j * PAGE, score, LOW))
        scores.append(jnp.concatenate(tiles, axis=1))
        keys = k_ref[r, head_ref[0]].astype(jnp.float32)
        wide = query.astype(jnp.float32)
        news = [jnp.sum(wide * keys[u:u + 1], axis=1, keepdims=True) * SCALE for u in range(STEPS)]
        fresh.append([jnp.where(u <= step, x, LOW) for u, x in enumerate(news)])
    score = jnp.concatenate(scores, axis=0)
    fresh = [jnp.concatenate([x[u] for x in fresh], axis=0) for u in range(STEPS)]
    top = functools.reduce(jnp.maximum, fresh + [jnp.max(score, axis=1, keepdims=True)])
    terms = jnp.exp(score - top)
    fresh = [jnp.exp(x - top) for x in fresh]
    total = functools.reduce(jnp.add, fresh + [jnp.sum(terms, axis=1, keepdims=True)])
    high = terms.astype(jnp.bfloat16)
    low = (terms - high.astype(jnp.float32)).astype(jnp.bfloat16)
    for r in range(requests):
        rows = slice(r * width, (r + 1) * width)
        new_values = v_ref[r, head_ref[0]].astype(jnp.float32)
        mixed = functools.reduce(
            jnp.add, [fresh[u][rows] * new_values[u:u + 1] for u in range(STEPS)]
        )
        for j, at in enumerate(pages[r]):
            values = pool_ref[at[0], at[1], 1]
            columns = slice(j * PAGE, (j + 1) * PAGE)
            mixed = mixed + dot(high[rows, columns], values) + dot(low[rows, columns], values)
        o_ref[r] = (mixed / total[rows]).astype(jnp.bfloat16)


def decoded(facts, head, pool, query, new_key, new_value, lanes):
    requests, here = query.shape[1], QH // lanes
    query = jnp.transpose(query.reshape(STEPS, requests, here, HD), (1, 2, 0, 3))
    query = query.reshape(requests, here * STEPS, HD)
    fresh = [
        jnp.transpose(x.reshape(STEPS, requests, KVH, HD), (1, 2, 0, 3)) for x in (new_key, new_value)
    ]
    out = pl.pallas_call(
        decode_kernel,
        out_shape=jax.ShapeDtypeStruct(query.shape, jnp.bfloat16),
        in_specs=[SMEM, SMEM, VMEM, VMEM, VMEM, VMEM],
        out_specs=VMEM,
        name="decode_attention",
        **params(32),
    )(facts, head, pool, query, *fresh)
    out = jnp.transpose(out.reshape(requests, here, STEPS, HD), (2, 0, 1, 3))
    return out.reshape(STEPS, requests, here * HD)


def after(x, *earlier):
    return lax.optimization_barrier((x, *earlier))[0]


def on_device(
    prefill_query, prefill_key, prefill_value, counts, fills, dec_query, dec_key, dec_value
):
    lanes = lax.axis_size("tp")
    query, key, value = prefill_query[0], prefill_key[0], prefill_value[0]
    facts = jnp.concatenate([counts, fills], axis=1)
    head = (lax.axis_index("tp") * (QH // lanes) // GROUP).reshape(1)
    bases = [sum(CHUNKS[:g]) for g in range(len(CHUNKS))]

    ahead = [(i, i + 2) for i in range(lanes - 2)]
    ahead_again = [(i, i + 2) for i in range(2, lanes - 2)]
    beside = [(i, i + 1) for i in range(0, lanes, 2)]
    trade = [(i, i ^ 1) for i in range(2, lanes)]
    back = [(i, i - 1) for i in range(5, lanes, 2)]
    mine = []
    for base, n in zip(bases, CHUNKS):
        mine.append(pack(base, n, after(key, *mine), value))
    received, out, arrived = [], None, None
    for g, block in enumerate(mine):
        a = lax.ppermute(block, "tp", ahead)
        b = lax.ppermute(after(block, received[0][2]) if g else block, "tp", beside)
        c = lax.ppermute(a if g else after(a, b), "tp", trade)
        d = lax.ppermute(jnp.concatenate([a[1:], c[:1]], axis=0), "tp", ahead_again)
        late = d
        if g:
            blocks = (mine[0], *received[0])
            out = prompt_heads(bases[0], CHUNKS[0], 0, CUTS[0], facts, query, blocks, None)
            late, done = after(d, out), out
            out = after(out, d)
            out = prompt_heads(bases[0], CHUNKS[0], CUTS[0], CHUNKS[0], facts, query, blocks, out)
        e = lax.ppermute(late[0], "tp", back)
        received.append((a, b, c, d, e))

    pages = pack(0, KVH, after(key, received[0][2]), value, by_head=True)
    pages = jnp.repeat(pages, lanes // KVH, axis=0)
    pages = after(pages, done)
    arrived = lax.all_to_all(pages, "tp", split_axis=0, concat_axis=0, tiled=True)
    blocks = (mine[1], *received[1])
    out = prompt_heads(bases[1], CHUNKS[1], 0, CUTS[1], facts, query, blocks, out)
    out = after(out, arrived)
    out = prompt_heads(bases[1], CHUNKS[1], CUTS[1], CHUNKS[1], facts, query, blocks, out)
    pool = lax.ppermute(arrived, "section", [(0, 1), (1, 0)])
    dec_out = decoded(facts, head, pool, dec_query[0], dec_key[0], dec_value[0], lanes)
    return (out[None], dec_out[None])


def solution(mesh):
    placed = (
        P("section", ("groups", "tp"), None),
        P("section", ("groups", "tp"), None),
        P("section", ("groups", "tp"), None),
        P(None, "groups"),
        P(None, "groups"),
        P("section", None, "groups", "tp"),
        P("section", None, "groups", None),
        P("section", None, "groups", None),
    )
    return jax.shard_map(
        on_device,
        mesh=mesh,
        in_specs=placed,
        out_specs=(P("section", ("groups", "tp"), None), P("section", None, "groups", "tp")),
        check_vma=False,
    )
```

```python
import functools
import math

import jax
import jax.numpy as jnp
from jax import lax
from jax.experimental import pallas as pl
from jax.experimental.pallas import tpu as pltpu
from jax.sharding import PartitionSpec as P

QH = 64
KVH = 8
HD = 128
PAGE = 128
MAXP = 8
STEPS = 4
GROUP = QH // KVH
SCALE = HD ** (-0.5)
EXP2_SCALE = SCALE * math.log2(math.e)
LOW = -1e30
CHUNKS = (4, 4)
ROWS = 256
SMEM = pl.BlockSpec(memory_space=pltpu.SMEM)
VMEM = pl.BlockSpec(memory_space=pltpu.VMEM)


def dot(a, b):
    return jnp.dot(a, b, preferred_element_type=jnp.float32)


def page_facts(facts, half, page):
    requests = facts.shape[1] // 2
    owner, first, live, end = -1, 0, PAGE, 0
    for r in range(requests):
        start, end = end, end + facts[half, r]
        begun = start <= page
        owner = jnp.where(begun, r, owner)
        first = jnp.where(begun, start, first)
        live = jnp.where(end - 1 == page, facts[half, requests + r], live)
    return owner, first, live


def params(limit):
    return dict(
        compiler_params=pltpu.CompilerParams(vmem_limit_bytes=limit << 20),
        cost_estimate=pl.CostEstimate(flops=1, bytes_accessed=1, transcendentals=0),
    )


def pack_kernel(base, k_ref, v_ref, *rest):
    o_ref, k_part, v_part, sems = rest[-4:]
    n = k_part.shape[1] // HD
    own = slice(base * HD, (base + n) * HD)
    copies = [
        pltpu.make_async_copy(source.at[:, own], part, sems.at[spot])
        for spot, (source, part) in enumerate(((k_ref, k_part), (v_ref, v_part)))
    ]
    for copy in copies:
        copy.start()
    for copy in copies:
        copy.wait()
    for j in range(n):
        columns = slice(j * HD, (j + 1) * HD)
        for p in range(2):
            rows = slice(p * PAGE, (p + 1) * PAGE)
            turned = jnp.transpose(k_part[rows, columns].astype(jnp.float32)).astype(jnp.bfloat16)
            o_ref[p, columns] = turned
            o_ref[p, (n + j) * HD:(n + j + 1) * HD] = v_part[rows, columns]


def pack(base, n, key, value):
    part = pltpu.VMEM((key.shape[0], n * HD), jnp.bfloat16)
    return pl.pallas_call(
        functools.partial(pack_kernel, base),
        out_shape=jax.ShapeDtypeStruct((2, 2 * n * HD, PAGE), jnp.bfloat16),
        in_specs=[pl.BlockSpec(memory_space=pl.ANY)] * 2,
        out_specs=VMEM,
        scratch_shapes=[part, part, pltpu.SemaphoreType.DMA((2,))],
        name="pack",
        **params(48),
    )(key, value)


def prompt_kernel(n, low, facts, q_ref, *rest):
    o_ref, keys, values, causal = rest[-4:]
    head = low + pl.program_id(0)
    spots = [pl.ds(pl.multiple_of((x + head) * HD, HD), HD) for x in (0, n)]
    mine, a, b, c, d = [[[x[p, at] for at in spots] for p in range(x.shape[0])] for x in rest[:5]]
    half, place = lax.axis_index("section"), lax.axis_index("tp")
    even = place % 2 == 0
    near, far = 2 * place - 2, 2 * place - 6
    page_c = jnp.where(even, near, far)
    page_be = jnp.where(even, far, near)
    choose = jnp.full((HD, PAGE), even)
    be = [[jnp.where(choose, x, y) for x, y in zip(d[1 + p], b[p])] for p in range(2)]
    row = lax.broadcasted_iota(jnp.int32, (PAGE, PAGE), 0)
    col = lax.broadcasted_iota(jnp.int32, (PAGE, PAGE), 1)
    causal[...] = jnp.where(col <= row, 0.0, LOW)
    one = jnp.ones((PAGE, HD), jnp.bfloat16)
    zero = jnp.zeros((PAGE, HD), jnp.bfloat16)
    lives = []

    for i in range(2):
        _, first, live = page_facts(facts, half, 2 * place + i)
        lives.append(live)
        stand_in = jnp.broadcast_to(mine[i][0][:, :1], (HD, PAGE))
        if i == 0:
            pages = [(*d[0], 2 * place - 7)]
        else:
            pages = [(*mine[0], 2 * place)]
        pages.append((*mine[i], None))
        pages += [(*a[p], 2 * place - 4 + p) for p in range(2)]
        pages += [(*c[p], page_c + p) for p in range(2)]
        pages += [(*be[p], page_be + p) for p in range(2)]
        for spot, (k, v, number) in enumerate(pages):
            count = one
            if number is not None:
                seen = jnp.full((PAGE, HD), number >= first)
                k = jnp.where(seen, k, stand_in)
                v = jnp.where(seen, v, zero)
                count = jnp.where(seen, one, zero)
            at = slice(spot * PAGE, (spot + 1) * PAGE)
            keys[i, :HD, at] = k
            keys[i, HD:, at] = k
            values[i, at, :HD] = v
            values[i, at, HD:] = count

    heads_at_once = ROWS // PAGE
    blocks = [(i, start) for i in range(2) for start in range(0, GROUP, heads_at_once)]

    def halves(query):
        query = query.astype(jnp.float32) * EXP2_SCALE
        high = query.astype(jnp.bfloat16)
        low = (query - high.astype(jnp.float32)).astype(jnp.bfloat16)
        return jnp.concatenate([high, low], axis=1)

    def queries(i, start):
        return halves(
            jnp.concatenate(
                [
                    q_ref[i * PAGE:(i + 1) * PAGE, h * HD:(h + 1) * HD]
                    for h in range(start, start + heads_at_once)
                ],
                axis=0,
            )
        )

    def divided(mixed, live):
        total = mixed[:, HD:]
        near = pl.reciprocal(total, approx=True)
        near = near * (2.0 - total * near)
        token = lax.broadcasted_iota(jnp.int32, (total.shape[0], HD), 0) % PAGE
        return jnp.where(token < live, mixed[:, :HD] * near, 0.0).astype(jnp.bfloat16)

    tiles = [slice(t, t + 2 * PAGE) for t in range(0, MAXP * PAGE, 2 * PAGE)]

    def own_scores(query, i, repeat):
        own = dot(query, keys[i, :, tiles[0]])
        bias = jnp.concatenate([causal[...]] * repeat, axis=0)
        return jnp.concatenate([own[:, :PAGE], own[:, PAGE:] + bias], axis=1)

    largest = jnp.zeros((ROWS, HD), jnp.float32)
    for i, start in blocks:
        query = queries(i, start)
        score = own_scores(query, i, heads_at_once)
        top = jnp.max(score, axis=1, keepdims=True)
        mixed = None
        for tile, at in enumerate(tiles):
            prob = jnp.exp2(score - top).astype(jnp.bfloat16)
            if tile + 1 < len(tiles):
                score = dot(query, keys[i, :, tiles[tile + 1]])
            part = dot(prob, values[i, at])
            mixed = part if mixed is None else mixed + part
        largest = jnp.maximum(largest, mixed[:, HD:])
        out = divided(mixed, lives[i])
        for number in range(heads_at_once):
            h = start + number
            o_ref[i * PAGE:(i + 1) * PAGE, h * HD:(h + 1) * HD] = out[number * PAGE:(number + 1) * PAGE]

    @pl.when(jnp.logical_not(jnp.max(largest) < 1e30))
    def _():
        def one(index, carry):
            i, h = index // GROUP, index % GROUP
            rows = pl.ds(pl.multiple_of(i * PAGE, PAGE), PAGE)
            columns = pl.ds(pl.multiple_of(h * HD, HD), HD)
            query = halves(q_ref[rows, columns])
            scores = [own_scores(query, i, 1)] + [dot(query, keys[i, :, at]) for at in tiles[1:]]
            top = jnp.max(functools.reduce(jnp.maximum, scores), axis=1, keepdims=True)
            mixed = jnp.zeros((PAGE, 2 * HD), jnp.float32)
            for score, at in zip(scores, tiles):
                mixed = mixed + dot(jnp.exp2(score - top).astype(jnp.bfloat16), values[i, at])
            o_ref[rows, columns] = divided(mixed, jnp.where(i == 0, lives[0], lives[1]))
            return carry

        lax.fori_loop(0, 2 * GROUP, one, 0)


def prompt_heads(base, n, low, high, facts, query, blocks, done):
    tok = query.shape[0]

    wide = pl.BlockSpec((tok, GROUP * HD), lambda j, *_: (0, base + low + j))
    operands = [facts, query, *blocks]
    specs = [wide] + [VMEM] * len(blocks)
    aliases = {}
    if done is not None:
        aliases = {len(operands): 0}
        operands.append(done)
        specs.append(pl.BlockSpec(memory_space=pl.ANY))
    return pl.pallas_call(
        functools.partial(prompt_kernel, n, low),
        out_shape=jax.ShapeDtypeStruct(query.shape, jnp.bfloat16),
        grid_spec=pltpu.PrefetchScalarGridSpec(
            num_scalar_prefetch=1,
            grid=(high - low,),
            in_specs=specs,
            out_specs=wide,
            scratch_shapes=[
                pltpu.VMEM((2, 2 * HD, MAXP * PAGE), jnp.bfloat16),
                pltpu.VMEM((2, MAXP * PAGE, 2 * HD), jnp.bfloat16),
                pltpu.VMEM((PAGE, PAGE), jnp.float32),
            ],
        ),
        input_output_aliases=aliases,
        name="prompt_attention",
        **params(48),
    )(*operands)


def stat_rows(rows):
    return 16 - rows % 16


def choose_kernel(facts, q_ref, o_ref, rows_ref, turned):
    requests, here = q_ref.shape[1], q_ref.shape[2] // HD
    other = 1 - lax.axis_index("section")
    for s in range(STEPS):
        query = q_ref[s].astype(jnp.float32)
        for r in range(requests):
            for h in range(here):
                row = h * STEPS + s
                turned[r, row:row + 1] = query[r:r + 1, h * HD:(h + 1) * HD]
    rows_ref[...] = turned[...].astype(jnp.bfloat16)

    def one(lane, carry):
        for i in range(2):
            owner = page_facts(facts, other, 2 * lane + i)[0]
            o_ref[lane, i] = turned[owner].astype(jnp.bfloat16)
        return carry

    lax.fori_loop(0, o_ref.shape[0], one, 0)


def chosen_queries(facts, query, lanes):
    rows = (query.shape[1], QH // lanes * STEPS, HD)
    return pl.pallas_call(
        choose_kernel,
        out_shape=(
            jax.ShapeDtypeStruct((lanes, 2, *rows[1:]), jnp.bfloat16),
            jax.ShapeDtypeStruct(rows, jnp.bfloat16),
        ),
        in_specs=[SMEM, VMEM],
        out_specs=(VMEM, VMEM),
        scratch_shapes=[pltpu.VMEM(rows, jnp.float32)],
        name="choose_queries",
        **params(32),
    )(facts, query)


def partial_kernel(lanes, facts, q_ref, *rest):
    *packed, o_ref = rest
    split = GROUP // (QH // lanes)
    width = QH // lanes * STEPS
    extra = stat_rows(2 * width)
    half, place = lax.axis_index("section"), lax.axis_index("tp")
    group = GROUP * STEPS
    height = 2 * KVH * group
    lane = lax.broadcasted_iota(jnp.int32, (height, PAGE), 1)
    later = lax.broadcasted_iota(jnp.int32, (height, PAGE), 0) // group % 2 == 1
    spot = lax.broadcasted_iota(jnp.int32, (2 * width, PAGE), 0)
    across = lax.broadcasted_iota(jnp.int32, (2 * width, PAGE), 1)
    line = lax.broadcasted_iota(jnp.int32, (extra, PAGE), 0)
    lives = [page_facts(facts, half, 2 * place + i)[2] for i in range(2)]
    places = [(block, j, n) for block, n in zip(packed, CHUNKS) for j in range(n)]
    scores, values = [], []
    for k, (block, j, n) in enumerate(places):
        for i in range(2):
            query = jnp.concatenate([q_ref[k * split + t, i] for t in range(split)], axis=0)
            scores.append(dot(query, block[i, j * HD:(j + 1) * HD]))
            values.append(block[i, (n + j) * HD:(n + j + 1) * HD])
    score = jnp.concatenate(scores, axis=0) * SCALE
    score = jnp.where(lane < jnp.where(later, lives[1], lives[0]), score, LOW)
    top = jnp.max(score, axis=1, keepdims=True)
    terms = jnp.exp(score - top)
    total = jnp.sum(terms, axis=1, keepdims=True)
    high = terms.astype(jnp.bfloat16)
    low = (terms - high.astype(jnp.float32)).astype(jnp.bfloat16)
    mixed = jnp.concatenate(
        [
            dot(high[m * group:(m + 1) * group], v) + dot(low[m * group:(m + 1) * group], v)
            for m, v in enumerate(values)
        ],
        axis=0,
    ) / total
    sums = top + jnp.log(total)
    for k in range(KVH):
        for t in range(split):
            begins = [(2 * k + i) * group + t * width for i in range(2)]
            both = jnp.concatenate([sums[at:at + width] for at in begins], axis=0)
            turned = jnp.sum(jnp.where(spot == across, both, 0.0), axis=0, keepdims=True)
            first = turned.astype(jnp.bfloat16).astype(jnp.float32)
            rest = turned - first
            second = rest.astype(jnp.bfloat16).astype(jnp.float32)
            stat = jnp.where(line == 0, first, jnp.where(line == 1, second, rest - second))
            stat = jnp.where(line < 3, stat, 0.0)
            block = jnp.concatenate([mixed[at:at + width] for at in begins] + [stat], axis=0)
            o_ref[k * split + t] = block.astype(jnp.bfloat16)


def partial_decode(facts, query, packed, lanes):
    rows = 2 * (QH // lanes) * STEPS
    return pl.pallas_call(
        functools.partial(partial_kernel, lanes),
        out_shape=jax.ShapeDtypeStruct((lanes, rows + stat_rows(rows), HD), jnp.bfloat16),
        in_specs=[SMEM, VMEM] + [VMEM] * len(packed),
        out_specs=VMEM,
        name="partial_decode",
        **params(32),
    )(facts, query, *packed)


def merge_kernel(lanes, facts, parts_ref, q_ref, k_ref, v_ref, o_ref):
    requests = q_ref.shape[0]
    width = (QH // lanes) * STEPS
    other, place = 1 - lax.axis_index("section"), lax.axis_index("tp")
    head = place * (QH // lanes) // GROUP
    spot = lax.broadcasted_iota(jnp.int32, (width, PAGE), 0)
    across = lax.broadcasted_iota(jnp.int32, (width, PAGE), 1)
    step = lax.broadcasted_iota(jnp.int32, (width, 1), 0) % STEPS
    end = 0
    for r in range(requests):
        start, end = end, end + facts[other, r]
        query = q_ref[r].astype(jnp.float32)
        keys = k_ref[r, head].astype(jnp.float32)
        values = v_ref[r, head].astype(jnp.float32)
        tops, vectors = [], []
        for u in range(STEPS):
            score = jnp.sum(query * keys[u:u + 1], axis=1, keepdims=True) * SCALE
            tops.append(jnp.where(u <= step, score, LOW))
            vectors.append(values[u:u + 1])
        for j in range(MAXP):
            page = jnp.minimum(start + j, 2 * lanes - 1)
            block = parts_ref[page // 2].astype(jnp.float32)
            later = jnp.full((width, HD), page % 2 == 1)
            vectors.append(jnp.where(later, block[width:2 * width], block[:width]))
            stat = jnp.sum(block[2 * width:2 * width + 8], axis=0, keepdims=True)
            stat = jnp.sum(
                jnp.where(across - page % 2 * width == spot, stat, 0.0), axis=1, keepdims=True
            )
            tops.append(jnp.where(jnp.full((width, 1), start + j < end), stat, LOW))
        top = functools.reduce(jnp.maximum, tops)
        weights = [jnp.exp(t - top) for t in tops]
        total = functools.reduce(jnp.add, weights)
        mixed = functools.reduce(jnp.add, [w * x for w, x in zip(weights, vectors)])
        o_ref[r] = (mixed / total).astype(jnp.bfloat16)


def merged(facts, parts, query, new_key, new_value, lanes):
    requests = query.shape[0]
    fresh = [
        jnp.transpose(x.reshape(STEPS, requests, KVH, HD), (1, 2, 0, 3)) for x in (new_key, new_value)
    ]
    out = pl.pallas_call(
        functools.partial(merge_kernel, lanes),
        out_shape=jax.ShapeDtypeStruct(query.shape, jnp.bfloat16),
        in_specs=[SMEM, VMEM, VMEM, VMEM, VMEM],
        out_specs=VMEM,
        name="merge_decode",
        **params(32),
    )(facts, parts, query, *fresh)
    out = jnp.transpose(out.reshape(requests, QH // lanes, STEPS, HD), (2, 0, 1, 3))
    return out.reshape(STEPS, requests, QH // lanes * HD)


def other_half(x):
    return lax.ppermute(x, "section", [(0, 1), (1, 0)])


def after(x, *earlier):
    return lax.optimization_barrier((x, *earlier))[0]


def on_device(
    prefill_query, prefill_key, prefill_value, counts, fills, dec_query, dec_key, dec_value
):
    lanes = lax.axis_size("tp")
    query, key, value = prefill_query[0], prefill_key[0], prefill_value[0]
    facts = jnp.concatenate([counts, fills], axis=1)
    ahead = [(i, i + 2) for i in range(lanes - 2)]
    ahead_again = [(i, i + 2) for i in range(2, lanes - 2)]
    beside = [(i, i + 1) for i in range(0, lanes, 2)]
    trade = [(i, i ^ 1) for i in range(2, lanes)]
    bases = [sum(CHUNKS[:g]) for g in range(len(CHUNKS))]
    mine = []
    for base, n in zip(bases, CHUNKS):
        mine.append(pack(base, n, after(key, *mine), value))

    chosen, dec_rows = chosen_queries(facts, dec_query[0], lanes)
    wanted = lax.all_to_all(chosen, "tp", split_axis=0, concat_axis=0, tiled=True)
    parts = partial_decode(facts, other_half(wanted), mine, lanes)
    parts = lax.all_to_all(parts, "tp", split_axis=0, concat_axis=0, tiled=True)
    dec_out = merged(facts, other_half(parts), dec_rows, dec_key[0], dec_value[0], lanes)

    received = []
    for g, block in enumerate(mine):
        a = lax.ppermute(after(block, wanted) if g else block, "tp", ahead)
        b = lax.ppermute(after(block, received[0][2]) if g else block, "tp", beside)
        c = lax.ppermute(a if g else after(a, b), "tp", trade)
        d = jnp.concatenate([a[1:], c], axis=0)
        d = lax.ppermute(after(d, parts) if g else d, "tp", ahead_again)
        received.append((a, b, c, d))
    out = None
    for g, (base, n) in enumerate(zip(bases, CHUNKS)):
        if g:
            out = after(out, dec_out)
        out = prompt_heads(base, n, 0, n, facts, query, (mine[g], *received[g]), out)
    return (out[None], dec_out[None])


def solution(mesh):
    placed = (
        P("section", ("groups", "tp"), None),
        P("section", ("groups", "tp"), None),
        P("section", ("groups", "tp"), None),
        P(None, "groups"),
        P(None, "groups"),
        P("section", None, "groups", "tp"),
        P("section", None, "groups", None),
        P("section", None, "groups", None),
    )
    return jax.shard_map(
        on_device,
        mesh=mesh,
        in_specs=placed,
        out_specs=(P("section", ("groups", "tp"), None), P("section", None, "groups", "tp")),
        check_vma=False,
    )
```

```python
import functools
import math

import jax
import jax.numpy as jnp
from jax import lax
from jax.experimental import pallas as pl
from jax.experimental.pallas import tpu as pltpu
from jax.sharding import PartitionSpec as P

QH = 64
KVH = 8
HD = 128
PAGE = 128
MAXP = 8
STEPS = 4
GROUP = QH // KVH
SCALE = HD ** (-0.5)
EXP2_SCALE = SCALE * math.log2(math.e)
LOW = -1e30
CHUNKS = (4, 4)
ROWS = 256
WIDTH = 512
SMEM = pl.BlockSpec(memory_space=pltpu.SMEM)
VMEM = pl.BlockSpec(memory_space=pltpu.VMEM)


def dot(a, b):
    return jnp.dot(a, b, preferred_element_type=jnp.float32)


def page_facts(facts, half, page):
    requests = facts.shape[1] // 2
    owner, first, live, end = -1, 0, PAGE, 0
    for r in range(requests):
        start, end = end, end + facts[half, r]
        begun = start <= page
        owner = jnp.where(begun, r, owner)
        first = jnp.where(begun, start, first)
        live = jnp.where(end - 1 == page, facts[half, requests + r], live)
    return owner, first, live


def params(limit):
    return dict(
        compiler_params=pltpu.CompilerParams(vmem_limit_bytes=limit << 20),
        cost_estimate=pl.CostEstimate(flops=1, bytes_accessed=1, transcendentals=0),
    )


def pack_kernel(base, k_ref, v_ref, *rest):
    o_ref, k_part, v_part, sems = rest[-4:]
    n = k_part.shape[1] // HD
    own = slice(base * HD, (base + n) * HD)
    copies = [
        pltpu.make_async_copy(source.at[:, own], part, sems.at[spot])
        for spot, (source, part) in enumerate(((k_ref, k_part), (v_ref, v_part)))
    ]
    for copy in copies:
        copy.start()
    for copy in copies:
        copy.wait()
    for j in range(n):
        columns = slice(j * HD, (j + 1) * HD)
        for p in range(2):
            rows = slice(p * PAGE, (p + 1) * PAGE)
            turned = jnp.transpose(k_part[rows, columns].astype(jnp.float32)).astype(jnp.bfloat16)
            o_ref[p, columns] = turned
            o_ref[p, (n + j) * HD:(n + j + 1) * HD] = v_part[rows, columns]


def pack(base, n, key, value):
    part = pltpu.VMEM((key.shape[0], n * HD), jnp.bfloat16)
    return pl.pallas_call(
        functools.partial(pack_kernel, base),
        out_shape=jax.ShapeDtypeStruct((2, 2 * n * HD, PAGE), jnp.bfloat16),
        in_specs=[pl.BlockSpec(memory_space=pl.ANY)] * 2,
        out_specs=VMEM,
        scratch_shapes=[part, part, pltpu.SemaphoreType.DMA((2,))],
        name="pack",
        **params(60),
    )(key, value)


def prompt_kernel(n, low, facts, q_ref, *rest):
    o_ref, keys, values, causal = rest[-4:]
    head = low + pl.program_id(0)
    spots = [pl.ds(pl.multiple_of((x + head) * HD, HD), HD) for x in (0, n)]
    mine, a, b, c, d = [[[x[p, at] for at in spots] for p in range(x.shape[0])] for x in rest[:5]]
    half, place = lax.axis_index("section"), lax.axis_index("tp")
    even = place % 2 == 0
    near, far = 2 * place - 2, 2 * place - 6
    page_c = jnp.where(even, near, far)
    page_be = jnp.where(even, far, near)
    choose = jnp.full((HD, PAGE), even)
    be = [[jnp.where(choose, x, y) for x, y in zip(d[1 + p], b[p])] for p in range(2)]
    row = lax.broadcasted_iota(jnp.int32, (PAGE, PAGE), 0)
    col = lax.broadcasted_iota(jnp.int32, (PAGE, PAGE), 1)
    causal[...] = jnp.where(col <= row, 0.0, LOW)
    one = jnp.ones((PAGE, HD), jnp.bfloat16)
    zero = jnp.zeros((PAGE, HD), jnp.bfloat16)
    lives = []

    for i in range(2):
        _, first, live = page_facts(facts, half, 2 * place + i)
        lives.append(live)
        stand_in = jnp.broadcast_to(mine[i][0][:, :1], (HD, PAGE))
        if i == 0:
            pages = [(*d[0], 2 * place - 7)]
        else:
            pages = [(*mine[0], 2 * place)]
        pages.append((*mine[i], None))
        pages += [(*a[p], 2 * place - 4 + p) for p in range(2)]
        pages += [(*c[p], page_c + p) for p in range(2)]
        pages += [(*be[p], page_be + p) for p in range(2)]
        for spot, (k, v, number) in enumerate(pages):
            count = one
            if number is not None:
                seen = jnp.full((PAGE, HD), number >= first)
                k = jnp.where(seen, k, stand_in)
                v = jnp.where(seen, v, zero)
                count = jnp.where(seen, one, zero)
            at = slice(spot * PAGE, (spot + 1) * PAGE)
            keys[i, :HD, at] = k
            keys[i, HD:, at] = k
            values[i, at, :HD] = v
            values[i, at, HD:] = count

    heads_at_once = ROWS // PAGE
    blocks = [(i, start) for i in range(2) for start in range(0, GROUP, heads_at_once)]

    def halves(query):
        query = query.astype(jnp.float32) * EXP2_SCALE
        high = query.astype(jnp.bfloat16)
        low = (query - high.astype(jnp.float32)).astype(jnp.bfloat16)
        return jnp.concatenate([high, low], axis=1)

    def queries(i, start):
        return halves(
            jnp.concatenate(
                [
                    q_ref[i * PAGE:(i + 1) * PAGE, h * HD:(h + 1) * HD]
                    for h in range(start, start + heads_at_once)
                ],
                axis=0,
            )
        )

    def divided(mixed, live):
        total = mixed[:, HD:]
        near = pl.reciprocal(total, approx=True)
        near = near * (2.0 - total * near)
        token = lax.broadcasted_iota(jnp.int32, (total.shape[0], HD), 0) % PAGE
        return jnp.where(token < live, mixed[:, :HD] * near, 0.0).astype(jnp.bfloat16)

    tiles = [slice(t, t + WIDTH) for t in range(0, MAXP * PAGE, WIDTH)]

    def own_scores(query, i, repeat):
        own = dot(query, keys[i, :, tiles[0]])
        bias = jnp.concatenate([causal[...]] * repeat, axis=0)
        second = own[:, PAGE:2 * PAGE] + bias
        return jnp.concatenate([own[:, :PAGE], second, own[:, 2 * PAGE:]], axis=1)

    largest = jnp.zeros((ROWS, HD), jnp.float32)
    for i, start in blocks:
        query = queries(i, start)
        score = own_scores(query, i, heads_at_once)
        top = jnp.max(score, axis=1, keepdims=True)
        mixed = None
        for tile, at in enumerate(tiles):
            prob = jnp.exp2(score - top).astype(jnp.bfloat16)
            if tile + 1 < len(tiles):
                score = dot(query, keys[i, :, tiles[tile + 1]])
            part = dot(prob, values[i, at])
            mixed = part if mixed is None else mixed + part
        largest = jnp.maximum(largest, mixed[:, HD:])
        out = divided(mixed, lives[i])
        for number in range(heads_at_once):
            h = start + number
            o_ref[i * PAGE:(i + 1) * PAGE, h * HD:(h + 1) * HD] = out[number * PAGE:(number + 1) * PAGE]

    @pl.when(jnp.logical_not(jnp.max(largest) < 1e30))
    def _():
        def one(index, carry):
            i, h = index // GROUP, index % GROUP
            rows = pl.ds(pl.multiple_of(i * PAGE, PAGE), PAGE)
            columns = pl.ds(pl.multiple_of(h * HD, HD), HD)
            query = halves(q_ref[rows, columns])
            scores = [own_scores(query, i, 1)] + [dot(query, keys[i, :, at]) for at in tiles[1:]]
            top = jnp.max(functools.reduce(jnp.maximum, scores), axis=1, keepdims=True)
            mixed = jnp.zeros((PAGE, 2 * HD), jnp.float32)
            for score, at in zip(scores, tiles):
                mixed = mixed + dot(jnp.exp2(score - top).astype(jnp.bfloat16), values[i, at])
            o_ref[rows, columns] = divided(mixed, jnp.where(i == 0, lives[0], lives[1]))
            return carry

        lax.fori_loop(0, 2 * GROUP, one, 0)


def prompt_heads(base, n, low, high, facts, query, blocks, done):
    tok = query.shape[0]

    wide = pl.BlockSpec((tok, GROUP * HD), lambda j, *_: (0, base + low + j))
    operands = [facts, query, *blocks]
    specs = [wide] + [VMEM] * len(blocks)
    aliases = {}
    if done is not None:
        aliases = {len(operands): 0}
        operands.append(done)
        specs.append(pl.BlockSpec(memory_space=pl.ANY))
    return pl.pallas_call(
        functools.partial(prompt_kernel, n, low),
        out_shape=jax.ShapeDtypeStruct(query.shape, jnp.bfloat16),
        grid_spec=pltpu.PrefetchScalarGridSpec(
            num_scalar_prefetch=1,
            grid=(high - low,),
            in_specs=specs,
            out_specs=wide,
            scratch_shapes=[
                pltpu.VMEM((2, 2 * HD, MAXP * PAGE), jnp.bfloat16),
                pltpu.VMEM((2, MAXP * PAGE, 2 * HD), jnp.bfloat16),
                pltpu.VMEM((PAGE, PAGE), jnp.float32),
            ],
        ),
        input_output_aliases=aliases,
        name="prompt_attention",
        **params(48),
    )(*operands)


def stat_rows(rows):
    return 16 - rows % 16


def choose_kernel(facts, q_ref, o_ref, rows_ref, turned):
    requests, here = q_ref.shape[1], q_ref.shape[2] // HD
    other = 1 - lax.axis_index("section")
    for s in range(STEPS):
        query = q_ref[s].astype(jnp.float32)
        for r in range(requests):
            for h in range(here):
                row = h * STEPS + s
                turned[r, row:row + 1] = query[r:r + 1, h * HD:(h + 1) * HD]
    rows_ref[...] = turned[...].astype(jnp.bfloat16)

    def one(lane, carry):
        for i in range(2):
            owner = page_facts(facts, other, 2 * lane + i)[0]
            o_ref[lane, i] = turned[owner].astype(jnp.bfloat16)
        return carry

    lax.fori_loop(0, o_ref.shape[0], one, 0)


def chosen_queries(facts, query, lanes):
    rows = (query.shape[1], QH // lanes * STEPS, HD)
    return pl.pallas_call(
        choose_kernel,
        out_shape=(
            jax.ShapeDtypeStruct((lanes, 2, *rows[1:]), jnp.bfloat16),
            jax.ShapeDtypeStruct(rows, jnp.bfloat16),
        ),
        in_specs=[SMEM, VMEM],
        out_specs=(VMEM, VMEM),
        scratch_shapes=[pltpu.VMEM(rows, jnp.float32)],
        name="choose_queries",
        **params(32),
    )(facts, query)


def partial_kernel(lanes, facts, q_ref, *rest):
    *packed, o_ref = rest
    split = GROUP // (QH // lanes)
    width = QH // lanes * STEPS
    extra = stat_rows(2 * width)
    half, place = lax.axis_index("section"), lax.axis_index("tp")
    group = GROUP * STEPS
    height = 2 * KVH * group
    lane = lax.broadcasted_iota(jnp.int32, (height, PAGE), 1)
    later = lax.broadcasted_iota(jnp.int32, (height, PAGE), 0) // group % 2 == 1
    spot = lax.broadcasted_iota(jnp.int32, (2 * width, PAGE), 0)
    across = lax.broadcasted_iota(jnp.int32, (2 * width, PAGE), 1)
    line = lax.broadcasted_iota(jnp.int32, (extra, PAGE), 0)
    lives = [page_facts(facts, half, 2 * place + i)[2] for i in range(2)]
    places = [(block, j, n) for block, n in zip(packed, CHUNKS) for j in range(n)]
    scores, values = [], []
    for k, (block, j, n) in enumerate(places):
        for i in range(2):
            query = jnp.concatenate([q_ref[k * split + t, i] for t in range(split)], axis=0)
            scores.append(dot(query, block[i, j * HD:(j + 1) * HD]))
            values.append(block[i, (n + j) * HD:(n + j + 1) * HD])
    score = jnp.concatenate(scores, axis=0) * SCALE
    score = jnp.where(lane < jnp.where(later, lives[1], lives[0]), score, LOW)
    top = jnp.max(score, axis=1, keepdims=True)
    terms = jnp.exp(score - top)
    total = jnp.sum(terms, axis=1, keepdims=True)
    high = terms.astype(jnp.bfloat16)
    low = (terms - high.astype(jnp.float32)).astype(jnp.bfloat16)
    mixed = jnp.concatenate(
        [
            dot(high[m * group:(m + 1) * group], v) + dot(low[m * group:(m + 1) * group], v)
            for m, v in enumerate(values)
        ],
        axis=0,
    ) / total
    sums = top + jnp.log(total)
    for k in range(KVH):
        for t in range(split):
            begins = [(2 * k + i) * group + t * width for i in range(2)]
            both = jnp.concatenate([sums[at:at + width] for at in begins], axis=0)
            turned = jnp.sum(jnp.where(spot == across, both, 0.0), axis=0, keepdims=True)
            first = turned.astype(jnp.bfloat16).astype(jnp.float32)
            rest = turned - first
            second = rest.astype(jnp.bfloat16).astype(jnp.float32)
            stat = jnp.where(line == 0, first, jnp.where(line == 1, second, rest - second))
            stat = jnp.where(line < 3, stat, 0.0)
            block = jnp.concatenate([mixed[at:at + width] for at in begins] + [stat], axis=0)
            o_ref[k * split + t] = block.astype(jnp.bfloat16)


def partial_decode(facts, query, packed, lanes):
    rows = 2 * (QH // lanes) * STEPS
    return pl.pallas_call(
        functools.partial(partial_kernel, lanes),
        out_shape=jax.ShapeDtypeStruct((lanes, rows + stat_rows(rows), HD), jnp.bfloat16),
        in_specs=[SMEM, VMEM] + [VMEM] * len(packed),
        out_specs=VMEM,
        name="partial_decode",
        **params(32),
    )(facts, query, *packed)


def merge_kernel(lanes, facts, parts_ref, q_ref, k_ref, v_ref, o_ref):
    requests = q_ref.shape[0]
    width = (QH // lanes) * STEPS
    other, place = 1 - lax.axis_index("section"), lax.axis_index("tp")
    head = place * (QH // lanes) // GROUP
    spot = lax.broadcasted_iota(jnp.int32, (width, PAGE), 0)
    across = lax.broadcasted_iota(jnp.int32, (width, PAGE), 1)
    step = lax.broadcasted_iota(jnp.int32, (width, 1), 0) % STEPS
    end = 0
    for r in range(requests):
        start, end = end, end + facts[other, r]
        query = q_ref[r].astype(jnp.float32)
        keys = k_ref[r, head].astype(jnp.float32)
        values = v_ref[r, head].astype(jnp.float32)
        tops, vectors = [], []
        for u in range(STEPS):
            score = jnp.sum(query * keys[u:u + 1], axis=1, keepdims=True) * SCALE
            tops.append(jnp.where(u <= step, score, LOW))
            vectors.append(values[u:u + 1])
        for j in range(MAXP):
            page = jnp.minimum(start + j, 2 * lanes - 1)
            block = parts_ref[page // 2].astype(jnp.float32)
            later = jnp.full((width, HD), page % 2 == 1)
            vectors.append(jnp.where(later, block[width:2 * width], block[:width]))
            stat = jnp.sum(block[2 * width:2 * width + 8], axis=0, keepdims=True)
            stat = jnp.sum(
                jnp.where(across - page % 2 * width == spot, stat, 0.0), axis=1, keepdims=True
            )
            tops.append(jnp.where(jnp.full((width, 1), start + j < end), stat, LOW))
        top = functools.reduce(jnp.maximum, tops)
        weights = [jnp.exp(t - top) for t in tops]
        total = functools.reduce(jnp.add, weights)
        mixed = functools.reduce(jnp.add, [w * x for w, x in zip(weights, vectors)])
        o_ref[r] = (mixed / total).astype(jnp.bfloat16)


def merged(facts, parts, query, new_key, new_value, lanes):
    requests = query.shape[0]
    fresh = [
        jnp.transpose(x.reshape(STEPS, requests, KVH, HD), (1, 2, 0, 3)) for x in (new_key, new_value)
    ]
    out = pl.pallas_call(
        functools.partial(merge_kernel, lanes),
        out_shape=jax.ShapeDtypeStruct(query.shape, jnp.bfloat16),
        in_specs=[SMEM, VMEM, VMEM, VMEM, VMEM],
        out_specs=VMEM,
        name="merge_decode",
        **params(32),
    )(facts, parts, query, *fresh)
    out = jnp.transpose(out.reshape(requests, QH // lanes, STEPS, HD), (2, 0, 1, 3))
    return out.reshape(STEPS, requests, QH // lanes * HD)


def other_half(x):
    return lax.ppermute(x, "section", [(0, 1), (1, 0)])


def after(x, *earlier):
    return lax.optimization_barrier((x, *earlier))[0]


def on_device(
    prefill_query, prefill_key, prefill_value, counts, fills, dec_query, dec_key, dec_value
):
    lanes = lax.axis_size("tp")
    query, key, value = prefill_query[0], prefill_key[0], prefill_value[0]
    facts = jnp.concatenate([counts, fills], axis=1)
    ahead = [(i, i + 2) for i in range(lanes - 2)]
    ahead_again = [(i, i + 2) for i in range(2, lanes - 2)]
    beside = [(i, i + 1) for i in range(0, lanes, 2)]
    trade = [(i, i ^ 1) for i in range(2, lanes)]
    bases = [sum(CHUNKS[:g]) for g in range(len(CHUNKS))]
    mine = []
    for base, n in zip(bases, CHUNKS):
        mine.append(pack(base, n, after(key, *mine), value))

    first_hops = [lax.ppermute(block, "tp", ahead) for block in mine]
    b = lax.ppermute(mine[0], "tp", beside)
    c = lax.ppermute(after(first_hops[0], b), "tp", trade)

    chosen, dec_rows = chosen_queries(facts, after(dec_query[0], first_hops[0]), lanes)
    wanted = lax.all_to_all(chosen, "tp", split_axis=0, concat_axis=0, tiled=True)
    wanted = other_half(after(wanted, c))
    parts = partial_decode(facts, wanted, mine, lanes)
    parts = lax.all_to_all(parts, "tp", split_axis=0, concat_axis=0, tiled=True)
    dec_out = merged(facts, other_half(parts), dec_rows, dec_key[0], dec_value[0], lanes)

    received = []
    for g, (block, a) in enumerate(zip(mine, first_hops)):
        if g:
            b = lax.ppermute(after(block, received[0][2]), "tp", beside)
            c = lax.ppermute(a, "tp", trade)
        d = jnp.concatenate([a[1:], c], axis=0)
        d = lax.ppermute(after(d, parts) if g else d, "tp", ahead_again)
        received.append((a, b, c, d))
    out = None
    for g, (base, n) in enumerate(zip(bases, CHUNKS)):
        if g:
            out = after(out, dec_out)
        out = prompt_heads(base, n, 0, n, facts, query, (mine[g], *received[g]), out)
    return (out[None], dec_out[None])


def solution(mesh):
    placed = (
        P("section", ("groups", "tp"), None),
        P("section", ("groups", "tp"), None),
        P("section", ("groups", "tp"), None),
        P(None, "groups"),
        P(None, "groups"),
        P("section", None, "groups", "tp"),
        P("section", None, "groups", None),
        P("section", None, "groups", None),
    )
    return jax.shard_map(
        on_device,
        mesh=mesh,
        in_specs=placed,
        out_specs=(P("section", ("groups", "tp"), None), P("section", None, "groups", "tp")),
        check_vma=False,
    )
```

```python
import functools
import math

import jax
import jax.numpy as jnp
from jax import lax
from jax.experimental import pallas as pl
from jax.experimental.pallas import tpu as pltpu
from jax.sharding import PartitionSpec as P

QH = 64
KVH = 8
HD = 128
PAGE = 128
MAXP = 8
STEPS = 4
GROUP = QH // KVH
SCALE = HD ** (-0.5)
EXP2_SCALE = SCALE * math.log2(math.e)
LOW = -1e30
CHUNKS = (4, 4)
CUTS = (2, 2)
ROWS = 256
LN2 = math.log(2.0)
SMEM = pl.BlockSpec(memory_space=pltpu.SMEM)
VMEM = pl.BlockSpec(memory_space=pltpu.VMEM)


def dot(a, b):
    return jnp.dot(a, b, preferred_element_type=jnp.float32)


def page_facts(facts, half, page):
    requests = facts.shape[1] // 2
    owner, first, live, end = -1, 0, PAGE, 0
    for r in range(requests):
        start, end = end, end + facts[half, r]
        begun = start <= page
        owner = jnp.where(begun, r, owner)
        first = jnp.where(begun, start, first)
        live = jnp.where(end - 1 == page, facts[half, requests + r], live)
    return owner, first, live


def params(limit):
    return dict(
        compiler_params=pltpu.CompilerParams(vmem_limit_bytes=limit << 20),
        cost_estimate=pl.CostEstimate(flops=1, bytes_accessed=1, transcendentals=0),
    )


def pack_kernel(base, by_head, k_ref, v_ref, *rest):
    o_ref, k_part, v_part, sems = rest[-4:]
    n = k_part.shape[1] // HD
    own = slice(base * HD, (base + n) * HD)
    copies = [
        pltpu.make_async_copy(source.at[:, own], part, sems.at[spot])
        for spot, (source, part) in enumerate(((k_ref, k_part), (v_ref, v_part)))
    ]
    for copy in copies:
        copy.start()
    for copy in copies:
        copy.wait()
    for j in range(n):
        columns = slice(j * HD, (j + 1) * HD)
        for p in range(2):
            rows = slice(p * PAGE, (p + 1) * PAGE)
            turned = jnp.transpose(k_part[rows, columns].astype(jnp.float32)).astype(jnp.bfloat16)
            if by_head:
                o_ref[j, p, 0] = turned
                o_ref[j, p, 1] = v_part[rows, columns]
            else:
                o_ref[p, columns] = turned
                o_ref[p, (n + j) * HD:(n + j + 1) * HD] = v_part[rows, columns]


def pack(base, n, key, value, by_head=False):
    shape = (n, 2, 2, HD, PAGE) if by_head else (2, 2 * n * HD, PAGE)
    part = pltpu.VMEM((key.shape[0], n * HD), jnp.bfloat16)
    return pl.pallas_call(
        functools.partial(pack_kernel, base, by_head),
        out_shape=jax.ShapeDtypeStruct(shape, jnp.bfloat16),
        in_specs=[pl.BlockSpec(memory_space=pl.ANY)] * 2,
        out_specs=VMEM,
        scratch_shapes=[part, part, pltpu.SemaphoreType.DMA((2,))],
        name="pack",
        **params(48),
    )(key, value)


def prompt_kernel(n, low, facts, q_ref, *rest):
    o_ref, keys, values, causal = rest[-4:]
    head = low + pl.program_id(0)
    spots = [pl.ds(pl.multiple_of((x + head) * HD, HD), HD) for x in (0, n)]
    mine, a, b, c, d = [[[x[p, at] for at in spots] for p in range(2)] for x in rest[:5]]
    e = [rest[5][at] for at in spots]
    half, place = lax.axis_index("section"), lax.axis_index("tp")
    even = place % 2 == 0
    near, far = 2 * place - 2, 2 * place - 6
    page_c = jnp.where(even, near, far)
    page_be = jnp.where(even, far, near)
    choose = jnp.full((HD, PAGE), even)
    be = [
        [jnp.where(choose, x, y) for x, y in zip(late, b[p])] for p, late in enumerate((d[1], e))
    ]
    row = lax.broadcasted_iota(jnp.int32, (PAGE, PAGE), 0)
    col = lax.broadcasted_iota(jnp.int32, (PAGE, PAGE), 1)
    causal[...] = jnp.where(col <= row, 0.0, LOW)
    one = jnp.ones((PAGE, HD), jnp.bfloat16)
    zero = jnp.zeros((PAGE, HD), jnp.bfloat16)
    lives = []

    for i in range(2):
        _, first, live = page_facts(facts, half, 2 * place + i)
        lives.append(live)
        stand_in = jnp.broadcast_to(mine[i][0][:, :1], (HD, PAGE))
        if i == 0:
            pages = [(*d[0], 2 * place - 7)]
        else:
            pages = [(*mine[0], 2 * place)]
        pages.append((*mine[i], None))
        pages += [(*a[p], 2 * place - 4 + p) for p in range(2)]
        pages += [(*c[p], page_c + p) for p in range(2)]
        pages += [(*be[p], page_be + p) for p in range(2)]
        for spot, (k, v, number) in enumerate(pages):
            count = one
            if number is not None:
                seen = jnp.full((PAGE, HD), number >= first)
                k = jnp.where(seen, k, stand_in)
                v = jnp.where(seen, v, zero)
                count = jnp.where(seen, one, zero)
            at = slice(spot * PAGE, (spot + 1) * PAGE)
            keys[i, :HD, at] = k
            keys[i, HD:, at] = k
            values[i, at, :HD] = v
            values[i, at, HD:] = count

    heads_at_once = ROWS // PAGE
    blocks = [(i, start) for i in range(2) for start in range(0, GROUP, heads_at_once)]

    def halves(query):
        query = query.astype(jnp.float32) * EXP2_SCALE
        high = query.astype(jnp.bfloat16)
        low = (query - high.astype(jnp.float32)).astype(jnp.bfloat16)
        return jnp.concatenate([high, low], axis=1)

    def queries(i, start):
        return halves(
            jnp.concatenate(
                [
                    q_ref[i * PAGE:(i + 1) * PAGE, h * HD:(h + 1) * HD]
                    for h in range(start, start + heads_at_once)
                ],
                axis=0,
            )
        )

    def divided(mixed, live):
        total = mixed[:, HD:]
        near = pl.reciprocal(total, approx=True)
        near = near * (2.0 - total * near)
        token = lax.broadcasted_iota(jnp.int32, (total.shape[0], HD), 0) % PAGE
        return jnp.where(token < live, mixed[:, :HD] * near, 0.0).astype(jnp.bfloat16)

    tiles = [slice(t, t + 2 * PAGE) for t in range(0, MAXP * PAGE, 2 * PAGE)]

    def soft(score, top):
        score = score - top
        near = score.astype(jnp.bfloat16)
        step = (score - near.astype(jnp.float32)) * LN2 + 1.0
        return (jnp.exp2(near).astype(jnp.float32) * step).astype(jnp.bfloat16)

    for i, start in blocks:
        query = queries(i, start)
        scores = [dot(query, keys[i, :, at]) for at in tiles]
        bias = jnp.concatenate([causal[...]] * heads_at_once, axis=0)
        scores[0] = jnp.concatenate([scores[0][:, :PAGE], scores[0][:, PAGE:] + bias], axis=1)
        top = jnp.max(functools.reduce(jnp.maximum, scores), axis=1, keepdims=True)
        probs = jnp.concatenate([soft(score, top) for score in scores], axis=1)
        out = divided(dot(probs, values[i]), lives[i])
        for number in range(heads_at_once):
            h = start + number
            o_ref[i * PAGE:(i + 1) * PAGE, h * HD:(h + 1) * HD] = out[number * PAGE:(number + 1) * PAGE]


def prompt_heads(base, n, low, high, facts, query, blocks, done):
    tok = query.shape[0]

    wide = pl.BlockSpec((tok, GROUP * HD), lambda j, *_: (0, base + low + j))
    operands = [facts, query, *blocks]
    specs = [wide] + [VMEM] * len(blocks)
    aliases = {}
    if done is not None:
        aliases = {len(operands): 0}
        operands.append(done)
        specs.append(pl.BlockSpec(memory_space=pl.ANY))
    return pl.pallas_call(
        functools.partial(prompt_kernel, n, low),
        out_shape=jax.ShapeDtypeStruct(query.shape, jnp.bfloat16),
        grid_spec=pltpu.PrefetchScalarGridSpec(
            num_scalar_prefetch=1,
            grid=(high - low,),
            in_specs=specs,
            out_specs=wide,
            scratch_shapes=[
                pltpu.VMEM((2, 2 * HD, MAXP * PAGE), jnp.bfloat16),
                pltpu.VMEM((2, MAXP * PAGE, 2 * HD), jnp.bfloat16),
                pltpu.VMEM((PAGE, PAGE), jnp.float32),
            ],
        ),
        input_output_aliases=aliases,
        name="prompt_attention",
        compiler_params=pltpu.CompilerParams(vmem_limit_bytes=48 << 20),
        cost_estimate=pl.CostEstimate(
            flops=(high - low) * QH // KVH * tok * 8 * PAGE * HD * 8,
            bytes_accessed=4 * (high - low) * tok * GROUP * HD,
            transcendentals=0,
        ),
    )(*operands)


def decode_kernel(facts, head_ref, pool_ref, q_ref, k_ref, v_ref, o_ref):
    requests, width = q_ref.shape[:2]
    last = 2 * pool_ref.shape[0] - 1
    other = 1 - lax.axis_index("section")
    lane = lax.broadcasted_iota(jnp.int32, (width, PAGE), 1)
    step = lax.broadcasted_iota(jnp.int32, (width, 1), 0) % STEPS
    scores, fresh, pages = [], [], []
    end = 0
    for r in range(requests):
        start, end = end, end + facts[other, r]
        length = PAGE * (end - start - 1) + facts[other, requests + r]
        query = q_ref[r]
        numbers = [jnp.minimum(start + j, last) for j in range(MAXP)]
        pages.append([(number // 2, number % 2) for number in numbers])
        tiles = []
        for j, at in enumerate(pages[r]):
            score = dot(query, pool_ref[at[0], at[1], 0]) * SCALE
            tiles.append(jnp.where(lane < length - j * PAGE, score, LOW))
        scores.append(jnp.concatenate(tiles, axis=1))
        keys = k_ref[r, head_ref[0]].astype(jnp.float32)
        wide = query.astype(jnp.float32)
        news = [jnp.sum(wide * keys[u:u + 1], axis=1, keepdims=True) * SCALE for u in range(STEPS)]
        fresh.append([jnp.where(u <= step, x, LOW) for u, x in enumerate(news)])
    score = jnp.concatenate(scores, axis=0)
    fresh = [jnp.concatenate([x[u] for x in fresh], axis=0) for u in range(STEPS)]
    top = functools.reduce(jnp.maximum, fresh + [jnp.max(score, axis=1, keepdims=True)])
    terms = jnp.exp(score - top)
    fresh = [jnp.exp(x - top) for x in fresh]
    total = functools.reduce(jnp.add, fresh + [jnp.sum(terms, axis=1, keepdims=True)])
    high = terms.astype(jnp.bfloat16)
    low = (terms - high.astype(jnp.float32)).astype(jnp.bfloat16)
    for r in range(requests):
        rows = slice(r * width, (r + 1) * width)
        new_values = v_ref[r, head_ref[0]].astype(jnp.float32)
        mixed = functools.reduce(
            jnp.add, [fresh[u][rows] * new_values[u:u + 1] for u in range(STEPS)]
        )
        for j, at in enumerate(pages[r]):
            values = pool_ref[at[0], at[1], 1]
            columns = slice(j * PAGE, (j + 1) * PAGE)
            mixed = mixed + dot(high[rows, columns], values) + dot(low[rows, columns], values)
        o_ref[r] = (mixed / total[rows]).astype(jnp.bfloat16)


def decoded(facts, head, pool, query, new_key, new_value, lanes):
    requests, here = query.shape[1], QH // lanes
    query = jnp.transpose(query.reshape(STEPS, requests, here, HD), (1, 2, 0, 3))
    query = query.reshape(requests, here * STEPS, HD)
    fresh = [
        jnp.transpose(x.reshape(STEPS, requests, KVH, HD), (1, 2, 0, 3)) for x in (new_key, new_value)
    ]
    out = pl.pallas_call(
        decode_kernel,
        out_shape=jax.ShapeDtypeStruct(query.shape, jnp.bfloat16),
        in_specs=[SMEM, SMEM, VMEM, VMEM, VMEM, VMEM],
        out_specs=VMEM,
        name="decode_attention",
        **params(32),
    )(facts, head, pool, query, *fresh)
    out = jnp.transpose(out.reshape(requests, here, STEPS, HD), (2, 0, 1, 3))
    return out.reshape(STEPS, requests, here * HD)


def after(x, *earlier):
    return lax.optimization_barrier((x, *earlier))[0]


def on_device(
    prefill_query, prefill_key, prefill_value, counts, fills, dec_query, dec_key, dec_value
):
    lanes = lax.axis_size("tp")
    query, key, value = prefill_query[0], prefill_key[0], prefill_value[0]
    facts = jnp.concatenate([counts, fills], axis=1)
    head = (lax.axis_index("tp") * (QH // lanes) // GROUP).reshape(1)
    bases = [sum(CHUNKS[:g]) for g in range(len(CHUNKS))]

    ahead = [(i, i + 2) for i in range(lanes - 2)]
    ahead_again = [(i, i + 2) for i in range(2, lanes - 2)]
    beside = [(i, i + 1) for i in range(0, lanes, 2)]
    trade = [(i, i ^ 1) for i in range(2, lanes)]
    back = [(i, i - 1) for i in range(5, lanes, 2)]
    mine = []
    for base, n in zip(bases, CHUNKS):
        mine.append(pack(base, n, after(key, *mine), value))
    first_hops = [lax.ppermute(block, "tp", ahead) for block in mine]
    across = []
    for g, (block, a) in enumerate(zip(mine, first_hops)):
        b = lax.ppermute(after(block, across[0][1]) if g else block, "tp", beside)
        across.append((b, lax.ppermute(a if g else after(a, b), "tp", trade)))
    received, out = [], None
    for g, (a, (b, c)) in enumerate(zip(first_hops, across)):
        d = jnp.concatenate([a[1:], c[:1]], axis=0)
        d = lax.ppermute(d if g else after(d, first_hops[1]), "tp", ahead_again)
        if g:
            blocks = (mine[0], *received[0])
            out = prompt_heads(bases[0], CHUNKS[0], 0, CUTS[0], facts, query, blocks, None)
            late = after(d, out)
            out = after(out, d)
            out = prompt_heads(bases[0], CHUNKS[0], CUTS[0], CHUNKS[0], facts, query, blocks, out)
        else:
            late = after(d, across[1][1])
        e = lax.ppermute(late[0], "tp", back)
        received.append((a, b, c, d, e))

    pages = pack(0, KVH, after(key, across[0][1]), value, by_head=True)
    pages = jnp.repeat(pages, lanes // KVH, axis=0)
    arrived = lax.all_to_all(
        after(pages, received[0][3]), "tp", split_axis=0, concat_axis=0, tiled=True
    )
    blocks = (mine[1], *received[1])
    out = prompt_heads(bases[1], CHUNKS[1], 0, CUTS[1], facts, query, blocks, out)
    arrived, out = lax.optimization_barrier((arrived, out))
    pool = lax.ppermute(arrived, "section", [(0, 1), (1, 0)])
    out = prompt_heads(bases[1], CHUNKS[1], CUTS[1], CHUNKS[1], facts, query, blocks, out)
    dec_out = decoded(facts, head, pool, dec_query[0], dec_key[0], dec_value[0], lanes)
    return (out[None], dec_out[None])


def solution(mesh):
    placed = (
        P("section", ("groups", "tp"), None),
        P("section", ("groups", "tp"), None),
        P("section", ("groups", "tp"), None),
        P(None, "groups"),
        P(None, "groups"),
        P("section", None, "groups", "tp"),
        P("section", None, "groups", None),
        P("section", None, "groups", None),
    )
    return jax.shard_map(
        on_device,
        mesh=mesh,
        in_specs=placed,
        out_specs=(P("section", ("groups", "tp"), None), P("section", None, "groups", "tp")),
        check_vma=False,
    )
```

```python
import functools
import math

import jax
import jax.numpy as jnp
from jax import lax
from jax.experimental import pallas as pl
from jax.experimental.pallas import tpu as pltpu
from jax.sharding import PartitionSpec as P

QH = 64
KVH = 8
HD = 128
PAGE = 128
MAXP = 8
STEPS = 4
GROUP = QH // KVH
SCALE = HD ** (-0.5)
EXP2_SCALE = SCALE * math.log2(math.e)
LOW = -1e30
CHUNKS = (4, 4)
CUTS = (2, 2)
ROWS = 512
SMEM = pl.BlockSpec(memory_space=pltpu.SMEM)
VMEM = pl.BlockSpec(memory_space=pltpu.VMEM)


def dot(a, b):
    return jnp.dot(a, b, preferred_element_type=jnp.float32)


def page_facts(facts, half, page):
    requests = facts.shape[1] // 2
    owner, first, live, end = -1, 0, PAGE, 0
    for r in range(requests):
        start, end = end, end + facts[half, r]
        begun = start <= page
        owner = jnp.where(begun, r, owner)
        first = jnp.where(begun, start, first)
        live = jnp.where(end - 1 == page, facts[half, requests + r], live)
    return owner, first, live


def params(limit):
    return dict(
        compiler_params=pltpu.CompilerParams(vmem_limit_bytes=limit << 20),
        cost_estimate=pl.CostEstimate(flops=1, bytes_accessed=1, transcendentals=0),
    )


def pack_kernel(base, by_head, k_ref, v_ref, *rest):
    o_ref, k_part, v_part, sems = rest[-4:]
    n = k_part.shape[1] // HD
    own = slice(base * HD, (base + n) * HD)
    copies = [
        pltpu.make_async_copy(source.at[:, own], part, sems.at[spot])
        for spot, (source, part) in enumerate(((k_ref, k_part), (v_ref, v_part)))
    ]
    for copy in copies:
        copy.start()
    for copy in copies:
        copy.wait()
    for j in range(n):
        columns = slice(j * HD, (j + 1) * HD)
        for p in range(2):
            rows = slice(p * PAGE, (p + 1) * PAGE)
            turned = jnp.transpose(k_part[rows, columns].astype(jnp.float32)).astype(jnp.bfloat16)
            if by_head:
                o_ref[j, p, 0] = turned
                o_ref[j, p, 1] = v_part[rows, columns]
            else:
                o_ref[p, columns] = turned
                o_ref[p, (n + j) * HD:(n + j + 1) * HD] = v_part[rows, columns]


def pack(base, n, key, value, by_head=False):
    shape = (n, 2, 2, HD, PAGE) if by_head else (2, 2 * n * HD, PAGE)
    part = pltpu.VMEM((key.shape[0], n * HD), jnp.bfloat16)
    return pl.pallas_call(
        functools.partial(pack_kernel, base, by_head),
        out_shape=jax.ShapeDtypeStruct(shape, jnp.bfloat16),
        in_specs=[pl.BlockSpec(memory_space=pl.ANY)] * 2,
        out_specs=VMEM,
        scratch_shapes=[part, part, pltpu.SemaphoreType.DMA((2,))],
        name="pack",
        **params(48),
    )(key, value)


def prompt_kernel(facts, side, q_ref, *rest):
    o_ref, keys, values, causal = rest[-4:]
    pairs = list(zip(rest[:12:2], rest[1:12:2]))
    mine, b, d = [[[x[p] for x in pairs[w]] for p in range(2)] for w in (0, 3, 4)]
    a, c = [[[x[0, p] for x in pairs[w]] for p in range(2)] for w in (1, 2)]
    e = [x[...] for x in pairs[5]]
    half, place = lax.axis_index("section"), lax.axis_index("tp")
    even = place % 2 == 0
    near, far = 2 * place - 2, 2 * place - 6
    page_c = jnp.where(even, near, far)
    page_be = jnp.where(even, far, near)
    choose = jnp.full((HD, PAGE), even)
    be = [
        [jnp.where(choose, x, y) for x, y in zip(late, b[p])] for p, late in enumerate((d[1], e))
    ]
    row = lax.broadcasted_iota(jnp.int32, (PAGE, PAGE), 0)
    col = lax.broadcasted_iota(jnp.int32, (PAGE, PAGE), 1)
    causal[...] = jnp.where(col <= row, 0.0, LOW)
    one = jnp.ones((PAGE, HD), jnp.bfloat16)
    zero = jnp.zeros((PAGE, HD), jnp.bfloat16)
    lives = []

    for i in range(2):
        _, first, live = page_facts(facts, half, 2 * place + i)
        lives.append(live)
        stand_in = jnp.broadcast_to(mine[i][0][:, :1], (HD, PAGE))
        if i == 0:
            pages = [(*d[0], 2 * place - 7)]
        else:
            pages = [(*mine[0], 2 * place)]
        pages.append((*mine[i], None))
        pages += [(*a[p], 2 * place - 4 + p) for p in range(2)]
        pages += [(*c[p], page_c + p) for p in range(2)]
        pages += [(*be[p], page_be + p) for p in range(2)]
        for spot, (k, v, number) in enumerate(pages):
            count = one
            if number is not None:
                seen = jnp.full((PAGE, HD), number >= first)
                k = jnp.where(seen, k, stand_in)
                v = jnp.where(seen, v, zero)
                count = jnp.where(seen, one, zero)
            at = slice(spot * PAGE, (spot + 1) * PAGE)
            keys[i, :HD, at] = k
            keys[i, HD:, at] = k
            values[i, at, :HD] = v
            values[i, at, HD:] = count

    heads_at_once = ROWS // PAGE
    blocks = [(i, start) for i in range(2) for start in range(0, GROUP, heads_at_once)]

    def halves(query):
        query = query.astype(jnp.float32) * EXP2_SCALE
        high = query.astype(jnp.bfloat16)
        low = (query - high.astype(jnp.float32)).astype(jnp.bfloat16)
        return jnp.concatenate([high, low], axis=1)

    def queries(i, start):
        return halves(
            jnp.concatenate(
                [
                    q_ref[i * PAGE:(i + 1) * PAGE, h * HD:(h + 1) * HD]
                    for h in range(start, start + heads_at_once)
                ],
                axis=0,
            )
        )

    def divided(mixed, live):
        total = mixed[:, HD:]
        near = pl.reciprocal(total, approx=True)
        near = near * (2.0 - total * near)
        token = lax.broadcasted_iota(jnp.int32, (total.shape[0], HD), 0) % PAGE
        return jnp.where(token < live, mixed[:, :HD] * near, 0.0).astype(jnp.bfloat16)

    tiles = [slice(t, t + 2 * PAGE) for t in range(0, MAXP * PAGE, 2 * PAGE)]

    def scores(i, start):
        query = queries(i, start)
        scores = [dot(query, keys[i, :, at]) for at in tiles]
        bias = jnp.concatenate([causal[...]] * heads_at_once, axis=0)
        scores[0] = jnp.concatenate([scores[0][:, :PAGE], scores[0][:, PAGE:] + bias], axis=1)
        return scores

    def finish(i, start, scores):
        top = jnp.max(functools.reduce(jnp.maximum, scores), axis=1, keepdims=True)
        mixed = None
        for score, at in zip(scores, tiles):
            part = dot(jnp.exp2(score - top).astype(jnp.bfloat16), values[i, at])
            mixed = part if mixed is None else mixed + part
        out = divided(mixed, lives[i])
        for number in range(heads_at_once):
            h = start + number
            o_ref[i * PAGE:(i + 1) * PAGE, h * HD:(h + 1) * HD] = out[number * PAGE:(number + 1) * PAGE]

    ready = scores(*blocks[0])
    for index, block in enumerate(blocks):
        following = scores(*blocks[index + 1]) if index + 1 < len(blocks) else None
        finish(*block, ready)
        ready = following


def prompt_heads(base, n, low, high, facts, side, query, blocks, done):
    tok = query.shape[0]
    firsts = (low, n + low)

    def block(first):
        return pl.BlockSpec((2, HD, PAGE), lambda j, *_: (0, first + j, 0))

    def half_block(first):
        return pl.BlockSpec((HD, PAGE), lambda j, *_: (first + j, 0))

    def of_pair(first, which):
        return pl.BlockSpec(
            (1, 2, HD, PAGE), lambda j, facts, side: (jnp.abs(side[0] - which), 0, first + j, 0)
        )

    wide = pl.BlockSpec((tok, GROUP * HD), lambda j, *_: (0, base + low + j))
    mine, pair, b, d, e = blocks
    operands = [facts, side, query, mine, mine, pair, pair, pair, pair, b, b, d, d, e, e]
    specs = [wide] + [block(x) for x in firsts]
    specs += [of_pair(x, which) for which in range(2) for x in firsts]
    specs += [block(x) for x in firsts] * 2 + [half_block(x) for x in firsts]
    aliases = {}
    if done is not None:
        aliases = {len(operands): 0}
        operands.append(done)
        specs.append(pl.BlockSpec(memory_space=pl.ANY))
    return pl.pallas_call(
        prompt_kernel,
        out_shape=jax.ShapeDtypeStruct(query.shape, jnp.bfloat16),
        grid_spec=pltpu.PrefetchScalarGridSpec(
            num_scalar_prefetch=2,
            grid=(high - low,),
            in_specs=specs,
            out_specs=wide,
            scratch_shapes=[
                pltpu.VMEM((2, 2 * HD, MAXP * PAGE), jnp.bfloat16),
                pltpu.VMEM((2, MAXP * PAGE, 2 * HD), jnp.bfloat16),
                pltpu.VMEM((PAGE, PAGE), jnp.float32),
            ],
        ),
        input_output_aliases=aliases,
        name="prompt_attention",
        compiler_params=pltpu.CompilerParams(vmem_limit_bytes=48 << 20),
        cost_estimate=pl.CostEstimate(
            flops=(high - low) * QH // KVH * tok * 8 * PAGE * HD * 8,
            bytes_accessed=4 * (high - low) * tok * GROUP * HD,
            transcendentals=0,
        ),
    )(*operands)


def decode_kernel(facts, head_ref, pool_ref, q_ref, k_ref, v_ref, o_ref):
    requests, width = q_ref.shape[:2]
    last = 2 * pool_ref.shape[0] - 1
    other = 1 - lax.axis_index("section")
    lane = lax.broadcasted_iota(jnp.int32, (width, PAGE), 1)
    step = lax.broadcasted_iota(jnp.int32, (width, 1), 0) % STEPS
    scores, fresh, pages = [], [], []
    end = 0
    for r in range(requests):
        start, end = end, end + facts[other, r]
        length = PAGE * (end - start - 1) + facts[other, requests + r]
        query = q_ref[r]
        numbers = [jnp.minimum(start + j, last) for j in range(MAXP)]
        pages.append([(number // 2, number % 2) for number in numbers])
        tiles = []
        for j, at in enumerate(pages[r]):
            score = dot(query, pool_ref[at[0], at[1], 0]) * SCALE
            tiles.append(jnp.where(lane < length - j * PAGE, score, LOW))
        scores.append(jnp.concatenate(tiles, axis=1))
        keys = k_ref[r, head_ref[0]].astype(jnp.float32)
        wide = query.astype(jnp.float32)
        news = [jnp.sum(wide * keys[u:u + 1], axis=1, keepdims=True) * SCALE for u in range(STEPS)]
        fresh.append([jnp.where(u <= step, x, LOW) for u, x in enumerate(news)])
    score = jnp.concatenate(scores, axis=0)
    fresh = [jnp.concatenate([x[u] for x in fresh], axis=0) for u in range(STEPS)]
    top = functools.reduce(jnp.maximum, fresh + [jnp.max(score, axis=1, keepdims=True)])
    terms = jnp.exp(score - top)
    fresh = [jnp.exp(x - top) for x in fresh]
    total = functools.reduce(jnp.add, fresh + [jnp.sum(terms, axis=1, keepdims=True)])
    high = terms.astype(jnp.bfloat16)
    low = (terms - high.astype(jnp.float32)).astype(jnp.bfloat16)
    for r in range(requests):
        rows = slice(r * width, (r + 1) * width)
        new_values = v_ref[r, head_ref[0]].astype(jnp.float32)
        mixed = functools.reduce(
            jnp.add, [fresh[u][rows] * new_values[u:u + 1] for u in range(STEPS)]
        )
        for j, at in enumerate(pages[r]):
            values = pool_ref[at[0], at[1], 1]
            columns = slice(j * PAGE, (j + 1) * PAGE)
            mixed = mixed + dot(high[rows, columns], values) + dot(low[rows, columns], values)
        o_ref[r] = (mixed / total[rows]).astype(jnp.bfloat16)


def decoded(facts, head, pool, query, new_key, new_value, lanes):
    requests, here = query.shape[1], QH // lanes
    query = jnp.transpose(query.reshape(STEPS, requests, here, HD), (1, 2, 0, 3))
    query = query.reshape(requests, here * STEPS, HD)
    fresh = [
        jnp.transpose(x.reshape(STEPS, requests, KVH, HD), (1, 2, 0, 3)) for x in (new_key, new_value)
    ]
    out = pl.pallas_call(
        decode_kernel,
        out_shape=jax.ShapeDtypeStruct(query.shape, jnp.bfloat16),
        in_specs=[SMEM, SMEM, VMEM, VMEM, VMEM, VMEM],
        out_specs=VMEM,
        name="decode_attention",
        **params(32),
    )(facts, head, pool, query, *fresh)
    out = jnp.transpose(out.reshape(requests, here, STEPS, HD), (2, 0, 1, 3))
    return out.reshape(STEPS, requests, here * HD)


def after(x, *earlier):
    return lax.optimization_barrier((x, *earlier))[0]


def on_device(
    prefill_query, prefill_key, prefill_value, counts, fills, dec_query, dec_key, dec_value
):
    lanes = lax.axis_size("tp")
    query, key, value = prefill_query[0], prefill_key[0], prefill_value[0]
    facts = jnp.concatenate([counts, fills], axis=1)
    head = (lax.axis_index("tp") * (QH // lanes) // GROUP).reshape(1)
    bases = [sum(CHUNKS[:g]) for g in range(len(CHUNKS))]

    ahead = [(i, i + 2) for i in range(lanes - 2)]
    ahead_again = [(i, i + 2) for i in range(2, lanes - 2)]
    beside = [(i, i + 1) for i in range(0, lanes, 2)]
    back = [(i, i - 1) for i in range(5, lanes, 2)]
    mine = []
    for base, n in zip(bases, CHUNKS):
        mine.append(pack(base, n, after(key, *mine), value))
    side = (lax.axis_index("tp") % 2).reshape(1)
    couples = [[i, i + 1] for i in range(0, lanes, 2)]
    first_hops = [lax.ppermute(block, "tp", ahead) for block in mine]
    b = lax.ppermute(mine[0], "tp", beside)
    pairs = [after(first_hops[0], b), first_hops[1]]
    pairs = [lax.all_gather(a, "tp", axis_index_groups=couples) for a in pairs]
    received, out = [], None
    for g, (block, a, pair) in enumerate(zip(mine, first_hops, pairs)):
        if g:
            b = lax.ppermute(after(block, pairs[0]), "tp", beside)
        d = jnp.concatenate([a[1:], pair[1, :1]], axis=0)
        d = lax.ppermute(d if g else after(d, first_hops[1]), "tp", ahead_again)
        if g:
            blocks = (mine[0], pairs[0], *received[0])
            out = prompt_heads(bases[0], CHUNKS[0], 0, CUTS[0], facts, side, query, blocks, None)
            late, done = after(d, out), out
            out = after(out, d)
            out = prompt_heads(
                bases[0], CHUNKS[0], CUTS[0], CHUNKS[0], facts, side, query, blocks, out
            )
        else:
            late = after(d, pairs[1])
        e = lax.ppermute(late[0], "tp", back)
        received.append((b, d, e))

    pages = pack(0, KVH, after(key, pairs[0]), value, by_head=True)
    pages = jnp.repeat(pages, lanes // KVH, axis=0)
    arrived = lax.all_to_all(after(pages, done), "tp", split_axis=0, concat_axis=0, tiled=True)
    blocks = (mine[1], pairs[1], *received[1])
    out = prompt_heads(bases[1], CHUNKS[1], 0, CUTS[1], facts, side, query, blocks, out)
    arrived, out = lax.optimization_barrier((arrived, out))
    pool = lax.ppermute(arrived, "section", [(0, 1), (1, 0)])
    out = prompt_heads(bases[1], CHUNKS[1], CUTS[1], CHUNKS[1], facts, side, query, blocks, out)
    dec_out = decoded(facts, head, pool, dec_query[0], dec_key[0], dec_value[0], lanes)
    return (out[None], dec_out[None])


def solution(mesh):
    placed = (
        P("section", ("groups", "tp"), None),
        P("section", ("groups", "tp"), None),
        P("section", ("groups", "tp"), None),
        P(None, "groups"),
        P(None, "groups"),
        P("section", None, "groups", "tp"),
        P("section", None, "groups", None),
        P("section", None, "groups", None),
    )
    return jax.shard_map(
        on_device,
        mesh=mesh,
        in_specs=placed,
        out_specs=(P("section", ("groups", "tp"), None), P("section", None, "groups", "tp")),
        check_vma=False,
    )
```

```python
import functools
import math

import jax
import jax.numpy as jnp
from jax import lax
from jax.experimental import pallas as pl
from jax.experimental.pallas import tpu as pltpu
from jax.sharding import PartitionSpec as P

QH = 64
KVH = 8
HD = 128
PAGE = 128
MAXP = 8
STEPS = 4
GROUP = QH // KVH
SCALE = HD ** (-0.5)
EXP2_SCALE = SCALE * math.log2(math.e)
LOW = -1e30
CHUNKS = (4, 4)
ROWS = 512
SMEM = pl.BlockSpec(memory_space=pltpu.SMEM)
VMEM = pl.BlockSpec(memory_space=pltpu.VMEM)


def dot(a, b):
    return jnp.dot(a, b, preferred_element_type=jnp.float32)


def page_facts(counts, fills, half, page):
    requests = counts.shape[1]
    owner, first, live, end = -1, 0, PAGE, 0
    for r in range(requests):
        start, end = end, end + counts[half, r]
        begun = start <= page
        owner = jnp.where(begun, r, owner)
        first = jnp.where(begun, start, first)
        live = jnp.where(end - 1 == page, fills[half, r], live)
    return owner, first, live


def params(limit):
    return dict(
        compiler_params=pltpu.CompilerParams(vmem_limit_bytes=limit << 20),
        cost_estimate=pl.CostEstimate(flops=1, bytes_accessed=1, transcendentals=0),
    )


def pack_kernel(base, by_head, k_ref, v_ref, *rest):
    o_ref, k_part, v_part, sems = rest[-4:]
    n = k_part.shape[1] // HD
    own = slice(base * HD, (base + n) * HD)
    copies = [
        pltpu.make_async_copy(source.at[:, own], part, sems.at[spot])
        for spot, (source, part) in enumerate(((k_ref, k_part), (v_ref, v_part)))
    ]
    for copy in copies:
        copy.start()
    for copy in copies:
        copy.wait()
    for j in range(n):
        columns = slice(j * HD, (j + 1) * HD)
        for p in range(2):
            rows = slice(p * PAGE, (p + 1) * PAGE)
            turned = jnp.transpose(k_part[rows, columns].astype(jnp.float32)).astype(jnp.bfloat16)
            if by_head:
                o_ref[j, p, 0] = turned
                o_ref[j, p, 1] = v_part[rows, columns]
            else:
                o_ref[p, columns] = turned
                o_ref[p, (n + j) * HD:(n + j + 1) * HD] = v_part[rows, columns]


def pack(base, n, key, value, by_head=False):
    shape = (n, 2, 2, HD, PAGE) if by_head else (2, 2 * n * HD, PAGE)
    part = pltpu.VMEM((key.shape[0], n * HD), jnp.bfloat16)
    return pl.pallas_call(
        functools.partial(pack_kernel, base, by_head),
        out_shape=jax.ShapeDtypeStruct(shape, jnp.bfloat16),
        in_specs=[pl.BlockSpec(memory_space=pl.ANY)] * 2,
        out_specs=VMEM,
        scratch_shapes=[part, part, pltpu.SemaphoreType.DMA((2,))],
        name="pack",
        **params(48),
    )(key, value)


def flags_kernel(counts, fills, o_ref):
    half, place = lax.axis_index("section"), lax.axis_index("tp")
    even = place % 2 == 0
    near, far = 2 * place - 2, 2 * place - 6
    line = lax.broadcasted_iota(jnp.int32, o_ref.shape, 0)
    out = jnp.zeros(o_ref.shape, jnp.float32)
    for i in range(2):
        _, first, live = page_facts(counts, fills, half, 2 * place + i)
        numbers = [2 * place - 7 if i == 0 else 2 * place, 2 * place + i]
        for page in (2 * place - 4, jnp.where(even, near, far), jnp.where(even, far, near)):
            numbers += [page, page + 1]
        for spot, number in enumerate(numbers):
            out = jnp.where(line == i * MAXP + spot, jnp.where(number >= first, 1.0, 0.0), out)
        out = jnp.where(line == 2 * MAXP + i, live.astype(jnp.float32), out)
    o_ref[...] = out


def page_flags(counts, fills):
    return pl.pallas_call(
        flags_kernel,
        out_shape=jax.ShapeDtypeStruct((2 * MAXP + 8, PAGE), jnp.float32),
        in_specs=[SMEM, SMEM],
        out_specs=VMEM,
        name="page_flags",
        **params(48),
    )(counts, fills)


def prompt_kernel(n, low, flags, q_ref, *rest):
    o_ref, keys, values, causal, *probs = rest[-6:]
    head = low + pl.program_id(0)
    spots = [pl.ds(pl.multiple_of((x + head) * HD, HD), HD) for x in (0, n)]
    mine, a, b, c, d = [[[x[p, at] for at in spots] for p in range(x.shape[0])] for x in rest[:5]]
    choose = jnp.full((HD, PAGE), lax.axis_index("tp") % 2 == 0)
    be = [[jnp.where(choose, x, y) for x, y in zip(d[1 + p], b[p])] for p in range(2)]
    row = lax.broadcasted_iota(jnp.int32, (PAGE, PAGE), 0)
    col = lax.broadcasted_iota(jnp.int32, (PAGE, PAGE), 1)
    causal[...] = jnp.where(col <= row, 0.0, LOW)
    one = jnp.ones((PAGE, HD), jnp.bfloat16)
    zero = jnp.zeros((PAGE, HD), jnp.bfloat16)
    lives = [flags[2 * MAXP + i:2 * MAXP + i + 1, :] for i in range(2)]

    for i in range(2):
        stand_in = jnp.broadcast_to(mine[i][0][:, :1], (HD, PAGE))
        pages = [d[0] if i == 0 else mine[0], mine[i], *a, *c, *be]
        for spot, (k, v) in enumerate(pages):
            line = i * MAXP + spot
            seen = jnp.broadcast_to(flags[line:line + 1, :], (PAGE, HD)) > 0.0
            at = slice(spot * PAGE, (spot + 1) * PAGE)
            k = jnp.where(seen, k, stand_in)
            keys[i, :HD, at] = k
            keys[i, HD:, at] = k
            values[i, at, :HD] = jnp.where(seen, v, zero)
            values[i, at, HD:] = jnp.where(seen, one, zero)

    heads_at_once = ROWS // PAGE
    blocks = [(i, start) for i in range(2) for start in range(0, GROUP, heads_at_once)]

    def halves(query):
        query = query.astype(jnp.float32) * EXP2_SCALE
        high = query.astype(jnp.bfloat16)
        low = (query - high.astype(jnp.float32)).astype(jnp.bfloat16)
        return jnp.concatenate([high, low], axis=1)

    def queries(i, start):
        return halves(
            jnp.concatenate(
                [
                    q_ref[i * PAGE:(i + 1) * PAGE, h * HD:(h + 1) * HD]
                    for h in range(start, start + heads_at_once)
                ],
                axis=0,
            )
        )

    def divided(mixed, live):
        total = mixed[:, HD:]
        near = pl.reciprocal(total, approx=True)
        near = near * (2.0 - total * near)
        token = lax.broadcasted_iota(jnp.int32, (total.shape[0], HD), 0) % PAGE
        return jnp.where(token.astype(jnp.float32) < live, mixed[:, :HD] * near, 0.0).astype(jnp.bfloat16)

    tiles = [slice(t, t + 2 * PAGE) for t in range(0, MAXP * PAGE, 2 * PAGE)]

    def own_scores(query, i, repeat):
        own = dot(query, keys[i, :, tiles[0]])
        bias = jnp.concatenate([causal[...]] * repeat, axis=0)
        return jnp.concatenate([own[:, :PAGE], own[:, PAGE:] + bias], axis=1)

    def mix(block, slot, largest):
        i, start = block
        mixed = dot(probs[slot][...], values[i])
        out = divided(mixed, lives[i])
        for number in range(heads_at_once):
            h = start + number
            o_ref[i * PAGE:(i + 1) * PAGE, h * HD:(h + 1) * HD] = out[number * PAGE:(number + 1) * PAGE]
        return jnp.maximum(largest, mixed[:, HD:])

    largest = jnp.zeros((ROWS, HD), jnp.float32)
    for index in range(len(blocks) + 1):
        if index < len(blocks):
            i, slot = blocks[index][0], index % 2
            query = queries(*blocks[index])
            own = own_scores(query, i, heads_at_once)
            top = jnp.max(own, axis=1, keepdims=True)
            probs[slot][:, tiles[0]] = jnp.exp2(own - top).astype(jnp.bfloat16)
        if index > 0:
            largest = mix(blocks[index - 1], 1 - slot if index < len(blocks) else slot, largest)
        if index < len(blocks):
            for at in tiles[1:]:
                other = dot(query, keys[i, :, at])
                probs[slot][:, at] = jnp.exp2(other - top).astype(jnp.bfloat16)

    @pl.when(jnp.logical_not(jnp.max(largest) < 1e30))
    def _():
        def one(index, carry):
            i, h = index // GROUP, index % GROUP
            rows = pl.ds(pl.multiple_of(i * PAGE, PAGE), PAGE)
            columns = pl.ds(pl.multiple_of(h * HD, HD), HD)
            query = halves(q_ref[rows, columns])
            scores = [own_scores(query, i, 1)] + [dot(query, keys[i, :, at]) for at in tiles[1:]]
            top = jnp.max(functools.reduce(jnp.maximum, scores), axis=1, keepdims=True)
            mixed = jnp.zeros((PAGE, 2 * HD), jnp.float32)
            for score, at in zip(scores, tiles):
                mixed = mixed + dot(jnp.exp2(score - top).astype(jnp.bfloat16), values[i, at])
            o_ref[rows, columns] = divided(mixed, jnp.where(i == 0, lives[0], lives[1]))
            return carry

        lax.fori_loop(0, 2 * GROUP, one, 0)


def prompt_heads(base, n, low, high, flags, query, blocks, done):
    tok = query.shape[0]

    wide = pl.BlockSpec((tok, GROUP * HD), lambda j: (0, base + low + j))
    operands = [flags, query, *blocks]
    specs = [VMEM, wide] + [VMEM] * len(blocks)
    aliases = {}
    if done is not None:
        aliases = {len(operands): 0}
        operands.append(done)
        specs.append(pl.BlockSpec(memory_space=pl.ANY))
    return pl.pallas_call(
        functools.partial(prompt_kernel, n, low),
        out_shape=jax.ShapeDtypeStruct(query.shape, jnp.bfloat16),
        grid=(high - low,),
        in_specs=specs,
        out_specs=wide,
        scratch_shapes=[
            pltpu.VMEM((2, 2 * HD, MAXP * PAGE), jnp.bfloat16),
            pltpu.VMEM((2, MAXP * PAGE, 2 * HD), jnp.bfloat16),
            pltpu.VMEM((PAGE, PAGE), jnp.float32),
            pltpu.VMEM((ROWS, MAXP * PAGE), jnp.bfloat16),
            pltpu.VMEM((ROWS, MAXP * PAGE), jnp.bfloat16),
        ],
        input_output_aliases=aliases,
        name="prompt_attention",
        **params(48),
    )(*operands)


def decode_kernel(lanes, facts, pool_ref, q_ref, k_ref, v_ref, o_ref):
    requests, width = q_ref.shape[:2]
    last = 2 * pool_ref.shape[0] - 1
    other = 1 - lax.axis_index("section")
    head = lax.axis_index("tp") * (QH // lanes) // GROUP
    lane = lax.broadcasted_iota(jnp.int32, (width, PAGE), 1)
    step = lax.broadcasted_iota(jnp.int32, (width, 1), 0) % STEPS
    scores, fresh, pages = [], [], []
    end = 0
    for r in range(requests):
        start, end = end, end + facts[other, r]
        length = PAGE * (end - start - 1) + facts[other, requests + r]
        query = q_ref[r]
        numbers = [jnp.minimum(start + j, last) for j in range(MAXP)]
        pages.append([(number // 2, number % 2) for number in numbers])
        tiles = []
        for j, at in enumerate(pages[r]):
            score = dot(query, pool_ref[at[0], at[1], 0]) * SCALE
            tiles.append(jnp.where(lane < length - j * PAGE, score, LOW))
        scores.append(jnp.concatenate(tiles, axis=1))
        keys = k_ref[r, head].astype(jnp.float32)
        wide = query.astype(jnp.float32)
        news = [jnp.sum(wide * keys[u:u + 1], axis=1, keepdims=True) * SCALE for u in range(STEPS)]
        fresh.append([jnp.where(u <= step, x, LOW) for u, x in enumerate(news)])
    score = jnp.concatenate(scores, axis=0)
    fresh = [jnp.concatenate([x[u] for x in fresh], axis=0) for u in range(STEPS)]
    top = functools.reduce(jnp.maximum, fresh + [jnp.max(score, axis=1, keepdims=True)])
    terms = jnp.exp(score - top)
    fresh = [jnp.exp(x - top) for x in fresh]
    total = functools.reduce(jnp.add, fresh + [jnp.sum(terms, axis=1, keepdims=True)])
    high = terms.astype(jnp.bfloat16)
    low = (terms - high.astype(jnp.float32)).astype(jnp.bfloat16)
    for r in range(requests):
        rows = slice(r * width, (r + 1) * width)
        new_values = v_ref[r, head].astype(jnp.float32)
        mixed = functools.reduce(
            jnp.add, [fresh[u][rows] * new_values[u:u + 1] for u in range(STEPS)]
        )
        for j, at in enumerate(pages[r]):
            values = pool_ref[at[0], at[1], 1]
            columns = slice(j * PAGE, (j + 1) * PAGE)
            mixed = mixed + dot(high[rows, columns], values) + dot(low[rows, columns], values)
        o_ref[r] = (mixed / total[rows]).astype(jnp.bfloat16)


def decoded(facts, pool, query, new_key, new_value, lanes):
    requests, here = query.shape[1], QH // lanes
    query = jnp.transpose(query.reshape(STEPS, requests, here, HD), (1, 2, 0, 3))
    query = query.reshape(requests, here * STEPS, HD)
    fresh = [
        jnp.transpose(x.reshape(STEPS, requests, KVH, HD), (1, 2, 0, 3)) for x in (new_key, new_value)
    ]
    out = pl.pallas_call(
        functools.partial(decode_kernel, lanes),
        out_shape=jax.ShapeDtypeStruct(query.shape, jnp.bfloat16),
        in_specs=[SMEM, VMEM, VMEM, VMEM, VMEM],
        out_specs=VMEM,
        name="decode_attention",
        **params(32),
    )(facts, pool, query, *fresh)
    out = jnp.transpose(out.reshape(requests, here, STEPS, HD), (2, 0, 1, 3))
    return out.reshape(STEPS, requests, here * HD)


def after(x, *earlier):
    return lax.optimization_barrier((x, *earlier))[0]


def on_device(
    prefill_query, prefill_key, prefill_value, counts, fills, dec_query, dec_key, dec_value
):
    lanes = lax.axis_size("tp")
    query, key, value = prefill_query[0], prefill_key[0], prefill_value[0]
    facts = jnp.concatenate([counts, fills], axis=1)
    flags = page_flags(counts, fills)
    bases = [sum(CHUNKS[:g]) for g in range(len(CHUNKS))]

    ahead = [(i, i + 2) for i in range(lanes - 2)]
    ahead_again = [(i, i + 2) for i in range(2, lanes - 2)]
    beside = [(i, i + 1) for i in range(0, lanes, 2)]
    trade = [(i, i ^ 1) for i in range(2, lanes)]
    mine = []
    for base, n in zip(bases, CHUNKS):
        mine.append(pack(base, n, after(key, *mine), value))
    first_hops = [lax.ppermute(block, "tp", ahead) for block in mine]
    across = []
    for g, (block, a) in enumerate(zip(mine, first_hops)):
        b = lax.ppermute(after(block, across[0][1]) if g else block, "tp", beside)
        across.append((b, lax.ppermute(a if g else after(a, b, mine[1]), "tp", trade)))
    received = []
    for g, (a, (b, c)) in enumerate(zip(first_hops, across)):
        d = jnp.concatenate([a[1:], c], axis=0)
        d = lax.ppermute(d if g else after(d, first_hops[1]), "tp", ahead_again)
        received.append((a, b, c, d))

    pages = pack(0, KVH, after(key, across[0][1]), value, by_head=True)
    pages = jnp.repeat(pages, lanes // KVH, axis=0)
    pages = after(pages, received[0][3])
    arrived = lax.all_to_all(pages, "tp", split_axis=0, concat_axis=0, tiled=True)

    out = None
    for g, (base, n) in enumerate(zip(bases, CHUNKS)):
        out = prompt_heads(base, n, 0, n, flags, query, (mine[g], *received[g]), out)
    pool = lax.ppermute(after(arrived, out), "section", [(0, 1), (1, 0)])
    dec_out = decoded(facts, pool, dec_query[0], dec_key[0], dec_value[0], lanes)
    return (out[None], dec_out[None])


def solution(mesh):
    placed = (
        P("section", ("groups", "tp"), None),
        P("section", ("groups", "tp"), None),
        P("section", ("groups", "tp"), None),
        P(None, "groups"),
        P(None, "groups"),
        P("section", None, "groups", "tp"),
        P("section", None, "groups", None),
        P("section", None, "groups", None),
    )
    return jax.shard_map(
        on_device,
        mesh=mesh,
        in_specs=placed,
        out_specs=(P("section", ("groups", "tp"), None), P("section", None, "groups", "tp")),
        check_vma=False,
    )
```

```python
import functools
import math

import jax
import jax.numpy as jnp
from jax import lax
from jax.experimental import pallas as pl
from jax.experimental.pallas import tpu as pltpu
from jax.sharding import PartitionSpec as P

QH = 64
KVH = 8
HD = 128
PAGE = 128
MAXP = 8
STEPS = 4
GROUP = QH // KVH
SCALE = HD ** (-0.5)
EXP2_SCALE = SCALE * math.log2(math.e)
LOW = -1e30
CHUNKS = (4, 4)
ROWS = 512
SMEM = pl.BlockSpec(memory_space=pltpu.SMEM)
VMEM = pl.BlockSpec(memory_space=pltpu.VMEM)


def dot(a, b):
    return jnp.dot(a, b, preferred_element_type=jnp.float32)


def page_facts(counts, fills, half, page):
    requests = counts.shape[1]
    owner, first, live, end = -1, 0, PAGE, 0
    for r in range(requests):
        start, end = end, end + counts[half, r]
        begun = start <= page
        owner = jnp.where(begun, r, owner)
        first = jnp.where(begun, start, first)
        live = jnp.where(end - 1 == page, fills[half, r], live)
    return owner, first, live


def params(limit):
    return dict(
        compiler_params=pltpu.CompilerParams(vmem_limit_bytes=limit << 20),
        cost_estimate=pl.CostEstimate(flops=1, bytes_accessed=1, transcendentals=0),
    )


def pack_kernel(base, by_head, k_ref, v_ref, *rest):
    o_ref, k_part, v_part, sems = rest[-4:]
    n = k_part.shape[1] // HD
    own = slice(base * HD, (base + n) * HD)
    copies = [
        pltpu.make_async_copy(source.at[:, own], part, sems.at[spot])
        for spot, (source, part) in enumerate(((k_ref, k_part), (v_ref, v_part)))
    ]
    for copy in copies:
        copy.start()
    for copy in copies:
        copy.wait()
    for j in range(n):
        columns = slice(j * HD, (j + 1) * HD)
        for p in range(2):
            rows = slice(p * PAGE, (p + 1) * PAGE)
            turned = jnp.transpose(k_part[rows, columns].astype(jnp.float32)).astype(jnp.bfloat16)
            if by_head:
                o_ref[j, p, 0] = turned
                o_ref[j, p, 1] = v_part[rows, columns]
            else:
                o_ref[p, columns] = turned
                o_ref[p, (n + j) * HD:(n + j + 1) * HD] = v_part[rows, columns]


def pack(base, n, key, value, by_head=False):
    shape = (n, 2, 2, HD, PAGE) if by_head else (2, 2 * n * HD, PAGE)
    part = pltpu.VMEM((key.shape[0], n * HD), jnp.bfloat16)
    return pl.pallas_call(
        functools.partial(pack_kernel, base, by_head),
        out_shape=jax.ShapeDtypeStruct(shape, jnp.bfloat16),
        in_specs=[pl.BlockSpec(memory_space=pl.ANY)] * 2,
        out_specs=VMEM,
        scratch_shapes=[part, part, pltpu.SemaphoreType.DMA((2,))],
        name="pack",
        **params(48),
    )(key, value)


def flags_kernel(counts, fills, o_ref):
    half, place = lax.axis_index("section"), lax.axis_index("tp")
    even = place % 2 == 0
    near, far = 2 * place - 2, 2 * place - 6
    line = lax.broadcasted_iota(jnp.int32, o_ref.shape, 0)
    out = jnp.zeros(o_ref.shape, jnp.float32)
    for i in range(2):
        _, first, live = page_facts(counts, fills, half, 2 * place + i)
        numbers = [2 * place - 7 if i == 0 else 2 * place, 2 * place + i]
        for page in (2 * place - 4, jnp.where(even, near, far), jnp.where(even, far, near)):
            numbers += [page, page + 1]
        for spot, number in enumerate(numbers):
            out = jnp.where(line == i * MAXP + spot, jnp.where(number >= first, 1.0, 0.0), out)
        out = jnp.where(line == 2 * MAXP + i, live.astype(jnp.float32), out)
    o_ref[...] = out


def page_flags(counts, fills):
    return pl.pallas_call(
        flags_kernel,
        out_shape=jax.ShapeDtypeStruct((2 * MAXP + 8, PAGE), jnp.float32),
        in_specs=[SMEM, SMEM],
        out_specs=VMEM,
        name="page_flags",
        **params(48),
    )(counts, fills)


def prompt_kernel(n, low, flags, q_ref, *rest):
    o_ref, keys, values, causal, *probs = rest[-6:]
    head = low + pl.program_id(0)
    spots = [pl.ds(pl.multiple_of((x + head) * HD, HD), HD) for x in (0, n)]
    mine, a, b, c, d = [[[x[p, at] for at in spots] for p in range(x.shape[0])] for x in rest[:5]]
    choose = jnp.full((HD, PAGE), lax.axis_index("tp") % 2 == 0)
    be = [[jnp.where(choose, x, y) for x, y in zip(d[1 + p], b[p])] for p in range(2)]
    row = lax.broadcasted_iota(jnp.int32, (PAGE, PAGE), 0)
    col = lax.broadcasted_iota(jnp.int32, (PAGE, PAGE), 1)
    causal[...] = jnp.where(col <= row, 0.0, LOW)
    one = jnp.ones((PAGE, HD), jnp.bfloat16)
    zero = jnp.zeros((PAGE, HD), jnp.bfloat16)
    lives = [flags[2 * MAXP + i:2 * MAXP + i + 1, :] for i in range(2)]

    for i in range(2):
        stand_in = jnp.broadcast_to(mine[i][0][:, :1], (HD, PAGE))
        pages = [d[0] if i == 0 else mine[0], mine[i], *a, *c, *be]
        for spot, (k, v) in enumerate(pages):
            line = i * MAXP + spot
            seen = jnp.broadcast_to(flags[line:line + 1, :], (PAGE, HD)) > 0.0
            at = slice(spot * PAGE, (spot + 1) * PAGE)
            k = jnp.where(seen, k, stand_in)
            keys[i, :HD, at] = k
            keys[i, HD:, at] = k
            values[i, at, :HD] = jnp.where(seen, v, zero)
            values[i, at, HD:] = jnp.where(seen, one, zero)

    heads_at_once = ROWS // PAGE
    blocks = [(i, start) for i in range(2) for start in range(0, GROUP, heads_at_once)]

    def halves(query):
        query = query.astype(jnp.float32) * EXP2_SCALE
        high = query.astype(jnp.bfloat16)
        low = (query - high.astype(jnp.float32)).astype(jnp.bfloat16)
        return jnp.concatenate([high, low], axis=1)

    def queries(i, start):
        return halves(
            jnp.concatenate(
                [
                    q_ref[i * PAGE:(i + 1) * PAGE, h * HD:(h + 1) * HD]
                    for h in range(start, start + heads_at_once)
                ],
                axis=0,
            )
        )

    def divided(mixed, live):
        total = mixed[:, HD:]
        near = pl.reciprocal(total, approx=True)
        near = near * (2.0 - total * near)
        token = lax.broadcasted_iota(jnp.int32, (total.shape[0], HD), 0) % PAGE
        return jnp.where(token.astype(jnp.float32) < live, mixed[:, :HD] * near, 0.0).astype(jnp.bfloat16)

    tiles = [slice(t, t + 2 * PAGE) for t in range(0, MAXP * PAGE, 2 * PAGE)]

    def own_scores(query, i, repeat):
        own = dot(query, keys[i, :, tiles[0]])
        bias = jnp.concatenate([causal[...]] * repeat, axis=0)
        return jnp.concatenate([own[:, :PAGE], own[:, PAGE:] + bias], axis=1)

    def mix(block, slot, largest):
        i, start = block
        mixed = dot(probs[slot][...], values[i])
        out = divided(mixed, lives[i])
        for number in range(heads_at_once):
            h = start + number
            o_ref[i * PAGE:(i + 1) * PAGE, h * HD:(h + 1) * HD] = out[number * PAGE:(number + 1) * PAGE]
        return jnp.maximum(largest, mixed[:, HD:])

    largest = jnp.zeros((ROWS, HD), jnp.float32)
    for index in range(len(blocks) + 1):
        if index < len(blocks):
            i, slot = blocks[index][0], index % 2
            query = queries(*blocks[index])
            own = own_scores(query, i, heads_at_once)
            top = jnp.max(own, axis=1, keepdims=True)
            probs[slot][:, tiles[0]] = jnp.exp2(own - top).astype(jnp.bfloat16)
        if index > 0:
            largest = mix(blocks[index - 1], 1 - slot if index < len(blocks) else slot, largest)
        if index < len(blocks):
            for at in tiles[1:]:
                other = dot(query, keys[i, :, at])
                probs[slot][:, at] = jnp.exp2(other - top).astype(jnp.bfloat16)

    @pl.when(jnp.logical_not(jnp.max(largest) < 1e30))
    def _():
        def one(index, carry):
            i, h = index // GROUP, index % GROUP
            rows = pl.ds(pl.multiple_of(i * PAGE, PAGE), PAGE)
            columns = pl.ds(pl.multiple_of(h * HD, HD), HD)
            query = halves(q_ref[rows, columns])
            scores = [own_scores(query, i, 1)] + [dot(query, keys[i, :, at]) for at in tiles[1:]]
            top = jnp.max(functools.reduce(jnp.maximum, scores), axis=1, keepdims=True)
            mixed = jnp.zeros((PAGE, 2 * HD), jnp.float32)
            for score, at in zip(scores, tiles):
                mixed = mixed + dot(jnp.exp2(score - top).astype(jnp.bfloat16), values[i, at])
            o_ref[rows, columns] = divided(mixed, jnp.where(i == 0, lives[0], lives[1]))
            return carry

        lax.fori_loop(0, 2 * GROUP, one, 0)


def prompt_heads(base, n, low, high, flags, query, blocks, done):
    tok = query.shape[0]

    wide = pl.BlockSpec((tok, GROUP * HD), lambda j: (0, base + low + j))
    operands = [flags, query, *blocks]
    specs = [VMEM, wide] + [VMEM] * len(blocks)
    aliases = {}
    if done is not None:
        aliases = {len(operands): 0}
        operands.append(done)
        specs.append(pl.BlockSpec(memory_space=pl.ANY))
    return pl.pallas_call(
        functools.partial(prompt_kernel, n, low),
        out_shape=jax.ShapeDtypeStruct(query.shape, jnp.bfloat16),
        grid=(high - low,),
        in_specs=specs,
        out_specs=wide,
        scratch_shapes=[
            pltpu.VMEM((2, 2 * HD, MAXP * PAGE), jnp.bfloat16),
            pltpu.VMEM((2, MAXP * PAGE, 2 * HD), jnp.bfloat16),
            pltpu.VMEM((PAGE, PAGE), jnp.float32),
            pltpu.VMEM((ROWS, MAXP * PAGE), jnp.bfloat16),
            pltpu.VMEM((ROWS, MAXP * PAGE), jnp.bfloat16),
        ],
        input_output_aliases=aliases,
        name="prompt_attention",
        **params(48),
    )(*operands)


def decode_kernel(lanes, facts, pool_ref, q_ref, k_ref, v_ref, o_ref):
    requests, width = q_ref.shape[:2]
    last = 2 * pool_ref.shape[0] - 1
    other = 1 - lax.axis_index("section")
    head = lax.axis_index("tp") * (QH // lanes) // GROUP
    lane = lax.broadcasted_iota(jnp.int32, (width, PAGE), 1)
    step = lax.broadcasted_iota(jnp.int32, (width, 1), 0) % STEPS
    scores, fresh, pages = [], [], []
    end = 0
    for r in range(requests):
        start, end = end, end + facts[other, r]
        length = PAGE * (end - start - 1) + facts[other, requests + r]
        query = q_ref[r]
        numbers = [jnp.minimum(start + j, last) for j in range(MAXP)]
        pages.append([(number // 2, number % 2) for number in numbers])
        tiles = []
        for j, at in enumerate(pages[r]):
            score = dot(query, pool_ref[at[0], at[1], 0]) * SCALE
            tiles.append(jnp.where(lane < length - j * PAGE, score, LOW))
        scores.append(jnp.concatenate(tiles, axis=1))
        keys = k_ref[r, head].astype(jnp.float32)
        wide = query.astype(jnp.float32)
        news = [jnp.sum(wide * keys[u:u + 1], axis=1, keepdims=True) * SCALE for u in range(STEPS)]
        fresh.append([jnp.where(u <= step, x, LOW) for u, x in enumerate(news)])
    score = jnp.concatenate(scores, axis=0)
    fresh = [jnp.concatenate([x[u] for x in fresh], axis=0) for u in range(STEPS)]
    top = functools.reduce(jnp.maximum, fresh + [jnp.max(score, axis=1, keepdims=True)])
    terms = jnp.exp(score - top)
    fresh = [jnp.exp(x - top) for x in fresh]
    total = functools.reduce(jnp.add, fresh + [jnp.sum(terms, axis=1, keepdims=True)])
    high = terms.astype(jnp.bfloat16)
    low = (terms - high.astype(jnp.float32)).astype(jnp.bfloat16)
    for r in range(requests):
        rows = slice(r * width, (r + 1) * width)
        new_values = v_ref[r, head].astype(jnp.float32)
        mixed = functools.reduce(
            jnp.add, [fresh[u][rows] * new_values[u:u + 1] for u in range(STEPS)]
        )
        for j, at in enumerate(pages[r]):
            values = pool_ref[at[0], at[1], 1]
            columns = slice(j * PAGE, (j + 1) * PAGE)
            mixed = mixed + dot(high[rows, columns], values) + dot(low[rows, columns], values)
        o_ref[r] = (mixed / total[rows]).astype(jnp.bfloat16)


def decoded(facts, pool, query, new_key, new_value, lanes):
    requests, here = query.shape[1], QH // lanes
    query = jnp.transpose(query.reshape(STEPS, requests, here, HD), (1, 2, 0, 3))
    query = query.reshape(requests, here * STEPS, HD)
    fresh = [
        jnp.transpose(x.reshape(STEPS, requests, KVH, HD), (1, 2, 0, 3)) for x in (new_key, new_value)
    ]
    out = pl.pallas_call(
        functools.partial(decode_kernel, lanes),
        out_shape=jax.ShapeDtypeStruct(query.shape, jnp.bfloat16),
        in_specs=[SMEM, VMEM, VMEM, VMEM, VMEM],
        out_specs=VMEM,
        name="decode_attention",
        **params(32),
    )(facts, pool, query, *fresh)
    out = jnp.transpose(out.reshape(requests, here, STEPS, HD), (2, 0, 1, 3))
    return out.reshape(STEPS, requests, here * HD)


def after(x, *earlier):
    return lax.optimization_barrier((x, *earlier))[0]


def on_device(
    prefill_query, prefill_key, prefill_value, counts, fills, dec_query, dec_key, dec_value
):
    lanes = lax.axis_size("tp")
    query, key, value = prefill_query[0], prefill_key[0], prefill_value[0]
    facts = jnp.concatenate([counts, fills], axis=1)
    flags = page_flags(counts, fills)
    bases = [sum(CHUNKS[:g]) for g in range(len(CHUNKS))]

    ahead = [(i, i + 2) for i in range(lanes - 2)]
    ahead_again = [(i, i + 2) for i in range(2, lanes - 2)]
    beside = [(i, i + 1) for i in range(0, lanes, 2)]
    trade = [(i, i ^ 1) for i in range(2, lanes)]
    mine = []
    for base, n in zip(bases, CHUNKS):
        mine.append(pack(base, n, after(key, *mine), value))
    first_hops = [lax.ppermute(block, "tp", ahead) for block in mine]
    across = []
    for g, (block, a) in enumerate(zip(mine, first_hops)):
        b = lax.ppermute(after(block, across[0][1]) if g else block, "tp", beside)
        across.append((b, lax.ppermute(a if g else after(a, b), "tp", trade)))
    received = []
    for g, (a, (b, c)) in enumerate(zip(first_hops, across)):
        joined = jnp.concatenate([a[1:], c], axis=0)
        d = lax.ppermute(joined if g else after(joined, first_hops[1]), "tp", ahead_again)
        received.append((a, b, c, d))

    pages = pack(0, KVH, after(key, across[0][1]), value, by_head=True)
    pages = jnp.repeat(pages, lanes // KVH, axis=0)
    pages = after(pages, joined)
    arrived = lax.all_to_all(pages, "tp", split_axis=0, concat_axis=0, tiled=True)

    out, flags = None, after(flags, across[1][1])
    for g, (base, n) in enumerate(zip(bases, CHUNKS)):
        out = prompt_heads(base, n, 0, n, flags, query, (mine[g], *received[g]), out)
    pool = lax.ppermute(after(arrived, out), "section", [(0, 1), (1, 0)])
    dec_out = decoded(facts, pool, dec_query[0], dec_key[0], dec_value[0], lanes)
    return (out[None], dec_out[None])


def solution(mesh):
    placed = (
        P("section", ("groups", "tp"), None),
        P("section", ("groups", "tp"), None),
        P("section", ("groups", "tp"), None),
        P(None, "groups"),
        P(None, "groups"),
        P("section", None, "groups", "tp"),
        P("section", None, "groups", None),
        P("section", None, "groups", None),
    )
    return jax.shard_map(
        on_device,
        mesh=mesh,
        in_specs=placed,
        out_specs=(P("section", ("groups", "tp"), None), P("section", None, "groups", "tp")),
        check_vma=False,
    )
```

```python
import functools
import math

import jax
import jax.numpy as jnp
from jax import lax
from jax.experimental import pallas as pl
from jax.experimental.pallas import tpu as pltpu
from jax.sharding import PartitionSpec as P

QH = 64
KVH = 8
HD = 128
PAGE = 128
MAXP = 8
STEPS = 4
GROUP = QH // KVH
SCALE = HD ** (-0.5)
EXP2_SCALE = SCALE * math.log2(math.e)
LOW = -1e30
CHUNKS = (4, 4)
ROWS = 512
SMEM = pl.BlockSpec(memory_space=pltpu.SMEM)
VMEM = pl.BlockSpec(memory_space=pltpu.VMEM)


def dot(a, b):
    return jnp.dot(a, b, preferred_element_type=jnp.float32)


def page_facts(facts, half, page):
    requests = facts.shape[1] // 2
    owner, first, live, end = -1, 0, PAGE, 0
    for r in range(requests):
        start, end = end, end + facts[half, r]
        begun = start <= page
        owner = jnp.where(begun, r, owner)
        first = jnp.where(begun, start, first)
        live = jnp.where(end - 1 == page, facts[half, requests + r], live)
    return owner, first, live


def params(limit):
    return dict(
        compiler_params=pltpu.CompilerParams(vmem_limit_bytes=limit << 20),
        cost_estimate=pl.CostEstimate(flops=1, bytes_accessed=1, transcendentals=0),
    )


def pack_kernel(base, k_ref, v_ref, *rest):
    o_ref, k_part, v_part, sems = rest[-4:]
    n = k_part.shape[1] // HD
    own = slice(base * HD, (base + n) * HD)
    copies = [
        pltpu.make_async_copy(source.at[:, own], part, sems.at[spot])
        for spot, (source, part) in enumerate(((k_ref, k_part), (v_ref, v_part)))
    ]
    for copy in copies:
        copy.start()
    for copy in copies:
        copy.wait()
    for j in range(n):
        columns = slice(j * HD, (j + 1) * HD)
        for p in range(2):
            rows = slice(p * PAGE, (p + 1) * PAGE)
            turned = jnp.transpose(k_part[rows, columns].astype(jnp.float32)).astype(jnp.bfloat16)
            o_ref[p, columns] = turned
            o_ref[p, (n + j) * HD:(n + j + 1) * HD] = v_part[rows, columns]


def pack(base, n, key, value):
    part = pltpu.VMEM((key.shape[0], n * HD), jnp.bfloat16)
    return pl.pallas_call(
        functools.partial(pack_kernel, base),
        out_shape=jax.ShapeDtypeStruct((2, 2 * n * HD, PAGE), jnp.bfloat16),
        in_specs=[pl.BlockSpec(memory_space=pl.ANY)] * 2,
        out_specs=VMEM,
        scratch_shapes=[part, part, pltpu.SemaphoreType.DMA((2,))],
        name="pack",
        **params(48),
    )(key, value)


def flags_kernel(facts, o_ref):
    half, place = lax.axis_index("section"), lax.axis_index("tp")
    even = place % 2 == 0
    near, far = 2 * place - 2, 2 * place - 6
    line = lax.broadcasted_iota(jnp.int32, o_ref.shape, 0)
    out = jnp.zeros(o_ref.shape, jnp.float32)
    for i in range(2):
        _, first, live = page_facts(facts, half, 2 * place + i)
        numbers = [2 * place - 7 if i == 0 else 2 * place, 2 * place + i]
        for page in (2 * place - 4, jnp.where(even, near, far), jnp.where(even, far, near)):
            numbers += [page, page + 1]
        for spot, number in enumerate(numbers):
            out = jnp.where(line == i * MAXP + spot, jnp.where(number >= first, 1.0, 0.0), out)
        out = jnp.where(line == 2 * MAXP + i, live.astype(jnp.float32), out)
    o_ref[...] = out


def page_flags(facts):
    return pl.pallas_call(
        flags_kernel,
        out_shape=jax.ShapeDtypeStruct((2 * MAXP + 8, PAGE), jnp.float32),
        in_specs=[SMEM],
        out_specs=VMEM,
        name="page_flags",
        **params(48),
    )(facts)


def prompt_kernel(n, low, flags, q_ref, *rest):
    o_ref, keys, values, causal, *probs = rest[-6:]
    head = low + pl.program_id(0)
    spots = [pl.ds(pl.multiple_of((x + head) * HD, HD), HD) for x in (0, n)]
    mine, a, b, c, d = [[[x[p, at] for at in spots] for p in range(x.shape[0])] for x in rest[:5]]
    choose = jnp.full((HD, PAGE), lax.axis_index("tp") % 2 == 0)
    be = [[jnp.where(choose, x, y) for x, y in zip(d[1 + p], b[p])] for p in range(2)]
    row = lax.broadcasted_iota(jnp.int32, (PAGE, PAGE), 0)
    col = lax.broadcasted_iota(jnp.int32, (PAGE, PAGE), 1)
    causal[...] = jnp.where(col <= row, 0.0, LOW)
    one = jnp.ones((PAGE, HD), jnp.bfloat16)
    zero = jnp.zeros((PAGE, HD), jnp.bfloat16)
    lives = [flags[2 * MAXP + i:2 * MAXP + i + 1, :] for i in range(2)]

    for i in range(2):
        stand_in = jnp.broadcast_to(mine[i][0][:, :1], (HD, PAGE))
        pages = [d[0] if i == 0 else mine[0], mine[i], *a, *c, *be]
        for spot, (k, v) in enumerate(pages):
            line = i * MAXP + spot
            seen = jnp.broadcast_to(flags[line:line + 1, :], (PAGE, HD)) > 0.0
            at = slice(spot * PAGE, (spot + 1) * PAGE)
            k = jnp.where(seen, k, stand_in)
            keys[i, :HD, at] = k
            keys[i, HD:, at] = k
            values[i, at, :HD] = jnp.where(seen, v, zero)
            values[i, at, HD:] = jnp.where(seen, one, zero)

    heads_at_once = ROWS // PAGE
    blocks = [(i, start) for i in range(2) for start in range(0, GROUP, heads_at_once)]

    def halves(query):
        query = query.astype(jnp.float32) * EXP2_SCALE
        high = query.astype(jnp.bfloat16)
        low = (query - high.astype(jnp.float32)).astype(jnp.bfloat16)
        return jnp.concatenate([high, low], axis=1)

    def queries(i, start):
        return halves(
            jnp.concatenate(
                [
                    q_ref[i * PAGE:(i + 1) * PAGE, h * HD:(h + 1) * HD]
                    for h in range(start, start + heads_at_once)
                ],
                axis=0,
            )
        )

    def divided(mixed, live):
        total = mixed[:, HD:]
        near = pl.reciprocal(total, approx=True)
        near = near * (2.0 - total * near)
        token = lax.broadcasted_iota(jnp.int32, (total.shape[0], HD), 0) % PAGE
        return jnp.where(token.astype(jnp.float32) < live, mixed[:, :HD] * near, 0.0).astype(jnp.bfloat16)

    tiles = [slice(t, t + 2 * PAGE) for t in range(0, MAXP * PAGE, 2 * PAGE)]

    def own_scores(query, i, repeat):
        own = dot(query, keys[i, :, tiles[0]])
        bias = jnp.concatenate([causal[...]] * repeat, axis=0)
        return jnp.concatenate([own[:, :PAGE], own[:, PAGE:] + bias], axis=1)

    def mix(block, slot, largest):
        i, start = block
        mixed = dot(probs[slot][...], values[i])
        out = divided(mixed, lives[i])
        for number in range(heads_at_once):
            h = start + number
            o_ref[i * PAGE:(i + 1) * PAGE, h * HD:(h + 1) * HD] = out[number * PAGE:(number + 1) * PAGE]
        return jnp.maximum(largest, mixed[:, HD:])

    largest = jnp.zeros((ROWS, HD), jnp.float32)
    for index in range(len(blocks) + 1):
        if index < len(blocks):
            i, slot = blocks[index][0], index % 2
            query = queries(*blocks[index])
            own = own_scores(query, i, heads_at_once)
            top = jnp.max(own, axis=1, keepdims=True)
            probs[slot][:, tiles[0]] = jnp.exp2(own - top).astype(jnp.bfloat16)
        if index > 0:
            largest = mix(blocks[index - 1], 1 - slot if index < len(blocks) else slot, largest)
        if index < len(blocks):
            for at in tiles[1:]:
                other = dot(query, keys[i, :, at])
                probs[slot][:, at] = jnp.exp2(other - top).astype(jnp.bfloat16)

    @pl.when(jnp.logical_not(jnp.max(largest) < 1e30))
    def _():
        def one(index, carry):
            i, h = index // GROUP, index % GROUP
            rows = pl.ds(pl.multiple_of(i * PAGE, PAGE), PAGE)
            columns = pl.ds(pl.multiple_of(h * HD, HD), HD)
            query = halves(q_ref[rows, columns])
            scores = [own_scores(query, i, 1)] + [dot(query, keys[i, :, at]) for at in tiles[1:]]
            top = jnp.max(functools.reduce(jnp.maximum, scores), axis=1, keepdims=True)
            mixed = jnp.zeros((PAGE, 2 * HD), jnp.float32)
            for score, at in zip(scores, tiles):
                mixed = mixed + dot(jnp.exp2(score - top).astype(jnp.bfloat16), values[i, at])
            o_ref[rows, columns] = divided(mixed, jnp.where(i == 0, lives[0], lives[1]))
            return carry

        lax.fori_loop(0, 2 * GROUP, one, 0)


def prompt_heads(base, n, low, high, flags, query, blocks, done):
    tok = query.shape[0]

    wide = pl.BlockSpec((tok, GROUP * HD), lambda j: (0, base + low + j))
    operands = [flags, query, *blocks]
    specs = [VMEM, wide] + [VMEM] * len(blocks)
    aliases = {}
    if done is not None:
        aliases = {len(operands): 0}
        operands.append(done)
        specs.append(pl.BlockSpec(memory_space=pl.ANY))
    return pl.pallas_call(
        functools.partial(prompt_kernel, n, low),
        out_shape=jax.ShapeDtypeStruct(query.shape, jnp.bfloat16),
        grid=(high - low,),
        in_specs=specs,
        out_specs=wide,
        scratch_shapes=[
            pltpu.VMEM((2, 2 * HD, MAXP * PAGE), jnp.bfloat16),
            pltpu.VMEM((2, MAXP * PAGE, 2 * HD), jnp.bfloat16),
            pltpu.VMEM((PAGE, PAGE), jnp.float32),
            pltpu.VMEM((ROWS, MAXP * PAGE), jnp.bfloat16),
            pltpu.VMEM((ROWS, MAXP * PAGE), jnp.bfloat16),
        ],
        input_output_aliases=aliases,
        name="prompt_attention",
        compiler_params=pltpu.CompilerParams(vmem_limit_bytes=48 << 20),
        cost_estimate=pl.CostEstimate(
            flops=(high - low) * GROUP * tok * MAXP * PAGE * HD * 8,
            bytes_accessed=4 * (high - low) * tok * GROUP * HD,
            transcendentals=0,
        ),
    )(*operands)


def stat_rows(rows):
    return 16 - rows % 16


def choose_kernel(facts, q_ref, o_ref, rows_ref, turned):
    requests, here = q_ref.shape[1], q_ref.shape[2] // HD
    other = 1 - lax.axis_index("section")
    for s in range(STEPS):
        query = q_ref[s].astype(jnp.float32)
        for r in range(requests):
            for h in range(here):
                row = h * STEPS + s
                turned[r, row:row + 1] = query[r:r + 1, h * HD:(h + 1) * HD]
    rows_ref[...] = turned[...].astype(jnp.bfloat16)

    def one(lane, carry):
        for i in range(2):
            owner = page_facts(facts, other, 2 * lane + i)[0]
            o_ref[lane, i] = turned[owner].astype(jnp.bfloat16)
        return carry

    lax.fori_loop(0, o_ref.shape[0], one, 0)


def chosen_queries(facts, query, lanes):
    rows = (query.shape[1], QH // lanes * STEPS, HD)
    return pl.pallas_call(
        choose_kernel,
        out_shape=(
            jax.ShapeDtypeStruct((lanes, 2, *rows[1:]), jnp.bfloat16),
            jax.ShapeDtypeStruct(rows, jnp.bfloat16),
        ),
        in_specs=[SMEM, VMEM],
        out_specs=(VMEM, VMEM),
        scratch_shapes=[pltpu.VMEM(rows, jnp.float32)],
        name="choose_queries",
        **params(32),
    )(facts, query)


def partial_kernel(lanes, facts, q_ref, *rest):
    *packed, o_ref = rest
    split = GROUP // (QH // lanes)
    width = QH // lanes * STEPS
    extra = stat_rows(2 * width)
    half, place = lax.axis_index("section"), lax.axis_index("tp")
    group = GROUP * STEPS
    height = 2 * KVH * group
    lane = lax.broadcasted_iota(jnp.int32, (height, PAGE), 1)
    later = lax.broadcasted_iota(jnp.int32, (height, PAGE), 0) // group % 2 == 1
    spot = lax.broadcasted_iota(jnp.int32, (2 * width, PAGE), 0)
    across = lax.broadcasted_iota(jnp.int32, (2 * width, PAGE), 1)
    line = lax.broadcasted_iota(jnp.int32, (extra, PAGE), 0)
    lives = [page_facts(facts, half, 2 * place + i)[2] for i in range(2)]
    places = [(block, j, n) for block, n in zip(packed, CHUNKS) for j in range(n)]
    scores, values = [], []
    for k, (block, j, n) in enumerate(places):
        for i in range(2):
            query = jnp.concatenate([q_ref[k * split + t, i] for t in range(split)], axis=0)
            scores.append(dot(query, block[i, j * HD:(j + 1) * HD]))
            values.append(block[i, (n + j) * HD:(n + j + 1) * HD])
    score = jnp.concatenate(scores, axis=0) * SCALE
    score = jnp.where(lane < jnp.where(later, lives[1], lives[0]), score, LOW)
    top = jnp.max(score, axis=1, keepdims=True)
    terms = jnp.exp(score - top)
    total = jnp.sum(terms, axis=1, keepdims=True)
    high = terms.astype(jnp.bfloat16)
    low = (terms - high.astype(jnp.float32)).astype(jnp.bfloat16)
    mixed = jnp.concatenate(
        [
            dot(high[m * group:(m + 1) * group], v) + dot(low[m * group:(m + 1) * group], v)
            for m, v in enumerate(values)
        ],
        axis=0,
    ) / total
    sums = top + jnp.log(total)
    for k in range(KVH):
        for t in range(split):
            begins = [(2 * k + i) * group + t * width for i in range(2)]
            both = jnp.concatenate([sums[at:at + width] for at in begins], axis=0)
            turned = jnp.sum(jnp.where(spot == across, both, 0.0), axis=0, keepdims=True)
            first = turned.astype(jnp.bfloat16).astype(jnp.float32)
            rest = turned - first
            second = rest.astype(jnp.bfloat16).astype(jnp.float32)
            stat = jnp.where(line == 0, first, jnp.where(line == 1, second, rest - second))
            stat = jnp.where(line < 3, stat, 0.0)
            block = jnp.concatenate([mixed[at:at + width] for at in begins] + [stat], axis=0)
            o_ref[k * split + t] = block.astype(jnp.bfloat16)


def partial_decode(facts, query, packed, lanes):
    rows = 2 * (QH // lanes) * STEPS
    return pl.pallas_call(
        functools.partial(partial_kernel, lanes),
        out_shape=jax.ShapeDtypeStruct((lanes, rows + stat_rows(rows), HD), jnp.bfloat16),
        in_specs=[SMEM, VMEM] + [VMEM] * len(packed),
        out_specs=VMEM,
        name="partial_decode",
        **params(32),
    )(facts, query, *packed)


def merge_kernel(lanes, facts, parts_ref, q_ref, k_ref, v_ref, o_ref):
    requests = q_ref.shape[0]
    width = (QH // lanes) * STEPS
    other, place = 1 - lax.axis_index("section"), lax.axis_index("tp")
    head = place * (QH // lanes) // GROUP
    spot = lax.broadcasted_iota(jnp.int32, (width, PAGE), 0)
    across = lax.broadcasted_iota(jnp.int32, (width, PAGE), 1)
    step = lax.broadcasted_iota(jnp.int32, (width, 1), 0) % STEPS
    end = 0
    for r in range(requests):
        start, end = end, end + facts[other, r]
        query = q_ref[r].astype(jnp.float32)
        keys = k_ref[r, head].astype(jnp.float32)
        values = v_ref[r, head].astype(jnp.float32)
        tops, vectors = [], []
        for u in range(STEPS):
            score = jnp.sum(query * keys[u:u + 1], axis=1, keepdims=True) * SCALE
            tops.append(jnp.where(u <= step, score, LOW))
            vectors.append(values[u:u + 1])
        for j in range(MAXP):
            page = jnp.minimum(start + j, 2 * lanes - 1)
            block = parts_ref[page // 2].astype(jnp.float32)
            later = jnp.full((width, HD), page % 2 == 1)
            vectors.append(jnp.where(later, block[width:2 * width], block[:width]))
            stat = jnp.sum(block[2 * width:2 * width + 8], axis=0, keepdims=True)
            stat = jnp.sum(
                jnp.where(across - page % 2 * width == spot, stat, 0.0), axis=1, keepdims=True
            )
            tops.append(jnp.where(jnp.full((width, 1), start + j < end), stat, LOW))
        top = functools.reduce(jnp.maximum, tops)
        weights = [jnp.exp(t - top) for t in tops]
        total = functools.reduce(jnp.add, weights)
        mixed = functools.reduce(jnp.add, [w * x for w, x in zip(weights, vectors)])
        o_ref[r] = (mixed / total).astype(jnp.bfloat16)


def merged(facts, parts, query, new_key, new_value, lanes):
    requests = query.shape[0]
    fresh = [
        jnp.transpose(x.reshape(STEPS, requests, KVH, HD), (1, 2, 0, 3)) for x in (new_key, new_value)
    ]
    out = pl.pallas_call(
        functools.partial(merge_kernel, lanes),
        out_shape=jax.ShapeDtypeStruct(query.shape, jnp.bfloat16),
        in_specs=[SMEM, VMEM, VMEM, VMEM, VMEM],
        out_specs=VMEM,
        name="merge_decode",
        **params(32),
    )(facts, parts, query, *fresh)
    out = jnp.transpose(out.reshape(requests, QH // lanes, STEPS, HD), (2, 0, 1, 3))
    return out.reshape(STEPS, requests, QH // lanes * HD)


def other_half(x):
    return lax.ppermute(x, "section", [(0, 1), (1, 0)])


def after(x, *earlier):
    return lax.optimization_barrier((x, *earlier))[0]


def on_device(
    prefill_query, prefill_key, prefill_value, counts, fills, dec_query, dec_key, dec_value
):
    lanes = lax.axis_size("tp")
    query, key, value = prefill_query[0], prefill_key[0], prefill_value[0]
    facts = jnp.concatenate([counts, fills], axis=1)
    flags = page_flags(facts)
    ahead = [(i, i + 2) for i in range(lanes - 2)]
    ahead_again = [(i, i + 2) for i in range(2, lanes - 2)]
    beside = [(i, i + 1) for i in range(0, lanes, 2)]
    trade = [(i, i ^ 1) for i in range(2, lanes)]
    bases = [sum(CHUNKS[:g]) for g in range(len(CHUNKS))]
    mine = []
    for base, n in zip(bases, CHUNKS):
        mine.append(pack(base, n, after(key, *mine), value))

    first_hops = [lax.ppermute(block, "tp", ahead) for block in mine]

    asked = after(dec_query[0], mine[0])
    chosen, dec_rows = chosen_queries(facts, asked, lanes)
    wanted = lax.all_to_all(chosen, "tp", split_axis=0, concat_axis=0, tiled=True)
    parts = partial_decode(facts, other_half(wanted), mine, lanes)
    parts = lax.all_to_all(parts, "tp", split_axis=0, concat_axis=0, tiled=True)
    dec_out = merged(facts, other_half(parts), dec_rows, dec_key[0], dec_value[0], lanes)

    received = []
    for g, (block, a) in enumerate(zip(mine, first_hops)):
        b = lax.ppermute(after(block, received[0][2]) if g else block, "tp", beside)
        c = lax.ppermute(a if g else after(a, b, wanted), "tp", trade)
        d = jnp.concatenate([a[1:], c], axis=0)
        d = lax.ppermute(d if g else after(d, first_hops[1], parts), "tp", ahead_again)
        received.append((a, b, c, d))
    out = None
    for g, (base, n) in enumerate(zip(bases, CHUNKS)):
        if g:
            out = after(out, dec_out)
        out = prompt_heads(base, n, 0, n, flags, query, (mine[g], *received[g]), out)
    return (out[None], dec_out[None])


def solution(mesh):
    placed = (
        P("section", ("groups", "tp"), None),
        P("section", ("groups", "tp"), None),
        P("section", ("groups", "tp"), None),
        P(None, "groups"),
        P(None, "groups"),
        P("section", None, "groups", "tp"),
        P("section", None, "groups", None),
        P("section", None, "groups", None),
    )
    return jax.shard_map(
        on_device,
        mesh=mesh,
        in_specs=placed,
        out_specs=(P("section", ("groups", "tp"), None), P("section", None, "groups", "tp")),
        check_vma=False,
    )
```

```python
import functools
import math

import jax
import jax.numpy as jnp
from jax import lax
from jax.experimental import pallas as pl
from jax.experimental.pallas import tpu as pltpu
from jax.sharding import PartitionSpec as P

QH = 64
KVH = 8
HD = 128
PAGE = 128
MAXP = 8
STEPS = 4
GROUP = QH // KVH
SCALE = HD ** (-0.5)
EXP2_SCALE = SCALE * math.log2(math.e)
LOW = -1e30
CHUNKS = (4, 4)
ROWS = 512
SMEM = pl.BlockSpec(memory_space=pltpu.SMEM)
VMEM = pl.BlockSpec(memory_space=pltpu.VMEM)


def dot(a, b):
    return jnp.dot(a, b, preferred_element_type=jnp.float32)


def page_facts(facts, half, page):
    requests = facts.shape[1] // 2
    owner, first, live, end = -1, 0, PAGE, 0
    for r in range(requests):
        start, end = end, end + facts[half, r]
        begun = start <= page
        owner = jnp.where(begun, r, owner)
        first = jnp.where(begun, start, first)
        live = jnp.where(end - 1 == page, facts[half, requests + r], live)
    return owner, first, live


def params(limit):
    return dict(
        compiler_params=pltpu.CompilerParams(vmem_limit_bytes=limit << 20),
        cost_estimate=pl.CostEstimate(flops=1, bytes_accessed=1, transcendentals=0),
    )


def pack_kernel(base, k_ref, v_ref, *rest):
    o_ref, k_part, v_part, sems = rest[-4:]
    n = k_part.shape[1] // HD
    own = slice(base * HD, (base + n) * HD)
    copies = [
        pltpu.make_async_copy(source.at[:, own], part, sems.at[spot])
        for spot, (source, part) in enumerate(((k_ref, k_part), (v_ref, v_part)))
    ]
    for copy in copies:
        copy.start()
    for copy in copies:
        copy.wait()
    for j in range(n):
        columns = slice(j * HD, (j + 1) * HD)
        for p in range(2):
            rows = slice(p * PAGE, (p + 1) * PAGE)
            turned = jnp.transpose(k_part[rows, columns].astype(jnp.float32)).astype(jnp.bfloat16)
            o_ref[p, columns] = turned
            o_ref[p, (n + j) * HD:(n + j + 1) * HD] = v_part[rows, columns]


def pack(base, n, key, value):
    part = pltpu.VMEM((key.shape[0], n * HD), jnp.bfloat16)
    return pl.pallas_call(
        functools.partial(pack_kernel, base),
        out_shape=jax.ShapeDtypeStruct((2, 2 * n * HD, PAGE), jnp.bfloat16),
        in_specs=[pl.BlockSpec(memory_space=pl.ANY)] * 2,
        out_specs=VMEM,
        scratch_shapes=[part, part, pltpu.SemaphoreType.DMA((2,))],
        name="pack",
        **params(48),
    )(key, value)


def flags_kernel(facts, o_ref):
    half, place = lax.axis_index("section"), lax.axis_index("tp")
    even = place % 2 == 0
    near, far = 2 * place - 2, 2 * place - 6
    line = lax.broadcasted_iota(jnp.int32, o_ref.shape, 0)
    out = jnp.zeros(o_ref.shape, jnp.float32)
    for i in range(2):
        _, first, live = page_facts(facts, half, 2 * place + i)
        numbers = [2 * place - 7 if i == 0 else 2 * place, 2 * place + i]
        for page in (2 * place - 4, jnp.where(even, near, far), jnp.where(even, far, near)):
            numbers += [page, page + 1]
        for spot, number in enumerate(numbers):
            out = jnp.where(line == i * MAXP + spot, jnp.where(number >= first, 1.0, 0.0), out)
        out = jnp.where(line == 2 * MAXP + i, live.astype(jnp.float32), out)
    o_ref[...] = out


def page_flags(facts):
    return pl.pallas_call(
        flags_kernel,
        out_shape=jax.ShapeDtypeStruct((2 * MAXP + 8, PAGE), jnp.float32),
        in_specs=[SMEM],
        out_specs=VMEM,
        name="page_flags",
        **params(48),
    )(facts)


def prompt_kernel(n, low, flags, q_ref, *rest):
    o_ref, keys, values, causal, *probs = rest[-6:]
    head = low + pl.program_id(0)
    spots = [pl.ds(pl.multiple_of((x + head) * HD, HD), HD) for x in (0, n)]
    mine, a, b, c, d = [[[x[p, at] for at in spots] for p in range(x.shape[0])] for x in rest[:5]]
    choose = jnp.full((HD, PAGE), lax.axis_index("tp") % 2 == 0)
    be = [[jnp.where(choose, x, y) for x, y in zip(d[1 + p], b[p])] for p in range(2)]
    row = lax.broadcasted_iota(jnp.int32, (PAGE, PAGE), 0)
    col = lax.broadcasted_iota(jnp.int32, (PAGE, PAGE), 1)
    causal[...] = jnp.where(col <= row, 0.0, LOW)
    one = jnp.ones((PAGE, HD), jnp.bfloat16)
    zero = jnp.zeros((PAGE, HD), jnp.bfloat16)
    lives = [flags[2 * MAXP + i:2 * MAXP + i + 1, :] for i in range(2)]

    for i in range(2):
        stand_in = jnp.broadcast_to(mine[i][0][:, :1], (HD, PAGE))
        pages = [d[0] if i == 0 else mine[0], mine[i], *a, *c, *be]
        for spot, (k, v) in enumerate(pages):
            line = i * MAXP + spot
            seen = jnp.broadcast_to(flags[line:line + 1, :], (PAGE, HD)) > 0.0
            at = slice(spot * PAGE, (spot + 1) * PAGE)
            k = jnp.where(seen, k, stand_in)
            keys[i, :HD, at] = k
            keys[i, HD:, at] = k
            values[i, at, :HD] = jnp.where(seen, v, zero)
            values[i, at, HD:] = jnp.where(seen, one, zero)

    heads_at_once = ROWS // PAGE
    blocks = [(i, start) for i in range(2) for start in range(0, GROUP, heads_at_once)]

    def halves(query):
        query = query.astype(jnp.float32) * EXP2_SCALE
        high = query.astype(jnp.bfloat16)
        low = (query - high.astype(jnp.float32)).astype(jnp.bfloat16)
        return jnp.concatenate([high, low], axis=1)

    def queries(i, start):
        return halves(
            jnp.concatenate(
                [
                    q_ref[i * PAGE:(i + 1) * PAGE, h * HD:(h + 1) * HD]
                    for h in range(start, start + heads_at_once)
                ],
                axis=0,
            )
        )

    def divided(mixed, live):
        total = mixed[:, HD:]
        near = pl.reciprocal(total, approx=True)
        near = near * (2.0 - total * near)
        token = lax.broadcasted_iota(jnp.int32, (total.shape[0], HD), 0) % PAGE
        return jnp.where(token.astype(jnp.float32) < live, mixed[:, :HD] * near, 0.0).astype(jnp.bfloat16)

    tiles = [slice(t, t + 2 * PAGE) for t in range(0, MAXP * PAGE, 2 * PAGE)]

    def own_scores(query, i, repeat):
        own = dot(query, keys[i, :, tiles[0]])
        bias = jnp.concatenate([causal[...]] * repeat, axis=0)
        return jnp.concatenate([own[:, :PAGE], own[:, PAGE:] + bias], axis=1)

    def mix(block, slot, largest):
        i, start = block
        mixed = dot(probs[slot][...], values[i])
        out = divided(mixed, lives[i])
        for number in range(heads_at_once):
            h = start + number
            o_ref[i * PAGE:(i + 1) * PAGE, h * HD:(h + 1) * HD] = out[number * PAGE:(number + 1) * PAGE]
        return jnp.maximum(largest, mixed[:, HD:])

    largest = jnp.zeros((ROWS, HD), jnp.float32)
    for index in range(len(blocks) + 1):
        if index < len(blocks):
            i, slot = blocks[index][0], index % 2
            query = queries(*blocks[index])
            own = own_scores(query, i, heads_at_once)
            top = jnp.max(own, axis=1, keepdims=True)
            probs[slot][:, tiles[0]] = jnp.exp2(own - top).astype(jnp.bfloat16)
        if index > 0:
            largest = mix(blocks[index - 1], 1 - slot if index < len(blocks) else slot, largest)
        if index < len(blocks):
            for at in tiles[1:]:
                other = dot(query, keys[i, :, at])
                probs[slot][:, at] = jnp.exp2(other - top).astype(jnp.bfloat16)

    @pl.when(jnp.logical_not(jnp.max(largest) < 1e30))
    def _():
        def one(index, carry):
            i, h = index // GROUP, index % GROUP
            rows = pl.ds(pl.multiple_of(i * PAGE, PAGE), PAGE)
            columns = pl.ds(pl.multiple_of(h * HD, HD), HD)
            query = halves(q_ref[rows, columns])
            scores = [own_scores(query, i, 1)] + [dot(query, keys[i, :, at]) for at in tiles[1:]]
            top = jnp.max(functools.reduce(jnp.maximum, scores), axis=1, keepdims=True)
            mixed = jnp.zeros((PAGE, 2 * HD), jnp.float32)
            for score, at in zip(scores, tiles):
                mixed = mixed + dot(jnp.exp2(score - top).astype(jnp.bfloat16), values[i, at])
            o_ref[rows, columns] = divided(mixed, jnp.where(i == 0, lives[0], lives[1]))
            return carry

        lax.fori_loop(0, 2 * GROUP, one, 0)


def prompt_heads(base, n, low, high, flags, query, blocks, done):
    tok = query.shape[0]

    wide = pl.BlockSpec((tok, GROUP * HD), lambda j: (0, base + low + j))
    operands = [flags, query, *blocks]
    specs = [VMEM, wide] + [VMEM] * len(blocks)
    aliases = {}
    if done is not None:
        aliases = {len(operands): 0}
        operands.append(done)
        specs.append(pl.BlockSpec(memory_space=pl.ANY))
    return pl.pallas_call(
        functools.partial(prompt_kernel, n, low),
        out_shape=jax.ShapeDtypeStruct(query.shape, jnp.bfloat16),
        grid=(high - low,),
        in_specs=specs,
        out_specs=wide,
        scratch_shapes=[
            pltpu.VMEM((2, 2 * HD, MAXP * PAGE), jnp.bfloat16),
            pltpu.VMEM((2, MAXP * PAGE, 2 * HD), jnp.bfloat16),
            pltpu.VMEM((PAGE, PAGE), jnp.float32),
            pltpu.VMEM((ROWS, MAXP * PAGE), jnp.bfloat16),
            pltpu.VMEM((ROWS, MAXP * PAGE), jnp.bfloat16),
        ],
        input_output_aliases=aliases,
        name="prompt_attention",
        compiler_params=pltpu.CompilerParams(vmem_limit_bytes=48 << 20),
        cost_estimate=pl.CostEstimate(
            flops=(high - low) * GROUP * tok * MAXP * PAGE * HD * 8,
            bytes_accessed=4 * (high - low) * tok * GROUP * HD,
            transcendentals=0,
        ),
    )(*operands)


def stat_rows(rows):
    return 16 - rows % 16


def choose_kernel(facts, q_ref, o_ref, rows_ref, turned):
    requests, here = q_ref.shape[1], q_ref.shape[2] // HD
    other = 1 - lax.axis_index("section")
    for s in range(STEPS):
        query = q_ref[s].astype(jnp.float32)
        for r in range(requests):
            for h in range(here):
                row = h * STEPS + s
                turned[r, row:row + 1] = query[r:r + 1, h * HD:(h + 1) * HD]
    rows_ref[...] = turned[...].astype(jnp.bfloat16)

    def one(lane, carry):
        for i in range(2):
            owner = page_facts(facts, other, 2 * lane + i)[0]
            o_ref[lane, i] = turned[owner].astype(jnp.bfloat16)
        return carry

    lax.fori_loop(0, o_ref.shape[0], one, 0)


def chosen_queries(facts, query, lanes):
    rows = (query.shape[1], QH // lanes * STEPS, HD)
    return pl.pallas_call(
        choose_kernel,
        out_shape=(
            jax.ShapeDtypeStruct((lanes, 2, *rows[1:]), jnp.bfloat16),
            jax.ShapeDtypeStruct(rows, jnp.bfloat16),
        ),
        in_specs=[SMEM, VMEM],
        out_specs=(VMEM, VMEM),
        scratch_shapes=[pltpu.VMEM(rows, jnp.float32)],
        name="choose_queries",
        **params(32),
    )(facts, query)


def partial_kernel(lanes, facts, q_ref, *rest):
    *packed, o_ref = rest
    split = GROUP // (QH // lanes)
    width = QH // lanes * STEPS
    extra = stat_rows(2 * width)
    half, place = lax.axis_index("section"), lax.axis_index("tp")
    group = GROUP * STEPS
    height = 2 * KVH * group
    lane = lax.broadcasted_iota(jnp.int32, (height, PAGE), 1)
    later = lax.broadcasted_iota(jnp.int32, (height, PAGE), 0) // group % 2 == 1
    spot = lax.broadcasted_iota(jnp.int32, (2 * width, PAGE), 0)
    across = lax.broadcasted_iota(jnp.int32, (2 * width, PAGE), 1)
    line = lax.broadcasted_iota(jnp.int32, (extra, PAGE), 0)
    lives = [page_facts(facts, half, 2 * place + i)[2] for i in range(2)]
    places = [(block, j, n) for block, n in zip(packed, CHUNKS) for j in range(n)]
    scores, values = [], []
    for k, (block, j, n) in enumerate(places):
        for i in range(2):
            query = jnp.concatenate([q_ref[k * split + t, i] for t in range(split)], axis=0)
            scores.append(dot(query, block[i, j * HD:(j + 1) * HD]))
            values.append(block[i, (n + j) * HD:(n + j + 1) * HD])
    score = jnp.concatenate(scores, axis=0) * SCALE
    score = jnp.where(lane < jnp.where(later, lives[1], lives[0]), score, LOW)
    top = jnp.max(score, axis=1, keepdims=True)
    terms = jnp.exp(score - top)
    total = jnp.sum(terms, axis=1, keepdims=True)
    high = terms.astype(jnp.bfloat16)
    low = (terms - high.astype(jnp.float32)).astype(jnp.bfloat16)
    mixed = jnp.concatenate(
        [
            dot(high[m * group:(m + 1) * group], v) + dot(low[m * group:(m + 1) * group], v)
            for m, v in enumerate(values)
        ],
        axis=0,
    ) / total
    sums = top + jnp.log(total)
    for k in range(KVH):
        for t in range(split):
            begins = [(2 * k + i) * group + t * width for i in range(2)]
            both = jnp.concatenate([sums[at:at + width] for at in begins], axis=0)
            turned = jnp.sum(jnp.where(spot == across, both, 0.0), axis=0, keepdims=True)
            first = turned.astype(jnp.bfloat16).astype(jnp.float32)
            rest = turned - first
            second = rest.astype(jnp.bfloat16).astype(jnp.float32)
            stat = jnp.where(line == 0, first, jnp.where(line == 1, second, rest - second))
            stat = jnp.where(line < 3, stat, 0.0)
            block = jnp.concatenate([mixed[at:at + width] for at in begins] + [stat], axis=0)
            o_ref[k * split + t] = block.astype(jnp.bfloat16)


def partial_decode(facts, query, packed, lanes):
    rows = 2 * (QH // lanes) * STEPS
    return pl.pallas_call(
        functools.partial(partial_kernel, lanes),
        out_shape=jax.ShapeDtypeStruct((lanes, rows + stat_rows(rows), HD), jnp.bfloat16),
        in_specs=[SMEM, VMEM] + [VMEM] * len(packed),
        out_specs=VMEM,
        name="partial_decode",
        **params(32),
    )(facts, query, *packed)


def merge_kernel(lanes, facts, parts_ref, q_ref, k_ref, v_ref, o_ref):
    requests = q_ref.shape[0]
    width = (QH // lanes) * STEPS
    other, place = 1 - lax.axis_index("section"), lax.axis_index("tp")
    head = place * (QH // lanes) // GROUP
    spot = lax.broadcasted_iota(jnp.int32, (width, PAGE), 0)
    across = lax.broadcasted_iota(jnp.int32, (width, PAGE), 1)
    step = lax.broadcasted_iota(jnp.int32, (width, 1), 0) % STEPS
    end = 0
    for r in range(requests):
        start, end = end, end + facts[other, r]
        query = q_ref[r].astype(jnp.float32)
        keys = k_ref[r, head].astype(jnp.float32)
        values = v_ref[r, head].astype(jnp.float32)
        tops, vectors = [], []
        for u in range(STEPS):
            score = jnp.sum(query * keys[u:u + 1], axis=1, keepdims=True) * SCALE
            tops.append(jnp.where(u <= step, score, LOW))
            vectors.append(values[u:u + 1])
        for j in range(MAXP):
            page = jnp.minimum(start + j, 2 * lanes - 1)
            block = parts_ref[page // 2].astype(jnp.float32)
            later = jnp.full((width, HD), page % 2 == 1)
            vectors.append(jnp.where(later, block[width:2 * width], block[:width]))
            stat = jnp.sum(block[2 * width:2 * width + 8], axis=0, keepdims=True)
            stat = jnp.sum(
                jnp.where(across - page % 2 * width == spot, stat, 0.0), axis=1, keepdims=True
            )
            tops.append(jnp.where(jnp.full((width, 1), start + j < end), stat, LOW))
        top = functools.reduce(jnp.maximum, tops)
        weights = [jnp.exp(t - top) for t in tops]
        total = functools.reduce(jnp.add, weights)
        mixed = functools.reduce(jnp.add, [w * x for w, x in zip(weights, vectors)])
        o_ref[r] = (mixed / total).astype(jnp.bfloat16)


def merged(facts, parts, query, new_key, new_value, lanes):
    requests = query.shape[0]
    fresh = [
        jnp.transpose(x.reshape(STEPS, requests, KVH, HD), (1, 2, 0, 3)) for x in (new_key, new_value)
    ]
    out = pl.pallas_call(
        functools.partial(merge_kernel, lanes),
        out_shape=jax.ShapeDtypeStruct(query.shape, jnp.bfloat16),
        in_specs=[SMEM, VMEM, VMEM, VMEM, VMEM],
        out_specs=VMEM,
        name="merge_decode",
        **params(32),
    )(facts, parts, query, *fresh)
    out = jnp.transpose(out.reshape(requests, QH // lanes, STEPS, HD), (2, 0, 1, 3))
    return out.reshape(STEPS, requests, QH // lanes * HD)


def other_half(x):
    return lax.ppermute(x, "section", [(0, 1), (1, 0)])


def after(x, *earlier):
    return lax.optimization_barrier((x, *earlier))[0]


def on_device(
    prefill_query, prefill_key, prefill_value, counts, fills, dec_query, dec_key, dec_value
):
    lanes = lax.axis_size("tp")
    query, key, value = prefill_query[0], prefill_key[0], prefill_value[0]
    facts = jnp.concatenate([counts, fills], axis=1)
    flags = page_flags(facts)
    ahead = [(i, i + 2) for i in range(lanes - 2)]
    ahead_again = [(i, i + 2) for i in range(2, lanes - 2)]
    beside = [(i, i + 1) for i in range(0, lanes, 2)]
    trade = [(i, i ^ 1) for i in range(2, lanes)]
    bases = [sum(CHUNKS[:g]) for g in range(len(CHUNKS))]
    mine = []
    for base, n in zip(bases, CHUNKS):
        mine.append(pack(base, n, after(key, *mine), value))

    first_hops = [lax.ppermute(block, "tp", ahead) for block in mine]

    asked = after(dec_query[0], mine[0])
    chosen, dec_rows = chosen_queries(facts, asked, lanes)
    wanted = lax.all_to_all(chosen, "tp", split_axis=0, concat_axis=0, tiled=True)
    parts = partial_decode(facts, other_half(wanted), mine, lanes)
    parts = lax.all_to_all(parts, "tp", split_axis=0, concat_axis=0, tiled=True)
    dec_out = merged(facts, other_half(parts), dec_rows, dec_key[0], dec_value[0], lanes)

    received = []
    for g, (block, a) in enumerate(zip(mine, first_hops)):
        b = lax.ppermute(after(block, received[0][2]) if g else block, "tp", beside)
        c = lax.ppermute(a if g else after(a, wanted, mine[1]), "tp", trade)
        d = jnp.concatenate([a[1:], c], axis=0)
        d = lax.ppermute(d if g else after(d, first_hops[1], parts), "tp", ahead_again)
        received.append((a, b, c, d))
    out = None
    for g, (base, n) in enumerate(zip(bases, CHUNKS)):
        if g:
            out = after(out, dec_out)
        out = prompt_heads(base, n, 0, n, flags, query, (mine[g], *received[g]), out)
    return (out[None], dec_out[None])


def solution(mesh):
    placed = (
        P("section", ("groups", "tp"), None),
        P("section", ("groups", "tp"), None),
        P("section", ("groups", "tp"), None),
        P(None, "groups"),
        P(None, "groups"),
        P("section", None, "groups", "tp"),
        P("section", None, "groups", None),
        P("section", None, "groups", None),
    )
    return jax.shard_map(
        on_device,
        mesh=mesh,
        in_specs=placed,
        out_specs=(P("section", ("groups", "tp"), None), P("section", None, "groups", "tp")),
        check_vma=False,
    )
```

```python
import functools
import math

import jax
import jax.numpy as jnp
from jax import lax
from jax.experimental import pallas as pl
from jax.experimental.pallas import tpu as pltpu
from jax.sharding import PartitionSpec as P

QH = 64
KVH = 8
HD = 128
PAGE = 128
MAXP = 8
STEPS = 4
GROUP = QH // KVH
SCALE = HD ** (-0.5)
EXP2_SCALE = SCALE * math.log2(math.e)
LOW = -1e30
CHUNKS = (4, 4)
ROWS = 512
SMEM = pl.BlockSpec(memory_space=pltpu.SMEM)
VMEM = pl.BlockSpec(memory_space=pltpu.VMEM)


def dot(a, b):
    return jnp.dot(a, b, preferred_element_type=jnp.float32)


def page_facts(facts, half, page):
    requests = facts.shape[1] // 2
    owner, first, live, end = -1, 0, PAGE, 0
    for r in range(requests):
        start, end = end, end + facts[half, r]
        begun = start <= page
        owner = jnp.where(begun, r, owner)
        first = jnp.where(begun, start, first)
        live = jnp.where(end - 1 == page, facts[half, requests + r], live)
    return owner, first, live


def params(limit):
    return dict(
        compiler_params=pltpu.CompilerParams(vmem_limit_bytes=limit << 20),
        cost_estimate=pl.CostEstimate(flops=1, bytes_accessed=1, transcendentals=0),
    )


def pack_kernel(base, k_ref, v_ref, *rest):
    o_ref, k_part, v_part, sems = rest[-4:]
    n = k_part.shape[1] // HD
    own = slice(base * HD, (base + n) * HD)
    copies = [
        pltpu.make_async_copy(source.at[:, own], part, sems.at[spot])
        for spot, (source, part) in enumerate(((k_ref, k_part), (v_ref, v_part)))
    ]
    for copy in copies:
        copy.start()
    for copy in copies:
        copy.wait()
    for j in range(n):
        columns = slice(j * HD, (j + 1) * HD)
        for p in range(2):
            rows = slice(p * PAGE, (p + 1) * PAGE)
            turned = jnp.transpose(k_part[rows, columns].astype(jnp.float32)).astype(jnp.bfloat16)
            o_ref[p, columns] = turned
            o_ref[p, (n + j) * HD:(n + j + 1) * HD] = v_part[rows, columns]


def pack(base, n, key, value):
    part = pltpu.VMEM((key.shape[0], n * HD), jnp.bfloat16)
    return pl.pallas_call(
        functools.partial(pack_kernel, base),
        out_shape=jax.ShapeDtypeStruct((2, 2 * n * HD, PAGE), jnp.bfloat16),
        in_specs=[pl.BlockSpec(memory_space=pl.ANY)] * 2,
        out_specs=VMEM,
        scratch_shapes=[part, part, pltpu.SemaphoreType.DMA((2,))],
        name="pack",
        **params(48),
    )(key, value)


def flags_kernel(facts, o_ref):
    half, place = lax.axis_index("section"), lax.axis_index("tp")
    even = place % 2 == 0
    near, far = 2 * place - 2, 2 * place - 6
    line = lax.broadcasted_iota(jnp.int32, o_ref.shape, 0)
    out = jnp.zeros(o_ref.shape, jnp.float32)
    for i in range(2):
        _, first, live = page_facts(facts, half, 2 * place + i)
        numbers = [2 * place - 7 if i == 0 else 2 * place, 2 * place + i]
        for page in (2 * place - 4, jnp.where(even, near, far), jnp.where(even, far, near)):
            numbers += [page, page + 1]
        for spot, number in enumerate(numbers):
            out = jnp.where(line == i * MAXP + spot, jnp.where(number >= first, 1.0, 0.0), out)
        out = jnp.where(line == 2 * MAXP + i, live.astype(jnp.float32), out)
    o_ref[...] = out


def page_flags(facts):
    return pl.pallas_call(
        flags_kernel,
        out_shape=jax.ShapeDtypeStruct((2 * MAXP + 8, PAGE), jnp.float32),
        in_specs=[SMEM],
        out_specs=VMEM,
        name="page_flags",
        **params(48),
    )(facts)


def prompt_kernel(n, low, flags, q_ref, *rest):
    o_ref, keys, values, causal, *probs = rest[-6:]
    head = low + pl.program_id(0)
    spots = [pl.ds(pl.multiple_of((x + head) * HD, HD), HD) for x in (0, n)]
    mine, a, b, c, d = [[[x[p, at] for at in spots] for p in range(x.shape[0])] for x in rest[:5]]
    choose = jnp.full((HD, PAGE), lax.axis_index("tp") % 2 == 0)
    be = [[jnp.where(choose, x, y) for x, y in zip(d[1 + p], b[p])] for p in range(2)]
    row = lax.broadcasted_iota(jnp.int32, (PAGE, PAGE), 0)
    col = lax.broadcasted_iota(jnp.int32, (PAGE, PAGE), 1)
    causal[...] = jnp.where(col <= row, 0.0, LOW)
    one = jnp.ones((PAGE, HD), jnp.bfloat16)
    zero = jnp.zeros((PAGE, HD), jnp.bfloat16)
    lives = [flags[2 * MAXP + i:2 * MAXP + i + 1, :] for i in range(2)]

    for i in range(2):
        stand_in = jnp.broadcast_to(mine[i][0][:, :1], (HD, PAGE))
        pages = [d[0] if i == 0 else mine[0], mine[i], *a, *c, *be]
        for spot, (k, v) in enumerate(pages):
            line = i * MAXP + spot
            seen = jnp.broadcast_to(flags[line:line + 1, :], (PAGE, HD)) > 0.0
            at = slice(spot * PAGE, (spot + 1) * PAGE)
            k = jnp.where(seen, k, stand_in)
            keys[i, :HD, at] = k
            keys[i, HD:, at] = k
            values[i, at, :HD] = jnp.where(seen, v, zero)
            values[i, at, HD:] = jnp.where(seen, one, zero)

    heads_at_once = ROWS // PAGE
    blocks = [(i, start) for i in range(2) for start in range(0, GROUP, heads_at_once)]

    def halves(query):
        query = query.astype(jnp.float32) * EXP2_SCALE
        high = query.astype(jnp.bfloat16)
        low = (query - high.astype(jnp.float32)).astype(jnp.bfloat16)
        return jnp.concatenate([high, low], axis=1)

    def queries(i, start):
        return halves(
            jnp.concatenate(
                [
                    q_ref[i * PAGE:(i + 1) * PAGE, h * HD:(h + 1) * HD]
                    for h in range(start, start + heads_at_once)
                ],
                axis=0,
            )
        )

    def divided(mixed, live):
        total = mixed[:, HD:]
        near = pl.reciprocal(total, approx=True)
        near = near * (2.0 - total * near)
        token = lax.broadcasted_iota(jnp.int32, (total.shape[0], HD), 0) % PAGE
        return jnp.where(token.astype(jnp.float32) < live, mixed[:, :HD] * near, 0.0).astype(jnp.bfloat16)

    tiles = [slice(t, t + 2 * PAGE) for t in range(0, MAXP * PAGE, 2 * PAGE)]

    def own_scores(query, i, repeat):
        own = dot(query, keys[i, :, tiles[0]])
        bias = jnp.concatenate([causal[...]] * repeat, axis=0)
        return jnp.concatenate([own[:, :PAGE], own[:, PAGE:] + bias], axis=1)

    def mix(block, slot, largest):
        i, start = block
        mixed = dot(probs[slot][...], values[i])
        out = divided(mixed, lives[i])
        for number in range(heads_at_once):
            h = start + number
            o_ref[i * PAGE:(i + 1) * PAGE, h * HD:(h + 1) * HD] = out[number * PAGE:(number + 1) * PAGE]
        return jnp.maximum(largest, mixed[:, HD:])

    largest = jnp.zeros((ROWS, HD), jnp.float32)
    for index in range(len(blocks) + 1):
        if index < len(blocks):
            i, slot = blocks[index][0], index % 2
            query = queries(*blocks[index])
            own = own_scores(query, i, heads_at_once)
            top = jnp.max(own, axis=1, keepdims=True)
            probs[slot][:, tiles[0]] = jnp.exp2(own - top).astype(jnp.bfloat16)
        if index > 0:
            largest = mix(blocks[index - 1], 1 - slot if index < len(blocks) else slot, largest)
        if index < len(blocks):
            for at in tiles[1:]:
                other = dot(query, keys[i, :, at])
                probs[slot][:, at] = jnp.exp2(other - top).astype(jnp.bfloat16)

    @pl.when(jnp.logical_not(jnp.max(largest) < 1e30))
    def _():
        def one(index, carry):
            i, h = index // GROUP, index % GROUP
            rows = pl.ds(pl.multiple_of(i * PAGE, PAGE), PAGE)
            columns = pl.ds(pl.multiple_of(h * HD, HD), HD)
            query = halves(q_ref[rows, columns])
            scores = [own_scores(query, i, 1)] + [dot(query, keys[i, :, at]) for at in tiles[1:]]
            top = jnp.max(functools.reduce(jnp.maximum, scores), axis=1, keepdims=True)
            mixed = jnp.zeros((PAGE, 2 * HD), jnp.float32)
            for score, at in zip(scores, tiles):
                mixed = mixed + dot(jnp.exp2(score - top).astype(jnp.bfloat16), values[i, at])
            o_ref[rows, columns] = divided(mixed, jnp.where(i == 0, lives[0], lives[1]))
            return carry

        lax.fori_loop(0, 2 * GROUP, one, 0)


def prompt_heads(base, n, low, high, flags, query, blocks, done):
    tok = query.shape[0]

    wide = pl.BlockSpec((tok, GROUP * HD), lambda j: (0, base + low + j))
    operands = [flags, query, *blocks]
    specs = [VMEM, wide] + [VMEM] * len(blocks)
    aliases = {}
    if done is not None:
        aliases = {len(operands): 0}
        operands.append(done)
        specs.append(pl.BlockSpec(memory_space=pl.ANY))
    return pl.pallas_call(
        functools.partial(prompt_kernel, n, low),
        out_shape=jax.ShapeDtypeStruct(query.shape, jnp.bfloat16),
        grid=(high - low,),
        in_specs=specs,
        out_specs=wide,
        scratch_shapes=[
            pltpu.VMEM((2, 2 * HD, MAXP * PAGE), jnp.bfloat16),
            pltpu.VMEM((2, MAXP * PAGE, 2 * HD), jnp.bfloat16),
            pltpu.VMEM((PAGE, PAGE), jnp.float32),
            pltpu.VMEM((ROWS, MAXP * PAGE), jnp.bfloat16),
            pltpu.VMEM((ROWS, MAXP * PAGE), jnp.bfloat16),
        ],
        input_output_aliases=aliases,
        name="prompt_attention",
        compiler_params=pltpu.CompilerParams(vmem_limit_bytes=48 << 20),
        cost_estimate=pl.CostEstimate(
            flops=(high - low) * GROUP * tok * MAXP * PAGE * HD * 8,
            bytes_accessed=4 * (high - low) * tok * GROUP * HD,
            transcendentals=0,
        ),
    )(*operands)


def stat_rows(rows):
    return 16 - rows % 16


def choose_kernel(facts, q_ref, o_ref, rows_ref, turned):
    requests, here = q_ref.shape[1], q_ref.shape[2] // HD
    other = 1 - lax.axis_index("section")
    for s in range(STEPS):
        query = q_ref[s].astype(jnp.float32)
        for r in range(requests):
            for h in range(here):
                row = h * STEPS + s
                turned[r, row:row + 1] = query[r:r + 1, h * HD:(h + 1) * HD]
    rows_ref[...] = turned[...].astype(jnp.bfloat16)

    def one(lane, carry):
        for i in range(2):
            owner = page_facts(facts, other, 2 * lane + i)[0]
            o_ref[lane, i] = turned[owner].astype(jnp.bfloat16)
        return carry

    lax.fori_loop(0, o_ref.shape[0], one, 0)


def chosen_queries(facts, query, lanes):
    rows = (query.shape[1], QH // lanes * STEPS, HD)
    return pl.pallas_call(
        choose_kernel,
        out_shape=(
            jax.ShapeDtypeStruct((lanes, 2, *rows[1:]), jnp.bfloat16),
            jax.ShapeDtypeStruct(rows, jnp.bfloat16),
        ),
        in_specs=[SMEM, VMEM],
        out_specs=(VMEM, VMEM),
        scratch_shapes=[pltpu.VMEM(rows, jnp.float32)],
        name="choose_queries",
        **params(32),
    )(facts, query)


def partial_kernel(lanes, facts, q_ref, *rest):
    *packed, o_ref = rest
    split = GROUP // (QH // lanes)
    width = QH // lanes * STEPS
    extra = stat_rows(2 * width)
    half, place = lax.axis_index("section"), lax.axis_index("tp")
    group = GROUP * STEPS
    height = 2 * KVH * group
    lane = lax.broadcasted_iota(jnp.int32, (height, PAGE), 1)
    later = lax.broadcasted_iota(jnp.int32, (height, PAGE), 0) // group % 2 == 1
    spot = lax.broadcasted_iota(jnp.int32, (2 * width, PAGE), 0)
    across = lax.broadcasted_iota(jnp.int32, (2 * width, PAGE), 1)
    line = lax.broadcasted_iota(jnp.int32, (extra, PAGE), 0)
    lives = [page_facts(facts, half, 2 * place + i)[2] for i in range(2)]
    places = [(block, j, n) for block, n in zip(packed, CHUNKS) for j in range(n)]
    scores, values = [], []
    for k, (block, j, n) in enumerate(places):
        for i in range(2):
            query = jnp.concatenate([q_ref[k * split + t, i] for t in range(split)], axis=0)
            scores.append(dot(query, block[i, j * HD:(j + 1) * HD]))
            values.append(block[i, (n + j) * HD:(n + j + 1) * HD])
    score = jnp.concatenate(scores, axis=0) * SCALE
    score = jnp.where(lane < jnp.where(later, lives[1], lives[0]), score, LOW)
    top = jnp.max(score, axis=1, keepdims=True)
    terms = jnp.exp(score - top)
    total = jnp.sum(terms, axis=1, keepdims=True)
    high = terms.astype(jnp.bfloat16)
    low = (terms - high.astype(jnp.float32)).astype(jnp.bfloat16)
    mixed = jnp.concatenate(
        [
            dot(high[m * group:(m + 1) * group], v) + dot(low[m * group:(m + 1) * group], v)
            for m, v in enumerate(values)
        ],
        axis=0,
    ) / total
    sums = top + jnp.log(total)
    for k in range(KVH):
        for t in range(split):
            begins = [(2 * k + i) * group + t * width for i in range(2)]
            both = jnp.concatenate([sums[at:at + width] for at in begins], axis=0)
            turned = jnp.sum(jnp.where(spot == across, both, 0.0), axis=0, keepdims=True)
            first = turned.astype(jnp.bfloat16).astype(jnp.float32)
            rest = turned - first
            second = rest.astype(jnp.bfloat16).astype(jnp.float32)
            stat = jnp.where(line == 0, first, jnp.where(line == 1, second, rest - second))
            stat = jnp.where(line < 3, stat, 0.0)
            block = jnp.concatenate([mixed[at:at + width] for at in begins] + [stat], axis=0)
            o_ref[k * split + t] = block.astype(jnp.bfloat16)


def partial_decode(facts, query, packed, lanes):
    rows = 2 * (QH // lanes) * STEPS
    return pl.pallas_call(
        functools.partial(partial_kernel, lanes),
        out_shape=jax.ShapeDtypeStruct((lanes, rows + stat_rows(rows), HD), jnp.bfloat16),
        in_specs=[SMEM, VMEM] + [VMEM] * len(packed),
        out_specs=VMEM,
        name="partial_decode",
        **params(32),
    )(facts, query, *packed)


def merge_kernel(lanes, facts, parts_ref, q_ref, k_ref, v_ref, o_ref):
    requests = q_ref.shape[0]
    width = (QH // lanes) * STEPS
    other, place = 1 - lax.axis_index("section"), lax.axis_index("tp")
    head = place * (QH // lanes) // GROUP
    spot = lax.broadcasted_iota(jnp.int32, (width, PAGE), 0)
    across = lax.broadcasted_iota(jnp.int32, (width, PAGE), 1)
    step = lax.broadcasted_iota(jnp.int32, (width, 1), 0) % STEPS
    end = 0
    for r in range(requests):
        start, end = end, end + facts[other, r]
        query = q_ref[r].astype(jnp.float32)
        keys = k_ref[r, head].astype(jnp.float32)
        values = v_ref[r, head].astype(jnp.float32)
        tops, vectors = [], []
        for u in range(STEPS):
            score = jnp.sum(query * keys[u:u + 1], axis=1, keepdims=True) * SCALE
            tops.append(jnp.where(u <= step, score, LOW))
            vectors.append(values[u:u + 1])
        for j in range(MAXP):
            page = jnp.minimum(start + j, 2 * lanes - 1)
            block = parts_ref[page // 2].astype(jnp.float32)
            later = jnp.full((width, HD), page % 2 == 1)
            vectors.append(jnp.where(later, block[width:2 * width], block[:width]))
            stat = jnp.sum(block[2 * width:2 * width + 8], axis=0, keepdims=True)
            stat = jnp.sum(
                jnp.where(across - page % 2 * width == spot, stat, 0.0), axis=1, keepdims=True
            )
            tops.append(jnp.where(jnp.full((width, 1), start + j < end), stat, LOW))
        top = functools.reduce(jnp.maximum, tops)
        weights = [jnp.exp(t - top) for t in tops]
        total = functools.reduce(jnp.add, weights)
        mixed = functools.reduce(jnp.add, [w * x for w, x in zip(weights, vectors)])
        o_ref[r] = (mixed / total).astype(jnp.bfloat16)


def merged(facts, parts, query, new_key, new_value, lanes):
    requests = query.shape[0]
    fresh = [
        jnp.transpose(x.reshape(STEPS, requests, KVH, HD), (1, 2, 0, 3)) for x in (new_key, new_value)
    ]
    out = pl.pallas_call(
        functools.partial(merge_kernel, lanes),
        out_shape=jax.ShapeDtypeStruct(query.shape, jnp.bfloat16),
        in_specs=[SMEM, VMEM, VMEM, VMEM, VMEM],
        out_specs=VMEM,
        name="merge_decode",
        **params(32),
    )(facts, parts, query, *fresh)
    out = jnp.transpose(out.reshape(requests, QH // lanes, STEPS, HD), (2, 0, 1, 3))
    return out.reshape(STEPS, requests, QH // lanes * HD)


def other_half(x):
    return lax.ppermute(x, "section", [(0, 1), (1, 0)])


def after(x, *earlier):
    return lax.optimization_barrier((x, *earlier))[0]


def on_device(
    prefill_query, prefill_key, prefill_value, counts, fills, dec_query, dec_key, dec_value
):
    lanes = lax.axis_size("tp")
    query, key, value = prefill_query[0], prefill_key[0], prefill_value[0]
    facts = jnp.concatenate([counts, fills], axis=1)
    flags = page_flags(facts)
    ahead = [(i, i + 2) for i in range(lanes - 2)]
    ahead_again = [(i, i + 2) for i in range(2, lanes - 2)]
    beside = [(i, i + 1) for i in range(0, lanes, 2)]
    trade = [(i, i ^ 1) for i in range(2, lanes)]
    bases = [sum(CHUNKS[:g]) for g in range(len(CHUNKS))]
    mine = []
    for base, n in zip(bases, CHUNKS):
        mine.append(pack(base, n, after(key, *mine), value))

    first_hops = [lax.ppermute(block, "tp", ahead) for block in mine]

    asked = after(dec_query[0], mine[0])
    chosen, dec_rows = chosen_queries(facts, asked, lanes)
    wanted = lax.all_to_all(chosen, "tp", split_axis=0, concat_axis=0, tiled=True)
    parts = partial_decode(facts, other_half(wanted), mine, lanes)
    parts = lax.all_to_all(parts, "tp", split_axis=0, concat_axis=0, tiled=True)
    dec_out = merged(facts, other_half(parts), dec_rows, dec_key[0], dec_value[0], lanes)

    received = []
    for g, (block, a) in enumerate(zip(mine, first_hops)):
        b = lax.ppermute(after(block, received[0][2]) if g else block, "tp", beside)
        c = lax.ppermute(a if g else after(a, b, mine[1]), "tp", trade)
        d = jnp.concatenate([a[1:], c], axis=0)
        d = lax.ppermute(after(d, parts if g else first_hops[1]), "tp", ahead_again)
        received.append((a, b, c, d))
    out, flags = None, after(flags, received[1][2])
    for g, (base, n) in enumerate(zip(bases, CHUNKS)):
        if g:
            out = after(out, dec_out)
        out = prompt_heads(base, n, 0, n, flags, query, (mine[g], *received[g]), out)
    return (out[None], dec_out[None])


def solution(mesh):
    placed = (
        P("section", ("groups", "tp"), None),
        P("section", ("groups", "tp"), None),
        P("section", ("groups", "tp"), None),
        P(None, "groups"),
        P(None, "groups"),
        P("section", None, "groups", "tp"),
        P("section", None, "groups", None),
        P("section", None, "groups", None),
    )
    return jax.shard_map(
        on_device,
        mesh=mesh,
        in_specs=placed,
        out_specs=(P("section", ("groups", "tp"), None), P("section", None, "groups", "tp")),
        check_vma=False,
    )
```

```python
import functools
import math

import jax
import jax.numpy as jnp
from jax import lax
from jax.experimental import pallas as pl
from jax.experimental.pallas import tpu as pltpu
from jax.sharding import PartitionSpec as P

QH = 64
KVH = 8
HD = 128
PAGE = 128
MAXP = 8
STEPS = 4
GROUP = QH // KVH
SCALE = HD ** (-0.5)
EXP2_SCALE = SCALE * math.log2(math.e)
LOW = -1e30
CHUNKS = (4, 4)
ROWS = 512
SMEM = pl.BlockSpec(memory_space=pltpu.SMEM)
VMEM = pl.BlockSpec(memory_space=pltpu.VMEM)


def dot(a, b):
    return jnp.dot(a, b, preferred_element_type=jnp.float32)


def page_facts(facts, half, page):
    requests = facts.shape[1] // 2
    owner, first, live, end = -1, 0, PAGE, 0
    for r in range(requests):
        start, end = end, end + facts[half, r]
        begun = start <= page
        owner = jnp.where(begun, r, owner)
        first = jnp.where(begun, start, first)
        live = jnp.where(end - 1 == page, facts[half, requests + r], live)
    return owner, first, live


def params(limit):
    return dict(
        compiler_params=pltpu.CompilerParams(vmem_limit_bytes=limit << 20),
        cost_estimate=pl.CostEstimate(flops=1, bytes_accessed=1, transcendentals=0),
    )


def pack_kernel(base, k_ref, v_ref, *rest):
    o_ref, k_part, v_part, sems = rest[-4:]
    n = k_part.shape[1] // HD
    own = slice(base * HD, (base + n) * HD)
    copies = [
        pltpu.make_async_copy(source.at[:, own], part, sems.at[spot])
        for spot, (source, part) in enumerate(((k_ref, k_part), (v_ref, v_part)))
    ]
    for copy in copies:
        copy.start()
    for copy in copies:
        copy.wait()
    for j in range(n):
        columns = slice(j * HD, (j + 1) * HD)
        for p in range(2):
            rows = slice(p * PAGE, (p + 1) * PAGE)
            turned = jnp.transpose(k_part[rows, columns].astype(jnp.float32)).astype(jnp.bfloat16)
            o_ref[p, columns] = turned
            o_ref[p, (n + j) * HD:(n + j + 1) * HD] = v_part[rows, columns]


def pack(base, n, key, value):
    part = pltpu.VMEM((key.shape[0], n * HD), jnp.bfloat16)
    return pl.pallas_call(
        functools.partial(pack_kernel, base),
        out_shape=jax.ShapeDtypeStruct((2, 2 * n * HD, PAGE), jnp.bfloat16),
        in_specs=[pl.BlockSpec(memory_space=pl.ANY)] * 2,
        out_specs=VMEM,
        scratch_shapes=[part, part, pltpu.SemaphoreType.DMA((2,))],
        name="pack",
        **params(48),
    )(key, value)


def flags_kernel(facts, o_ref):
    half, place = lax.axis_index("section"), lax.axis_index("tp")
    even = place % 2 == 0
    near, far = 2 * place - 2, 2 * place - 6
    line = lax.broadcasted_iota(jnp.int32, o_ref.shape, 0)
    out = jnp.zeros(o_ref.shape, jnp.float32)
    for i in range(2):
        _, first, live = page_facts(facts, half, 2 * place + i)
        numbers = [2 * place - 7 if i == 0 else 2 * place, 2 * place + i]
        for page in (2 * place - 4, jnp.where(even, near, far), jnp.where(even, far, near)):
            numbers += [page, page + 1]
        for spot, number in enumerate(numbers):
            out = jnp.where(line == i * MAXP + spot, jnp.where(number >= first, 1.0, 0.0), out)
        out = jnp.where(line == 2 * MAXP + i, live.astype(jnp.float32), out)
    o_ref[...] = out


def page_flags(facts):
    return pl.pallas_call(
        flags_kernel,
        out_shape=jax.ShapeDtypeStruct((2 * MAXP + 8, PAGE), jnp.float32),
        in_specs=[SMEM],
        out_specs=VMEM,
        name="page_flags",
        **params(48),
    )(facts)


def prompt_kernel(n, low, flags, q_ref, *rest):
    o_ref, keys, values, causal, *probs = rest[-6:]
    head = low + pl.program_id(0)
    spots = [pl.ds(pl.multiple_of((x + head) * HD, HD), HD) for x in (0, n)]
    mine, a, b, c, d = [[[x[p, at] for at in spots] for p in range(x.shape[0])] for x in rest[:5]]
    choose = jnp.full((HD, PAGE), lax.axis_index("tp") % 2 == 0)
    be = [[jnp.where(choose, x, y) for x, y in zip(d[1 + p], b[p])] for p in range(2)]
    row = lax.broadcasted_iota(jnp.int32, (PAGE, PAGE), 0)
    col = lax.broadcasted_iota(jnp.int32, (PAGE, PAGE), 1)
    causal[...] = jnp.where(col <= row, 0.0, LOW)
    one = jnp.ones((PAGE, HD), jnp.bfloat16)
    zero = jnp.zeros((PAGE, HD), jnp.bfloat16)
    lives = [flags[2 * MAXP + i:2 * MAXP + i + 1, :] for i in range(2)]

    for i in range(2):
        stand_in = jnp.broadcast_to(mine[i][0][:, :1], (HD, PAGE))
        pages = [d[0] if i == 0 else mine[0], mine[i], *a, *c, *be]
        for spot, (k, v) in enumerate(pages):
            line = i * MAXP + spot
            seen = jnp.broadcast_to(flags[line:line + 1, :], (PAGE, HD)) > 0.0
            at = slice(spot * PAGE, (spot + 1) * PAGE)
            k = jnp.where(seen, k, stand_in)
            keys[i, :HD, at] = k
            keys[i, HD:, at] = k
            values[i, at, :HD] = jnp.where(seen, v, zero)
            values[i, at, HD:] = jnp.where(seen, one, zero)

    heads_at_once = ROWS // PAGE
    blocks = [(i, start) for i in range(2) for start in range(0, GROUP, heads_at_once)]

    def halves(query):
        query = query.astype(jnp.float32) * EXP2_SCALE
        high = query.astype(jnp.bfloat16)
        low = (query - high.astype(jnp.float32)).astype(jnp.bfloat16)
        return jnp.concatenate([high, low], axis=1)

    def queries(i, start):
        return halves(
            jnp.concatenate(
                [
                    q_ref[i * PAGE:(i + 1) * PAGE, h * HD:(h + 1) * HD]
                    for h in range(start, start + heads_at_once)
                ],
                axis=0,
            )
        )

    def divided(mixed, live):
        total = mixed[:, HD:]
        near = pl.reciprocal(total, approx=True)
        near = near * (2.0 - total * near)
        token = lax.broadcasted_iota(jnp.int32, (total.shape[0], HD), 0) % PAGE
        return jnp.where(token.astype(jnp.float32) < live, mixed[:, :HD] * near, 0.0).astype(jnp.bfloat16)

    tiles = [slice(t, t + 2 * PAGE) for t in range(0, MAXP * PAGE, 2 * PAGE)]

    def own_scores(query, i, repeat):
        own = dot(query, keys[i, :, tiles[0]])
        bias = jnp.concatenate([causal[...]] * repeat, axis=0)
        return jnp.concatenate([own[:, :PAGE], own[:, PAGE:] + bias], axis=1)

    def mix(block, slot, largest):
        i, start = block
        mixed = dot(probs[slot][...], values[i])
        out = divided(mixed, lives[i])
        for number in range(heads_at_once):
            h = start + number
            o_ref[i * PAGE:(i + 1) * PAGE, h * HD:(h + 1) * HD] = out[number * PAGE:(number + 1) * PAGE]
        return jnp.maximum(largest, mixed[:, HD:])

    largest = jnp.zeros((ROWS, HD), jnp.float32)
    for index in range(len(blocks) + 1):
        if index < len(blocks):
            i, slot = blocks[index][0], index % 2
            query = queries(*blocks[index])
            own = own_scores(query, i, heads_at_once)
            top = jnp.max(own, axis=1, keepdims=True)
            probs[slot][:, tiles[0]] = jnp.exp2(own - top).astype(jnp.bfloat16)
        if index > 0:
            largest = mix(blocks[index - 1], 1 - slot if index < len(blocks) else slot, largest)
        if index < len(blocks):
            for at in tiles[1:]:
                other = dot(query, keys[i, :, at])
                probs[slot][:, at] = jnp.exp2(other - top).astype(jnp.bfloat16)

    @pl.when(jnp.logical_not(jnp.max(largest) < 1e30))
    def _():
        def one(index, carry):
            i, h = index // GROUP, index % GROUP
            rows = pl.ds(pl.multiple_of(i * PAGE, PAGE), PAGE)
            columns = pl.ds(pl.multiple_of(h * HD, HD), HD)
            query = halves(q_ref[rows, columns])
            scores = [own_scores(query, i, 1)] + [dot(query, keys[i, :, at]) for at in tiles[1:]]
            top = jnp.max(functools.reduce(jnp.maximum, scores), axis=1, keepdims=True)
            mixed = jnp.zeros((PAGE, 2 * HD), jnp.float32)
            for score, at in zip(scores, tiles):
                mixed = mixed + dot(jnp.exp2(score - top).astype(jnp.bfloat16), values[i, at])
            o_ref[rows, columns] = divided(mixed, jnp.where(i == 0, lives[0], lives[1]))
            return carry

        lax.fori_loop(0, 2 * GROUP, one, 0)


def prompt_heads(base, n, low, high, flags, query, blocks, done):
    tok = query.shape[0]

    wide = pl.BlockSpec((tok, GROUP * HD), lambda j: (0, base + low + j))
    operands = [flags, query, *blocks]
    specs = [VMEM, wide] + [VMEM] * len(blocks)
    aliases = {}
    if done is not None:
        aliases = {len(operands): 0}
        operands.append(done)
        specs.append(pl.BlockSpec(memory_space=pl.ANY))
    return pl.pallas_call(
        functools.partial(prompt_kernel, n, low),
        out_shape=jax.ShapeDtypeStruct(query.shape, jnp.bfloat16),
        grid=(high - low,),
        in_specs=specs,
        out_specs=wide,
        scratch_shapes=[
            pltpu.VMEM((2, 2 * HD, MAXP * PAGE), jnp.bfloat16),
            pltpu.VMEM((2, MAXP * PAGE, 2 * HD), jnp.bfloat16),
            pltpu.VMEM((PAGE, PAGE), jnp.float32),
            pltpu.VMEM((ROWS, MAXP * PAGE), jnp.bfloat16),
            pltpu.VMEM((ROWS, MAXP * PAGE), jnp.bfloat16),
        ],
        input_output_aliases=aliases,
        name="prompt_attention",
        compiler_params=pltpu.CompilerParams(vmem_limit_bytes=48 << 20),
        cost_estimate=pl.CostEstimate(
            flops=(high - low) * GROUP * tok * MAXP * PAGE * HD * 8,
            bytes_accessed=4 * (high - low) * tok * GROUP * HD,
            transcendentals=0,
        ),
    )(*operands)


def stat_rows(rows):
    return 16 - rows % 16


def choose_kernel(facts, q_ref, o_ref, rows_ref, turned):
    requests, here = q_ref.shape[1], q_ref.shape[2] // HD
    other = 1 - lax.axis_index("section")
    for s in range(STEPS):
        query = q_ref[s].astype(jnp.float32)
        for r in range(requests):
            for h in range(here):
                row = h * STEPS + s
                turned[r, row:row + 1] = query[r:r + 1, h * HD:(h + 1) * HD]
    rows_ref[...] = turned[...].astype(jnp.bfloat16)

    def one(lane, carry):
        for i in range(2):
            owner = page_facts(facts, other, 2 * lane + i)[0]
            o_ref[lane, i] = turned[owner].astype(jnp.bfloat16)
        return carry

    lax.fori_loop(0, o_ref.shape[0], one, 0)


def chosen_queries(facts, query, lanes):
    rows = (query.shape[1], QH // lanes * STEPS, HD)
    return pl.pallas_call(
        choose_kernel,
        out_shape=(
            jax.ShapeDtypeStruct((lanes, 2, *rows[1:]), jnp.bfloat16),
            jax.ShapeDtypeStruct(rows, jnp.bfloat16),
        ),
        in_specs=[SMEM, VMEM],
        out_specs=(VMEM, VMEM),
        scratch_shapes=[pltpu.VMEM(rows, jnp.float32)],
        name="choose_queries",
        **params(32),
    )(facts, query)


def partial_kernel(lanes, facts, q_ref, *rest):
    *packed, o_ref = rest
    split = GROUP // (QH // lanes)
    width = QH // lanes * STEPS
    extra = stat_rows(2 * width)
    half, place = lax.axis_index("section"), lax.axis_index("tp")
    group = GROUP * STEPS
    height = 2 * KVH * group
    lane = lax.broadcasted_iota(jnp.int32, (height, PAGE), 1)
    later = lax.broadcasted_iota(jnp.int32, (height, PAGE), 0) // group % 2 == 1
    spot = lax.broadcasted_iota(jnp.int32, (2 * width, PAGE), 0)
    across = lax.broadcasted_iota(jnp.int32, (2 * width, PAGE), 1)
    line = lax.broadcasted_iota(jnp.int32, (extra, PAGE), 0)
    lives = [page_facts(facts, half, 2 * place + i)[2] for i in range(2)]
    places = [(block, j, n) for block, n in zip(packed, CHUNKS) for j in range(n)]
    scores, values = [], []
    for k, (block, j, n) in enumerate(places):
        for i in range(2):
            query = jnp.concatenate([q_ref[k * split + t, i] for t in range(split)], axis=0)
            scores.append(dot(query, block[i, j * HD:(j + 1) * HD]))
            values.append(block[i, (n + j) * HD:(n + j + 1) * HD])
    score = jnp.concatenate(scores, axis=0) * SCALE
    score = jnp.where(lane < jnp.where(later, lives[1], lives[0]), score, LOW)
    top = jnp.max(score, axis=1, keepdims=True)
    terms = jnp.exp(score - top)
    total = jnp.sum(terms, axis=1, keepdims=True)
    high = terms.astype(jnp.bfloat16)
    low = (terms - high.astype(jnp.float32)).astype(jnp.bfloat16)
    mixed = jnp.concatenate(
        [
            dot(high[m * group:(m + 1) * group], v) + dot(low[m * group:(m + 1) * group], v)
            for m, v in enumerate(values)
        ],
        axis=0,
    ) / total
    sums = top + jnp.log(total)
    for k in range(KVH):
        for t in range(split):
            begins = [(2 * k + i) * group + t * width for i in range(2)]
            both = jnp.concatenate([sums[at:at + width] for at in begins], axis=0)
            turned = jnp.sum(jnp.where(spot == across, both, 0.0), axis=0, keepdims=True)
            first = turned.astype(jnp.bfloat16).astype(jnp.float32)
            rest = turned - first
            second = rest.astype(jnp.bfloat16).astype(jnp.float32)
            stat = jnp.where(line == 0, first, jnp.where(line == 1, second, rest - second))
            stat = jnp.where(line < 3, stat, 0.0)
            block = jnp.concatenate([mixed[at:at + width] for at in begins] + [stat], axis=0)
            o_ref[k * split + t] = block.astype(jnp.bfloat16)


def partial_decode(facts, query, packed, lanes):
    rows = 2 * (QH // lanes) * STEPS
    return pl.pallas_call(
        functools.partial(partial_kernel, lanes),
        out_shape=jax.ShapeDtypeStruct((lanes, rows + stat_rows(rows), HD), jnp.bfloat16),
        in_specs=[SMEM, VMEM] + [VMEM] * len(packed),
        out_specs=VMEM,
        name="partial_decode",
        **params(32),
    )(facts, query, *packed)


def merge_kernel(lanes, facts, parts_ref, q_ref, k_ref, v_ref, o_ref):
    requests = q_ref.shape[0]
    width = (QH // lanes) * STEPS
    other, place = 1 - lax.axis_index("section"), lax.axis_index("tp")
    head = place * (QH // lanes) // GROUP
    spot = lax.broadcasted_iota(jnp.int32, (width, PAGE), 0)
    across = lax.broadcasted_iota(jnp.int32, (width, PAGE), 1)
    step = lax.broadcasted_iota(jnp.int32, (width, 1), 0) % STEPS
    end = 0
    for r in range(requests):
        start, end = end, end + facts[other, r]
        query = q_ref[r].astype(jnp.float32)
        keys = k_ref[r, head].astype(jnp.float32)
        values = v_ref[r, head].astype(jnp.float32)
        tops, vectors = [], []
        for u in range(STEPS):
            score = jnp.sum(query * keys[u:u + 1], axis=1, keepdims=True) * SCALE
            tops.append(jnp.where(u <= step, score, LOW))
            vectors.append(values[u:u + 1])
        for j in range(MAXP):
            page = jnp.minimum(start + j, 2 * lanes - 1)
            block = parts_ref[page // 2].astype(jnp.float32)
            later = jnp.full((width, HD), page % 2 == 1)
            vectors.append(jnp.where(later, block[width:2 * width], block[:width]))
            stat = jnp.sum(block[2 * width:2 * width + 8], axis=0, keepdims=True)
            stat = jnp.sum(
                jnp.where(across - page % 2 * width == spot, stat, 0.0), axis=1, keepdims=True
            )
            tops.append(jnp.where(jnp.full((width, 1), start + j < end), stat, LOW))
        top = functools.reduce(jnp.maximum, tops)
        weights = [jnp.exp(t - top) for t in tops]
        total = functools.reduce(jnp.add, weights)
        mixed = functools.reduce(jnp.add, [w * x for w, x in zip(weights, vectors)])
        o_ref[r] = (mixed / total).astype(jnp.bfloat16)


def merged(facts, parts, query, new_key, new_value, lanes):
    requests = query.shape[0]
    fresh = [
        jnp.transpose(x.reshape(STEPS, requests, KVH, HD), (1, 2, 0, 3)) for x in (new_key, new_value)
    ]
    out = pl.pallas_call(
        functools.partial(merge_kernel, lanes),
        out_shape=jax.ShapeDtypeStruct(query.shape, jnp.bfloat16),
        in_specs=[SMEM, VMEM, VMEM, VMEM, VMEM],
        out_specs=VMEM,
        name="merge_decode",
        **params(32),
    )(facts, parts, query, *fresh)
    out = jnp.transpose(out.reshape(requests, QH // lanes, STEPS, HD), (2, 0, 1, 3))
    return out.reshape(STEPS, requests, QH // lanes * HD)


def other_half(x):
    return lax.ppermute(x, "section", [(0, 1), (1, 0)])


def after(x, *earlier):
    return lax.optimization_barrier((x, *earlier))[0]


def on_device(
    prefill_query, prefill_key, prefill_value, counts, fills, dec_query, dec_key, dec_value
):
    lanes = lax.axis_size("tp")
    query, key, value = prefill_query[0], prefill_key[0], prefill_value[0]
    facts = jnp.concatenate([counts, fills], axis=1)
    flags = page_flags(facts)
    ahead = [(i, i + 2) for i in range(lanes - 2)]
    ahead_again = [(i, i + 2) for i in range(2, lanes - 2)]
    beside = [(i, i + 1) for i in range(0, lanes, 2)]
    trade = [(i, i ^ 1) for i in range(2, lanes)]
    bases = [sum(CHUNKS[:g]) for g in range(len(CHUNKS))]
    mine = []
    for base, n in zip(bases, CHUNKS):
        mine.append(pack(base, n, after(key, *mine), value))

    first_hops = [lax.ppermute(block, "tp", ahead) for block in mine]

    asked = after(dec_query[0], mine[0])
    chosen, dec_rows = chosen_queries(facts, asked, lanes)
    wanted = lax.all_to_all(chosen, "tp", split_axis=0, concat_axis=0, tiled=True)
    parts = partial_decode(facts, other_half(wanted), mine, lanes)
    parts = lax.all_to_all(parts, "tp", split_axis=0, concat_axis=0, tiled=True)
    dec_out = merged(facts, other_half(parts), dec_rows, dec_key[0], dec_value[0], lanes)

    received = []
    for g, (block, a) in enumerate(zip(mine, first_hops)):
        b = lax.ppermute(after(block, received[0][2]) if g else block, "tp", beside)
        c = lax.ppermute(a if g else after(a, b), "tp", trade)
        d = jnp.concatenate([a[1:], c], axis=0)
        d = lax.ppermute(d if g else after(d, first_hops[1]), "tp", ahead_again)
        received.append((a, b, c, d))
    out, flags = None, after(flags, received[1][2], parts)
    for g, (base, n) in enumerate(zip(bases, CHUNKS)):
        if g:
            out = after(out, dec_out)
        out = prompt_heads(base, n, 0, n, flags, query, (mine[g], *received[g]), out)
    return (out[None], dec_out[None])


def solution(mesh):
    placed = (
        P("section", ("groups", "tp"), None),
        P("section", ("groups", "tp"), None),
        P("section", ("groups", "tp"), None),
        P(None, "groups"),
        P(None, "groups"),
        P("section", None, "groups", "tp"),
        P("section", None, "groups", None),
        P("section", None, "groups", None),
    )
    return jax.shard_map(
        on_device,
        mesh=mesh,
        in_specs=placed,
        out_specs=(P("section", ("groups", "tp"), None), P("section", None, "groups", "tp")),
        check_vma=False,
    )
```

```python
import functools
import math

import jax
import jax.numpy as jnp
from jax import lax
from jax.experimental import pallas as pl
from jax.experimental.pallas import tpu as pltpu
from jax.sharding import PartitionSpec as P

QH = 64
KVH = 8
HD = 128
PAGE = 128
MAXP = 8
STEPS = 4
GROUP = QH // KVH
SCALE = HD ** (-0.5)
EXP2_SCALE = SCALE * math.log2(math.e)
LOW = -1e30
CHUNKS = (4, 4)
ROWS = 512
SMEM = pl.BlockSpec(memory_space=pltpu.SMEM)
VMEM = pl.BlockSpec(memory_space=pltpu.VMEM)


def dot(a, b):
    return jnp.dot(a, b, preferred_element_type=jnp.float32)


def page_facts(facts, half, page):
    requests = facts.shape[1] // 2
    owner, first, live, end = -1, 0, PAGE, 0
    for r in range(requests):
        start, end = end, end + facts[half, r]
        begun = start <= page
        owner = jnp.where(begun, r, owner)
        first = jnp.where(begun, start, first)
        live = jnp.where(end - 1 == page, facts[half, requests + r], live)
    return owner, first, live


def params(limit):
    return dict(
        compiler_params=pltpu.CompilerParams(vmem_limit_bytes=limit << 20),
        cost_estimate=pl.CostEstimate(flops=1, bytes_accessed=1, transcendentals=0),
    )


def pack_kernel(base, k_ref, v_ref, *rest):
    o_ref, k_part, v_part, sems = rest[-4:]
    n = k_part.shape[1] // HD
    own = slice(base * HD, (base + n) * HD)
    copies = [
        pltpu.make_async_copy(source.at[:, own], part, sems.at[spot])
        for spot, (source, part) in enumerate(((k_ref, k_part), (v_ref, v_part)))
    ]
    for copy in copies:
        copy.start()
    for copy in copies:
        copy.wait()
    for j in range(n):
        columns = slice(j * HD, (j + 1) * HD)
        for p in range(2):
            rows = slice(p * PAGE, (p + 1) * PAGE)
            turned = jnp.transpose(k_part[rows, columns].astype(jnp.float32)).astype(jnp.bfloat16)
            o_ref[p, columns] = turned
            o_ref[p, (n + j) * HD:(n + j + 1) * HD] = v_part[rows, columns]


def pack(base, n, key, value):
    part = pltpu.VMEM((key.shape[0], n * HD), jnp.bfloat16)
    return pl.pallas_call(
        functools.partial(pack_kernel, base),
        out_shape=jax.ShapeDtypeStruct((2, 2 * n * HD, PAGE), jnp.bfloat16),
        in_specs=[pl.BlockSpec(memory_space=pl.ANY)] * 2,
        out_specs=VMEM,
        scratch_shapes=[part, part, pltpu.SemaphoreType.DMA((2,))],
        name="pack",
        **params(48),
    )(key, value)


def flags_kernel(facts, o_ref):
    half, place = lax.axis_index("section"), lax.axis_index("tp")
    even = place % 2 == 0
    near, far = 2 * place - 2, 2 * place - 6
    line = lax.broadcasted_iota(jnp.int32, o_ref.shape, 0)
    out = jnp.zeros(o_ref.shape, jnp.float32)
    for i in range(2):
        _, first, live = page_facts(facts, half, 2 * place + i)
        numbers = [2 * place - 7 if i == 0 else 2 * place, 2 * place + i]
        for page in (2 * place - 4, jnp.where(even, near, far), jnp.where(even, far, near)):
            numbers += [page, page + 1]
        for spot, number in enumerate(numbers):
            out = jnp.where(line == i * MAXP + spot, jnp.where(number >= first, 1.0, 0.0), out)
        out = jnp.where(line == 2 * MAXP + i, live.astype(jnp.float32), out)
    o_ref[...] = out


def page_flags(facts):
    return pl.pallas_call(
        flags_kernel,
        out_shape=jax.ShapeDtypeStruct((2 * MAXP + 8, PAGE), jnp.float32),
        in_specs=[SMEM],
        out_specs=VMEM,
        name="page_flags",
        **params(48),
    )(facts)


def prompt_kernel(n, low, flags, q_ref, *rest):
    o_ref, keys, values, causal, *probs = rest[-6:]
    head = low + pl.program_id(0)
    spots = [pl.ds(pl.multiple_of((x + head) * HD, HD), HD) for x in (0, n)]
    mine, a, b, c, d = [[[x[p, at] for at in spots] for p in range(x.shape[0])] for x in rest[:5]]
    choose = jnp.full((HD, PAGE), lax.axis_index("tp") % 2 == 0)
    be = [[jnp.where(choose, x, y) for x, y in zip(d[1 + p], b[p])] for p in range(2)]
    row = lax.broadcasted_iota(jnp.int32, (PAGE, PAGE), 0)
    col = lax.broadcasted_iota(jnp.int32, (PAGE, PAGE), 1)
    causal[...] = jnp.where(col <= row, 0.0, LOW)
    one = jnp.ones((PAGE, HD), jnp.bfloat16)
    zero = jnp.zeros((PAGE, HD), jnp.bfloat16)
    lives = [flags[2 * MAXP + i:2 * MAXP + i + 1, :] for i in range(2)]

    for i in range(2):
        stand_in = jnp.broadcast_to(mine[i][0][:, :1], (HD, PAGE))
        pages = [d[0] if i == 0 else mine[0], mine[i], *a, *c, *be]
        for spot, (k, v) in enumerate(pages):
            line = i * MAXP + spot
            seen = jnp.broadcast_to(flags[line:line + 1, :], (PAGE, HD)) > 0.0
            at = slice(spot * PAGE, (spot + 1) * PAGE)
            k = jnp.where(seen, k, stand_in)
            keys[i, :HD, at] = k
            keys[i, HD:, at] = k
            values[i, at, :HD] = jnp.where(seen, v, zero)
            values[i, at, HD:] = jnp.where(seen, one, zero)

    heads_at_once = ROWS // PAGE
    blocks = [(i, start) for i in range(2) for start in range(0, GROUP, heads_at_once)]

    def halves(query):
        query = query.astype(jnp.float32) * EXP2_SCALE
        high = query.astype(jnp.bfloat16)
        low = (query - high.astype(jnp.float32)).astype(jnp.bfloat16)
        return jnp.concatenate([high, low], axis=1)

    def queries(i, start):
        return halves(
            jnp.concatenate(
                [
                    q_ref[i * PAGE:(i + 1) * PAGE, h * HD:(h + 1) * HD]
                    for h in range(start, start + heads_at_once)
                ],
                axis=0,
            )
        )

    def divided(mixed, live):
        total = mixed[:, HD:]
        near = pl.reciprocal(total, approx=True)
        near = near * (2.0 - total * near)
        token = lax.broadcasted_iota(jnp.int32, (total.shape[0], HD), 0) % PAGE
        return jnp.where(token.astype(jnp.float32) < live, mixed[:, :HD] * near, 0.0).astype(jnp.bfloat16)

    tiles = [slice(t, t + 2 * PAGE) for t in range(0, MAXP * PAGE, 2 * PAGE)]

    def own_scores(query, i, repeat):
        own = dot(query, keys[i, :, tiles[0]])
        bias = jnp.concatenate([causal[...]] * repeat, axis=0)
        return jnp.concatenate([own[:, :PAGE], own[:, PAGE:] + bias], axis=1)

    def mix(block, slot, largest):
        i, start = block
        mixed = dot(probs[slot][...], values[i])
        out = divided(mixed, lives[i])
        for number in range(heads_at_once):
            h = start + number
            o_ref[i * PAGE:(i + 1) * PAGE, h * HD:(h + 1) * HD] = out[number * PAGE:(number + 1) * PAGE]
        return jnp.maximum(largest, mixed[:, HD:])

    largest = jnp.zeros((ROWS, HD), jnp.float32)
    for index in range(len(blocks) + 1):
        if index < len(blocks):
            i, slot = blocks[index][0], index % 2
            query = queries(*blocks[index])
            own = own_scores(query, i, heads_at_once)
            top = jnp.max(own, axis=1, keepdims=True)
            probs[slot][:, tiles[0]] = jnp.exp2(own - top).astype(jnp.bfloat16)
        if index > 0:
            largest = mix(blocks[index - 1], 1 - slot if index < len(blocks) else slot, largest)
        if index < len(blocks):
            for at in tiles[1:]:
                other = dot(query, keys[i, :, at])
                probs[slot][:, at] = jnp.exp2(other - top).astype(jnp.bfloat16)

    @pl.when(jnp.logical_not(jnp.max(largest) < 1e30))
    def _():
        def one(index, carry):
            i, h = index // GROUP, index % GROUP
            rows = pl.ds(pl.multiple_of(i * PAGE, PAGE), PAGE)
            columns = pl.ds(pl.multiple_of(h * HD, HD), HD)
            query = halves(q_ref[rows, columns])
            scores = [own_scores(query, i, 1)] + [dot(query, keys[i, :, at]) for at in tiles[1:]]
            top = jnp.max(functools.reduce(jnp.maximum, scores), axis=1, keepdims=True)
            mixed = jnp.zeros((PAGE, 2 * HD), jnp.float32)
            for score, at in zip(scores, tiles):
                mixed = mixed + dot(jnp.exp2(score - top).astype(jnp.bfloat16), values[i, at])
            o_ref[rows, columns] = divided(mixed, jnp.where(i == 0, lives[0], lives[1]))
            return carry

        lax.fori_loop(0, 2 * GROUP, one, 0)


def prompt_heads(base, n, low, high, flags, query, blocks, done):
    tok = query.shape[0]

    wide = pl.BlockSpec((tok, GROUP * HD), lambda j: (0, base + low + j))
    operands = [flags, query, *blocks]
    specs = [VMEM, wide] + [VMEM] * len(blocks)
    aliases = {}
    if done is not None:
        aliases = {len(operands): 0}
        operands.append(done)
        specs.append(pl.BlockSpec(memory_space=pl.ANY))
    return pl.pallas_call(
        functools.partial(prompt_kernel, n, low),
        out_shape=jax.ShapeDtypeStruct(query.shape, jnp.bfloat16),
        grid=(high - low,),
        in_specs=specs,
        out_specs=wide,
        scratch_shapes=[
            pltpu.VMEM((2, 2 * HD, MAXP * PAGE), jnp.bfloat16),
            pltpu.VMEM((2, MAXP * PAGE, 2 * HD), jnp.bfloat16),
            pltpu.VMEM((PAGE, PAGE), jnp.float32),
            pltpu.VMEM((ROWS, MAXP * PAGE), jnp.bfloat16),
            pltpu.VMEM((ROWS, MAXP * PAGE), jnp.bfloat16),
        ],
        input_output_aliases=aliases,
        name="prompt_attention",
        compiler_params=pltpu.CompilerParams(vmem_limit_bytes=48 << 20),
        cost_estimate=pl.CostEstimate(
            flops=(high - low) * GROUP * tok * MAXP * PAGE * HD * 8,
            bytes_accessed=4 * (high - low) * tok * GROUP * HD,
            transcendentals=0,
        ),
    )(*operands)


def stat_rows(rows):
    return 16 - rows % 16


def choose_kernel(facts, q_ref, o_ref, rows_ref, turned):
    requests, here = q_ref.shape[1], q_ref.shape[2] // HD
    other = 1 - lax.axis_index("section")
    for s in range(STEPS):
        query = q_ref[s].astype(jnp.float32)
        for r in range(requests):
            for h in range(here):
                row = h * STEPS + s
                turned[r, row:row + 1] = query[r:r + 1, h * HD:(h + 1) * HD]
    rows_ref[...] = turned[...].astype(jnp.bfloat16)

    def one(lane, carry):
        for i in range(2):
            owner = page_facts(facts, other, 2 * lane + i)[0]
            o_ref[lane, i] = turned[owner].astype(jnp.bfloat16)
        return carry

    lax.fori_loop(0, o_ref.shape[0], one, 0)


def chosen_queries(facts, query, lanes):
    rows = (query.shape[1], QH // lanes * STEPS, HD)
    return pl.pallas_call(
        choose_kernel,
        out_shape=(
            jax.ShapeDtypeStruct((lanes, 2, *rows[1:]), jnp.bfloat16),
            jax.ShapeDtypeStruct(rows, jnp.bfloat16),
        ),
        in_specs=[SMEM, VMEM],
        out_specs=(VMEM, VMEM),
        scratch_shapes=[pltpu.VMEM(rows, jnp.float32)],
        name="choose_queries",
        **params(32),
    )(facts, query)


def partial_kernel(lanes, facts, q_ref, *rest):
    *packed, o_ref = rest
    split = GROUP // (QH // lanes)
    width = QH // lanes * STEPS
    extra = stat_rows(2 * width)
    half, place = lax.axis_index("section"), lax.axis_index("tp")
    group = GROUP * STEPS
    height = 2 * KVH * group
    lane = lax.broadcasted_iota(jnp.int32, (height, PAGE), 1)
    later = lax.broadcasted_iota(jnp.int32, (height, PAGE), 0) // group % 2 == 1
    spot = lax.broadcasted_iota(jnp.int32, (2 * width, PAGE), 0)
    across = lax.broadcasted_iota(jnp.int32, (2 * width, PAGE), 1)
    line = lax.broadcasted_iota(jnp.int32, (extra, PAGE), 0)
    lives = [page_facts(facts, half, 2 * place + i)[2] for i in range(2)]
    places = [(block, j, n) for block, n in zip(packed, CHUNKS) for j in range(n)]
    scores, values = [], []
    for k, (block, j, n) in enumerate(places):
        for i in range(2):
            query = jnp.concatenate([q_ref[k * split + t, i] for t in range(split)], axis=0)
            scores.append(dot(query, block[i, j * HD:(j + 1) * HD]))
            values.append(block[i, (n + j) * HD:(n + j + 1) * HD])
    score = jnp.concatenate(scores, axis=0) * SCALE
    score = jnp.where(lane < jnp.where(later, lives[1], lives[0]), score, LOW)
    top = jnp.max(score, axis=1, keepdims=True)
    terms = jnp.exp(score - top)
    total = jnp.sum(terms, axis=1, keepdims=True)
    high = terms.astype(jnp.bfloat16)
    low = (terms - high.astype(jnp.float32)).astype(jnp.bfloat16)
    mixed = jnp.concatenate(
        [
            dot(high[m * group:(m + 1) * group], v) + dot(low[m * group:(m + 1) * group], v)
            for m, v in enumerate(values)
        ],
        axis=0,
    ) / total
    sums = top + jnp.log(total)
    for k in range(KVH):
        for t in range(split):
            begins = [(2 * k + i) * group + t * width for i in range(2)]
            both = jnp.concatenate([sums[at:at + width] for at in begins], axis=0)
            turned = jnp.sum(jnp.where(spot == across, both, 0.0), axis=0, keepdims=True)
            first = turned.astype(jnp.bfloat16).astype(jnp.float32)
            rest = turned - first
            second = rest.astype(jnp.bfloat16).astype(jnp.float32)
            stat = jnp.where(line == 0, first, jnp.where(line == 1, second, rest - second))
            stat = jnp.where(line < 3, stat, 0.0)
            block = jnp.concatenate([mixed[at:at + width] for at in begins] + [stat], axis=0)
            o_ref[k * split + t] = block.astype(jnp.bfloat16)


def partial_decode(facts, query, packed, lanes):
    rows = 2 * (QH // lanes) * STEPS
    return pl.pallas_call(
        functools.partial(partial_kernel, lanes),
        out_shape=jax.ShapeDtypeStruct((lanes, rows + stat_rows(rows), HD), jnp.bfloat16),
        in_specs=[SMEM, VMEM] + [VMEM] * len(packed),
        out_specs=VMEM,
        name="partial_decode",
        **params(32),
    )(facts, query, *packed)


def merge_kernel(lanes, facts, parts_ref, q_ref, k_ref, v_ref, o_ref):
    requests = q_ref.shape[0]
    width = (QH // lanes) * STEPS
    other, place = 1 - lax.axis_index("section"), lax.axis_index("tp")
    head = place * (QH // lanes) // GROUP
    spot = lax.broadcasted_iota(jnp.int32, (width, PAGE), 0)
    across = lax.broadcasted_iota(jnp.int32, (width, PAGE), 1)
    step = lax.broadcasted_iota(jnp.int32, (width, 1), 0) % STEPS
    end = 0
    for r in range(requests):
        start, end = end, end + facts[other, r]
        query = q_ref[r].astype(jnp.float32)
        keys = k_ref[r, head].astype(jnp.float32)
        values = v_ref[r, head].astype(jnp.float32)
        tops, vectors = [], []
        for u in range(STEPS):
            score = jnp.sum(query * keys[u:u + 1], axis=1, keepdims=True) * SCALE
            tops.append(jnp.where(u <= step, score, LOW))
            vectors.append(values[u:u + 1])
        for j in range(MAXP):
            page = jnp.minimum(start + j, 2 * lanes - 1)
            block = parts_ref[page // 2].astype(jnp.float32)
            later = jnp.full((width, HD), page % 2 == 1)
            vectors.append(jnp.where(later, block[width:2 * width], block[:width]))
            stat = jnp.sum(block[2 * width:2 * width + 8], axis=0, keepdims=True)
            stat = jnp.sum(
                jnp.where(across - page % 2 * width == spot, stat, 0.0), axis=1, keepdims=True
            )
            tops.append(jnp.where(jnp.full((width, 1), start + j < end), stat, LOW))
        top = functools.reduce(jnp.maximum, tops)
        weights = [jnp.exp(t - top) for t in tops]
        total = functools.reduce(jnp.add, weights)
        mixed = functools.reduce(jnp.add, [w * x for w, x in zip(weights, vectors)])
        o_ref[r] = (mixed / total).astype(jnp.bfloat16)


def merged(facts, parts, query, new_key, new_value, lanes):
    requests = query.shape[0]
    fresh = [
        jnp.transpose(x.reshape(STEPS, requests, KVH, HD), (1, 2, 0, 3)) for x in (new_key, new_value)
    ]
    out = pl.pallas_call(
        functools.partial(merge_kernel, lanes),
        out_shape=jax.ShapeDtypeStruct(query.shape, jnp.bfloat16),
        in_specs=[SMEM, VMEM, VMEM, VMEM, VMEM],
        out_specs=VMEM,
        name="merge_decode",
        **params(32),
    )(facts, parts, query, *fresh)
    out = jnp.transpose(out.reshape(requests, QH // lanes, STEPS, HD), (2, 0, 1, 3))
    return out.reshape(STEPS, requests, QH // lanes * HD)


def other_half(x):
    return lax.ppermute(x, "section", [(0, 1), (1, 0)])


def after(x, *earlier):
    return lax.optimization_barrier((x, *earlier))[0]


def on_device(
    prefill_query, prefill_key, prefill_value, counts, fills, dec_query, dec_key, dec_value
):
    lanes = lax.axis_size("tp")
    query, key, value = prefill_query[0], prefill_key[0], prefill_value[0]
    facts = jnp.concatenate([counts, fills], axis=1)
    flags = page_flags(facts)
    ahead = [(i, i + 2) for i in range(lanes - 2)]
    ahead_again = [(i, i + 2) for i in range(2, lanes - 2)]
    beside = [(i, i + 1) for i in range(0, lanes, 2)]
    trade = [(i, i ^ 1) for i in range(2, lanes)]
    bases = [sum(CHUNKS[:g]) for g in range(len(CHUNKS))]
    mine = []
    for base, n in zip(bases, CHUNKS):
        mine.append(pack(base, n, after(key, *mine), value))

    first_hops = [lax.ppermute(block, "tp", ahead) for block in mine]

    asked = after(dec_query[0], mine[0])
    chosen, dec_rows = chosen_queries(facts, asked, lanes)
    wanted = lax.all_to_all(chosen, "tp", split_axis=0, concat_axis=0, tiled=True)
    b = lax.ppermute(mine[0], "tp", beside)
    parts = partial_decode(facts, other_half(after(wanted, b)), mine, lanes)
    parts = lax.all_to_all(parts, "tp", split_axis=0, concat_axis=0, tiled=True)
    dec_out = merged(facts, other_half(parts), dec_rows, dec_key[0], dec_value[0], lanes)

    received = []
    for g, (block, a) in enumerate(zip(mine, first_hops)):
        if g:
            b = lax.ppermute(after(block, received[0][2]), "tp", beside)
        c = lax.ppermute(a if g else after(a, wanted, mine[1]), "tp", trade)
        d = jnp.concatenate([a[1:], c], axis=0)
        d = lax.ppermute(d if g else after(d, first_hops[1], parts), "tp", ahead_again)
        received.append((a, b, c, d))
    out = None
    for g, (base, n) in enumerate(zip(bases, CHUNKS)):
        if g:
            out = after(out, dec_out)
        out = prompt_heads(base, n, 0, n, flags, query, (mine[g], *received[g]), out)
    return (out[None], dec_out[None])


def solution(mesh):
    placed = (
        P("section", ("groups", "tp"), None),
        P("section", ("groups", "tp"), None),
        P("section", ("groups", "tp"), None),
        P(None, "groups"),
        P(None, "groups"),
        P("section", None, "groups", "tp"),
        P("section", None, "groups", None),
        P("section", None, "groups", None),
    )
    return jax.shard_map(
        on_device,
        mesh=mesh,
        in_specs=placed,
        out_specs=(P("section", ("groups", "tp"), None), P("section", None, "groups", "tp")),
        check_vma=False,
    )
```

```python
import functools
import math

import jax
import jax.numpy as jnp
from jax import lax
from jax.experimental import pallas as pl
from jax.experimental.pallas import tpu as pltpu
from jax.sharding import PartitionSpec as P

QH = 64
KVH = 8
HD = 128
PAGE = 128
MAXP = 8
STEPS = 4
GROUP = QH // KVH
SCALE = HD ** (-0.5)
EXP2_SCALE = SCALE * math.log2(math.e)
LOW = -1e30
CHUNKS = (4, 4)
ROWS = 512
SMEM = pl.BlockSpec(memory_space=pltpu.SMEM)
VMEM = pl.BlockSpec(memory_space=pltpu.VMEM)


def dot(a, b):
    return jnp.dot(a, b, preferred_element_type=jnp.float32)


def page_facts(facts, half, page):
    requests = facts.shape[1] // 2
    owner, first, live, end = -1, 0, PAGE, 0
    for r in range(requests):
        start, end = end, end + facts[half, r]
        begun = start <= page
        owner = jnp.where(begun, r, owner)
        first = jnp.where(begun, start, first)
        live = jnp.where(end - 1 == page, facts[half, requests + r], live)
    return owner, first, live


def params(limit):
    return dict(
        compiler_params=pltpu.CompilerParams(vmem_limit_bytes=limit << 20),
        cost_estimate=pl.CostEstimate(flops=1, bytes_accessed=1, transcendentals=0),
    )


def pack_kernel(base, k_ref, v_ref, *rest):
    o_ref, k_part, v_part, sems = rest[-4:]
    n = k_part.shape[1] // HD
    own = slice(base * HD, (base + n) * HD)
    copies = [
        pltpu.make_async_copy(source.at[:, own], part, sems.at[spot])
        for spot, (source, part) in enumerate(((k_ref, k_part), (v_ref, v_part)))
    ]
    for copy in copies:
        copy.start()
    for copy in copies:
        copy.wait()
    for j in range(n):
        columns = slice(j * HD, (j + 1) * HD)
        for p in range(2):
            rows = slice(p * PAGE, (p + 1) * PAGE)
            turned = jnp.transpose(k_part[rows, columns].astype(jnp.float32)).astype(jnp.bfloat16)
            o_ref[p, columns] = turned
            o_ref[p, (n + j) * HD:(n + j + 1) * HD] = v_part[rows, columns]


def pack(base, n, key, value):
    part = pltpu.VMEM((key.shape[0], n * HD), jnp.bfloat16)
    return pl.pallas_call(
        functools.partial(pack_kernel, base),
        out_shape=jax.ShapeDtypeStruct((2, 2 * n * HD, PAGE), jnp.bfloat16),
        in_specs=[pl.BlockSpec(memory_space=pl.ANY)] * 2,
        out_specs=VMEM,
        scratch_shapes=[part, part, pltpu.SemaphoreType.DMA((2,))],
        name="pack",
        **params(48),
    )(key, value)


def flags_kernel(facts, o_ref):
    half, place = lax.axis_index("section"), lax.axis_index("tp")
    even = place % 2 == 0
    near, far = 2 * place - 2, 2 * place - 6
    line = lax.broadcasted_iota(jnp.int32, o_ref.shape, 0)
    out = jnp.zeros(o_ref.shape, jnp.float32)
    for i in range(2):
        _, first, live = page_facts(facts, half, 2 * place + i)
        numbers = [2 * place - 7 if i == 0 else 2 * place, 2 * place + i]
        for page in (2 * place - 4, jnp.where(even, near, far), jnp.where(even, far, near)):
            numbers += [page, page + 1]
        for spot, number in enumerate(numbers):
            out = jnp.where(line == i * MAXP + spot, jnp.where(number >= first, 1.0, 0.0), out)
        out = jnp.where(line == 2 * MAXP + i, live.astype(jnp.float32), out)
    o_ref[...] = out


def page_flags(facts):
    return pl.pallas_call(
        flags_kernel,
        out_shape=jax.ShapeDtypeStruct((2 * MAXP + 8, PAGE), jnp.float32),
        in_specs=[SMEM],
        out_specs=VMEM,
        name="page_flags",
        **params(48),
    )(facts)


def prompt_kernel(n, low, flags, q_ref, *rest):
    o_ref, keys, values, causal, *probs = rest[-6:]
    head = low + pl.program_id(0)
    spots = [pl.ds(pl.multiple_of((x + head) * HD, HD), HD) for x in (0, n)]
    mine, a, b, c, d = [[[x[p, at] for at in spots] for p in range(x.shape[0])] for x in rest[:5]]
    choose = jnp.full((HD, PAGE), lax.axis_index("tp") % 2 == 0)
    be = [[jnp.where(choose, x, y) for x, y in zip(d[1 + p], b[p])] for p in range(2)]
    row = lax.broadcasted_iota(jnp.int32, (PAGE, PAGE), 0)
    col = lax.broadcasted_iota(jnp.int32, (PAGE, PAGE), 1)
    causal[...] = jnp.where(col <= row, 0.0, LOW)
    one = jnp.ones((PAGE, HD), jnp.bfloat16)
    zero = jnp.zeros((PAGE, HD), jnp.bfloat16)
    lives = [flags[2 * MAXP + i:2 * MAXP + i + 1, :] for i in range(2)]

    for i in range(2):
        stand_in = jnp.broadcast_to(mine[i][0][:, :1], (HD, PAGE))
        pages = [d[0] if i == 0 else mine[0], mine[i], *a, *c, *be]
        for spot, (k, v) in enumerate(pages):
            line = i * MAXP + spot
            seen = jnp.broadcast_to(flags[line:line + 1, :], (PAGE, HD)) > 0.0
            at = slice(spot * PAGE, (spot + 1) * PAGE)
            k = jnp.where(seen, k, stand_in)
            keys[i, :HD, at] = k
            keys[i, HD:, at] = k
            values[i, at, :HD] = jnp.where(seen, v, zero)
            values[i, at, HD:] = jnp.where(seen, one, zero)

    heads_at_once = ROWS // PAGE
    blocks = [(i, start) for i in range(2) for start in range(0, GROUP, heads_at_once)]

    def halves(query):
        query = query.astype(jnp.float32) * EXP2_SCALE
        high = query.astype(jnp.bfloat16)
        low = (query - high.astype(jnp.float32)).astype(jnp.bfloat16)
        return jnp.concatenate([high, low], axis=1)

    def queries(i, start):
        return halves(
            jnp.concatenate(
                [
                    q_ref[i * PAGE:(i + 1) * PAGE, h * HD:(h + 1) * HD]
                    for h in range(start, start + heads_at_once)
                ],
                axis=0,
            )
        )

    def divided(mixed, live):
        total = mixed[:, HD:]
        near = pl.reciprocal(total, approx=True)
        near = near * (2.0 - total * near)
        token = lax.broadcasted_iota(jnp.int32, (total.shape[0], HD), 0) % PAGE
        return jnp.where(token.astype(jnp.float32) < live, mixed[:, :HD] * near, 0.0).astype(jnp.bfloat16)

    tiles = [slice(t, t + 2 * PAGE) for t in range(0, MAXP * PAGE, 2 * PAGE)]

    def own_scores(query, i, repeat):
        own = dot(query, keys[i, :, tiles[0]])
        bias = jnp.concatenate([causal[...]] * repeat, axis=0)
        return jnp.concatenate([own[:, :PAGE], own[:, PAGE:] + bias], axis=1)

    def mix(block, slot, largest):
        i, start = block
        mixed = dot(probs[slot][...], values[i])
        out = divided(mixed, lives[i])
        for number in range(heads_at_once):
            h = start + number
            o_ref[i * PAGE:(i + 1) * PAGE, h * HD:(h + 1) * HD] = out[number * PAGE:(number + 1) * PAGE]
        return jnp.maximum(largest, mixed[:, HD:])

    largest = jnp.zeros((ROWS, HD), jnp.float32)
    for index in range(len(blocks) + 1):
        if index < len(blocks):
            i, slot = blocks[index][0], index % 2
            query = queries(*blocks[index])
            own = own_scores(query, i, heads_at_once)
            top = jnp.max(own, axis=1, keepdims=True)
            probs[slot][:, tiles[0]] = jnp.exp2(own - top).astype(jnp.bfloat16)
        if index > 0:
            largest = mix(blocks[index - 1], 1 - slot if index < len(blocks) else slot, largest)
        if index < len(blocks):
            for at in tiles[1:]:
                other = dot(query, keys[i, :, at])
                probs[slot][:, at] = jnp.exp2(other - top).astype(jnp.bfloat16)

    @pl.when(jnp.logical_not(jnp.max(largest) < 1e30))
    def _():
        def one(index, carry):
            i, h = index // GROUP, index % GROUP
            rows = pl.ds(pl.multiple_of(i * PAGE, PAGE), PAGE)
            columns = pl.ds(pl.multiple_of(h * HD, HD), HD)
            query = halves(q_ref[rows, columns])
            scores = [own_scores(query, i, 1)] + [dot(query, keys[i, :, at]) for at in tiles[1:]]
            top = jnp.max(functools.reduce(jnp.maximum, scores), axis=1, keepdims=True)
            mixed = jnp.zeros((PAGE, 2 * HD), jnp.float32)
            for score, at in zip(scores, tiles):
                mixed = mixed + dot(jnp.exp2(score - top).astype(jnp.bfloat16), values[i, at])
            o_ref[rows, columns] = divided(mixed, jnp.where(i == 0, lives[0], lives[1]))
            return carry

        lax.fori_loop(0, 2 * GROUP, one, 0)


def prompt_heads(base, n, low, high, flags, query, blocks, done):
    tok = query.shape[0]

    wide = pl.BlockSpec((tok, GROUP * HD), lambda j: (0, base + low + j))
    operands = [flags, query, *blocks]
    specs = [VMEM, wide] + [VMEM] * len(blocks)
    aliases = {}
    if done is not None:
        aliases = {len(operands): 0}
        operands.append(done)
        specs.append(pl.BlockSpec(memory_space=pl.ANY))
    return pl.pallas_call(
        functools.partial(prompt_kernel, n, low),
        out_shape=jax.ShapeDtypeStruct(query.shape, jnp.bfloat16),
        grid=(high - low,),
        in_specs=specs,
        out_specs=wide,
        scratch_shapes=[
            pltpu.VMEM((2, 2 * HD, MAXP * PAGE), jnp.bfloat16),
            pltpu.VMEM((2, MAXP * PAGE, 2 * HD), jnp.bfloat16),
            pltpu.VMEM((PAGE, PAGE), jnp.float32),
            pltpu.VMEM((ROWS, MAXP * PAGE), jnp.bfloat16),
            pltpu.VMEM((ROWS, MAXP * PAGE), jnp.bfloat16),
        ],
        input_output_aliases=aliases,
        name="prompt_attention",
        compiler_params=pltpu.CompilerParams(vmem_limit_bytes=48 << 20),
        cost_estimate=pl.CostEstimate(
            flops=(high - low) * GROUP * tok * MAXP * PAGE * HD * 8,
            bytes_accessed=4 * (high - low) * tok * GROUP * HD,
            transcendentals=0,
        ),
    )(*operands)


def stat_rows(rows):
    return 16 - rows % 16


def choose_kernel(facts, q_ref, o_ref, rows_ref, turned):
    requests, here = q_ref.shape[1], q_ref.shape[2] // HD
    other = 1 - lax.axis_index("section")
    for s in range(STEPS):
        query = q_ref[s].astype(jnp.float32)
        for r in range(requests):
            for h in range(here):
                row = h * STEPS + s
                turned[r, row:row + 1] = query[r:r + 1, h * HD:(h + 1) * HD]
    rows_ref[...] = turned[...].astype(jnp.bfloat16)

    def one(lane, carry):
        for i in range(2):
            owner = page_facts(facts, other, 2 * lane + i)[0]
            o_ref[lane, i] = turned[owner].astype(jnp.bfloat16)
        return carry

    lax.fori_loop(0, o_ref.shape[0], one, 0)


def chosen_queries(facts, query, lanes):
    rows = (query.shape[1], QH // lanes * STEPS, HD)
    return pl.pallas_call(
        choose_kernel,
        out_shape=(
            jax.ShapeDtypeStruct((lanes, 2, *rows[1:]), jnp.bfloat16),
            jax.ShapeDtypeStruct(rows, jnp.bfloat16),
        ),
        in_specs=[SMEM, VMEM],
        out_specs=(VMEM, VMEM),
        scratch_shapes=[pltpu.VMEM(rows, jnp.float32)],
        name="choose_queries",
        **params(32),
    )(facts, query)


def partial_kernel(lanes, facts, q_ref, *rest):
    *packed, o_ref = rest
    split = GROUP // (QH // lanes)
    width = QH // lanes * STEPS
    extra = stat_rows(2 * width)
    half, place = lax.axis_index("section"), lax.axis_index("tp")
    group = GROUP * STEPS
    height = 2 * KVH * group
    lane = lax.broadcasted_iota(jnp.int32, (height, PAGE), 1)
    later = lax.broadcasted_iota(jnp.int32, (height, PAGE), 0) // group % 2 == 1
    spot = lax.broadcasted_iota(jnp.int32, (2 * width, PAGE), 0)
    across = lax.broadcasted_iota(jnp.int32, (2 * width, PAGE), 1)
    line = lax.broadcasted_iota(jnp.int32, (extra, PAGE), 0)
    lives = [page_facts(facts, half, 2 * place + i)[2] for i in range(2)]
    places = [(block, j, n) for block, n in zip(packed, CHUNKS) for j in range(n)]
    scores, values = [], []
    for k, (block, j, n) in enumerate(places):
        for i in range(2):
            query = jnp.concatenate([q_ref[k * split + t, i] for t in range(split)], axis=0)
            scores.append(dot(query, block[i, j * HD:(j + 1) * HD]))
            values.append(block[i, (n + j) * HD:(n + j + 1) * HD])
    score = jnp.concatenate(scores, axis=0) * SCALE
    score = jnp.where(lane < jnp.where(later, lives[1], lives[0]), score, LOW)
    top = jnp.max(score, axis=1, keepdims=True)
    terms = jnp.exp(score - top)
    total = jnp.sum(terms, axis=1, keepdims=True)
    high = terms.astype(jnp.bfloat16)
    low = (terms - high.astype(jnp.float32)).astype(jnp.bfloat16)
    mixed = jnp.concatenate(
        [
            dot(high[m * group:(m + 1) * group], v) + dot(low[m * group:(m + 1) * group], v)
            for m, v in enumerate(values)
        ],
        axis=0,
    ) / total
    sums = top + jnp.log(total)
    for k in range(KVH):
        for t in range(split):
            begins = [(2 * k + i) * group + t * width for i in range(2)]
            both = jnp.concatenate([sums[at:at + width] for at in begins], axis=0)
            turned = jnp.sum(jnp.where(spot == across, both, 0.0), axis=0, keepdims=True)
            first = turned.astype(jnp.bfloat16).astype(jnp.float32)
            rest = turned - first
            second = rest.astype(jnp.bfloat16).astype(jnp.float32)
            stat = jnp.where(line == 0, first, jnp.where(line == 1, second, rest - second))
            stat = jnp.where(line < 3, stat, 0.0)
            block = jnp.concatenate([mixed[at:at + width] for at in begins] + [stat], axis=0)
            o_ref[k * split + t] = block.astype(jnp.bfloat16)


def partial_decode(facts, query, packed, lanes):
    rows = 2 * (QH // lanes) * STEPS
    return pl.pallas_call(
        functools.partial(partial_kernel, lanes),
        out_shape=jax.ShapeDtypeStruct((lanes, rows + stat_rows(rows), HD), jnp.bfloat16),
        in_specs=[SMEM, VMEM] + [VMEM] * len(packed),
        out_specs=VMEM,
        name="partial_decode",
        **params(32),
    )(facts, query, *packed)


def merge_kernel(lanes, facts, parts_ref, q_ref, k_ref, v_ref, o_ref):
    requests = q_ref.shape[0]
    width = (QH // lanes) * STEPS
    other, place = 1 - lax.axis_index("section"), lax.axis_index("tp")
    head = place * (QH // lanes) // GROUP
    spot = lax.broadcasted_iota(jnp.int32, (width, PAGE), 0)
    across = lax.broadcasted_iota(jnp.int32, (width, PAGE), 1)
    step = lax.broadcasted_iota(jnp.int32, (width, 1), 0) % STEPS
    end = 0
    for r in range(requests):
        start, end = end, end + facts[other, r]
        query = q_ref[r].astype(jnp.float32)
        keys = k_ref[r, head].astype(jnp.float32)
        values = v_ref[r, head].astype(jnp.float32)
        tops, vectors = [], []
        for u in range(STEPS):
            score = jnp.sum(query * keys[u:u + 1], axis=1, keepdims=True) * SCALE
            tops.append(jnp.where(u <= step, score, LOW))
            vectors.append(values[u:u + 1])
        for j in range(MAXP):
            page = jnp.minimum(start + j, 2 * lanes - 1)
            block = parts_ref[page // 2].astype(jnp.float32)
            later = jnp.full((width, HD), page % 2 == 1)
            vectors.append(jnp.where(later, block[width:2 * width], block[:width]))
            stat = jnp.sum(block[2 * width:2 * width + 8], axis=0, keepdims=True)
            stat = jnp.sum(
                jnp.where(across - page % 2 * width == spot, stat, 0.0), axis=1, keepdims=True
            )
            tops.append(jnp.where(jnp.full((width, 1), start + j < end), stat, LOW))
        top = functools.reduce(jnp.maximum, tops)
        weights = [jnp.exp(t - top) for t in tops]
        total = functools.reduce(jnp.add, weights)
        mixed = functools.reduce(jnp.add, [w * x for w, x in zip(weights, vectors)])
        o_ref[r] = (mixed / total).astype(jnp.bfloat16)


def merged(facts, parts, query, new_key, new_value, lanes):
    requests = query.shape[0]
    fresh = [
        jnp.transpose(x.reshape(STEPS, requests, KVH, HD), (1, 2, 0, 3)) for x in (new_key, new_value)
    ]
    out = pl.pallas_call(
        functools.partial(merge_kernel, lanes),
        out_shape=jax.ShapeDtypeStruct(query.shape, jnp.bfloat16),
        in_specs=[SMEM, VMEM, VMEM, VMEM, VMEM],
        out_specs=VMEM,
        name="merge_decode",
        **params(32),
    )(facts, parts, query, *fresh)
    out = jnp.transpose(out.reshape(requests, QH // lanes, STEPS, HD), (2, 0, 1, 3))
    return out.reshape(STEPS, requests, QH // lanes * HD)


def other_half(x):
    return lax.ppermute(x, "section", [(0, 1), (1, 0)])


def after(x, *earlier):
    return lax.optimization_barrier((x, *earlier))[0]


def on_device(
    prefill_query, prefill_key, prefill_value, counts, fills, dec_query, dec_key, dec_value
):
    lanes = lax.axis_size("tp")
    query, key, value = prefill_query[0], prefill_key[0], prefill_value[0]
    facts = jnp.concatenate([counts, fills], axis=1)
    flags = page_flags(facts)
    ahead = [(i, i + 2) for i in range(lanes - 2)]
    ahead_again = [(i, i + 2) for i in range(2, lanes - 2)]
    beside = [(i, i + 1) for i in range(0, lanes, 2)]
    trade = [(i, i ^ 1) for i in range(2, lanes)]
    bases = [sum(CHUNKS[:g]) for g in range(len(CHUNKS))]
    mine = []
    for base, n in zip(bases, CHUNKS):
        mine.append(pack(base, n, after(key, *mine), value))

    first_hops = [lax.ppermute(block, "tp", ahead) for block in mine]

    asked = after(dec_query[0], mine[0])
    chosen, dec_rows = chosen_queries(facts, asked, lanes)
    wanted = lax.all_to_all(chosen, "tp", split_axis=0, concat_axis=0, tiled=True)
    b = lax.ppermute(mine[0], "tp", beside)
    parts = partial_decode(facts, other_half(after(wanted, b)), mine, lanes)
    parts = lax.all_to_all(parts, "tp", split_axis=0, concat_axis=0, tiled=True)
    dec_out = merged(facts, other_half(parts), dec_rows, dec_key[0], dec_value[0], lanes)

    received = []
    for g, (block, a) in enumerate(zip(mine, first_hops)):
        if g:
            b = lax.ppermute(after(block, received[0][2]), "tp", beside)
        c = lax.ppermute(after(a, parts) if g else after(a, wanted, mine[1]), "tp", trade)
        d = lax.ppermute(jnp.concatenate([a[1:], c], axis=0), "tp", ahead_again)
        received.append((a, b, c, d))
    out, flags = None, after(flags, received[1][2])
    for g, (base, n) in enumerate(zip(bases, CHUNKS)):
        if g:
            out = after(out, dec_out)
        out = prompt_heads(base, n, 0, n, flags, query, (mine[g], *received[g]), out)
    return (out[None], dec_out[None])


def solution(mesh):
    placed = (
        P("section", ("groups", "tp"), None),
        P("section", ("groups", "tp"), None),
        P("section", ("groups", "tp"), None),
        P(None, "groups"),
        P(None, "groups"),
        P("section", None, "groups", "tp"),
        P("section", None, "groups", None),
        P("section", None, "groups", None),
    )
    return jax.shard_map(
        on_device,
        mesh=mesh,
        in_specs=placed,
        out_specs=(P("section", ("groups", "tp"), None), P("section", None, "groups", "tp")),
        check_vma=False,
    )
```

```python
import functools
import math

import jax
import jax.numpy as jnp
from jax import lax
from jax.experimental import pallas as pl
from jax.experimental.pallas import tpu as pltpu
from jax.sharding import PartitionSpec as P

QH = 64
KVH = 8
HD = 128
PAGE = 128
MAXP = 8
STEPS = 4
GROUP = QH // KVH
SCALE = HD ** (-0.5)
EXP2_SCALE = SCALE * math.log2(math.e)
LOW = -1e30
CHUNKS = (4, 4)
ROWS = 512
SMEM = pl.BlockSpec(memory_space=pltpu.SMEM)
VMEM = pl.BlockSpec(memory_space=pltpu.VMEM)


def dot(a, b):
    return jnp.dot(a, b, preferred_element_type=jnp.float32)


def page_facts(facts, half, page):
    requests = facts.shape[1] // 2
    owner, first, live, end = -1, 0, PAGE, 0
    for r in range(requests):
        start, end = end, end + facts[half, r]
        begun = start <= page
        owner = jnp.where(begun, r, owner)
        first = jnp.where(begun, start, first)
        live = jnp.where(end - 1 == page, facts[half, requests + r], live)
    return owner, first, live


def params(limit):
    return dict(
        compiler_params=pltpu.CompilerParams(vmem_limit_bytes=limit << 20),
        cost_estimate=pl.CostEstimate(flops=1, bytes_accessed=1, transcendentals=0),
    )


def pack_kernel(base, k_ref, v_ref, *rest):
    o_ref, k_part, v_part, sems = rest[-4:]
    n = k_part.shape[1] // HD
    own = slice(base * HD, (base + n) * HD)
    copies = [
        pltpu.make_async_copy(source.at[:, own], part, sems.at[spot])
        for spot, (source, part) in enumerate(((k_ref, k_part), (v_ref, v_part)))
    ]
    for copy in copies:
        copy.start()
    for copy in copies:
        copy.wait()
    for j in range(n):
        columns = slice(j * HD, (j + 1) * HD)
        for p in range(2):
            rows = slice(p * PAGE, (p + 1) * PAGE)
            turned = jnp.transpose(k_part[rows, columns].astype(jnp.float32)).astype(jnp.bfloat16)
            o_ref[p, columns] = turned
            o_ref[p, (n + j) * HD:(n + j + 1) * HD] = v_part[rows, columns]


def pack(base, n, key, value):
    part = pltpu.VMEM((key.shape[0], n * HD), jnp.bfloat16)
    return pl.pallas_call(
        functools.partial(pack_kernel, base),
        out_shape=jax.ShapeDtypeStruct((2, 2 * n * HD, PAGE), jnp.bfloat16),
        in_specs=[pl.BlockSpec(memory_space=pl.ANY)] * 2,
        out_specs=VMEM,
        scratch_shapes=[part, part, pltpu.SemaphoreType.DMA((2,))],
        name="pack",
        **params(48),
    )(key, value)


def flags_kernel(facts, o_ref):
    half, place = lax.axis_index("section"), lax.axis_index("tp")
    even = place % 2 == 0
    near, far = 2 * place - 2, 2 * place - 6
    line = lax.broadcasted_iota(jnp.int32, o_ref.shape, 0)
    out = jnp.zeros(o_ref.shape, jnp.float32)
    for i in range(2):
        _, first, live = page_facts(facts, half, 2 * place + i)
        numbers = [2 * place - 7 if i == 0 else 2 * place, 2 * place + i]
        for page in (2 * place - 4, jnp.where(even, near, far), jnp.where(even, far, near)):
            numbers += [page, page + 1]
        for spot, number in enumerate(numbers):
            out = jnp.where(line == i * MAXP + spot, jnp.where(number >= first, 1.0, 0.0), out)
        out = jnp.where(line == 2 * MAXP + i, live.astype(jnp.float32), out)
    o_ref[...] = out


def page_flags(facts):
    return pl.pallas_call(
        flags_kernel,
        out_shape=jax.ShapeDtypeStruct((2 * MAXP + 8, PAGE), jnp.float32),
        in_specs=[SMEM],
        out_specs=VMEM,
        name="page_flags",
        **params(48),
    )(facts)


def prompt_kernel(n, low, flags, q_ref, *rest):
    o_ref, keys, values, causal, *probs = rest[-6:]
    head = low + pl.program_id(0)
    spots = [pl.ds(pl.multiple_of((x + head) * HD, HD), HD) for x in (0, n)]
    mine, a, b, c, d = [[[x[p, at] for at in spots] for p in range(x.shape[0])] for x in rest[:5]]
    choose = jnp.full((HD, PAGE), lax.axis_index("tp") % 2 == 0)
    be = [[jnp.where(choose, x, y) for x, y in zip(d[1 + p], b[p])] for p in range(2)]
    row = lax.broadcasted_iota(jnp.int32, (PAGE, PAGE), 0)
    col = lax.broadcasted_iota(jnp.int32, (PAGE, PAGE), 1)
    causal[...] = jnp.where(col <= row, 0.0, LOW)
    one = jnp.ones((PAGE, HD), jnp.bfloat16)
    zero = jnp.zeros((PAGE, HD), jnp.bfloat16)
    lives = [flags[2 * MAXP + i:2 * MAXP + i + 1, :] for i in range(2)]

    for i in range(2):
        stand_in = jnp.broadcast_to(mine[i][0][:, :1], (HD, PAGE))
        pages = [d[0] if i == 0 else mine[0], mine[i], *a, *c, *be]
        for spot, (k, v) in enumerate(pages):
            line = i * MAXP + spot
            seen = jnp.broadcast_to(flags[line:line + 1, :], (PAGE, HD)) > 0.0
            at = slice(spot * PAGE, (spot + 1) * PAGE)
            k = jnp.where(seen, k, stand_in)
            keys[i, :HD, at] = k
            keys[i, HD:, at] = k
            values[i, at, :HD] = jnp.where(seen, v, zero)
            values[i, at, HD:] = jnp.where(seen, one, zero)

    heads_at_once = ROWS // PAGE
    blocks = [(i, start) for i in range(2) for start in range(0, GROUP, heads_at_once)]

    def halves(query):
        query = query.astype(jnp.float32) * EXP2_SCALE
        high = query.astype(jnp.bfloat16)
        low = (query - high.astype(jnp.float32)).astype(jnp.bfloat16)
        return jnp.concatenate([high, low], axis=1)

    def queries(i, start):
        return halves(
            jnp.concatenate(
                [
                    q_ref[i * PAGE:(i + 1) * PAGE, h * HD:(h + 1) * HD]
                    for h in range(start, start + heads_at_once)
                ],
                axis=0,
            )
        )

    def divided(mixed, live):
        total = mixed[:, HD:]
        near = pl.reciprocal(total, approx=True)
        near = near * (2.0 - total * near)
        token = lax.broadcasted_iota(jnp.int32, (total.shape[0], HD), 0) % PAGE
        return jnp.where(token.astype(jnp.float32) < live, mixed[:, :HD] * near, 0.0).astype(jnp.bfloat16)

    tiles = [slice(t, t + 2 * PAGE) for t in range(0, MAXP * PAGE, 2 * PAGE)]

    def own_scores(query, i, repeat):
        own = dot(query, keys[i, :, tiles[0]])
        bias = jnp.concatenate([causal[...]] * repeat, axis=0)
        return jnp.concatenate([own[:, :PAGE], own[:, PAGE:] + bias], axis=1)

    def mix(block, slot, largest):
        i, start = block
        mixed = dot(probs[slot][...], values[i])
        out = divided(mixed, lives[i])
        for number in range(heads_at_once):
            h = start + number
            o_ref[i * PAGE:(i + 1) * PAGE, h * HD:(h + 1) * HD] = out[number * PAGE:(number + 1) * PAGE]
        return jnp.maximum(largest, mixed[:, HD:])

    largest = jnp.zeros((ROWS, HD), jnp.float32)
    for index in range(len(blocks) + 1):
        if index < len(blocks):
            i, slot = blocks[index][0], index % 2
            query = queries(*blocks[index])
            own = own_scores(query, i, heads_at_once)
            top = jnp.max(own, axis=1, keepdims=True)
            probs[slot][:, tiles[0]] = jnp.exp2(own - top).astype(jnp.bfloat16)
        if index > 0:
            largest = mix(blocks[index - 1], 1 - slot if index < len(blocks) else slot, largest)
        if index < len(blocks):
            for at in tiles[1:]:
                other = dot(query, keys[i, :, at])
                probs[slot][:, at] = jnp.exp2(other - top).astype(jnp.bfloat16)

    @pl.when(jnp.logical_not(jnp.max(largest) < 1e30))
    def _():
        def one(index, carry):
            i, h = index // GROUP, index % GROUP
            rows = pl.ds(pl.multiple_of(i * PAGE, PAGE), PAGE)
            columns = pl.ds(pl.multiple_of(h * HD, HD), HD)
            query = halves(q_ref[rows, columns])
            scores = [own_scores(query, i, 1)] + [dot(query, keys[i, :, at]) for at in tiles[1:]]
            top = jnp.max(functools.reduce(jnp.maximum, scores), axis=1, keepdims=True)
            mixed = jnp.zeros((PAGE, 2 * HD), jnp.float32)
            for score, at in zip(scores, tiles):
                mixed = mixed + dot(jnp.exp2(score - top).astype(jnp.bfloat16), values[i, at])
            o_ref[rows, columns] = divided(mixed, jnp.where(i == 0, lives[0], lives[1]))
            return carry

        lax.fori_loop(0, 2 * GROUP, one, 0)


def prompt_heads(base, n, low, high, flags, query, blocks, done):
    tok = query.shape[0]

    wide = pl.BlockSpec((tok, GROUP * HD), lambda j: (0, base + low + j))
    operands = [flags, query, *blocks]
    specs = [VMEM, wide] + [VMEM] * len(blocks)
    aliases = {}
    if done is not None:
        aliases = {len(operands): 0}
        operands.append(done)
        specs.append(pl.BlockSpec(memory_space=pl.ANY))
    return pl.pallas_call(
        functools.partial(prompt_kernel, n, low),
        out_shape=jax.ShapeDtypeStruct(query.shape, jnp.bfloat16),
        grid=(high - low,),
        in_specs=specs,
        out_specs=wide,
        scratch_shapes=[
            pltpu.VMEM((2, 2 * HD, MAXP * PAGE), jnp.bfloat16),
            pltpu.VMEM((2, MAXP * PAGE, 2 * HD), jnp.bfloat16),
            pltpu.VMEM((PAGE, PAGE), jnp.float32),
            pltpu.VMEM((ROWS, MAXP * PAGE), jnp.bfloat16),
            pltpu.VMEM((ROWS, MAXP * PAGE), jnp.bfloat16),
        ],
        input_output_aliases=aliases,
        name="prompt_attention",
        compiler_params=pltpu.CompilerParams(vmem_limit_bytes=48 << 20),
        cost_estimate=pl.CostEstimate(
            flops=(high - low) * GROUP * tok * MAXP * PAGE * HD * 8,
            bytes_accessed=4 * (high - low) * tok * GROUP * HD,
            transcendentals=0,
        ),
    )(*operands)


def stat_rows(rows):
    return 16 - rows % 16


def choose_kernel(facts, q_ref, o_ref, rows_ref, turned):
    requests, here = q_ref.shape[1], q_ref.shape[2] // HD
    other = 1 - lax.axis_index("section")
    for s in range(STEPS):
        query = q_ref[s].astype(jnp.float32)
        for r in range(requests):
            for h in range(here):
                row = h * STEPS + s
                turned[r, row:row + 1] = query[r:r + 1, h * HD:(h + 1) * HD]
    rows_ref[...] = turned[...].astype(jnp.bfloat16)

    def one(lane, carry):
        for i in range(2):
            owner = page_facts(facts, other, 2 * lane + i)[0]
            o_ref[lane, i] = turned[owner].astype(jnp.bfloat16)
        return carry

    lax.fori_loop(0, o_ref.shape[0], one, 0)


def chosen_queries(facts, query, lanes):
    rows = (query.shape[1], QH // lanes * STEPS, HD)
    return pl.pallas_call(
        choose_kernel,
        out_shape=(
            jax.ShapeDtypeStruct((lanes, 2, *rows[1:]), jnp.bfloat16),
            jax.ShapeDtypeStruct(rows, jnp.bfloat16),
        ),
        in_specs=[SMEM, VMEM],
        out_specs=(VMEM, VMEM),
        scratch_shapes=[pltpu.VMEM(rows, jnp.float32)],
        name="choose_queries",
        **params(32),
    )(facts, query)


def partial_kernel(lanes, facts, q_ref, *rest):
    *packed, o_ref = rest
    split = GROUP // (QH // lanes)
    width = QH // lanes * STEPS
    extra = stat_rows(2 * width)
    half, place = lax.axis_index("section"), lax.axis_index("tp")
    group = GROUP * STEPS
    height = 2 * KVH * group
    lane = lax.broadcasted_iota(jnp.int32, (height, PAGE), 1)
    later = lax.broadcasted_iota(jnp.int32, (height, PAGE), 0) // group % 2 == 1
    spot = lax.broadcasted_iota(jnp.int32, (2 * width, PAGE), 0)
    across = lax.broadcasted_iota(jnp.int32, (2 * width, PAGE), 1)
    line = lax.broadcasted_iota(jnp.int32, (extra, PAGE), 0)
    lives = [page_facts(facts, half, 2 * place + i)[2] for i in range(2)]
    places = [(block, j, n) for block, n in zip(packed, CHUNKS) for j in range(n)]
    scores, values = [], []
    for k, (block, j, n) in enumerate(places):
        for i in range(2):
            query = jnp.concatenate([q_ref[k * split + t, i] for t in range(split)], axis=0)
            scores.append(dot(query, block[i, j * HD:(j + 1) * HD]))
            values.append(block[i, (n + j) * HD:(n + j + 1) * HD])
    score = jnp.concatenate(scores, axis=0) * SCALE
    score = jnp.where(lane < jnp.where(later, lives[1], lives[0]), score, LOW)
    top = jnp.max(score, axis=1, keepdims=True)
    terms = jnp.exp(score - top)
    total = jnp.sum(terms, axis=1, keepdims=True)
    high = terms.astype(jnp.bfloat16)
    low = (terms - high.astype(jnp.float32)).astype(jnp.bfloat16)
    mixed = jnp.concatenate(
        [
            dot(high[m * group:(m + 1) * group], v) + dot(low[m * group:(m + 1) * group], v)
            for m, v in enumerate(values)
        ],
        axis=0,
    ) / total
    sums = top + jnp.log(total)
    for k in range(KVH):
        for t in range(split):
            begins = [(2 * k + i) * group + t * width for i in range(2)]
            both = jnp.concatenate([sums[at:at + width] for at in begins], axis=0)
            turned = jnp.sum(jnp.where(spot == across, both, 0.0), axis=0, keepdims=True)
            first = turned.astype(jnp.bfloat16).astype(jnp.float32)
            rest = turned - first
            second = rest.astype(jnp.bfloat16).astype(jnp.float32)
            stat = jnp.where(line == 0, first, jnp.where(line == 1, second, rest - second))
            stat = jnp.where(line < 3, stat, 0.0)
            block = jnp.concatenate([mixed[at:at + width] for at in begins] + [stat], axis=0)
            o_ref[k * split + t] = block.astype(jnp.bfloat16)


def partial_decode(facts, query, packed, lanes):
    rows = 2 * (QH // lanes) * STEPS
    return pl.pallas_call(
        functools.partial(partial_kernel, lanes),
        out_shape=jax.ShapeDtypeStruct((lanes, rows + stat_rows(rows), HD), jnp.bfloat16),
        in_specs=[SMEM, VMEM] + [VMEM] * len(packed),
        out_specs=VMEM,
        name="partial_decode",
        **params(32),
    )(facts, query, *packed)


def merge_kernel(lanes, facts, parts_ref, q_ref, k_ref, v_ref, o_ref):
    requests = q_ref.shape[0]
    width = (QH // lanes) * STEPS
    other, place = 1 - lax.axis_index("section"), lax.axis_index("tp")
    head = place * (QH // lanes) // GROUP
    spot = lax.broadcasted_iota(jnp.int32, (width, PAGE), 0)
    across = lax.broadcasted_iota(jnp.int32, (width, PAGE), 1)
    step = lax.broadcasted_iota(jnp.int32, (width, 1), 0) % STEPS
    end = 0
    for r in range(requests):
        start, end = end, end + facts[other, r]
        query = q_ref[r].astype(jnp.float32)
        keys = k_ref[r, head].astype(jnp.float32)
        values = v_ref[r, head].astype(jnp.float32)
        tops, vectors = [], []
        for u in range(STEPS):
            score = jnp.sum(query * keys[u:u + 1], axis=1, keepdims=True) * SCALE
            tops.append(jnp.where(u <= step, score, LOW))
            vectors.append(values[u:u + 1])
        for j in range(MAXP):
            page = jnp.minimum(start + j, 2 * lanes - 1)
            block = parts_ref[page // 2].astype(jnp.float32)
            later = jnp.full((width, HD), page % 2 == 1)
            vectors.append(jnp.where(later, block[width:2 * width], block[:width]))
            stat = jnp.sum(block[2 * width:2 * width + 8], axis=0, keepdims=True)
            stat = jnp.sum(
                jnp.where(across - page % 2 * width == spot, stat, 0.0), axis=1, keepdims=True
            )
            tops.append(jnp.where(jnp.full((width, 1), start + j < end), stat, LOW))
        top = functools.reduce(jnp.maximum, tops)
        weights = [jnp.exp(t - top) for t in tops]
        total = functools.reduce(jnp.add, weights)
        mixed = functools.reduce(jnp.add, [w * x for w, x in zip(weights, vectors)])
        o_ref[r] = (mixed / total).astype(jnp.bfloat16)


def merged(facts, parts, query, new_key, new_value, lanes):
    requests = query.shape[0]
    fresh = [
        jnp.transpose(x.reshape(STEPS, requests, KVH, HD), (1, 2, 0, 3)) for x in (new_key, new_value)
    ]
    out = pl.pallas_call(
        functools.partial(merge_kernel, lanes),
        out_shape=jax.ShapeDtypeStruct(query.shape, jnp.bfloat16),
        in_specs=[SMEM, VMEM, VMEM, VMEM, VMEM],
        out_specs=VMEM,
        name="merge_decode",
        **params(32),
    )(facts, parts, query, *fresh)
    out = jnp.transpose(out.reshape(requests, QH // lanes, STEPS, HD), (2, 0, 1, 3))
    return out.reshape(STEPS, requests, QH // lanes * HD)


def other_half(x):
    return lax.ppermute(x, "section", [(0, 1), (1, 0)])


def after(x, *earlier):
    return lax.optimization_barrier((x, *earlier))[0]


def on_device(
    prefill_query, prefill_key, prefill_value, counts, fills, dec_query, dec_key, dec_value
):
    lanes = lax.axis_size("tp")
    query, key, value = prefill_query[0], prefill_key[0], prefill_value[0]
    facts = jnp.concatenate([counts, fills], axis=1)
    flags = page_flags(facts)
    ahead = [(i, i + 2) for i in range(lanes - 2)]
    ahead_again = [(i, i + 2) for i in range(2, lanes - 2)]
    beside = [(i, i + 1) for i in range(0, lanes, 2)]
    trade = [(i, i ^ 1) for i in range(2, lanes)]
    bases = [sum(CHUNKS[:g]) for g in range(len(CHUNKS))]
    mine = []
    for base, n in zip(bases, CHUNKS):
        mine.append(pack(base, n, after(key, *mine), value))

    first_hops = [lax.ppermute(block, "tp", ahead) for block in mine]

    asked = after(dec_query[0], mine[0])
    chosen, dec_rows = chosen_queries(facts, asked, lanes)
    wanted = lax.all_to_all(chosen, "tp", split_axis=0, concat_axis=0, tiled=True)
    b = lax.ppermute(mine[0], "tp", beside)
    parts = partial_decode(facts, other_half(after(wanted, b)), mine, lanes)
    parts = lax.all_to_all(parts, "tp", split_axis=0, concat_axis=0, tiled=True)
    dec_out = merged(facts, other_half(parts), dec_rows, dec_key[0], dec_value[0], lanes)

    received = []
    for g, (block, a) in enumerate(zip(mine, first_hops)):
        if g:
            b = lax.ppermute(after(block, received[0][2]), "tp", beside)
        c = lax.ppermute(a if g else after(a, wanted, mine[1]), "tp", trade)
        d = lax.ppermute(jnp.concatenate([a[1:], c], axis=0), "tp", ahead_again)
        received.append((a, b, c, d))
    out, flags = None, after(flags, received[1][2], parts)
    for g, (base, n) in enumerate(zip(bases, CHUNKS)):
        if g:
            out = after(out, dec_out)
        out = prompt_heads(base, n, 0, n, flags, query, (mine[g], *received[g]), out)
    return (out[None], dec_out[None])


def solution(mesh):
    placed = (
        P("section", ("groups", "tp"), None),
        P("section", ("groups", "tp"), None),
        P("section", ("groups", "tp"), None),
        P(None, "groups"),
        P(None, "groups"),
        P("section", None, "groups", "tp"),
        P("section", None, "groups", None),
        P("section", None, "groups", None),
    )
    return jax.shard_map(
        on_device,
        mesh=mesh,
        in_specs=placed,
        out_specs=(P("section", ("groups", "tp"), None), P("section", None, "groups", "tp")),
        check_vma=False,
    )
```

```python
import functools
import math

import jax
import jax.numpy as jnp
from jax import lax
from jax.experimental import pallas as pl
from jax.experimental.pallas import tpu as pltpu
from jax.sharding import PartitionSpec as P

QH = 64
KVH = 8
HD = 128
PAGE = 128
MAXP = 8
STEPS = 4
GROUP = QH // KVH
SCALE = HD ** (-0.5)
EXP2_SCALE = SCALE * math.log2(math.e)
LOW = -1e30
CHUNKS = (4, 4)
ROWS = 512
SMEM = pl.BlockSpec(memory_space=pltpu.SMEM)
VMEM = pl.BlockSpec(memory_space=pltpu.VMEM)


def dot(a, b):
    return jnp.dot(a, b, preferred_element_type=jnp.float32)


def page_facts(facts, half, page):
    requests = facts.shape[1] // 2
    owner, first, live, end = -1, 0, PAGE, 0
    for r in range(requests):
        start, end = end, end + facts[half, r]
        begun = start <= page
        owner = jnp.where(begun, r, owner)
        first = jnp.where(begun, start, first)
        live = jnp.where(end - 1 == page, facts[half, requests + r], live)
    return owner, first, live


def params(limit):
    return dict(
        compiler_params=pltpu.CompilerParams(vmem_limit_bytes=limit << 20),
        cost_estimate=pl.CostEstimate(flops=1, bytes_accessed=1, transcendentals=0),
    )


def pack_kernel(base, k_ref, v_ref, *rest):
    o_ref, k_part, v_part, sems = rest[-4:]
    n = k_part.shape[1] // HD
    own = slice(base * HD, (base + n) * HD)
    copies = [
        pltpu.make_async_copy(source.at[:, own], part, sems.at[spot])
        for spot, (source, part) in enumerate(((k_ref, k_part), (v_ref, v_part)))
    ]
    for copy in copies:
        copy.start()
    for copy in copies:
        copy.wait()
    for j in range(n):
        columns = slice(j * HD, (j + 1) * HD)
        for p in range(2):
            rows = slice(p * PAGE, (p + 1) * PAGE)
            turned = jnp.transpose(k_part[rows, columns].astype(jnp.float32)).astype(jnp.bfloat16)
            o_ref[p, columns] = turned
            o_ref[p, (n + j) * HD:(n + j + 1) * HD] = v_part[rows, columns]


def pack(base, n, key, value):
    part = pltpu.VMEM((key.shape[0], n * HD), jnp.bfloat16)
    return pl.pallas_call(
        functools.partial(pack_kernel, base),
        out_shape=jax.ShapeDtypeStruct((2, 2 * n * HD, PAGE), jnp.bfloat16),
        in_specs=[pl.BlockSpec(memory_space=pl.ANY)] * 2,
        out_specs=VMEM,
        scratch_shapes=[part, part, pltpu.SemaphoreType.DMA((2,))],
        name="pack",
        **params(48),
    )(key, value)


def flags_kernel(facts, o_ref):
    half, place = lax.axis_index("section"), lax.axis_index("tp")
    even = place % 2 == 0
    near, far = 2 * place - 2, 2 * place - 6
    line = lax.broadcasted_iota(jnp.int32, o_ref.shape, 0)
    out = jnp.zeros(o_ref.shape, jnp.float32)
    for i in range(2):
        _, first, live = page_facts(facts, half, 2 * place + i)
        numbers = [2 * place - 7 if i == 0 else 2 * place, 2 * place + i]
        for page in (2 * place - 4, jnp.where(even, near, far), jnp.where(even, far, near)):
            numbers += [page, page + 1]
        for spot, number in enumerate(numbers):
            out = jnp.where(line == i * MAXP + spot, jnp.where(number >= first, 1.0, 0.0), out)
        out = jnp.where(line == 2 * MAXP + i, live.astype(jnp.float32), out)
    o_ref[...] = out


def page_flags(facts):
    return pl.pallas_call(
        flags_kernel,
        out_shape=jax.ShapeDtypeStruct((2 * MAXP + 8, PAGE), jnp.float32),
        in_specs=[SMEM],
        out_specs=VMEM,
        name="page_flags",
        **params(48),
    )(facts)


def prompt_kernel(n, low, flags, q_ref, *rest):
    o_ref, keys, values, causal, *probs = rest[-6:]
    head = low + pl.program_id(0)
    spots = [pl.ds(pl.multiple_of((x + head) * HD, HD), HD) for x in (0, n)]
    mine, a, c, d = [[[x[p, at] for at in spots] for p in range(x.shape[0])] for x in rest[:4]]
    b = [[x[p] for x in rest[4:6]] for p in range(2)]
    choose = jnp.full((HD, PAGE), lax.axis_index("tp") % 2 == 0)
    be = [[jnp.where(choose, x, y) for x, y in zip(d[1 + p], b[p])] for p in range(2)]
    row = lax.broadcasted_iota(jnp.int32, (PAGE, PAGE), 0)
    col = lax.broadcasted_iota(jnp.int32, (PAGE, PAGE), 1)
    causal[...] = jnp.where(col <= row, 0.0, LOW)
    one = jnp.ones((PAGE, HD), jnp.bfloat16)
    zero = jnp.zeros((PAGE, HD), jnp.bfloat16)
    lives = [flags[2 * MAXP + i:2 * MAXP + i + 1, :] for i in range(2)]

    for i in range(2):
        stand_in = jnp.broadcast_to(mine[i][0][:, :1], (HD, PAGE))
        pages = [d[0] if i == 0 else mine[0], mine[i], *a, *c, *be]
        for spot, (k, v) in enumerate(pages):
            line = i * MAXP + spot
            seen = jnp.broadcast_to(flags[line:line + 1, :], (PAGE, HD)) > 0.0
            at = slice(spot * PAGE, (spot + 1) * PAGE)
            k = jnp.where(seen, k, stand_in)
            keys[i, :HD, at] = k
            keys[i, HD:, at] = k
            values[i, at, :HD] = jnp.where(seen, v, zero)
            values[i, at, HD:] = jnp.where(seen, one, zero)

    heads_at_once = ROWS // PAGE
    blocks = [(i, start) for i in range(2) for start in range(0, GROUP, heads_at_once)]

    def halves(query):
        query = query.astype(jnp.float32) * EXP2_SCALE
        high = query.astype(jnp.bfloat16)
        low = (query - high.astype(jnp.float32)).astype(jnp.bfloat16)
        return jnp.concatenate([high, low], axis=1)

    def queries(i, start):
        return halves(
            jnp.concatenate(
                [
                    q_ref[i * PAGE:(i + 1) * PAGE, h * HD:(h + 1) * HD]
                    for h in range(start, start + heads_at_once)
                ],
                axis=0,
            )
        )

    def divided(mixed, live):
        total = mixed[:, HD:]
        near = pl.reciprocal(total, approx=True)
        near = near * (2.0 - total * near)
        token = lax.broadcasted_iota(jnp.int32, (total.shape[0], HD), 0) % PAGE
        return jnp.where(token.astype(jnp.float32) < live, mixed[:, :HD] * near, 0.0).astype(jnp.bfloat16)

    tiles = [slice(t, t + 2 * PAGE) for t in range(0, MAXP * PAGE, 2 * PAGE)]

    def own_scores(query, i, repeat):
        own = dot(query, keys[i, :, tiles[0]])
        bias = jnp.concatenate([causal[...]] * repeat, axis=0)
        return jnp.concatenate([own[:, :PAGE], own[:, PAGE:] + bias], axis=1)

    def mix(block, slot, largest):
        i, start = block
        mixed = dot(probs[slot][...], values[i])
        out = divided(mixed, lives[i])
        for number in range(heads_at_once):
            h = start + number
            o_ref[i * PAGE:(i + 1) * PAGE, h * HD:(h + 1) * HD] = out[number * PAGE:(number + 1) * PAGE]
        return jnp.maximum(largest, mixed[:, HD:])

    largest = jnp.zeros((ROWS, HD), jnp.float32)
    for index in range(len(blocks) + 1):
        if index < len(blocks):
            i, slot = blocks[index][0], index % 2
            query = queries(*blocks[index])
            own = own_scores(query, i, heads_at_once)
            top = jnp.max(own, axis=1, keepdims=True)
            probs[slot][:, tiles[0]] = jnp.exp2(own - top).astype(jnp.bfloat16)
        if index > 0:
            largest = mix(blocks[index - 1], 1 - slot if index < len(blocks) else slot, largest)
        if index < len(blocks):
            for at in tiles[1:]:
                other = dot(query, keys[i, :, at])
                probs[slot][:, at] = jnp.exp2(other - top).astype(jnp.bfloat16)

    @pl.when(jnp.logical_not(jnp.max(largest) < 1e30))
    def _():
        def one(index, carry):
            i, h = index // GROUP, index % GROUP
            rows = pl.ds(pl.multiple_of(i * PAGE, PAGE), PAGE)
            columns = pl.ds(pl.multiple_of(h * HD, HD), HD)
            query = halves(q_ref[rows, columns])
            scores = [own_scores(query, i, 1)] + [dot(query, keys[i, :, at]) for at in tiles[1:]]
            top = jnp.max(functools.reduce(jnp.maximum, scores), axis=1, keepdims=True)
            mixed = jnp.zeros((PAGE, 2 * HD), jnp.float32)
            for score, at in zip(scores, tiles):
                mixed = mixed + dot(jnp.exp2(score - top).astype(jnp.bfloat16), values[i, at])
            o_ref[rows, columns] = divided(mixed, jnp.where(i == 0, lives[0], lives[1]))
            return carry

        lax.fori_loop(0, 2 * GROUP, one, 0)


def prompt_heads(base, n, low, high, flags, query, blocks, done):
    tok = query.shape[0]

    wide = pl.BlockSpec((tok, GROUP * HD), lambda j: (0, base + low + j))
    mine, a, b, c, d = blocks
    operands = [flags, query, mine, a, c, d, b, b]
    specs = [VMEM, wide] + [VMEM] * 4
    specs += [pl.BlockSpec((2, HD, PAGE), lambda j, x=x: (0, x + low + j, 0)) for x in (0, n)]
    aliases = {}
    if done is not None:
        aliases = {len(operands): 0}
        operands.append(done)
        specs.append(pl.BlockSpec(memory_space=pl.ANY))
    return pl.pallas_call(
        functools.partial(prompt_kernel, n, low),
        out_shape=jax.ShapeDtypeStruct(query.shape, jnp.bfloat16),
        grid=(high - low,),
        in_specs=specs,
        out_specs=wide,
        scratch_shapes=[
            pltpu.VMEM((2, 2 * HD, MAXP * PAGE), jnp.bfloat16),
            pltpu.VMEM((2, MAXP * PAGE, 2 * HD), jnp.bfloat16),
            pltpu.VMEM((PAGE, PAGE), jnp.float32),
            pltpu.VMEM((ROWS, MAXP * PAGE), jnp.bfloat16),
            pltpu.VMEM((ROWS, MAXP * PAGE), jnp.bfloat16),
        ],
        input_output_aliases=aliases,
        name="prompt_attention",
        compiler_params=pltpu.CompilerParams(vmem_limit_bytes=48 << 20),
        cost_estimate=pl.CostEstimate(
            flops=(high - low) * GROUP * tok * MAXP * PAGE * HD * 8,
            bytes_accessed=4 * (high - low) * tok * GROUP * HD,
            transcendentals=0,
        ),
    )(*operands)


def stat_rows(rows):
    return 16 - rows % 16


def choose_kernel(facts, q_ref, o_ref, rows_ref, turned):
    requests, here = q_ref.shape[1], q_ref.shape[2] // HD
    other = 1 - lax.axis_index("section")
    for s in range(STEPS):
        query = q_ref[s].astype(jnp.float32)
        for r in range(requests):
            for h in range(here):
                row = h * STEPS + s
                turned[r, row:row + 1] = query[r:r + 1, h * HD:(h + 1) * HD]
    rows_ref[...] = turned[...].astype(jnp.bfloat16)

    def one(lane, carry):
        for i in range(2):
            owner = page_facts(facts, other, 2 * lane + i)[0]
            o_ref[lane, i] = turned[owner].astype(jnp.bfloat16)
        return carry

    lax.fori_loop(0, o_ref.shape[0], one, 0)


def chosen_queries(facts, query, lanes):
    rows = (query.shape[1], QH // lanes * STEPS, HD)
    return pl.pallas_call(
        choose_kernel,
        out_shape=(
            jax.ShapeDtypeStruct((lanes, 2, *rows[1:]), jnp.bfloat16),
            jax.ShapeDtypeStruct(rows, jnp.bfloat16),
        ),
        in_specs=[SMEM, VMEM],
        out_specs=(VMEM, VMEM),
        scratch_shapes=[pltpu.VMEM(rows, jnp.float32)],
        name="choose_queries",
        **params(32),
    )(facts, query)


def partial_kernel(lanes, facts, q_ref, *rest):
    *packed, o_ref = rest
    split = GROUP // (QH // lanes)
    width = QH // lanes * STEPS
    extra = stat_rows(2 * width)
    half, place = lax.axis_index("section"), lax.axis_index("tp")
    group = GROUP * STEPS
    height = 2 * KVH * group
    lane = lax.broadcasted_iota(jnp.int32, (height, PAGE), 1)
    later = lax.broadcasted_iota(jnp.int32, (height, PAGE), 0) // group % 2 == 1
    spot = lax.broadcasted_iota(jnp.int32, (2 * width, PAGE), 0)
    across = lax.broadcasted_iota(jnp.int32, (2 * width, PAGE), 1)
    line = lax.broadcasted_iota(jnp.int32, (extra, PAGE), 0)
    lives = [page_facts(facts, half, 2 * place + i)[2] for i in range(2)]
    places = [(block, j, n) for block, n in zip(packed, CHUNKS) for j in range(n)]
    scores, values = [], []
    for k, (block, j, n) in enumerate(places):
        for i in range(2):
            query = jnp.concatenate([q_ref[k * split + t, i] for t in range(split)], axis=0)
            scores.append(dot(query, block[i, j * HD:(j + 1) * HD]))
            values.append(block[i, (n + j) * HD:(n + j + 1) * HD])
    score = jnp.concatenate(scores, axis=0) * SCALE
    score = jnp.where(lane < jnp.where(later, lives[1], lives[0]), score, LOW)
    top = jnp.max(score, axis=1, keepdims=True)
    terms = jnp.exp(score - top)
    total = jnp.sum(terms, axis=1, keepdims=True)
    high = terms.astype(jnp.bfloat16)
    low = (terms - high.astype(jnp.float32)).astype(jnp.bfloat16)
    mixed = jnp.concatenate(
        [
            dot(high[m * group:(m + 1) * group], v) + dot(low[m * group:(m + 1) * group], v)
            for m, v in enumerate(values)
        ],
        axis=0,
    ) / total
    sums = top + jnp.log(total)
    for k in range(KVH):
        for t in range(split):
            begins = [(2 * k + i) * group + t * width for i in range(2)]
            both = jnp.concatenate([sums[at:at + width] for at in begins], axis=0)
            turned = jnp.sum(jnp.where(spot == across, both, 0.0), axis=0, keepdims=True)
            first = turned.astype(jnp.bfloat16).astype(jnp.float32)
            rest = turned - first
            second = rest.astype(jnp.bfloat16).astype(jnp.float32)
            stat = jnp.where(line == 0, first, jnp.where(line == 1, second, rest - second))
            stat = jnp.where(line < 3, stat, 0.0)
            block = jnp.concatenate([mixed[at:at + width] for at in begins] + [stat], axis=0)
            o_ref[k * split + t] = block.astype(jnp.bfloat16)


def partial_decode(facts, query, packed, lanes):
    rows = 2 * (QH // lanes) * STEPS
    return pl.pallas_call(
        functools.partial(partial_kernel, lanes),
        out_shape=jax.ShapeDtypeStruct((lanes, rows + stat_rows(rows), HD), jnp.bfloat16),
        in_specs=[SMEM, VMEM] + [VMEM] * len(packed),
        out_specs=VMEM,
        name="partial_decode",
        **params(32),
    )(facts, query, *packed)


def merge_kernel(lanes, facts, parts_ref, q_ref, k_ref, v_ref, o_ref):
    requests = q_ref.shape[0]
    width = (QH // lanes) * STEPS
    other, place = 1 - lax.axis_index("section"), lax.axis_index("tp")
    head = place * (QH // lanes) // GROUP
    spot = lax.broadcasted_iota(jnp.int32, (width, PAGE), 0)
    across = lax.broadcasted_iota(jnp.int32, (width, PAGE), 1)
    step = lax.broadcasted_iota(jnp.int32, (width, 1), 0) % STEPS
    end = 0
    for r in range(requests):
        start, end = end, end + facts[other, r]
        query = q_ref[r].astype(jnp.float32)
        keys = k_ref[r, head].astype(jnp.float32)
        values = v_ref[r, head].astype(jnp.float32)
        tops, vectors = [], []
        for u in range(STEPS):
            score = jnp.sum(query * keys[u:u + 1], axis=1, keepdims=True) * SCALE
            tops.append(jnp.where(u <= step, score, LOW))
            vectors.append(values[u:u + 1])
        for j in range(MAXP):
            page = jnp.minimum(start + j, 2 * lanes - 1)
            block = parts_ref[page // 2].astype(jnp.float32)
            later = jnp.full((width, HD), page % 2 == 1)
            vectors.append(jnp.where(later, block[width:2 * width], block[:width]))
            stat = jnp.sum(block[2 * width:2 * width + 8], axis=0, keepdims=True)
            stat = jnp.sum(
                jnp.where(across - page % 2 * width == spot, stat, 0.0), axis=1, keepdims=True
            )
            tops.append(jnp.where(jnp.full((width, 1), start + j < end), stat, LOW))
        top = functools.reduce(jnp.maximum, tops)
        weights = [jnp.exp(t - top) for t in tops]
        total = functools.reduce(jnp.add, weights)
        mixed = functools.reduce(jnp.add, [w * x for w, x in zip(weights, vectors)])
        o_ref[r] = (mixed / total).astype(jnp.bfloat16)


def merged(facts, parts, query, new_key, new_value, lanes):
    requests = query.shape[0]
    fresh = [
        jnp.transpose(x.reshape(STEPS, requests, KVH, HD), (1, 2, 0, 3)) for x in (new_key, new_value)
    ]
    out = pl.pallas_call(
        functools.partial(merge_kernel, lanes),
        out_shape=jax.ShapeDtypeStruct(query.shape, jnp.bfloat16),
        in_specs=[SMEM, VMEM, VMEM, VMEM, VMEM],
        out_specs=VMEM,
        name="merge_decode",
        **params(32),
    )(facts, parts, query, *fresh)
    out = jnp.transpose(out.reshape(requests, QH // lanes, STEPS, HD), (2, 0, 1, 3))
    return out.reshape(STEPS, requests, QH // lanes * HD)


def other_half(x):
    return lax.ppermute(x, "section", [(0, 1), (1, 0)])


def after(x, *earlier):
    return lax.optimization_barrier((x, *earlier))[0]


def on_device(
    prefill_query, prefill_key, prefill_value, counts, fills, dec_query, dec_key, dec_value
):
    lanes = lax.axis_size("tp")
    query, key, value = prefill_query[0], prefill_key[0], prefill_value[0]
    facts = jnp.concatenate([counts, fills], axis=1)
    flags = page_flags(facts)
    ahead = [(i, i + 2) for i in range(lanes - 2)]
    ahead_again = [(i, i + 2) for i in range(2, lanes - 2)]
    beside = [(i, i + 1) for i in range(0, lanes, 2)]
    trade = [(i, i ^ 1) for i in range(2, lanes)]
    bases = [sum(CHUNKS[:g]) for g in range(len(CHUNKS))]
    mine = []
    for base, n in zip(bases, CHUNKS):
        mine.append(pack(base, n, after(key, *mine), value))

    first_hops = [lax.ppermute(block, "tp", ahead) for block in mine]

    asked = after(dec_query[0], mine[0])
    chosen, dec_rows = chosen_queries(facts, asked, lanes)
    wanted = lax.all_to_all(chosen, "tp", split_axis=0, concat_axis=0, tiled=True)
    b = lax.ppermute(after(mine[0], chosen), "tp", beside)
    found = partial_decode(facts, other_half(wanted), mine, lanes)
    parts = lax.all_to_all(found, "tp", split_axis=0, concat_axis=0, tiled=True)
    dec_out = merged(facts, other_half(parts), dec_rows, dec_key[0], dec_value[0], lanes)

    received = []
    for g, (block, a) in enumerate(zip(mine, first_hops)):
        if g:
            b = lax.ppermute(after(block, received[0][2]), "tp", beside)
        c = lax.ppermute(after(a, found) if g else after(a, wanted, b, mine[1]), "tp", trade)
        d = lax.ppermute(jnp.concatenate([a[1:], c], axis=0), "tp", ahead_again)
        received.append((a, b, c, d))
    out, flags = None, after(flags, received[1][2])
    for g, (base, n) in enumerate(zip(bases, CHUNKS)):
        if g:
            out = after(out, dec_out)
        out = prompt_heads(base, n, 0, n, flags, query, (mine[g], *received[g]), out)
    return (out[None], dec_out[None])


def solution(mesh):
    placed = (
        P("section", ("groups", "tp"), None),
        P("section", ("groups", "tp"), None),
        P("section", ("groups", "tp"), None),
        P(None, "groups"),
        P(None, "groups"),
        P("section", None, "groups", "tp"),
        P("section", None, "groups", None),
        P("section", None, "groups", None),
    )
    return jax.shard_map(
        on_device,
        mesh=mesh,
        in_specs=placed,
        out_specs=(P("section", ("groups", "tp"), None), P("section", None, "groups", "tp")),
        check_vma=False,
    )
```

```python
import functools
import math

import jax
import jax.numpy as jnp
from jax import lax
from jax.experimental import pallas as pl
from jax.experimental.pallas import tpu as pltpu
from jax.sharding import PartitionSpec as P

QH = 64
KVH = 8
HD = 128
PAGE = 128
MAXP = 8
STEPS = 4
GROUP = QH // KVH
SCALE = HD ** (-0.5)
EXP2_SCALE = SCALE * math.log2(math.e)
LOW = -1e30
CHUNKS = (4, 4)
ROWS = 512
SMEM = pl.BlockSpec(memory_space=pltpu.SMEM)
VMEM = pl.BlockSpec(memory_space=pltpu.VMEM)


def dot(a, b):
    return jnp.dot(a, b, preferred_element_type=jnp.float32)


def page_facts(facts, half, page):
    requests = facts.shape[1] // 2
    owner, first, live, end = -1, 0, PAGE, 0
    for r in range(requests):
        start, end = end, end + facts[half, r]
        begun = start <= page
        owner = jnp.where(begun, r, owner)
        first = jnp.where(begun, start, first)
        live = jnp.where(end - 1 == page, facts[half, requests + r], live)
    return owner, first, live


def params(limit):
    return dict(
        compiler_params=pltpu.CompilerParams(vmem_limit_bytes=limit << 20),
        cost_estimate=pl.CostEstimate(flops=1, bytes_accessed=1, transcendentals=0),
    )


def pack_kernel(base, k_ref, v_ref, *rest):
    o_ref, k_part, v_part, sems = rest[-4:]
    n = k_part.shape[1] // HD
    own = slice(base * HD, (base + n) * HD)
    copies = [
        pltpu.make_async_copy(source.at[:, own], part, sems.at[spot])
        for spot, (source, part) in enumerate(((k_ref, k_part), (v_ref, v_part)))
    ]
    for copy in copies:
        copy.start()
    for copy in copies:
        copy.wait()
    for j in range(n):
        columns = slice(j * HD, (j + 1) * HD)
        for p in range(2):
            rows = slice(p * PAGE, (p + 1) * PAGE)
            turned = jnp.transpose(k_part[rows, columns].astype(jnp.float32)).astype(jnp.bfloat16)
            o_ref[p, columns] = turned
            o_ref[p, (n + j) * HD:(n + j + 1) * HD] = v_part[rows, columns]


def pack(base, n, key, value):
    part = pltpu.VMEM((key.shape[0], n * HD), jnp.bfloat16)
    return pl.pallas_call(
        functools.partial(pack_kernel, base),
        out_shape=jax.ShapeDtypeStruct((2, 2 * n * HD, PAGE), jnp.bfloat16),
        in_specs=[pl.BlockSpec(memory_space=pl.ANY)] * 2,
        out_specs=VMEM,
        scratch_shapes=[part, part, pltpu.SemaphoreType.DMA((2,))],
        name="pack",
        **params(48),
    )(key, value)


def flags_kernel(facts, o_ref):
    half, place = lax.axis_index("section"), lax.axis_index("tp")
    even = place % 2 == 0
    near, far = 2 * place - 2, 2 * place - 6
    line = lax.broadcasted_iota(jnp.int32, o_ref.shape, 0)
    out = jnp.zeros(o_ref.shape, jnp.float32)
    for i in range(2):
        _, first, live = page_facts(facts, half, 2 * place + i)
        numbers = [2 * place - 7 if i == 0 else 2 * place, 2 * place + i]
        for page in (2 * place - 4, jnp.where(even, near, far), jnp.where(even, far, near)):
            numbers += [page, page + 1]
        for spot, number in enumerate(numbers):
            out = jnp.where(line == i * MAXP + spot, jnp.where(number >= first, 1.0, 0.0), out)
        out = jnp.where(line == 2 * MAXP + i, live.astype(jnp.float32), out)
    o_ref[...] = out


def page_flags(facts):
    return pl.pallas_call(
        flags_kernel,
        out_shape=jax.ShapeDtypeStruct((2 * MAXP + 8, PAGE), jnp.float32),
        in_specs=[SMEM],
        out_specs=VMEM,
        name="page_flags",
        **params(48),
    )(facts)


def prompt_kernel(n, low, flags, q_ref, *rest):
    o_ref, keys, values, causal, *probs = rest[-6:]
    head = low + pl.program_id(0)
    spots = [pl.ds(pl.multiple_of((x + head) * HD, HD), HD) for x in (0, n)]
    mine, a, c, d = [[[x[p, at] for at in spots] for p in range(x.shape[0])] for x in rest[:4]]
    b = [[x[p] for x in rest[4:6]] for p in range(2)]
    choose = jnp.full((HD, PAGE), lax.axis_index("tp") % 2 == 0)
    be = [[jnp.where(choose, x, y) for x, y in zip(d[1 + p], b[p])] for p in range(2)]
    row = lax.broadcasted_iota(jnp.int32, (PAGE, PAGE), 0)
    col = lax.broadcasted_iota(jnp.int32, (PAGE, PAGE), 1)
    causal[...] = jnp.where(col <= row, 0.0, LOW)
    one = jnp.ones((PAGE, HD), jnp.bfloat16)
    zero = jnp.zeros((PAGE, HD), jnp.bfloat16)
    lives = [flags[2 * MAXP + i:2 * MAXP + i + 1, :] for i in range(2)]

    for i in range(2):
        stand_in = jnp.broadcast_to(mine[i][0][:, :1], (HD, PAGE))
        pages = [d[0] if i == 0 else mine[0], mine[i], *a, *c, *be]
        for spot, (k, v) in enumerate(pages):
            line = i * MAXP + spot
            seen = jnp.broadcast_to(flags[line:line + 1, :], (PAGE, HD)) > 0.0
            at = slice(spot * PAGE, (spot + 1) * PAGE)
            k = jnp.where(seen, k, stand_in)
            keys[i, :, at] = k
            values[i, at, :HD] = jnp.where(seen, v, zero)
            values[i, at, HD:] = jnp.where(seen, one, zero)

    heads_at_once = ROWS // PAGE
    blocks = [(i, start) for i in range(2) for start in range(0, GROUP, heads_at_once)]

    def queries(i, start):
        return jnp.concatenate(
            [
                q_ref[i * PAGE:(i + 1) * PAGE, h * HD:(h + 1) * HD]
                for h in range(start, start + heads_at_once)
            ],
            axis=0,
        )

    def divided(mixed, live):
        total = mixed[:, HD:]
        near = pl.reciprocal(total, approx=True)
        near = near * (2.0 - total * near)
        token = lax.broadcasted_iota(jnp.int32, (total.shape[0], HD), 0) % PAGE
        return jnp.where(token.astype(jnp.float32) < live, mixed[:, :HD] * near, 0.0).astype(jnp.bfloat16)

    tiles = [slice(t, t + 2 * PAGE) for t in range(0, MAXP * PAGE, 2 * PAGE)]

    def own_scores(query, i, repeat):
        own = dot(query, keys[i, :, tiles[0]]) * EXP2_SCALE
        bias = jnp.concatenate([causal[...]] * repeat, axis=0)
        return jnp.concatenate([own[:, :PAGE], own[:, PAGE:] + bias], axis=1)

    def mix(block, slot, largest):
        i, start = block
        mixed = dot(probs[slot][...], values[i])
        out = divided(mixed, lives[i])
        for number in range(heads_at_once):
            h = start + number
            o_ref[i * PAGE:(i + 1) * PAGE, h * HD:(h + 1) * HD] = out[number * PAGE:(number + 1) * PAGE]
        return jnp.maximum(largest, mixed[:, HD:])

    largest = jnp.zeros((ROWS, HD), jnp.float32)
    for index in range(len(blocks) + 1):
        if index < len(blocks):
            i, slot = blocks[index][0], index % 2
            query = queries(*blocks[index])
            own = own_scores(query, i, heads_at_once)
            top = jnp.max(own, axis=1, keepdims=True)
            probs[slot][:, tiles[0]] = jnp.exp2(own - top).astype(jnp.bfloat16)
        if index > 0:
            largest = mix(blocks[index - 1], 1 - slot if index < len(blocks) else slot, largest)
        if index < len(blocks):
            for at in tiles[1:]:
                other = dot(query, keys[i, :, at]) * EXP2_SCALE
                probs[slot][:, at] = jnp.exp2(other - top).astype(jnp.bfloat16)

    @pl.when(jnp.logical_not(jnp.max(largest) < 1e30))
    def _():
        def one(index, carry):
            i, h = index // GROUP, index % GROUP
            rows = pl.ds(pl.multiple_of(i * PAGE, PAGE), PAGE)
            columns = pl.ds(pl.multiple_of(h * HD, HD), HD)
            query = q_ref[rows, columns]
            scores = [own_scores(query, i, 1)] + [dot(query, keys[i, :, at]) * EXP2_SCALE for at in tiles[1:]]
            top = jnp.max(functools.reduce(jnp.maximum, scores), axis=1, keepdims=True)
            mixed = jnp.zeros((PAGE, 2 * HD), jnp.float32)
            for score, at in zip(scores, tiles):
                mixed = mixed + dot(jnp.exp2(score - top).astype(jnp.bfloat16), values[i, at])
            o_ref[rows, columns] = divided(mixed, jnp.where(i == 0, lives[0], lives[1]))
            return carry

        lax.fori_loop(0, 2 * GROUP, one, 0)


def prompt_heads(base, n, low, high, flags, query, blocks, done):
    tok = query.shape[0]

    wide = pl.BlockSpec((tok, GROUP * HD), lambda j: (0, base + low + j))
    mine, a, b, c, d = blocks
    operands = [flags, query, mine, a, c, d, b, b]
    specs = [VMEM, wide] + [VMEM] * 4
    specs += [pl.BlockSpec((2, HD, PAGE), lambda j, x=x: (0, x + low + j, 0)) for x in (0, n)]
    aliases = {}
    if done is not None:
        aliases = {len(operands): 0}
        operands.append(done)
        specs.append(pl.BlockSpec(memory_space=pl.ANY))
    return pl.pallas_call(
        functools.partial(prompt_kernel, n, low),
        out_shape=jax.ShapeDtypeStruct(query.shape, jnp.bfloat16),
        grid=(high - low,),
        in_specs=specs,
        out_specs=wide,
        scratch_shapes=[
            pltpu.VMEM((2, HD, MAXP * PAGE), jnp.bfloat16),
            pltpu.VMEM((2, MAXP * PAGE, 2 * HD), jnp.bfloat16),
            pltpu.VMEM((PAGE, PAGE), jnp.float32),
            pltpu.VMEM((ROWS, MAXP * PAGE), jnp.bfloat16),
            pltpu.VMEM((ROWS, MAXP * PAGE), jnp.bfloat16),
        ],
        input_output_aliases=aliases,
        name="prompt_attention",
        compiler_params=pltpu.CompilerParams(vmem_limit_bytes=48 << 20),
        cost_estimate=pl.CostEstimate(
            flops=(high - low) * GROUP * tok * MAXP * PAGE * HD * 8,
            bytes_accessed=4 * (high - low) * tok * GROUP * HD,
            transcendentals=0,
        ),
    )(*operands)


def stat_rows(rows):
    return 16 - rows % 16


def choose_kernel(facts, q_ref, o_ref, rows_ref, turned):
    requests, here = q_ref.shape[1], q_ref.shape[2] // HD
    other = 1 - lax.axis_index("section")
    for s in range(STEPS):
        query = q_ref[s].astype(jnp.float32)
        for r in range(requests):
            for h in range(here):
                row = h * STEPS + s
                turned[r, row:row + 1] = query[r:r + 1, h * HD:(h + 1) * HD]
    rows_ref[...] = turned[...].astype(jnp.bfloat16)

    def one(lane, carry):
        for i in range(2):
            owner = page_facts(facts, other, 2 * lane + i)[0]
            o_ref[lane, i] = turned[owner].astype(jnp.bfloat16)
        return carry

    lax.fori_loop(0, o_ref.shape[0], one, 0)


def chosen_queries(facts, query, lanes):
    rows = (query.shape[1], QH // lanes * STEPS, HD)
    return pl.pallas_call(
        choose_kernel,
        out_shape=(
            jax.ShapeDtypeStruct((lanes, 2, *rows[1:]), jnp.bfloat16),
            jax.ShapeDtypeStruct(rows, jnp.bfloat16),
        ),
        in_specs=[SMEM, VMEM],
        out_specs=(VMEM, VMEM),
        scratch_shapes=[pltpu.VMEM(rows, jnp.float32)],
        name="choose_queries",
        **params(32),
    )(facts, query)


def partial_kernel(lanes, facts, q_ref, *rest):
    *packed, o_ref = rest
    split = GROUP // (QH // lanes)
    width = QH // lanes * STEPS
    extra = stat_rows(2 * width)
    half, place = lax.axis_index("section"), lax.axis_index("tp")
    group = GROUP * STEPS
    height = 2 * KVH * group
    lane = lax.broadcasted_iota(jnp.int32, (height, PAGE), 1)
    later = lax.broadcasted_iota(jnp.int32, (height, PAGE), 0) // group % 2 == 1
    spot = lax.broadcasted_iota(jnp.int32, (2 * width, PAGE), 0)
    across = lax.broadcasted_iota(jnp.int32, (2 * width, PAGE), 1)
    line = lax.broadcasted_iota(jnp.int32, (extra, PAGE), 0)
    lives = [page_facts(facts, half, 2 * place + i)[2] for i in range(2)]
    places = [(block, j, n) for block, n in zip(packed, CHUNKS) for j in range(n)]
    scores, values = [], []
    for k, (block, j, n) in enumerate(places):
        for i in range(2):
            query = jnp.concatenate([q_ref[k * split + t, i] for t in range(split)], axis=0)
            scores.append(dot(query, block[i, j * HD:(j + 1) * HD]))
            values.append(block[i, (n + j) * HD:(n + j + 1) * HD])
    score = jnp.concatenate(scores, axis=0) * SCALE
    score = jnp.where(lane < jnp.where(later, lives[1], lives[0]), score, LOW)
    top = jnp.max(score, axis=1, keepdims=True)
    terms = jnp.exp(score - top)
    total = jnp.sum(terms, axis=1, keepdims=True)
    high = terms.astype(jnp.bfloat16)
    low = (terms - high.astype(jnp.float32)).astype(jnp.bfloat16)
    mixed = jnp.concatenate(
        [
            dot(high[m * group:(m + 1) * group], v) + dot(low[m * group:(m + 1) * group], v)
            for m, v in enumerate(values)
        ],
        axis=0,
    ) / total
    sums = top + jnp.log(total)
    for k in range(KVH):
        for t in range(split):
            begins = [(2 * k + i) * group + t * width for i in range(2)]
            both = jnp.concatenate([sums[at:at + width] for at in begins], axis=0)
            turned = jnp.sum(jnp.where(spot == across, both, 0.0), axis=0, keepdims=True)
            first = turned.astype(jnp.bfloat16).astype(jnp.float32)
            rest = turned - first
            second = rest.astype(jnp.bfloat16).astype(jnp.float32)
            stat = jnp.where(line == 0, first, jnp.where(line == 1, second, rest - second))
            stat = jnp.where(line < 3, stat, 0.0)
            block = jnp.concatenate([mixed[at:at + width] for at in begins] + [stat], axis=0)
            o_ref[k * split + t] = block.astype(jnp.bfloat16)


def partial_decode(facts, query, packed, lanes):
    rows = 2 * (QH // lanes) * STEPS
    return pl.pallas_call(
        functools.partial(partial_kernel, lanes),
        out_shape=jax.ShapeDtypeStruct((lanes, rows + stat_rows(rows), HD), jnp.bfloat16),
        in_specs=[SMEM, VMEM] + [VMEM] * len(packed),
        out_specs=VMEM,
        name="partial_decode",
        **params(32),
    )(facts, query, *packed)


def merge_kernel(lanes, facts, parts_ref, q_ref, k_ref, v_ref, o_ref):
    requests = q_ref.shape[0]
    width = (QH // lanes) * STEPS
    other, place = 1 - lax.axis_index("section"), lax.axis_index("tp")
    head = place * (QH // lanes) // GROUP
    spot = lax.broadcasted_iota(jnp.int32, (width, PAGE), 0)
    across = lax.broadcasted_iota(jnp.int32, (width, PAGE), 1)
    step = lax.broadcasted_iota(jnp.int32, (width, 1), 0) % STEPS
    end = 0
    for r in range(requests):
        start, end = end, end + facts[other, r]
        query = q_ref[r].astype(jnp.float32)
        keys = k_ref[r, head].astype(jnp.float32)
        values = v_ref[r, head].astype(jnp.float32)
        tops, vectors = [], []
        for u in range(STEPS):
            score = jnp.sum(query * keys[u:u + 1], axis=1, keepdims=True) * SCALE
            tops.append(jnp.where(u <= step, score, LOW))
            vectors.append(values[u:u + 1])
        for j in range(MAXP):
            page = jnp.minimum(start + j, 2 * lanes - 1)
            block = parts_ref[page // 2].astype(jnp.float32)
            later = jnp.full((width, HD), page % 2 == 1)
            vectors.append(jnp.where(later, block[width:2 * width], block[:width]))
            stat = jnp.sum(block[2 * width:2 * width + 8], axis=0, keepdims=True)
            stat = jnp.sum(
                jnp.where(across - page % 2 * width == spot, stat, 0.0), axis=1, keepdims=True
            )
            tops.append(jnp.where(jnp.full((width, 1), start + j < end), stat, LOW))
        top = functools.reduce(jnp.maximum, tops)
        weights = [jnp.exp(t - top) for t in tops]
        total = functools.reduce(jnp.add, weights)
        mixed = functools.reduce(jnp.add, [w * x for w, x in zip(weights, vectors)])
        o_ref[r] = (mixed / total).astype(jnp.bfloat16)


def merged(facts, parts, query, new_key, new_value, lanes):
    requests = query.shape[0]
    fresh = [
        jnp.transpose(x.reshape(STEPS, requests, KVH, HD), (1, 2, 0, 3)) for x in (new_key, new_value)
    ]
    out = pl.pallas_call(
        functools.partial(merge_kernel, lanes),
        out_shape=jax.ShapeDtypeStruct(query.shape, jnp.bfloat16),
        in_specs=[SMEM, VMEM, VMEM, VMEM, VMEM],
        out_specs=VMEM,
        name="merge_decode",
        **params(32),
    )(facts, parts, query, *fresh)
    out = jnp.transpose(out.reshape(requests, QH // lanes, STEPS, HD), (2, 0, 1, 3))
    return out.reshape(STEPS, requests, QH // lanes * HD)


def other_half(x):
    return lax.ppermute(x, "section", [(0, 1), (1, 0)])


def after(x, *earlier):
    return lax.optimization_barrier((x, *earlier))[0]


def on_device(
    prefill_query, prefill_key, prefill_value, counts, fills, dec_query, dec_key, dec_value
):
    lanes = lax.axis_size("tp")
    query, key, value = prefill_query[0], prefill_key[0], prefill_value[0]
    facts = jnp.concatenate([counts, fills], axis=1)
    flags = page_flags(facts)
    ahead = [(i, i + 2) for i in range(lanes - 2)]
    ahead_again = [(i, i + 2) for i in range(2, lanes - 2)]
    beside = [(i, i + 1) for i in range(0, lanes, 2)]
    trade = [(i, i ^ 1) for i in range(2, lanes)]
    bases = [sum(CHUNKS[:g]) for g in range(len(CHUNKS))]
    mine = []
    for base, n in zip(bases, CHUNKS):
        mine.append(pack(base, n, after(key, *mine), value))

    first_hops = [lax.ppermute(block, "tp", ahead) for block in mine]

    asked = after(dec_query[0], mine[0])
    chosen, dec_rows = chosen_queries(facts, asked, lanes)
    wanted = lax.all_to_all(chosen, "tp", split_axis=0, concat_axis=0, tiled=True)
    b = lax.ppermute(mine[0], "tp", beside)
    parts = partial_decode(facts, other_half(after(wanted, b)), mine, lanes)
    parts = lax.all_to_all(parts, "tp", split_axis=0, concat_axis=0, tiled=True)
    dec_out = merged(facts, other_half(parts), dec_rows, dec_key[0], dec_value[0], lanes)

    received = []
    for g, (block, a) in enumerate(zip(mine, first_hops)):
        if g:
            b = lax.ppermute(after(block, received[0][2]), "tp", beside)
        c = lax.ppermute(after(a, parts) if g else after(a, wanted, mine[1]), "tp", trade)
        d = lax.ppermute(jnp.concatenate([a[1:], c], axis=0), "tp", ahead_again)
        received.append((a, b, c, d))
    out, flags = None, after(flags, received[1][2])
    for g, (base, n) in enumerate(zip(bases, CHUNKS)):
        if g:
            out = after(out, dec_out)
        out = prompt_heads(base, n, 0, n, flags, query, (mine[g], *received[g]), out)
    return (out[None], dec_out[None])


def solution(mesh):
    placed = (
        P("section", ("groups", "tp"), None),
        P("section", ("groups", "tp"), None),
        P("section", ("groups", "tp"), None),
        P(None, "groups"),
        P(None, "groups"),
        P("section", None, "groups", "tp"),
        P("section", None, "groups", None),
        P("section", None, "groups", None),
    )
    return jax.shard_map(
        on_device,
        mesh=mesh,
        in_specs=placed,
        out_specs=(P("section", ("groups", "tp"), None), P("section", None, "groups", "tp")),
        check_vma=False,
    )
```

```python
import functools
import math

import jax
import jax.numpy as jnp
from jax import lax
from jax.experimental import pallas as pl
from jax.experimental.pallas import tpu as pltpu
from jax.sharding import PartitionSpec as P

QH = 64
KVH = 8
HD = 128
PAGE = 128
MAXP = 8
STEPS = 4
GROUP = QH // KVH
SCALE = HD ** (-0.5)
EXP2_SCALE = SCALE * math.log2(math.e)
LOW = -1e30
CHUNKS = (4, 4)
ROWS = 512
SMEM = pl.BlockSpec(memory_space=pltpu.SMEM)
VMEM = pl.BlockSpec(memory_space=pltpu.VMEM)


def dot(a, b):
    return jnp.dot(a, b, preferred_element_type=jnp.float32)


def page_facts(facts, half, page):
    requests = facts.shape[1] // 2
    owner, first, live, end = -1, 0, PAGE, 0
    for r in range(requests):
        start, end = end, end + facts[half, r]
        begun = start <= page
        owner = jnp.where(begun, r, owner)
        first = jnp.where(begun, start, first)
        live = jnp.where(end - 1 == page, facts[half, requests + r], live)
    return owner, first, live


def params(limit):
    return dict(
        compiler_params=pltpu.CompilerParams(vmem_limit_bytes=limit << 20),
        cost_estimate=pl.CostEstimate(flops=1, bytes_accessed=1, transcendentals=0),
    )


def pack_kernel(base, k_ref, v_ref, *rest):
    o_ref, k_part, v_part, sems = rest[-4:]
    n = k_part.shape[1] // HD
    own = slice(base * HD, (base + n) * HD)
    copies = [
        pltpu.make_async_copy(source.at[:, own], part, sems.at[spot])
        for spot, (source, part) in enumerate(((k_ref, k_part), (v_ref, v_part)))
    ]
    for copy in copies:
        copy.start()
    for copy in copies:
        copy.wait()
    for j in range(n):
        columns = slice(j * HD, (j + 1) * HD)
        for p in range(2):
            rows = slice(p * PAGE, (p + 1) * PAGE)
            turned = jnp.transpose(k_part[rows, columns].astype(jnp.float32)).astype(jnp.bfloat16)
            o_ref[p, columns] = turned
            o_ref[p, (n + j) * HD:(n + j + 1) * HD] = v_part[rows, columns]


def pack(base, n, key, value):
    part = pltpu.VMEM((key.shape[0], n * HD), jnp.bfloat16)
    return pl.pallas_call(
        functools.partial(pack_kernel, base),
        out_shape=jax.ShapeDtypeStruct((2, 2 * n * HD, PAGE), jnp.bfloat16),
        in_specs=[pl.BlockSpec(memory_space=pl.ANY)] * 2,
        out_specs=VMEM,
        scratch_shapes=[part, part, pltpu.SemaphoreType.DMA((2,))],
        name="pack",
        **params(48),
    )(key, value)


def flags_kernel(facts, o_ref):
    half, place = lax.axis_index("section"), lax.axis_index("tp")
    even = place % 2 == 0
    near, far = 2 * place - 2, 2 * place - 6
    line = lax.broadcasted_iota(jnp.int32, o_ref.shape, 0)
    out = jnp.zeros(o_ref.shape, jnp.float32)
    for i in range(2):
        _, first, live = page_facts(facts, half, 2 * place + i)
        numbers = [2 * place - 7 if i == 0 else 2 * place, 2 * place + i]
        for page in (2 * place - 4, jnp.where(even, near, far), jnp.where(even, far, near)):
            numbers += [page, page + 1]
        for spot, number in enumerate(numbers):
            out = jnp.where(line == i * MAXP + spot, jnp.where(number >= first, 1.0, 0.0), out)
        out = jnp.where(line == 2 * MAXP + i, live.astype(jnp.float32), out)
    o_ref[...] = out


def page_flags(facts):
    return pl.pallas_call(
        flags_kernel,
        out_shape=jax.ShapeDtypeStruct((2 * MAXP + 8, PAGE), jnp.float32),
        in_specs=[SMEM],
        out_specs=VMEM,
        name="page_flags",
        **params(48),
    )(facts)


def prompt_kernel(n, low, flags, q_ref, *rest):
    o_ref, keys, values, causal, *probs = rest[-6:]
    head = low + pl.program_id(0)
    spots = [pl.ds(pl.multiple_of((x + head) * HD, HD), HD) for x in (0, n)]
    mine, a, c, d = [[[x[p, at] for at in spots] for p in range(x.shape[0])] for x in rest[:4]]
    b = [[x[p] for x in rest[4:6]] for p in range(2)]
    choose = jnp.full((HD, PAGE), lax.axis_index("tp") % 2 == 0)
    be = [[jnp.where(choose, x, y) for x, y in zip(d[1 + p], b[p])] for p in range(2)]
    row = lax.broadcasted_iota(jnp.int32, (PAGE, PAGE), 0)
    col = lax.broadcasted_iota(jnp.int32, (PAGE, PAGE), 1)
    causal[...] = jnp.where(col <= row, 0.0, LOW)
    one = jnp.ones((PAGE, HD), jnp.bfloat16)
    zero = jnp.zeros((PAGE, HD), jnp.bfloat16)
    lives = [flags[2 * MAXP + i:2 * MAXP + i + 1, :] for i in range(2)]

    for i in range(2):
        stand_in = jnp.broadcast_to(mine[i][0][:, :1], (HD, PAGE))
        pages = [d[0] if i == 0 else mine[0], mine[i], *a, *c, *be]
        for spot, (k, v) in enumerate(pages):
            line = i * MAXP + spot
            seen = jnp.broadcast_to(flags[line:line + 1, :], (PAGE, HD)) > 0.0
            at = slice(spot * PAGE, (spot + 1) * PAGE)
            k = jnp.where(seen, k, stand_in)
            keys[i, :, at] = k
            values[i, at, :HD] = jnp.where(seen, v, zero)
            values[i, at, HD:] = jnp.where(seen, one, zero)

    heads_at_once = ROWS // PAGE
    blocks = [(i, start) for i in range(2) for start in range(0, GROUP, heads_at_once)]

    def queries(i, start):
        return jnp.concatenate(
            [
                q_ref[i * PAGE:(i + 1) * PAGE, h * HD:(h + 1) * HD]
                for h in range(start, start + heads_at_once)
            ],
            axis=0,
        )

    def divided(mixed, live):
        total = mixed[:, HD:]
        near = pl.reciprocal(total, approx=True)
        near = near * (2.0 - total * near)
        token = lax.broadcasted_iota(jnp.int32, (total.shape[0], HD), 0) % PAGE
        return jnp.where(token.astype(jnp.float32) < live, mixed[:, :HD] * near, 0.0).astype(jnp.bfloat16)

    tiles = [slice(t, t + 2 * PAGE) for t in range(0, MAXP * PAGE, 2 * PAGE)]

    def own_scores(query, i, repeat):
        own = dot(query, keys[i, :, tiles[0]]) * EXP2_SCALE
        bias = jnp.concatenate([causal[...]] * repeat, axis=0)
        return jnp.concatenate([own[:, :PAGE], own[:, PAGE:] + bias], axis=1)

    def mix(block, slot, largest):
        i, start = block
        mixed = dot(probs[slot][...], values[i])
        out = divided(mixed, lives[i])
        for number in range(heads_at_once):
            h = start + number
            o_ref[i * PAGE:(i + 1) * PAGE, h * HD:(h + 1) * HD] = out[number * PAGE:(number + 1) * PAGE]
        return jnp.maximum(largest, mixed[:, HD:])

    largest = jnp.zeros((ROWS, HD), jnp.float32)
    for index in range(len(blocks) + 1):
        if index < len(blocks):
            i, slot = blocks[index][0], index % 2
            query = queries(*blocks[index])
            own = own_scores(query, i, heads_at_once)
            top = jnp.max(own, axis=1, keepdims=True)
            probs[slot][:, tiles[0]] = jnp.exp2(own - top).astype(jnp.bfloat16)
        if index > 0:
            largest = mix(blocks[index - 1], 1 - slot if index < len(blocks) else slot, largest)
        if index < len(blocks):
            for at in tiles[1:]:
                other = dot(query, keys[i, :, at]) * EXP2_SCALE
                probs[slot][:, at] = jnp.exp2(other - top).astype(jnp.bfloat16)

    @pl.when(jnp.logical_not(jnp.max(largest) < 1e30))
    def _():
        def one(index, carry):
            i, h = index // GROUP, index % GROUP
            rows = pl.ds(pl.multiple_of(i * PAGE, PAGE), PAGE)
            columns = pl.ds(pl.multiple_of(h * HD, HD), HD)
            query = q_ref[rows, columns]
            scores = [own_scores(query, i, 1)] + [dot(query, keys[i, :, at]) * EXP2_SCALE for at in tiles[1:]]
            top = jnp.max(functools.reduce(jnp.maximum, scores), axis=1, keepdims=True)
            mixed = jnp.zeros((PAGE, 2 * HD), jnp.float32)
            for score, at in zip(scores, tiles):
                mixed = mixed + dot(jnp.exp2(score - top).astype(jnp.bfloat16), values[i, at])
            o_ref[rows, columns] = divided(mixed, jnp.where(i == 0, lives[0], lives[1]))
            return carry

        lax.fori_loop(0, 2 * GROUP, one, 0)


def prompt_heads(base, n, low, high, flags, query, blocks, done):
    tok = query.shape[0]

    wide = pl.BlockSpec((tok, GROUP * HD), lambda j: (0, base + low + j))
    mine, a, b, c, d = blocks
    operands = [flags, query, mine, a, c, d, b, b]
    specs = [VMEM, wide] + [VMEM] * 4
    specs += [pl.BlockSpec((2, HD, PAGE), lambda j, x=x: (0, x + low + j, 0)) for x in (0, n)]
    aliases = {}
    if done is not None:
        aliases = {len(operands): 0}
        operands.append(done)
        specs.append(pl.BlockSpec(memory_space=pl.ANY))
    return pl.pallas_call(
        functools.partial(prompt_kernel, n, low),
        out_shape=jax.ShapeDtypeStruct(query.shape, jnp.bfloat16),
        grid=(high - low,),
        in_specs=specs,
        out_specs=wide,
        scratch_shapes=[
            pltpu.VMEM((2, HD, MAXP * PAGE), jnp.bfloat16),
            pltpu.VMEM((2, MAXP * PAGE, 2 * HD), jnp.bfloat16),
            pltpu.VMEM((PAGE, PAGE), jnp.float32),
            pltpu.VMEM((ROWS, MAXP * PAGE), jnp.bfloat16),
            pltpu.VMEM((ROWS, MAXP * PAGE), jnp.bfloat16),
        ],
        input_output_aliases=aliases,
        name="prompt_attention",
        compiler_params=pltpu.CompilerParams(vmem_limit_bytes=48 << 20),
        cost_estimate=pl.CostEstimate(
            flops=(high - low) * GROUP * tok * MAXP * PAGE * HD * 8,
            bytes_accessed=4 * (high - low) * tok * GROUP * HD,
            transcendentals=0,
        ),
    )(*operands)


def stat_rows(rows):
    return 16 - rows % 16


def choose_kernel(facts, q_ref, o_ref, rows_ref, turned):
    requests, here = q_ref.shape[1], q_ref.shape[2] // HD
    other = 1 - lax.axis_index("section")
    for s in range(STEPS):
        query = q_ref[s].astype(jnp.float32)
        for r in range(requests):
            for h in range(here):
                row = h * STEPS + s
                turned[r, row:row + 1] = query[r:r + 1, h * HD:(h + 1) * HD]
    rows_ref[...] = turned[...].astype(jnp.bfloat16)

    def one(lane, carry):
        for i in range(2):
            owner = page_facts(facts, other, 2 * lane + i)[0]
            o_ref[lane, i] = turned[owner].astype(jnp.bfloat16)
        return carry

    lax.fori_loop(0, o_ref.shape[0], one, 0)


def chosen_queries(facts, query, lanes):
    rows = (query.shape[1], QH // lanes * STEPS, HD)
    return pl.pallas_call(
        choose_kernel,
        out_shape=(
            jax.ShapeDtypeStruct((lanes, 2, *rows[1:]), jnp.bfloat16),
            jax.ShapeDtypeStruct(rows, jnp.bfloat16),
        ),
        in_specs=[SMEM, VMEM],
        out_specs=(VMEM, VMEM),
        scratch_shapes=[pltpu.VMEM(rows, jnp.float32)],
        name="choose_queries",
        **params(32),
    )(facts, query)


def partial_kernel(lanes, facts, q_ref, *rest):
    *packed, o_ref = rest
    split = GROUP // (QH // lanes)
    width = QH // lanes * STEPS
    extra = stat_rows(2 * width)
    half, place = lax.axis_index("section"), lax.axis_index("tp")
    group = GROUP * STEPS
    height = 2 * KVH * group
    lane = lax.broadcasted_iota(jnp.int32, (height, PAGE), 1)
    later = lax.broadcasted_iota(jnp.int32, (height, PAGE), 0) // group % 2 == 1
    spot = lax.broadcasted_iota(jnp.int32, (2 * width, PAGE), 0)
    across = lax.broadcasted_iota(jnp.int32, (2 * width, PAGE), 1)
    line = lax.broadcasted_iota(jnp.int32, (extra, PAGE), 0)
    lives = [page_facts(facts, half, 2 * place + i)[2] for i in range(2)]
    places = [(block, j, n) for block, n in zip(packed, CHUNKS) for j in range(n)]
    scores, values = [], []
    for k, (block, j, n) in enumerate(places):
        for i in range(2):
            query = jnp.concatenate([q_ref[k * split + t, i] for t in range(split)], axis=0)
            scores.append(dot(query, block[i, j * HD:(j + 1) * HD]))
            values.append(block[i, (n + j) * HD:(n + j + 1) * HD])
    score = jnp.concatenate(scores, axis=0) * SCALE
    score = jnp.where(lane < jnp.where(later, lives[1], lives[0]), score, LOW)
    top = jnp.max(score, axis=1, keepdims=True)
    terms = jnp.exp(score - top)
    total = jnp.sum(terms, axis=1, keepdims=True)
    high = terms.astype(jnp.bfloat16)
    low = (terms - high.astype(jnp.float32)).astype(jnp.bfloat16)
    mixed = jnp.concatenate(
        [
            dot(high[m * group:(m + 1) * group], v) + dot(low[m * group:(m + 1) * group], v)
            for m, v in enumerate(values)
        ],
        axis=0,
    ) / total
    sums = top + jnp.log(total)
    for k in range(KVH):
        for t in range(split):
            begins = [(2 * k + i) * group + t * width for i in range(2)]
            both = jnp.concatenate([sums[at:at + width] for at in begins], axis=0)
            turned = jnp.sum(jnp.where(spot == across, both, 0.0), axis=0, keepdims=True)
            first = turned.astype(jnp.bfloat16).astype(jnp.float32)
            rest = turned - first
            second = rest.astype(jnp.bfloat16).astype(jnp.float32)
            stat = jnp.where(line == 0, first, jnp.where(line == 1, second, rest - second))
            stat = jnp.where(line < 3, stat, 0.0)
            block = jnp.concatenate([mixed[at:at + width] for at in begins] + [stat], axis=0)
            o_ref[k * split + t] = block.astype(jnp.bfloat16)


def partial_decode(facts, query, packed, lanes):
    rows = 2 * (QH // lanes) * STEPS
    return pl.pallas_call(
        functools.partial(partial_kernel, lanes),
        out_shape=jax.ShapeDtypeStruct((lanes, rows + stat_rows(rows), HD), jnp.bfloat16),
        in_specs=[SMEM, VMEM] + [VMEM] * len(packed),
        out_specs=VMEM,
        name="partial_decode",
        **params(32),
    )(facts, query, *packed)


def merge_kernel(lanes, facts, parts_ref, q_ref, k_ref, v_ref, o_ref):
    requests = q_ref.shape[0]
    width = (QH // lanes) * STEPS
    other, place = 1 - lax.axis_index("section"), lax.axis_index("tp")
    head = place * (QH // lanes) // GROUP
    spot = lax.broadcasted_iota(jnp.int32, (width, PAGE), 0)
    across = lax.broadcasted_iota(jnp.int32, (width, PAGE), 1)
    step = lax.broadcasted_iota(jnp.int32, (width, 1), 0) % STEPS
    end = 0
    for r in range(requests):
        start, end = end, end + facts[other, r]
        query = q_ref[r].astype(jnp.float32)
        keys = k_ref[r, head].astype(jnp.float32)
        values = v_ref[r, head].astype(jnp.float32)
        tops, vectors = [], []
        for u in range(STEPS):
            score = jnp.sum(query * keys[u:u + 1], axis=1, keepdims=True) * SCALE
            tops.append(jnp.where(u <= step, score, LOW))
            vectors.append(values[u:u + 1])
        for j in range(MAXP):
            page = jnp.minimum(start + j, 2 * lanes - 1)
            block = parts_ref[page // 2].astype(jnp.float32)
            later = jnp.full((width, HD), page % 2 == 1)
            vectors.append(jnp.where(later, block[width:2 * width], block[:width]))
            stat = jnp.sum(block[2 * width:2 * width + 8], axis=0, keepdims=True)
            stat = jnp.sum(
                jnp.where(across - page % 2 * width == spot, stat, 0.0), axis=1, keepdims=True
            )
            tops.append(jnp.where(jnp.full((width, 1), start + j < end), stat, LOW))
        top = functools.reduce(jnp.maximum, tops)
        weights = [jnp.exp(t - top) for t in tops]
        total = functools.reduce(jnp.add, weights)
        mixed = functools.reduce(jnp.add, [w * x for w, x in zip(weights, vectors)])
        o_ref[r] = (mixed / total).astype(jnp.bfloat16)


def merged(facts, parts, query, new_key, new_value, lanes):
    requests = query.shape[0]
    fresh = [
        jnp.transpose(x.reshape(STEPS, requests, KVH, HD), (1, 2, 0, 3)) for x in (new_key, new_value)
    ]
    out = pl.pallas_call(
        functools.partial(merge_kernel, lanes),
        out_shape=jax.ShapeDtypeStruct(query.shape, jnp.bfloat16),
        in_specs=[SMEM, VMEM, VMEM, VMEM, VMEM],
        out_specs=VMEM,
        name="merge_decode",
        **params(32),
    )(facts, parts, query, *fresh)
    out = jnp.transpose(out.reshape(requests, QH // lanes, STEPS, HD), (2, 0, 1, 3))
    return out.reshape(STEPS, requests, QH // lanes * HD)


def other_half(x):
    return lax.ppermute(x, "section", [(0, 1), (1, 0)])


def after(x, *earlier):
    return lax.optimization_barrier((x, *earlier))[0]


def on_device(
    prefill_query, prefill_key, prefill_value, counts, fills, dec_query, dec_key, dec_value
):
    lanes = lax.axis_size("tp")
    query, key, value = prefill_query[0], prefill_key[0], prefill_value[0]
    facts = jnp.concatenate([counts, fills], axis=1)
    flags = page_flags(facts)
    ahead = [(i, i + 2) for i in range(lanes - 2)]
    ahead_again = [(i, i + 2) for i in range(2, lanes - 2)]
    beside = [(i, i + 1) for i in range(0, lanes, 2)]
    trade = [(i, i ^ 1) for i in range(2, lanes)]
    bases = [sum(CHUNKS[:g]) for g in range(len(CHUNKS))]
    mine = []
    for base, n in zip(bases, CHUNKS):
        mine.append(pack(base, n, after(key, *mine), value))

    first_hops = [lax.ppermute(block, "tp", ahead) for block in mine]

    asked = after(dec_query[0], mine[0])
    chosen, dec_rows = chosen_queries(facts, asked, lanes)
    wanted = lax.all_to_all(chosen, "tp", split_axis=0, concat_axis=0, tiled=True)
    b = lax.ppermute(mine[0], "tp", beside)
    parts = after(partial_decode(facts, other_half(wanted), mine, lanes), b)
    parts = lax.all_to_all(parts, "tp", split_axis=0, concat_axis=0, tiled=True)
    dec_out = merged(facts, other_half(parts), dec_rows, dec_key[0], dec_value[0], lanes)

    received = []
    for g, (block, a) in enumerate(zip(mine, first_hops)):
        if g:
            b = lax.ppermute(after(block, received[0][2]), "tp", beside)
        c = lax.ppermute(after(a, parts) if g else after(a, wanted, mine[1]), "tp", trade)
        d = lax.ppermute(jnp.concatenate([a[1:], c], axis=0), "tp", ahead_again)
        received.append((a, b, c, d))
    out, flags = None, after(flags, received[1][2])
    for g, (base, n) in enumerate(zip(bases, CHUNKS)):
        if g:
            out = after(out, dec_out)
        out = prompt_heads(base, n, 0, n, flags, query, (mine[g], *received[g]), out)
    return (out[None], dec_out[None])


def solution(mesh):
    placed = (
        P("section", ("groups", "tp"), None),
        P("section", ("groups", "tp"), None),
        P("section", ("groups", "tp"), None),
        P(None, "groups"),
        P(None, "groups"),
        P("section", None, "groups", "tp"),
        P("section", None, "groups", None),
        P("section", None, "groups", None),
    )
    return jax.shard_map(
        on_device,
        mesh=mesh,
        in_specs=placed,
        out_specs=(P("section", ("groups", "tp"), None), P("section", None, "groups", "tp")),
        check_vma=False,
    )
```

```python
import functools
import math

import jax
import jax.numpy as jnp
from jax import lax
from jax.experimental import pallas as pl
from jax.experimental.pallas import tpu as pltpu
from jax.sharding import PartitionSpec as P

QH = 64
KVH = 8
HD = 128
PAGE = 128
MAXP = 8
STEPS = 4
GROUP = QH // KVH
SCALE = HD ** (-0.5)
EXP2_SCALE = SCALE * math.log2(math.e)
LOW = -1e30
CHUNKS = (4, 4)
ROWS = 512
SMEM = pl.BlockSpec(memory_space=pltpu.SMEM)
VMEM = pl.BlockSpec(memory_space=pltpu.VMEM)


def dot(a, b):
    return jnp.dot(a, b, preferred_element_type=jnp.float32)


def page_facts(facts, half, page):
    requests = facts.shape[1] // 2
    owner, first, live, end = -1, 0, PAGE, 0
    for r in range(requests):
        start, end = end, end + facts[half, r]
        begun = start <= page
        owner = jnp.where(begun, r, owner)
        first = jnp.where(begun, start, first)
        live = jnp.where(end - 1 == page, facts[half, requests + r], live)
    return owner, first, live


def params(limit):
    return dict(
        compiler_params=pltpu.CompilerParams(vmem_limit_bytes=limit << 20),
        cost_estimate=pl.CostEstimate(flops=1, bytes_accessed=1, transcendentals=0),
    )


def pack_kernel(base, k_ref, v_ref, *rest):
    o_ref, k_part, v_part, sems = rest[-4:]
    n = k_part.shape[1] // HD
    own = slice(base * HD, (base + n) * HD)
    copies = [
        pltpu.make_async_copy(source.at[:, own], part, sems.at[spot])
        for spot, (source, part) in enumerate(((k_ref, k_part), (v_ref, v_part)))
    ]
    for copy in copies:
        copy.start()
    for copy in copies:
        copy.wait()
    for j in range(n):
        columns = slice(j * HD, (j + 1) * HD)
        for p in range(2):
            rows = slice(p * PAGE, (p + 1) * PAGE)
            turned = jnp.transpose(k_part[rows, columns].astype(jnp.float32)).astype(jnp.bfloat16)
            o_ref[p, columns] = turned
            o_ref[p, (n + j) * HD:(n + j + 1) * HD] = v_part[rows, columns]


def pack(base, n, key, value):
    part = pltpu.VMEM((key.shape[0], n * HD), jnp.bfloat16)
    return pl.pallas_call(
        functools.partial(pack_kernel, base),
        out_shape=jax.ShapeDtypeStruct((2, 2 * n * HD, PAGE), jnp.bfloat16),
        in_specs=[pl.BlockSpec(memory_space=pl.ANY)] * 2,
        out_specs=VMEM,
        scratch_shapes=[part, part, pltpu.SemaphoreType.DMA((2,))],
        name="pack",
        **params(48),
    )(key, value)


def flags_kernel(facts, o_ref):
    half, place = lax.axis_index("section"), lax.axis_index("tp")
    even = place % 2 == 0
    near, far = 2 * place - 2, 2 * place - 6
    line = lax.broadcasted_iota(jnp.int32, o_ref.shape, 0)
    out = jnp.zeros(o_ref.shape, jnp.float32)
    for i in range(2):
        _, first, live = page_facts(facts, half, 2 * place + i)
        numbers = [2 * place - 7 if i == 0 else 2 * place, 2 * place + i]
        for page in (2 * place - 4, jnp.where(even, near, far), jnp.where(even, far, near)):
            numbers += [page, page + 1]
        for spot, number in enumerate(numbers):
            out = jnp.where(line == i * MAXP + spot, jnp.where(number >= first, 1.0, 0.0), out)
        out = jnp.where(line == 2 * MAXP + i, live.astype(jnp.float32), out)
    o_ref[...] = out


def page_flags(facts):
    return pl.pallas_call(
        flags_kernel,
        out_shape=jax.ShapeDtypeStruct((2 * MAXP + 8, PAGE), jnp.float32),
        in_specs=[SMEM],
        out_specs=VMEM,
        name="page_flags",
        **params(48),
    )(facts)


def prompt_kernel(n, low, flags, q_ref, *rest):
    o_ref, keys, values, causal, *probs = rest[-6:]
    head = low + pl.program_id(0)
    spots = [pl.ds(pl.multiple_of((x + head) * HD, HD), HD) for x in (0, n)]
    mine, a, c, d = [[[x[p, at] for at in spots] for p in range(x.shape[0])] for x in rest[:4]]
    b = [[x[p] for x in rest[4:6]] for p in range(2)]
    choose = jnp.full((HD, PAGE), lax.axis_index("tp") % 2 == 0)
    be = [[jnp.where(choose, x, y) for x, y in zip(d[1 + p], b[p])] for p in range(2)]
    row = lax.broadcasted_iota(jnp.int32, (PAGE, PAGE), 0)
    col = lax.broadcasted_iota(jnp.int32, (PAGE, PAGE), 1)
    causal[...] = jnp.where(col <= row, 0.0, LOW)
    one = jnp.ones((PAGE, HD), jnp.bfloat16)
    zero = jnp.zeros((PAGE, HD), jnp.bfloat16)
    lives = [flags[2 * MAXP + i:2 * MAXP + i + 1, :] for i in range(2)]

    for i in range(2):
        stand_in = jnp.broadcast_to(mine[i][0][:, :1], (HD, PAGE))
        pages = [d[0] if i == 0 else mine[0], mine[i], *a, *c, *be]
        for spot, (k, v) in enumerate(pages):
            line = i * MAXP + spot
            seen = jnp.broadcast_to(flags[line:line + 1, :], (PAGE, HD)) > 0.0
            at = slice(spot * PAGE, (spot + 1) * PAGE)
            k = jnp.where(seen, k, stand_in)
            keys[i, :, at] = k
            values[i, at, :HD] = jnp.where(seen, v, zero)
            values[i, at, HD:] = jnp.where(seen, one, zero)

    heads_at_once = ROWS // PAGE
    blocks = [(i, start) for i in range(2) for start in range(0, GROUP, heads_at_once)]

    def queries(i, start):
        return jnp.concatenate(
            [
                q_ref[i * PAGE:(i + 1) * PAGE, h * HD:(h + 1) * HD]
                for h in range(start, start + heads_at_once)
            ],
            axis=0,
        )

    def divided(mixed, live):
        total = mixed[:, HD:]
        near = pl.reciprocal(total, approx=True)
        near = near * (2.0 - total * near)
        token = lax.broadcasted_iota(jnp.int32, (total.shape[0], HD), 0) % PAGE
        return jnp.where(token.astype(jnp.float32) < live, mixed[:, :HD] * near, 0.0).astype(jnp.bfloat16)

    tiles = [slice(t, t + 2 * PAGE) for t in range(0, MAXP * PAGE, 2 * PAGE)]

    def own_scores(query, i, repeat):
        own = dot(query, keys[i, :, tiles[0]]) * EXP2_SCALE
        bias = jnp.concatenate([causal[...]] * repeat, axis=0)
        return jnp.concatenate([own[:, :PAGE], own[:, PAGE:] + bias], axis=1)

    def mix(block, slot, largest):
        i, start = block
        mixed = dot(probs[slot][...], values[i])
        out = divided(mixed, lives[i])
        for number in range(heads_at_once):
            h = start + number
            o_ref[i * PAGE:(i + 1) * PAGE, h * HD:(h + 1) * HD] = out[number * PAGE:(number + 1) * PAGE]
        return jnp.maximum(largest, mixed[:, HD:])

    largest = jnp.zeros((ROWS, HD), jnp.float32)
    for index in range(len(blocks) + 1):
        if index < len(blocks):
            i, slot = blocks[index][0], index % 2
            query = queries(*blocks[index])
            own = own_scores(query, i, heads_at_once)
            top = jnp.max(own, axis=1, keepdims=True)
            probs[slot][:, tiles[0]] = jnp.exp2(own - top).astype(jnp.bfloat16)
        if index > 0:
            largest = mix(blocks[index - 1], 1 - slot if index < len(blocks) else slot, largest)
        if index < len(blocks):
            for at in tiles[1:]:
                other = dot(query, keys[i, :, at]) * EXP2_SCALE
                probs[slot][:, at] = jnp.exp2(other - top).astype(jnp.bfloat16)

    @pl.when(jnp.logical_not(jnp.max(largest) < 1e30))
    def _():
        def one(index, carry):
            i, h = index // GROUP, index % GROUP
            rows = pl.ds(pl.multiple_of(i * PAGE, PAGE), PAGE)
            columns = pl.ds(pl.multiple_of(h * HD, HD), HD)
            query = q_ref[rows, columns]
            scores = [own_scores(query, i, 1)] + [dot(query, keys[i, :, at]) * EXP2_SCALE for at in tiles[1:]]
            top = jnp.max(functools.reduce(jnp.maximum, scores), axis=1, keepdims=True)
            mixed = jnp.zeros((PAGE, 2 * HD), jnp.float32)
            for score, at in zip(scores, tiles):
                mixed = mixed + dot(jnp.exp2(score - top).astype(jnp.bfloat16), values[i, at])
            o_ref[rows, columns] = divided(mixed, jnp.where(i == 0, lives[0], lives[1]))
            return carry

        lax.fori_loop(0, 2 * GROUP, one, 0)


def prompt_heads(base, n, low, high, flags, query, blocks, done):
    tok = query.shape[0]

    wide = pl.BlockSpec((tok, GROUP * HD), lambda j: (0, base + low + j))
    mine, a, b, c, d = blocks
    operands = [flags, query, mine, a, c, d, b, b]
    specs = [VMEM, wide] + [VMEM] * 4
    specs += [pl.BlockSpec((2, HD, PAGE), lambda j, x=x: (0, x + low + j, 0)) for x in (0, n)]
    aliases = {}
    if done is not None:
        aliases = {len(operands): 0}
        operands.append(done)
        specs.append(pl.BlockSpec(memory_space=pl.ANY))
    return pl.pallas_call(
        functools.partial(prompt_kernel, n, low),
        out_shape=jax.ShapeDtypeStruct(query.shape, jnp.bfloat16),
        grid=(high - low,),
        in_specs=specs,
        out_specs=wide,
        scratch_shapes=[
            pltpu.VMEM((2, HD, MAXP * PAGE), jnp.bfloat16),
            pltpu.VMEM((2, MAXP * PAGE, 2 * HD), jnp.bfloat16),
            pltpu.VMEM((PAGE, PAGE), jnp.float32),
            pltpu.VMEM((ROWS, MAXP * PAGE), jnp.bfloat16),
            pltpu.VMEM((ROWS, MAXP * PAGE), jnp.bfloat16),
        ],
        input_output_aliases=aliases,
        name="prompt_attention",
        compiler_params=pltpu.CompilerParams(vmem_limit_bytes=48 << 20),
        cost_estimate=pl.CostEstimate(
            flops=(high - low) * GROUP * tok * MAXP * PAGE * HD * 8,
            bytes_accessed=4 * (high - low) * tok * GROUP * HD,
            transcendentals=0,
        ),
    )(*operands)


def stat_rows(rows):
    return 16 - rows % 16


def choose_kernel(facts, q_ref, o_ref, rows_ref, turned):
    requests, here = q_ref.shape[1], q_ref.shape[2] // HD
    other = 1 - lax.axis_index("section")
    for s in range(STEPS):
        query = q_ref[s].astype(jnp.float32)
        for r in range(requests):
            for h in range(here):
                row = h * STEPS + s
                turned[r, row:row + 1] = query[r:r + 1, h * HD:(h + 1) * HD]
    rows_ref[...] = turned[...].astype(jnp.bfloat16)

    def one(lane, carry):
        for i in range(2):
            owner = page_facts(facts, other, 2 * lane + i)[0]
            o_ref[lane, i] = turned[owner].astype(jnp.bfloat16)
        return carry

    lax.fori_loop(0, o_ref.shape[0], one, 0)


def chosen_queries(facts, query, lanes):
    rows = (query.shape[1], QH // lanes * STEPS, HD)
    return pl.pallas_call(
        choose_kernel,
        out_shape=(
            jax.ShapeDtypeStruct((lanes, 2, *rows[1:]), jnp.bfloat16),
            jax.ShapeDtypeStruct(rows, jnp.bfloat16),
        ),
        in_specs=[SMEM, VMEM],
        out_specs=(VMEM, VMEM),
        scratch_shapes=[pltpu.VMEM(rows, jnp.float32)],
        name="choose_queries",
        **params(32),
    )(facts, query)


def partial_kernel(lanes, facts, q_ref, *rest):
    *packed, o_ref = rest
    split = GROUP // (QH // lanes)
    width = QH // lanes * STEPS
    extra = stat_rows(2 * width)
    half, place = lax.axis_index("section"), lax.axis_index("tp")
    group = GROUP * STEPS
    height = 2 * KVH * group
    lane = lax.broadcasted_iota(jnp.int32, (height, PAGE), 1)
    later = lax.broadcasted_iota(jnp.int32, (height, PAGE), 0) // group % 2 == 1
    spot = lax.broadcasted_iota(jnp.int32, (2 * width, PAGE), 0)
    across = lax.broadcasted_iota(jnp.int32, (2 * width, PAGE), 1)
    line = lax.broadcasted_iota(jnp.int32, (extra, PAGE), 0)
    lives = [page_facts(facts, half, 2 * place + i)[2] for i in range(2)]
    places = [(block, j, n) for block, n in zip(packed, CHUNKS) for j in range(n)]
    scores, values = [], []
    for k, (block, j, n) in enumerate(places):
        for i in range(2):
            query = jnp.concatenate([q_ref[k * split + t, i] for t in range(split)], axis=0)
            scores.append(dot(query, block[i, j * HD:(j + 1) * HD]))
            values.append(block[i, (n + j) * HD:(n + j + 1) * HD])
    score = jnp.concatenate(scores, axis=0) * SCALE
    score = jnp.where(lane < jnp.where(later, lives[1], lives[0]), score, LOW)
    top = jnp.max(score, axis=1, keepdims=True)
    terms = jnp.exp(score - top)
    total = jnp.sum(terms, axis=1, keepdims=True)
    high = terms.astype(jnp.bfloat16)
    low = (terms - high.astype(jnp.float32)).astype(jnp.bfloat16)
    mixed = jnp.concatenate(
        [
            dot(high[m * group:(m + 1) * group], v) + dot(low[m * group:(m + 1) * group], v)
            for m, v in enumerate(values)
        ],
        axis=0,
    ) / total
    sums = top + jnp.log(total)
    for k in range(KVH):
        for t in range(split):
            begins = [(2 * k + i) * group + t * width for i in range(2)]
            both = jnp.concatenate([sums[at:at + width] for at in begins], axis=0)
            turned = jnp.sum(jnp.where(spot == across, both, 0.0), axis=0, keepdims=True)
            first = turned.astype(jnp.bfloat16).astype(jnp.float32)
            rest = turned - first
            second = rest.astype(jnp.bfloat16).astype(jnp.float32)
            stat = jnp.where(line == 0, first, jnp.where(line == 1, second, rest - second))
            stat = jnp.where(line < 3, stat, 0.0)
            block = jnp.concatenate([mixed[at:at + width] for at in begins] + [stat], axis=0)
            o_ref[k * split + t] = block.astype(jnp.bfloat16)


def partial_decode(facts, query, packed, lanes):
    rows = 2 * (QH // lanes) * STEPS
    return pl.pallas_call(
        functools.partial(partial_kernel, lanes),
        out_shape=jax.ShapeDtypeStruct((lanes, rows + stat_rows(rows), HD), jnp.bfloat16),
        in_specs=[SMEM, VMEM] + [VMEM] * len(packed),
        out_specs=VMEM,
        name="partial_decode",
        **params(32),
    )(facts, query, *packed)


def merge_kernel(lanes, facts, parts_ref, q_ref, k_ref, v_ref, o_ref):
    requests = q_ref.shape[0]
    width = (QH // lanes) * STEPS
    other, place = 1 - lax.axis_index("section"), lax.axis_index("tp")
    head = place * (QH // lanes) // GROUP
    spot = lax.broadcasted_iota(jnp.int32, (width, PAGE), 0)
    across = lax.broadcasted_iota(jnp.int32, (width, PAGE), 1)
    step = lax.broadcasted_iota(jnp.int32, (width, 1), 0) % STEPS
    end = 0
    for r in range(requests):
        start, end = end, end + facts[other, r]
        query = q_ref[r].astype(jnp.float32)
        keys = k_ref[r, head].astype(jnp.float32)
        values = v_ref[r, head].astype(jnp.float32)
        tops, vectors = [], []
        for u in range(STEPS):
            score = jnp.sum(query * keys[u:u + 1], axis=1, keepdims=True) * SCALE
            tops.append(jnp.where(u <= step, score, LOW))
            vectors.append(values[u:u + 1])
        for j in range(MAXP):
            page = jnp.minimum(start + j, 2 * lanes - 1)
            block = parts_ref[page // 2].astype(jnp.float32)
            later = jnp.full((width, HD), page % 2 == 1)
            vectors.append(jnp.where(later, block[width:2 * width], block[:width]))
            stat = jnp.sum(block[2 * width:2 * width + 8], axis=0, keepdims=True)
            stat = jnp.sum(
                jnp.where(across - page % 2 * width == spot, stat, 0.0), axis=1, keepdims=True
            )
            tops.append(jnp.where(jnp.full((width, 1), start + j < end), stat, LOW))
        top = functools.reduce(jnp.maximum, tops)
        weights = [jnp.exp(t - top) for t in tops]
        total = functools.reduce(jnp.add, weights)
        mixed = functools.reduce(jnp.add, [w * x for w, x in zip(weights, vectors)])
        o_ref[r] = (mixed / total).astype(jnp.bfloat16)


def merged(facts, parts, query, new_key, new_value, lanes):
    requests = query.shape[0]
    fresh = [
        jnp.transpose(x.reshape(STEPS, requests, KVH, HD), (1, 2, 0, 3)) for x in (new_key, new_value)
    ]
    out = pl.pallas_call(
        functools.partial(merge_kernel, lanes),
        out_shape=jax.ShapeDtypeStruct(query.shape, jnp.bfloat16),
        in_specs=[SMEM, VMEM, VMEM, VMEM, VMEM],
        out_specs=VMEM,
        name="merge_decode",
        **params(32),
    )(facts, parts, query, *fresh)
    out = jnp.transpose(out.reshape(requests, QH // lanes, STEPS, HD), (2, 0, 1, 3))
    return out.reshape(STEPS, requests, QH // lanes * HD)


def other_half(x):
    return lax.ppermute(x, "section", [(0, 1), (1, 0)])


def after(x, *earlier):
    return lax.optimization_barrier((x, *earlier))[0]


def on_device(
    prefill_query, prefill_key, prefill_value, counts, fills, dec_query, dec_key, dec_value
):
    lanes = lax.axis_size("tp")
    query, key, value = prefill_query[0], prefill_key[0], prefill_value[0]
    facts = jnp.concatenate([counts, fills], axis=1)
    flags = page_flags(facts)
    ahead = [(i, i + 2) for i in range(lanes - 2)]
    ahead_again = [(i, i + 2) for i in range(2, lanes - 2)]
    beside = [(i, i + 1) for i in range(0, lanes, 2)]
    trade = [(i, i ^ 1) for i in range(2, lanes)]
    bases = [sum(CHUNKS[:g]) for g in range(len(CHUNKS))]
    mine = []
    for base, n in zip(bases, CHUNKS):
        mine.append(pack(base, n, after(key, *mine), value))

    first_hops = [lax.ppermute(block, "tp", ahead) for block in mine]

    asked = after(dec_query[0], mine[0])
    chosen, dec_rows = chosen_queries(facts, asked, lanes)
    wanted = lax.all_to_all(chosen, "tp", split_axis=0, concat_axis=0, tiled=True)
    b = lax.ppermute(mine[0], "tp", beside)
    parts = after(partial_decode(facts, other_half(wanted), mine, lanes), b)
    parts = lax.all_to_all(parts, "tp", split_axis=0, concat_axis=0, tiled=True)
    dec_out = merged(facts, other_half(parts), dec_rows, dec_key[0], dec_value[0], lanes)

    received = []
    for g, (block, a) in enumerate(zip(mine, first_hops)):
        if g:
            b = lax.ppermute(after(block, received[0][2]), "tp", beside)
        c = lax.ppermute(after(a, parts) if g else after(a, wanted, b, mine[1]), "tp", trade)
        d = lax.ppermute(jnp.concatenate([a[1:], c], axis=0), "tp", ahead_again)
        received.append((a, b, c, d))
    out, flags = None, after(flags, received[1][2])
    for g, (base, n) in enumerate(zip(bases, CHUNKS)):
        if g:
            out = after(out, dec_out)
        out = prompt_heads(base, n, 0, n, flags, query, (mine[g], *received[g]), out)
    return (out[None], dec_out[None])


def solution(mesh):
    placed = (
        P("section", ("groups", "tp"), None),
        P("section", ("groups", "tp"), None),
        P("section", ("groups", "tp"), None),
        P(None, "groups"),
        P(None, "groups"),
        P("section", None, "groups", "tp"),
        P("section", None, "groups", None),
        P("section", None, "groups", None),
    )
    return jax.shard_map(
        on_device,
        mesh=mesh,
        in_specs=placed,
        out_specs=(P("section", ("groups", "tp"), None), P("section", None, "groups", "tp")),
        check_vma=False,
    )
```

```python
import functools
import math

import jax
import jax.numpy as jnp
from jax import lax
from jax.experimental import pallas as pl
from jax.experimental.pallas import tpu as pltpu
from jax.sharding import PartitionSpec as P

QH = 64
KVH = 8
HD = 128
PAGE = 128
MAXP = 8
STEPS = 4
GROUP = QH // KVH
SCALE = HD ** (-0.5)
EXP2_SCALE = SCALE * math.log2(math.e)
LOW = -1e30
CHUNKS = (4, 4)
ROWS = 512
SMEM = pl.BlockSpec(memory_space=pltpu.SMEM)
VMEM = pl.BlockSpec(memory_space=pltpu.VMEM)


def dot(a, b):
    return jnp.dot(a, b, preferred_element_type=jnp.float32)


def page_facts(facts, half, page):
    requests = facts.shape[1] // 2
    owner, first, live, end = -1, 0, PAGE, 0
    for r in range(requests):
        start, end = end, end + facts[half, r]
        begun = start <= page
        owner = jnp.where(begun, r, owner)
        first = jnp.where(begun, start, first)
        live = jnp.where(end - 1 == page, facts[half, requests + r], live)
    return owner, first, live


def params(limit):
    return dict(
        compiler_params=pltpu.CompilerParams(vmem_limit_bytes=limit << 20),
        cost_estimate=pl.CostEstimate(flops=1, bytes_accessed=1, transcendentals=0),
    )


def pack_kernel(base, k_ref, v_ref, *rest):
    o_ref, k_part, v_part, sems = rest[-4:]
    n = k_part.shape[1] // HD
    own = slice(base * HD, (base + n) * HD)
    copies = [
        pltpu.make_async_copy(source.at[:, own], part, sems.at[spot])
        for spot, (source, part) in enumerate(((k_ref, k_part), (v_ref, v_part)))
    ]
    for copy in copies:
        copy.start()
    for copy in copies:
        copy.wait()
    for j in range(n):
        columns = slice(j * HD, (j + 1) * HD)
        for p in range(2):
            rows = slice(p * PAGE, (p + 1) * PAGE)
            turned = jnp.transpose(k_part[rows, columns].astype(jnp.float32)).astype(jnp.bfloat16)
            o_ref[p, columns] = turned
            o_ref[p, (n + j) * HD:(n + j + 1) * HD] = v_part[rows, columns]


def pack(base, n, key, value):
    part = pltpu.VMEM((key.shape[0], n * HD), jnp.bfloat16)
    return pl.pallas_call(
        functools.partial(pack_kernel, base),
        out_shape=jax.ShapeDtypeStruct((2, 2 * n * HD, PAGE), jnp.bfloat16),
        in_specs=[pl.BlockSpec(memory_space=pl.ANY)] * 2,
        out_specs=VMEM,
        scratch_shapes=[part, part, pltpu.SemaphoreType.DMA((2,))],
        name="pack",
        **params(12),
    )(key, value)


def flags_kernel(facts, o_ref):
    half, place = lax.axis_index("section"), lax.axis_index("tp")
    even = place % 2 == 0
    near, far = 2 * place - 2, 2 * place - 6
    line = lax.broadcasted_iota(jnp.int32, o_ref.shape, 0)
    out = jnp.zeros(o_ref.shape, jnp.float32)
    for i in range(2):
        _, first, live = page_facts(facts, half, 2 * place + i)
        numbers = [2 * place - 7 if i == 0 else 2 * place, 2 * place + i]
        for page in (2 * place - 4, jnp.where(even, near, far), jnp.where(even, far, near)):
            numbers += [page, page + 1]
        for spot, number in enumerate(numbers):
            out = jnp.where(line == i * MAXP + spot, jnp.where(number >= first, 1.0, 0.0), out)
        out = jnp.where(line == 2 * MAXP + i, live.astype(jnp.float32), out)
    o_ref[...] = out


def page_flags(facts):
    return pl.pallas_call(
        flags_kernel,
        out_shape=jax.ShapeDtypeStruct((2 * MAXP + 8, PAGE), jnp.float32),
        in_specs=[SMEM],
        out_specs=VMEM,
        name="page_flags",
        **params(12),
    )(facts)


def prompt_kernel(n, low, flags, q_ref, *rest):
    o_ref, keys, values, causal, *probs = rest[-6:]
    head = low + pl.program_id(0)
    spots = [pl.ds(pl.multiple_of((x + head) * HD, HD), HD) for x in (0, n)]
    mine, a, c, d = [[[x[p, at] for at in spots] for p in range(x.shape[0])] for x in rest[:4]]
    b = [[x[p] for x in rest[4:6]] for p in range(2)]
    choose = jnp.full((HD, PAGE), lax.axis_index("tp") % 2 == 0)
    be = [[jnp.where(choose, x, y) for x, y in zip(d[1 + p], b[p])] for p in range(2)]
    row = lax.broadcasted_iota(jnp.int32, (PAGE, PAGE), 0)
    col = lax.broadcasted_iota(jnp.int32, (PAGE, PAGE), 1)
    causal[...] = jnp.where(col <= row, 0.0, LOW)
    one = jnp.ones((PAGE, HD), jnp.bfloat16)
    zero = jnp.zeros((PAGE, HD), jnp.bfloat16)
    lives = [flags[2 * MAXP + i:2 * MAXP + i + 1, :] for i in range(2)]

    for i in range(2):
        stand_in = jnp.broadcast_to(mine[i][0][:, :1], (HD, PAGE))
        pages = [d[0] if i == 0 else mine[0], mine[i], *a, *c, *be]
        for spot, (k, v) in enumerate(pages):
            line = i * MAXP + spot
            seen = jnp.broadcast_to(flags[line:line + 1, :], (PAGE, HD)) > 0.0
            at = slice(spot * PAGE, (spot + 1) * PAGE)
            k = jnp.where(seen, k, stand_in)
            keys[i, :, at] = k
            values[i, at, :HD] = jnp.where(seen, v, zero)
            values[i, at, HD:] = jnp.where(seen, one, zero)

    heads_at_once = ROWS // PAGE
    blocks = [(i, start) for i in range(2) for start in range(0, GROUP, heads_at_once)]

    def queries(i, start):
        return jnp.concatenate(
            [
                q_ref[i * PAGE:(i + 1) * PAGE, h * HD:(h + 1) * HD]
                for h in range(start, start + heads_at_once)
            ],
            axis=0,
        )

    def divided(mixed, live):
        total = mixed[:, HD:]
        near = pl.reciprocal(total, approx=True)
        near = near * (2.0 - total * near)
        token = lax.broadcasted_iota(jnp.int32, (total.shape[0], HD), 0) % PAGE
        return jnp.where(token.astype(jnp.float32) < live, mixed[:, :HD] * near, 0.0).astype(jnp.bfloat16)

    tiles = [slice(t, t + 2 * PAGE) for t in range(0, MAXP * PAGE, 2 * PAGE)]

    def own_scores(query, i, repeat):
        own = dot(query, keys[i, :, tiles[0]]) * EXP2_SCALE
        bias = jnp.concatenate([causal[...]] * repeat, axis=0)
        return jnp.concatenate([own[:, :PAGE], own[:, PAGE:] + bias], axis=1)

    def mix(block, slot, largest):
        i, start = block
        mixed = dot(probs[slot][...], values[i])
        out = divided(mixed, lives[i])
        for number in range(heads_at_once):
            h = start + number
            o_ref[i * PAGE:(i + 1) * PAGE, h * HD:(h + 1) * HD] = out[number * PAGE:(number + 1) * PAGE]
        return jnp.maximum(largest, mixed[:, HD:])

    largest = jnp.zeros((ROWS, HD), jnp.float32)
    for index in range(len(blocks) + 1):
        if index < len(blocks):
            i, slot = blocks[index][0], index % 2
            query = queries(*blocks[index])
            own = own_scores(query, i, heads_at_once)
            top = jnp.max(own, axis=1, keepdims=True)
            probs[slot][:, tiles[0]] = jnp.exp2(own - top).astype(jnp.bfloat16)
        if index > 0:
            largest = mix(blocks[index - 1], 1 - slot if index < len(blocks) else slot, largest)
        if index < len(blocks):
            for at in tiles[1:]:
                other = dot(query, keys[i, :, at]) * EXP2_SCALE
                probs[slot][:, at] = jnp.exp2(other - top).astype(jnp.bfloat16)

    @pl.when(jnp.logical_not(jnp.max(largest) < 1e30))
    def _():
        def one(index, carry):
            i, h = index // GROUP, index % GROUP
            rows = pl.ds(pl.multiple_of(i * PAGE, PAGE), PAGE)
            columns = pl.ds(pl.multiple_of(h * HD, HD), HD)
            query = q_ref[rows, columns]
            scores = [own_scores(query, i, 1)] + [dot(query, keys[i, :, at]) * EXP2_SCALE for at in tiles[1:]]
            top = jnp.max(functools.reduce(jnp.maximum, scores), axis=1, keepdims=True)
            mixed = jnp.zeros((PAGE, 2 * HD), jnp.float32)
            for score, at in zip(scores, tiles):
                mixed = mixed + dot(jnp.exp2(score - top).astype(jnp.bfloat16), values[i, at])
            o_ref[rows, columns] = divided(mixed, jnp.where(i == 0, lives[0], lives[1]))
            return carry

        lax.fori_loop(0, 2 * GROUP, one, 0)


def prompt_heads(base, n, low, high, flags, query, blocks, done):
    tok = query.shape[0]

    wide = pl.BlockSpec((tok, GROUP * HD), lambda j: (0, base + low + j))
    mine, a, b, c, d = blocks
    operands = [flags, query, mine, a, c, d, b, b]
    specs = [VMEM, wide] + [VMEM] * 4
    specs += [pl.BlockSpec((2, HD, PAGE), lambda j, x=x: (0, x + low + j, 0)) for x in (0, n)]
    aliases = {}
    if done is not None:
        aliases = {len(operands): 0}
        operands.append(done)
        specs.append(pl.BlockSpec(memory_space=pl.ANY))
    return pl.pallas_call(
        functools.partial(prompt_kernel, n, low),
        out_shape=jax.ShapeDtypeStruct(query.shape, jnp.bfloat16),
        grid=(high - low,),
        in_specs=specs,
        out_specs=wide,
        scratch_shapes=[
            pltpu.VMEM((2, HD, MAXP * PAGE), jnp.bfloat16),
            pltpu.VMEM((2, MAXP * PAGE, 2 * HD), jnp.bfloat16),
            pltpu.VMEM((PAGE, PAGE), jnp.float32),
            pltpu.VMEM((ROWS, MAXP * PAGE), jnp.bfloat16),
            pltpu.VMEM((ROWS, MAXP * PAGE), jnp.bfloat16),
        ],
        input_output_aliases=aliases,
        name="prompt_attention",
        compiler_params=pltpu.CompilerParams(vmem_limit_bytes=48 << 20),
        cost_estimate=pl.CostEstimate(
            flops=(high - low) * GROUP * tok * MAXP * PAGE * HD * 8,
            bytes_accessed=4 * (high - low) * tok * GROUP * HD,
            transcendentals=0,
        ),
    )(*operands)


def stat_rows(rows):
    return 16 - rows % 16


def choose_kernel(facts, q_ref, o_ref, rows_ref, turned):
    requests, here = q_ref.shape[1], q_ref.shape[2] // HD
    other = 1 - lax.axis_index("section")
    for s in range(STEPS):
        query = q_ref[s].astype(jnp.float32)
        for r in range(requests):
            for h in range(here):
                row = h * STEPS + s
                turned[r, row:row + 1] = query[r:r + 1, h * HD:(h + 1) * HD]
    rows_ref[...] = turned[...].astype(jnp.bfloat16)

    def one(lane, carry):
        for i in range(2):
            owner = page_facts(facts, other, 2 * lane + i)[0]
            o_ref[lane, i] = turned[owner].astype(jnp.bfloat16)
        return carry

    lax.fori_loop(0, o_ref.shape[0], one, 0)


def chosen_queries(facts, query, lanes):
    rows = (query.shape[1], QH // lanes * STEPS, HD)
    return pl.pallas_call(
        choose_kernel,
        out_shape=(
            jax.ShapeDtypeStruct((lanes, 2, *rows[1:]), jnp.bfloat16),
            jax.ShapeDtypeStruct(rows, jnp.bfloat16),
        ),
        in_specs=[SMEM, VMEM],
        out_specs=(VMEM, VMEM),
        scratch_shapes=[pltpu.VMEM(rows, jnp.float32)],
        name="choose_queries",
        **params(12),
    )(facts, query)


def partial_kernel(lanes, facts, q_ref, *rest):
    *packed, o_ref = rest
    split = GROUP // (QH // lanes)
    width = QH // lanes * STEPS
    extra = stat_rows(2 * width)
    half, place = lax.axis_index("section"), lax.axis_index("tp")
    group = GROUP * STEPS
    height = 2 * KVH * group
    lane = lax.broadcasted_iota(jnp.int32, (height, PAGE), 1)
    later = lax.broadcasted_iota(jnp.int32, (height, PAGE), 0) // group % 2 == 1
    spot = lax.broadcasted_iota(jnp.int32, (2 * width, PAGE), 0)
    across = lax.broadcasted_iota(jnp.int32, (2 * width, PAGE), 1)
    line = lax.broadcasted_iota(jnp.int32, (extra, PAGE), 0)
    lives = [page_facts(facts, half, 2 * place + i)[2] for i in range(2)]
    places = [(block, j, n) for block, n in zip(packed, CHUNKS) for j in range(n)]
    scores, values = [], []
    for k, (block, j, n) in enumerate(places):
        for i in range(2):
            query = jnp.concatenate([q_ref[k * split + t, i] for t in range(split)], axis=0)
            scores.append(dot(query, block[i, j * HD:(j + 1) * HD]))
            values.append(block[i, (n + j) * HD:(n + j + 1) * HD])
    score = jnp.concatenate(scores, axis=0) * SCALE
    score = jnp.where(lane < jnp.where(later, lives[1], lives[0]), score, LOW)
    top = jnp.max(score, axis=1, keepdims=True)
    terms = jnp.exp(score - top)
    total = jnp.sum(terms, axis=1, keepdims=True)
    high = terms.astype(jnp.bfloat16)
    low = (terms - high.astype(jnp.float32)).astype(jnp.bfloat16)
    mixed = jnp.concatenate(
        [
            dot(high[m * group:(m + 1) * group], v) + dot(low[m * group:(m + 1) * group], v)
            for m, v in enumerate(values)
        ],
        axis=0,
    ) / total
    sums = top + jnp.log(total)
    for k in range(KVH):
        for t in range(split):
            begins = [(2 * k + i) * group + t * width for i in range(2)]
            both = jnp.concatenate([sums[at:at + width] for at in begins], axis=0)
            turned = jnp.sum(jnp.where(spot == across, both, 0.0), axis=0, keepdims=True)
            first = turned.astype(jnp.bfloat16).astype(jnp.float32)
            rest = turned - first
            second = rest.astype(jnp.bfloat16).astype(jnp.float32)
            stat = jnp.where(line == 0, first, jnp.where(line == 1, second, rest - second))
            stat = jnp.where(line < 3, stat, 0.0)
            block = jnp.concatenate([mixed[at:at + width] for at in begins] + [stat], axis=0)
            o_ref[k * split + t] = block.astype(jnp.bfloat16)


def partial_decode(facts, query, packed, lanes):
    rows = 2 * (QH // lanes) * STEPS
    return pl.pallas_call(
        functools.partial(partial_kernel, lanes),
        out_shape=jax.ShapeDtypeStruct((lanes, rows + stat_rows(rows), HD), jnp.bfloat16),
        in_specs=[SMEM, VMEM] + [VMEM] * len(packed),
        out_specs=VMEM,
        name="partial_decode",
        **params(12),
    )(facts, query, *packed)


def merge_kernel(lanes, facts, parts_ref, q_ref, k_ref, v_ref, o_ref):
    requests = q_ref.shape[0]
    width = (QH // lanes) * STEPS
    other, place = 1 - lax.axis_index("section"), lax.axis_index("tp")
    head = place * (QH // lanes) // GROUP
    spot = lax.broadcasted_iota(jnp.int32, (width, PAGE), 0)
    across = lax.broadcasted_iota(jnp.int32, (width, PAGE), 1)
    step = lax.broadcasted_iota(jnp.int32, (width, 1), 0) % STEPS
    end = 0
    for r in range(requests):
        start, end = end, end + facts[other, r]
        query = q_ref[r].astype(jnp.float32)
        keys = k_ref[r, head].astype(jnp.float32)
        values = v_ref[r, head].astype(jnp.float32)
        tops, vectors = [], []
        for u in range(STEPS):
            score = jnp.sum(query * keys[u:u + 1], axis=1, keepdims=True) * SCALE
            tops.append(jnp.where(u <= step, score, LOW))
            vectors.append(values[u:u + 1])
        for j in range(MAXP):
            page = jnp.minimum(start + j, 2 * lanes - 1)
            block = parts_ref[page // 2].astype(jnp.float32)
            later = jnp.full((width, HD), page % 2 == 1)
            vectors.append(jnp.where(later, block[width:2 * width], block[:width]))
            stat = jnp.sum(block[2 * width:2 * width + 8], axis=0, keepdims=True)
            stat = jnp.sum(
                jnp.where(across - page % 2 * width == spot, stat, 0.0), axis=1, keepdims=True
            )
            tops.append(jnp.where(jnp.full((width, 1), start + j < end), stat, LOW))
        top = functools.reduce(jnp.maximum, tops)
        weights = [jnp.exp(t - top) for t in tops]
        total = functools.reduce(jnp.add, weights)
        mixed = functools.reduce(jnp.add, [w * x for w, x in zip(weights, vectors)])
        o_ref[r] = (mixed / total).astype(jnp.bfloat16)


def merged(facts, parts, query, new_key, new_value, lanes):
    requests = query.shape[0]
    fresh = [
        jnp.transpose(x.reshape(STEPS, requests, KVH, HD), (1, 2, 0, 3)) for x in (new_key, new_value)
    ]
    out = pl.pallas_call(
        functools.partial(merge_kernel, lanes),
        out_shape=jax.ShapeDtypeStruct(query.shape, jnp.bfloat16),
        in_specs=[SMEM, VMEM, VMEM, VMEM, VMEM],
        out_specs=VMEM,
        name="merge_decode",
        **params(12),
    )(facts, parts, query, *fresh)
    out = jnp.transpose(out.reshape(requests, QH // lanes, STEPS, HD), (2, 0, 1, 3))
    return out.reshape(STEPS, requests, QH // lanes * HD)


def other_half(x):
    return lax.ppermute(x, "section", [(0, 1), (1, 0)])


def after(x, *earlier):
    return lax.optimization_barrier((x, *earlier))[0]


def on_device(
    prefill_query, prefill_key, prefill_value, counts, fills, dec_query, dec_key, dec_value
):
    lanes = lax.axis_size("tp")
    query, key, value = prefill_query[0], prefill_key[0], prefill_value[0]
    facts = jnp.concatenate([counts, fills], axis=1)
    flags = page_flags(facts)
    ahead = [(i, i + 2) for i in range(lanes - 2)]
    ahead_again = [(i, i + 2) for i in range(2, lanes - 2)]
    beside = [(i, i + 1) for i in range(0, lanes, 2)]
    trade = [(i, i ^ 1) for i in range(2, lanes)]
    bases = [sum(CHUNKS[:g]) for g in range(len(CHUNKS))]
    mine = []
    for base, n in zip(bases, CHUNKS):
        mine.append(pack(base, n, after(key, *mine), value))

    first_hops = [lax.ppermute(block, "tp", ahead) for block in mine]

    asked = after(dec_query[0], mine[0])
    chosen, dec_rows = chosen_queries(facts, asked, lanes)
    wanted = lax.all_to_all(chosen, "tp", split_axis=0, concat_axis=0, tiled=True)
    b = lax.ppermute(mine[0], "tp", beside)
    parts = after(partial_decode(facts, other_half(wanted), mine, lanes), b)
    parts = lax.all_to_all(parts, "tp", split_axis=0, concat_axis=0, tiled=True)
    dec_out = merged(facts, other_half(parts), dec_rows, dec_key[0], dec_value[0], lanes)

    received = []
    for g, (block, a) in enumerate(zip(mine, first_hops)):
        if g:
            b = lax.ppermute(after(block, received[0][2]), "tp", beside)
        c = lax.ppermute(after(a, parts) if g else after(a, wanted, b, mine[1]), "tp", trade)
        d = lax.ppermute(jnp.concatenate([a[1:], c], axis=0), "tp", ahead_again)
        received.append((a, b, c, d))
    out, flags = None, after(flags, received[1][2])
    for g, (base, n) in enumerate(zip(bases, CHUNKS)):
        if g:
            out = after(out, dec_out)
        out = prompt_heads(base, n, 0, n, flags, query, (mine[g], *received[g]), out)
    return (out[None], dec_out[None])


def solution(mesh):
    placed = (
        P("section", ("groups", "tp"), None),
        P("section", ("groups", "tp"), None),
        P("section", ("groups", "tp"), None),
        P(None, "groups"),
        P(None, "groups"),
        P("section", None, "groups", "tp"),
        P("section", None, "groups", None),
        P("section", None, "groups", None),
    )
    return jax.shard_map(
        on_device,
        mesh=mesh,
        in_specs=placed,
        out_specs=(P("section", ("groups", "tp"), None), P("section", None, "groups", "tp")),
        check_vma=False,
    )
```
